32 devices in a mesh: groups: 2 (over y), seg: 4 (over z), slab: 2 (over x), comp: 2 (over core).
Axes of the slice: x: 2, y: 2, z: 4, core: 2. Of those that a mesh axis runs over, the one named last changes fastest.
Arguments:
- base: float32 [8, 3, 64, 4096], P(('groups', 'seg'), None, 'slab'), parts along dimension 0, may hold values from -6 to 6
- state: float32 [8, 2, 3, 64, 4096], P(('groups', 'seg'), 'comp', None, 'slab'), parts along dimension 0, may hold values from -6 to 6
- wavenumber: int32 [2], P('groups'), parts along dimension 0, may hold values from 1 to 4
- cutoff: int32 [6], P('groups'), parts along dimension 0, may hold values from 18 to 21, as said below
Outputs:
- base_gap: float32 [8, 3, 64, 4096], P(('groups', 'seg'), None, ('slab', 'comp')), parts along dimension 0
- state_gap: float32 [8, 2, 3, 64, 4096], P(('groups', 'seg'), 'comp', None, 'slab'), parts along dimension 0
The draws below stay inside these ranges and needn't reach their ends.
There are 2 independent parts, one for each index of `groups`. The reference program is written for one: setup_inputs(seed, part) draws one part's arguments, and reference() takes and returns one part's arrays. A program takes and returns all parts, laid end to end along the dimension named above; each array names one. Nothing has to cross between parts.
Inputs may be any that keep to these rules, and one draw needn't show every extreme that they name: `cutoff`: each entry is at most one third of 64, rounded down, and at least that minus three; one entry always equals it.
All inputs are finite; a program needn't handle non-finite values.
Results may differ from the reference program's by a relative error of at most 0.0001.
Values sent between devices are 32-bit elements; how exact they have to be, the bound alone decides.
No kernel may reach another device: no remote copies, remote signals or barrier semaphores. Data moves between devices by JAX's collectives and lax.ppermute only.
A program may use at most 128 MiB of HBM per device.

```python
import jax
import jax.numpy as jnp
from jax import lax

N = 64
SEG = 4


def draw_cutoff(key, part):
    first_key, second_key = jax.random.split(jax.random.fold_in(key, 17))
    offsets = jax.random.randint(first_key, (3,), 0, 4)
    chosen = jax.random.randint(second_key, (), 0, 3)
    offsets = jnp.where(jnp.arange(3) == chosen, 0, offsets)
    return (N // 3 - offsets).astype(jnp.int32)


def levels(stream_key, shape, pieces, least, top_value):
    factor_of, own = 1.0, jax.random.fold_in(stream_key, 6)
    for dim, parts in pieces:
        steps = jnp.exp(jax.random.uniform(jax.random.fold_in(own, dim), (parts,), jnp.float32, least / len(pieces), top_value / len(pieces)))
        factor_of = factor_of * jnp.repeat(steps, shape[dim] // parts).reshape([-1 if axis == dim else 1 for axis in range(len(shape))])
    return factor_of


def noise(own_key, dims, width, most, shards=(), kind=jnp.bfloat16):
    result = width * jax.random.normal(own_key, dims, jnp.float32)
    if shards:
        result = result * levels(own_key, dims, shards, -0.22, 0.18)
    return jnp.clip(result, -most, most).astype(kind)


def setup_inputs(seed: int = 0, part: int = 0) -> dict:
    keys = jax.random.split(jax.random.key(seed), 5)
    own_keys = jax.random.split(jax.random.fold_in(keys[4], part), 5)
    base = noise(own_keys[0], (SEG, 3, N, N * N), 1.0, 6.0, ((0, 4), (2, 2)), jnp.float32)
    state = noise(own_keys[1], (SEG, 2, 3, N, N * N), 1.0, 6.0, ((0, 4), (1, 2), (3, 2)), jnp.float32)
    wavenumber = jax.random.randint(own_keys[2], (1,), 1, 5).astype(jnp.int32)
    cutoff = draw_cutoff(jax.random.fold_in(jax.random.fold_in(keys[4], part), 71), part)
    return dict(base=base, state=state, wavenumber=wavenumber, cutoff=cutoff)


viscosity = 0.025
time_step = 0.02
forcing_amp = 10.0


def wavenumbers(grid_points):
    position = jnp.arange(grid_points, dtype=jnp.int32)
    return jnp.where(position < grid_points // 2, position, position - grid_points)


def transform(field):
    return jnp.fft.fftn(field, axes=(-3, -2, -1))


def restore(modes):
    return jnp.real(jnp.fft.ifftn(modes, axes=(-3, -2, -1)))


def reference(base, state, wavenumber, cutoff):
    base = base.reshape(SEG, 3, N, N, N)
    state = state.reshape(SEG, 2, 3, N, N, N)
    spectrum = wavenumbers(N)
    wave_x = jnp.broadcast_to(spectrum[:, None, None], (N, N, N))
    wave_y = jnp.broadcast_to(spectrum[None, :, None], (N, N, N))
    wave_z = jnp.broadcast_to(spectrum[None, None, :], (N, N, N))
    inside = (jnp.abs(wave_x) <= cutoff[0]) & (jnp.abs(wave_y) <= cutoff[1]) & (jnp.abs(wave_z) <= cutoff[2])
    keep_mask = inside.astype(jnp.float32)
    float_x = wave_x.astype(jnp.float32)
    float_y = wave_y.astype(jnp.float32)
    float_z = wave_z.astype(jnp.float32)
    waves_stack = jnp.stack([float_x, float_y, float_z])
    ksquare = float_x * float_x + float_y * float_y + float_z * float_z
    safe_square = jnp.where(ksquare > 0, ksquare, jnp.ones_like(ksquare))
    damping = 1.0 / (1.0 + viscosity * time_step * ksquare)

    def project(field):
        divergence = (float_x * field[0] + float_y * field[1] + float_z * field[2]) / safe_square
        return jnp.stack([field[0] - float_x * divergence, field[1] - float_y * divergence, field[2] - float_z * divergence])

    grid_index = jnp.arange(N, dtype=jnp.int32)
    phase = jnp.mod(wavenumber[0] * grid_index, N).astype(jnp.float32) * (2.0 * jnp.pi / N)
    forcing = jnp.broadcast_to(forcing_amp * jnp.sin(phase)[None, :, None], (N, N, N))

    def advance(segment):
        flow, paired = segment
        flow_hat = transform(flow) * keep_mask
        gradient = restore(1j * waves_stack[None, :] * flow_hat[:, None])
        base_drive = jnp.sum(gradient * flow[None, :], axis=1)
        base_drive = jnp.concatenate([base_drive[:1] - forcing[None], base_drive[1:]], axis=0)
        flow_new = restore(damping * project(flow_hat - time_step * keep_mask * transform(base_drive)))
        results = []
        for branch, orient in ((0, 1.0), (1, -1.0)):
            field = paired[branch]
            field_hat = transform(field) * keep_mask
            flux_hat = transform(field[:, None] * flow[None, :])
            divergence = jnp.sum(1j * waves_stack[None, :] * flux_hat, axis=1)
            if branch == 0:
                matrix = gradient
            else:
                matrix = jnp.swapaxes(gradient, 0, 1)
            coupling = jnp.sum(matrix * field[None, :], axis=1)
            state_drive = keep_mask * (orient * divergence + transform(coupling))
            results.append(restore(damping * project(field_hat - time_step * state_drive)))
        return flow_new, jnp.stack(results)

    flow_next, state_next = lax.map(advance, (base, state))
    base_gap = flow_next - jnp.roll(base, -1, axis=0)
    tangent_gap = state_next[:, 0] - jnp.roll(state[:, 0], -1, axis=0)
    adjoint_gap = state_next[:, 1] - jnp.roll(state[:, 1], 1, axis=0)
    state_gap = jnp.stack([tangent_gap, adjoint_gap], axis=1)
    return base_gap.reshape(SEG, 3, N, N * N).astype(jnp.float32), state_gap.reshape(SEG, 2, 3, N, N * N).astype(jnp.float32)
```

```python
import functools

import jax
import jax.numpy as jnp
import ml_dtypes
import numpy as np
from jax import lax
from jax.experimental import pallas as pl
from jax.experimental.pallas import tpu as pltpu
from jax.sharding import PartitionSpec as P

N = 64
HALF = 32
KEEP = N // 3
NKZ = KEEP + 1
NKY = 44
ROWS = 2 * NKY
PACKED = NKZ + 3
LANES = 128

viscosity = 0.025
time_step = 0.02
forcing_amp = 10.0

f32 = jnp.float32
bf16 = jnp.bfloat16


highest = lax.Precision.HIGHEST


def swapped(value, axis, apart):
    mask = 2**apart
    pairs = [(source, source ^ mask) for source in range(lax.axis_size(axis))]
    return lax.ppermute(value, axis, pairs)


def shifted(block, axis, distance):
    devices = range(lax.axis_size(axis))
    route = [((i - distance) % len(devices), i) for i in devices]
    return lax.ppermute(block, axis, route)


def wavenumbers(grid_points):
    position = jnp.arange(grid_points, dtype=jnp.int32)
    return jnp.where(position < grid_points // 2, position, position - grid_points)


def phases(first, second, grid_points):
    product = jnp.mod(first[:, None] * second[None, :], grid_points)
    return product.astype(jnp.float32) * (2.0 * jnp.pi / grid_points)


def combine(partial_value, columns):
    cosine_part = partial_value[0]
    sine_part = partial_value[1]
    real_part = cosine_part[..., :columns] - sine_part[..., columns:]
    imag_part = cosine_part[..., columns:] + sine_part[..., :columns]
    return jnp.concatenate([real_part, imag_part], axis=-1)


def times_unit(values, wave, columns):
    return jnp.concatenate([-wave * values[..., columns:], wave * values[..., :columns]], axis=-1)


def doubled(values):
    return jnp.concatenate([values, values], axis=-1)


def general_body(base, state, wavenumber, cutoff):
    grid_points = N
    base = base.reshape(base.shape[0], 3, base.shape[2], grid_points, grid_points)
    state = state.reshape(
        state.shape[0], state.shape[1], 3, state.shape[3], grid_points, grid_points
    )
    slab_rows = state.shape[3]
    half_rows = slab_rows // 2
    slab_count = lax.axis_size("slab")
    group_count = slab_count * lax.axis_size("comp")
    core_side = lax.axis_index("comp")
    block_number = lax.axis_index(("slab", "comp"))
    base_whole = base[0]
    base_half = lax.dynamic_slice_in_dim(base_whole, core_side * half_rows, half_rows, 1)
    own_state = state[0, 0]
    spectrum = wavenumbers(grid_points)
    one_third = grid_points // 3
    row_total = (2 * one_third + group_count) // group_count * group_count
    row_index = jnp.arange(row_total, dtype=jnp.int32)
    row_alive_mask = row_index <= 2 * one_third
    row_wave = jnp.where(row_index <= one_third, row_index, row_index - (2 * one_third + 1))
    row_wave = jnp.where(row_alive_mask, row_wave, 0)
    width = grid_points // 2
    rows_per_block = row_total // group_count
    alive_flags = row_alive_mask.astype(jnp.float32)
    grid_index = jnp.arange(grid_points, dtype=jnp.int32)
    column_index = grid_index[:width]
    angle_grid = phases(grid_index, grid_index, grid_points)
    angle_ahead = phases(grid_index, column_index, grid_points)
    angle_behind = phases(column_index, grid_index, grid_points)
    column_weight = jnp.where(column_index == 0, 1.0, 2.0).astype(jnp.float32)[:, None]
    forward_z = jnp.concatenate([jnp.cos(angle_ahead), -jnp.sin(angle_ahead)], axis=1)
    inverse_z = (
        jnp.concatenate(
            [jnp.cos(angle_behind) * column_weight, -jnp.sin(angle_behind) * column_weight], axis=0
        )
        / grid_points
    )
    phase_angle_rows = phases(row_wave, grid_index, grid_points)
    forward_transform_y = (
        jnp.stack([jnp.cos(phase_angle_rows), -jnp.sin(phase_angle_rows)])
        * alive_flags[None, :, None]
    )
    inverse_y = (
        jnp.stack([jnp.cos(phase_angle_rows).T, jnp.sin(phase_angle_rows).T])
        * alive_flags[None, None, :]
        / grid_points
    )
    forward_x = jnp.stack([jnp.cos(angle_grid), -jnp.sin(angle_grid)])
    inverse_x = jnp.stack([jnp.cos(angle_grid), jnp.sin(angle_grid)]) / grid_points
    table_ahead = forward_x.reshape(2, grid_points, slab_count, slab_rows)
    table_back = inverse_x.reshape(2, slab_count, slab_rows, grid_points)
    local_wave = lax.dynamic_slice_in_dim(row_wave, block_number * rows_per_block, rows_per_block)
    local_alive_mask = lax.dynamic_slice_in_dim(
        alive_flags, block_number * rows_per_block, rows_per_block
    )
    shape_local = (grid_points, rows_per_block, width)
    wave_x = jnp.broadcast_to(spectrum[:, None, None], shape_local)
    wave_y = jnp.broadcast_to(local_wave[None, :, None], shape_local)
    wave_z = jnp.broadcast_to(spectrum[:width][None, None, :], shape_local)
    inside = (
        (jnp.abs(wave_x) <= cutoff[0])
        & (jnp.abs(wave_y) <= cutoff[1])
        & (jnp.abs(wave_z) <= cutoff[2])
    )
    keep_mask = doubled(inside.astype(jnp.float32) * local_alive_mask[None, :, None])
    float_x = wave_x.astype(jnp.float32)
    float_y = wave_y.astype(jnp.float32)
    float_z = wave_z.astype(jnp.float32)
    ksquare = float_x * float_x + float_y * float_y + float_z * float_z
    safe_square = doubled(jnp.where(ksquare > 0, ksquare, jnp.ones_like(ksquare)))
    damping = doubled(1.0 / (1.0 + viscosity * time_step * ksquare))
    double_x = doubled(float_x)
    double_y = doubled(float_y)
    double_z = doubled(float_z)

    def project(field):
        divergence = (double_x * field[0] + double_y * field[1] + double_z * field[2]) / safe_square
        return jnp.stack(
            [
                field[0] - double_x * divergence,
                field[1] - double_y * divergence,
                field[2] - double_z * divergence,
            ]
        )

    def yz_forward(field):
        along_z = jnp.einsum("...z,zk->...k", field, forward_z, precision=highest)
        partial_value = jnp.einsum(
            "sry,...yk->s...rk", forward_transform_y, along_z, precision=highest
        )
        return combine(partial_value, width)

    def yz_inverse(modes):
        partial_value = jnp.einsum("syr,...rk->s...yk", inverse_y, modes, precision=highest)
        return jnp.einsum(
            "...k,kz->...z", combine(partial_value, width), inverse_z, precision=highest
        )

    def spectral(state_fields, base_fields):
        state_modes = yz_forward(state_fields)[:, :, None]
        base_modes = yz_forward(base_fields)[:, :, None]
        state_got = lax.all_to_all(
            state_modes, ("slab", "comp"), split_axis=4, concat_axis=2, tiled=True
        )
        base_got = lax.all_to_all(
            base_modes, ("slab", "comp"), split_axis=4, concat_axis=2, tiled=True
        )
        item_count = state_got.shape[0]
        part_count = state_got.shape[1]
        state_split = state_got.reshape(
            item_count, part_count, slab_count, 2, slab_rows, rows_per_block, 2 * width
        )
        state_partial = jnp.einsum(
            "srpx,ijpcxyk->sijcryk", table_ahead, state_split, precision=highest
        )
        base_lined = base_got.reshape(item_count, 1, grid_points, rows_per_block, 2 * width)
        base_partial = jnp.einsum("srx,ijxyk->sijryk", forward_x, base_lined, precision=highest)
        return (combine(state_partial, width), combine(base_partial, width))

    state_first, base_first = spectral(own_state[:, None], base_half[:, None])
    state_hat = state_first[:, 0] * keep_mask
    base_hat = base_first[:, 0] * keep_mask
    grad_hat = jnp.stack(
        [
            times_unit(base_hat, float_x, width),
            times_unit(base_hat, float_y, width),
            times_unit(base_hat, float_z, width),
        ],
        axis=1,
    )
    grad_hat = grad_hat.reshape(9, grid_points, rows_per_block, 2 * width)
    grad_partial = jnp.einsum("sxr,iryk->sixyk", inverse_x, grad_hat, precision=highest)
    grad_spread = combine(grad_partial, width).reshape(
        9, group_count, half_rows, rows_per_block, 2 * width
    )
    own_rows = yz_inverse(
        lax.all_to_all(grad_spread, ("slab", "comp"), split_axis=1, concat_axis=3, tiled=True)[:, 0]
    )
    other_rows = swapped(own_rows, "comp", 0)
    gradient = jnp.where(
        core_side == 0,
        jnp.concatenate([own_rows, other_rows], axis=1),
        jnp.concatenate([other_rows, own_rows], axis=1),
    )
    gradient = gradient.reshape(3, 3, slab_rows, grid_points, grid_points)
    gradient_half = lax.dynamic_slice_in_dim(gradient, core_side * half_rows, half_rows, 2)
    flux_terms = own_state[:, None] * base_whole[None, :]
    coupling_matrix = jnp.where(core_side == 0, gradient, jnp.swapaxes(gradient, 0, 1))
    coupling = jnp.sum(coupling_matrix * own_state[None, :], axis=1)
    forcing_phase = phases(wavenumber, grid_index, grid_points)[0]
    forcing = forcing_amp * jnp.sin(forcing_phase)[None, :, None]
    base_drive = jnp.sum(gradient_half * base_half[None, :], axis=1)
    base_drive = jnp.concatenate([base_drive[:1] - forcing[None], base_drive[1:]], axis=0)
    state_fields = jnp.concatenate([flux_terms, coupling[:, None]], axis=1)
    drive_modes, base_modes_two = spectral(state_fields, base_drive[:, None])
    orient = jnp.array([1.0, -1.0], dtype=jnp.float32)[None, :, None, None, None]
    divergence = (
        times_unit(drive_modes[:, 0], float_x, width)
        + times_unit(drive_modes[:, 1], float_y, width)
        + times_unit(drive_modes[:, 2], float_z, width)
    )
    state_drive = keep_mask * (orient * divergence + drive_modes[:, 3])
    new_hat = damping * project(state_hat - time_step * state_drive)
    base_new_hat = damping * project(base_hat - time_step * keep_mask * base_modes_two[:, 0])
    state_partial = jnp.einsum("spxr,icryk->sipcxyk", table_back, new_hat, precision=highest)
    state_back = combine(state_partial, width).reshape(
        3, group_count, slab_rows, rows_per_block, 2 * width
    )
    base_partial = jnp.einsum("sxr,iryk->sixyk", inverse_x, base_new_hat, precision=highest)
    base_back = combine(base_partial, width).reshape(
        3, group_count, half_rows, rows_per_block, 2 * width
    )
    state_got = lax.all_to_all(
        state_back, ("slab", "comp"), split_axis=1, concat_axis=3, tiled=True
    )
    base_got = lax.all_to_all(base_back, ("slab", "comp"), split_axis=1, concat_axis=3, tiled=True)
    state_new = yz_inverse(state_got[:, 0])
    base_new = yz_inverse(base_got[:, 0])
    base_later, later_state = shifted((base_half, own_state), "seg", -1)
    prior_state = shifted(own_state, "seg", 1)
    neighbour = jnp.where(core_side == 0, later_state, prior_state)
    base_gap = (base_new - base_later).reshape(1, 3, half_rows, grid_points * grid_points)
    state_gap = (state_new - neighbour).reshape(1, 1, 3, slab_rows, grid_points * grid_points)
    return (base_gap, state_gap)


def halves(table):
    high = table.astype(np.float32).astype(ml_dtypes.bfloat16)
    low = (table - high.astype(np.float64)).astype(ml_dtypes.bfloat16)
    return high, low


def left_table(table, depth):
    padded = np.zeros((table.shape[0], depth))
    padded[:, : table.shape[1]] = table
    high, low = halves(padded)
    return np.concatenate(
        [np.concatenate([high, high], 1), np.concatenate([low, np.zeros_like(low)], 1)], 0
    )


def right_table(table, depth):
    return np.ascontiguousarray(left_table(table.T, depth).T)


def ky_values():
    index = np.arange(NKY)
    wave = np.where(index <= KEEP, index, index - (2 * KEEP + 1))
    alive = (index <= 2 * KEEP).astype(np.float64)
    return wave * alive, alive


@functools.cache
def tables():
    out = {}
    z = np.arange(N)
    kz = np.arange(NKZ)
    angle = 2 * np.pi * kz[:, None] * z[None, :] / N
    weight = np.where(kz == 0, 1.0, 2.0)[:, None] / N
    forward = np.zeros((2, 2, NKZ, 2, N))
    inverse = np.zeros((NKZ, 2, 2, 2, N))
    turned = np.zeros((NKZ, 2, 2, 2, N))
    slope = np.zeros((NKZ, 2, 2, 2, N))
    for y2 in range(2):
        forward[y2, 0, :, y2] = np.cos(angle)
        forward[y2, 1, :, y2] = -np.sin(angle)
        inverse[:, y2, 0, y2] = weight * np.cos(angle)
        inverse[:, y2, 1, y2] = -weight * np.sin(angle)
        turned[:, y2, 0, y2] = weight * np.sin(angle)
        turned[:, y2, 1, y2] = weight * np.cos(angle)
        slope[:, y2, 0, y2] = -weight * kz[:, None] * np.sin(angle)
        slope[:, y2, 1, y2] = -weight * kz[:, None] * np.cos(angle)
    out["fz"] = left_table(forward.reshape(4 * NKZ, 2 * N), 128)
    out["iz"] = right_table(inverse.reshape(4 * NKZ, 2 * N), 128)
    out["izr"] = right_table(turned.reshape(4 * NKZ, 2 * N), 128)
    out["izd"] = right_table(slope.reshape(4 * NKZ, 2 * N), 128)
    ky, alive = ky_values()
    y = 2 * np.arange(HALF)[None, :] + np.arange(2)[:, None]
    phase = 2 * np.pi * ky[:, None, None] * y[None] / N
    cosine = np.cos(phase) * alive[:, None, None]
    sine = np.sin(phase) * alive[:, None, None]
    plain = np.zeros((2, NKY, 2, 2, HALF))
    plain[0, :, :, 0] = cosine
    plain[0, :, :, 1] = sine
    plain[1, :, :, 0] = -sine
    plain[1, :, :, 1] = cosine
    rotated = np.stack([-plain[1], plain[0]])
    out["fy"] = left_table(plain.reshape(ROWS, 128), 128)
    out["fyr"] = left_table(rotated.reshape(ROWS, 128), 128)
    back = np.zeros((2, 2, HALF, 2, NKY))
    cos_t = np.moveaxis(cosine, 0, -1) / N
    sin_t = np.moveaxis(sine, 0, -1) / N
    back[:, 0, :, 0] = cos_t
    back[:, 0, :, 1] = -sin_t
    back[:, 1, :, 0] = sin_t
    back[:, 1, :, 1] = cos_t
    back_slope = np.zeros_like(back)
    back_slope[..., 0, :] = ky * back[..., 1, :]
    back_slope[..., 1, :] = -ky * back[..., 0, :]
    out["iy"] = left_table(back.reshape(128, ROWS), 128)
    out["iyd"] = left_table(back_slope.reshape(128, ROWS), 128)
    grad_high, grad_low = [], []
    x = np.arange(N)
    apart = x[:HALF, None] - x[None, :]
    for cut in range(KEEP - 3, KEEP + 1):
        k = np.arange(cut + 1)
        wk = np.where(k == 0, 1.0, 2.0) / N
        arg = 2 * np.pi * apart[..., None] * k / N
        keep = (np.cos(arg) * wk).sum(-1)
        derive = (-np.sin(arg) * wk * k).sum(-1)
        table = np.zeros((2, 4, HALF, 2, 4, HALF))
        for comp in range(3):
            for side in range(2):
                rows = slice(side * HALF, (side + 1) * HALF)
                table[side, comp, :, 0, comp, :] = keep[:, rows].T
                table[side, comp, :, 1, comp, :] = derive[:, rows].T
        high, low = halves(table.reshape(256, 256))
        grad_high.append(high)
        grad_low.append(low)
    out["gxh"] = np.stack(grad_high)
    out["gxl"] = np.stack(grad_low)
    kx = np.arange(HALF)
    live = (kx <= KEEP).astype(np.float64)
    xl = np.arange(HALF)
    arg = 2 * np.pi * xl[:, None] * kx[None, :] / N
    value = np.concatenate([np.cos(arg) * live, np.sin(arg) * live], 1)
    change = np.concatenate([kx * np.sin(arg) * live, -kx * np.cos(arg) * live], 1)

    def d_of(block):
        return np.concatenate([kx * block[:, HALF:], -kx * block[:, :HALF]], 1)

    fx = np.zeros((4, 4, HALF, 4, 2, 2 * HALF))

    def put(tile, block, quantity, part, what):
        fx[tile, block, :, quantity, part] += what
        if quantity == 0:
            fx[tile, block, :, 1, part] += -d_of(what)

    put(0, 0, 2, 0, change)
    put(0, 1, 3, 0, change)
    put(0, 2, 0, 0, value)
    put(0, 3, 0, 0, value)
    put(1, 0, 2, 0, value)
    put(1, 1, 3, 0, value)
    put(1, 2, 2, 1, value)
    put(1, 3, 3, 1, value)
    put(2, 0, 0, 0, change)
    put(2, 1, 2, 0, value)
    put(2, 2, 3, 0, value)
    put(2, 3, 0, 0, value)
    put(3, 0, 2, 0, value)
    put(3, 1, 3, 0, value)
    put(3, 2, 0, 1, value)
    out["fxh"], out["fxl"] = halves(fx.reshape(512, 512))
    inv_high, inv_low = [], []
    wx = np.where(kx == 0, 1.0, 2.0) * live / N
    for core in range(2):
        ix = np.zeros((4, 2, 2 * HALF, 3 * LANES))
        for side in range(2):
            xs = np.arange(HALF) + side * HALF
            arg = 2 * np.pi * kx[:, None] * xs[None, :] / N
            give = np.concatenate([np.cos(arg) * wx[:, None], np.sin(arg) * wx[:, None]], 0)
            fall = np.concatenate(
                [np.sin(arg) * (wx * kx)[:, None], -np.cos(arg) * (wx * kx)[:, None]], 0
            )
            own = slice(core * 16, core * 16 + 16)
            at = side * LANES
            ix[0, 0, :, at : at + 32] = give
            ix[1, 0, :, at : at + 32] = fall
            ix[0, 1, :, at + 32 : at + 48] = give[:, own]
            ix[1, 1, :, at + 32 : at + 48] = fall[:, own]
            ix[2, 1, :, at + 48 : at + 64] = give[:, own]
            ix[2, 0, :, at + 64 : at + 96] = give
            ix[3, 0, :, at + 96 : at + 128] = give
            last = 2 * LANES + side * 16
            ix[3, 1, :, last : last + 16] = give[:, own]
        high, low = halves(ix.reshape(512, 3 * LANES))
        inv_high.append(high)
        inv_low.append(low)
    out["ixh"] = np.stack(inv_high)
    out["ixl"] = np.stack(inv_low)
    ky_rows = np.tile(ky, 2)[:, None]
    fixed = np.ones((3, ROWS, 4, HALF))
    by_kz = np.zeros((3, ROWS, 4, HALF))
    fixed[0, :, 2] = -ky_rows
    fixed[0, :, 3] = 0
    by_kz[0, :, 3] = -1
    fixed[1, :, 1] = ky_rows
    fixed[1, :, 2] = ky_rows
    fixed[2, :, 0] = 0
    fixed[2, :, 1] = 0
    by_kz[2, :, 0] = 1
    by_kz[2, :, 1] = 1
    out["fixed"] = fixed.reshape(3, ROWS, LANES).astype(np.float32)
    out["bykz"] = by_kz.reshape(3, ROWS, LANES).astype(np.float32)
    out["kyrow"] = np.broadcast_to(ky_rows, (ROWS, LANES)).astype(np.float32).copy()
    lane_kx = np.tile(kx * live, 4)
    out["kxlane"] = np.broadcast_to(lane_kx, (8, LANES)).astype(np.float32).copy()
    yy = np.arange(N)
    force = [forcing_amp * np.sin(2 * np.pi * ((w * yy) % N) / N) for w in range(1, 5)]
    force = np.repeat(np.stack(force).reshape(4, HALF, 2, 1), N, axis=3)
    out["force"] = force.reshape(4, HALF, LANES).astype(np.float32)
    return out


def split(values):
    high = values.astype(bf16)
    low = (values - high.astype(f32)).astype(bf16)
    return high, low


def dot(a, b):
    return jnp.dot(a, b, preferred_element_type=f32)


def dot_nt(a, b):
    return lax.dot_general(a, b, (((1,), (1,)), ((), ())), preferred_element_type=f32)


def stacked(values):
    high, low = split(values)
    return jnp.concatenate([high, low], 0)


def beside(values):
    high, low = split(values)
    return jnp.concatenate([high, low], 1)


def folded(result):
    rows = result.shape[0] // 2
    return result[:rows] + result[rows:]


def folded_lanes(result):
    return result[:, :LANES] + result[:, LANES:]


def padded(values, rows=128):
    return jnp.concatenate([values, jnp.zeros((rows - values.shape[0], values.shape[1]), f32)], 0)


def triple(values, high_ref, low_ref):
    high, low = split(values)
    return dot(high, high_ref) + dot(low, high_ref) + dot(high, low_ref)


def columns(yh):
    return pl.ds(pl.multiple_of(yh * LANES, LANES), LANES)


def along_y(ref, tile, kz):
    return jnp.concatenate(
        [ref[tile, pl.ds(q * NKZ + kz, HALF, stride=ROWS), :] for q in range(4)], 0
    )


def base_kernel(base_ref, fz_ref, fy_ref, out_ref, lines):
    def z_step(yh, _):
        rows = jnp.concatenate(
            [base_ref[i, :, columns(yh)] for i in range(3)] + [jnp.zeros((HALF, LANES), f32)], 0
        )
        got = folded(dot_nt(fz_ref[...], beside(rows)))
        lines[0, pl.ds(pl.multiple_of(yh * ROWS, 8), ROWS), :] = got
        return 0

    lax.fori_loop(0, HALF, z_step, 0, unroll=2)

    def y_step(kz, _):
        out_ref[kz] = folded(dot(fy_ref[...], stacked(along_y(lines, 0, kz))))
        return 0

    lax.fori_loop(0, NKZ, y_step, 0, unroll=2)


def main_kernel(
    core_ref, cutoff_ref, wave_ref, base_ref, state_ref, here_ref, there_ref,
    gxh_ref, gxl_ref, iy_ref, iyd_ref, iz_ref, izd_ref, fz_ref, fy_ref, fyr_ref,
    fxh_ref, fxl_ref, ixh_ref, ixl_ref, fixed_ref, bykz_ref, kyrow_ref, kxlane_ref, force_ref,
    near_ref, far_ref, planes, lines,
):
    core = core_ref[0]
    cut_x, cut_y, cut_z = cutoff_ref[0], cutoff_ref[1], cutoff_ref[2]
    which = jnp.clip(cut_x - (KEEP - 3), 0, 3)
    ky = kyrow_ref[...]
    keep_y = jnp.where(jnp.abs(ky) <= cut_y.astype(f32), 1.0, 0.0).astype(f32)
    high_x = gxh_ref[which]
    low_x = gxl_ref[which]

    def gradient_step(pair, _):
        kz = pair * 2
        parts = []
        for ref in (here_ref, there_ref):
            both = []
            for k in range(2):
                keep_z = jnp.where(kz + k <= cut_z, 1.0, 0.0).astype(f32)
                both.append(ref[kz + k] * (keep_y * keep_z))
            parts.append(jnp.concatenate(both, 0))
        got = triple(jnp.concatenate(parts, 1), high_x, low_x)
        for k in range(2):
            data = stacked(padded(got[k * ROWS : (k + 1) * ROWS]))
            even = folded(dot(iy_ref[...], data))
            odd = folded(dot(iyd_ref[...], data[:, :LANES]))
            rows = pl.ds(pl.multiple_of((kz + k) * LANES, LANES), LANES)
            planes[0, rows, :] = even[:, LANES:]
            planes[1, rows, :] = odd
            planes[2, rows, :] = even[:, :LANES]
        return 0

    lax.fori_loop(0, NKZ // 2, gradient_step, 0)
    sigma = jnp.where(core == 0, -time_step, time_step).astype(f32)
    force_at = jnp.clip(wave_ref[0] - 1, 0, 3)

    def physical_step(yh, _):
        grads = []
        for d in range(3):
            data = padded(planes[d, pl.ds(yh, ROWS, stride=HALF), :]).T
            table = izd_ref if d == 2 else iz_ref
            got = folded_lanes(dot(beside(data), table[...]))
            grads.append([got[HALF * i : HALF * (i + 1)] for i in range(3)])
        b = [base_ref[i, :, columns(yh)] for i in range(3)]
        s = [state_ref[i, :, columns(yh)] for i in range(3)]
        t = [sigma * v for v in s]
        comb, comb_base = [], []
        for i in range(3):
            coupling = sum(jnp.where(core == 0, grads[j][i], grads[i][j]) * s[j] for j in range(3))
            comb.append(s[i] - time_step * coupling)
            drive = sum(grads[j][i] * b[j] for j in range(3))
            if i == 0:
                drive = drive - force_ref[force_at, pl.ds(yh, 1), :]
            comb_base.append(b[i] - time_step * drive)
        blocks = [
            t[1] * b[0], t[2] * b[0], t[0] * b[1], t[0] * b[2],
            comb[1], comb[2], comb_base[1], comb_base[2],
            t[0] * b[0], t[1] * b[1], t[2] * b[1], comb[0],
            t[1] * b[2], t[2] * b[2], comb_base[0], jnp.zeros((HALF, LANES), f32),
        ]
        got = folded(dot_nt(fz_ref[...], beside(jnp.concatenate(blocks, 0))))
        rows = pl.ds(pl.multiple_of(yh * ROWS, 8), ROWS)
        for tile in range(4):
            lines[tile, rows, :] = got[:, tile * LANES : (tile + 1) * LANES]
        return 0

    lax.fori_loop(0, HALF, physical_step, 0)
    kx = kxlane_ref[0:1, :]
    keep_x = jnp.where(kx <= cut_x.astype(f32), 1.0, 0.0).astype(f32)
    keep_xy = keep_y * keep_x
    square_xy = ky * ky + kx * kx
    lane = lax.broadcasted_iota(jnp.int32, (ROWS, LANES), 1)
    for group in range(3):
        near_ref[NKZ + group] = jnp.zeros((ROWS, LANES), f32)
        far_ref[NKZ + group] = jnp.zeros((ROWS, LANES), f32)

    def spectral_step(pair, _):
        stack = []
        for k in range(2):
            kz = pair * 2 + k
            kzf = kz.astype(f32)
            first = jnp.concatenate([stacked(along_y(lines, t, kz)) for t in (0, 1)], 1)
            second = jnp.concatenate([stacked(along_y(lines, t, kz)) for t in (2, 3)], 1)
            even = folded(dot(fy_ref[...], first))
            odd = folded(dot(fyr_ref[...], second))
            factor = [fixed_ref[n] + kzf * bykz_ref[n] for n in range(3)]
            stack.append(
                jnp.concatenate(
                    [
                        even[:, :LANES] * factor[0],
                        even[:, LANES:],
                        odd[:, :LANES] * factor[1],
                        odd[:, LANES:] * factor[2],
                    ],
                    1,
                )
            )
        modes = triple(jnp.concatenate(stack, 0), fxh_ref[...], fxl_ref[...])
        results = []
        for k in range(2):
            kz = pair * 2 + k
            kzf = kz.astype(f32)
            vx, slope, uy, uz = (
                modes[k * ROWS : (k + 1) * ROWS, n * LANES : (n + 1) * LANES] for n in range(4)
            )
            square = square_xy + kzf * kzf
            keep_z = jnp.where(kz <= cut_z, 1.0, 0.0).astype(f32)
            factor = keep_xy * keep_z / (1.0 + viscosity * time_step * square)
            share = (slope + ky * uy + kzf * uz) / jnp.where(square > 0, square, 1.0)
            results.append(
                jnp.concatenate(
                    [
                        factor * vx,
                        factor * share,
                        factor * (uy - ky * share),
                        factor * (uz - kzf * share),
                    ],
                    1,
                )
            )
        got = triple(jnp.concatenate(results, 0), ixh_ref[core], ixl_ref[core])
        for k in range(2):
            kz = pair * 2 + k
            mine = got[k * ROWS : (k + 1) * ROWS]
            near_ref[kz] = mine[:, :LANES]
            far_ref[kz] = mine[:, LANES : 2 * LANES]
            last = mine[:, 2 * LANES :]
            group = NKZ + kz // 8
            shift = (kz % 8) * 16
            own = pltpu.roll(jnp.where(lane < 16, last, 0.0), shift, 1)
            other = jnp.where((lane >= 16) & (lane < 32), last, 0.0)
            other = pltpu.roll(other, (shift + LANES - 16) % LANES, 1)
            near_ref[group] += own
            far_ref[group] += other
        return 0

    lax.fori_loop(0, NKZ // 2, spectral_step, 0)


def final_kernel(
    near_ref, far_ref, state_ref, base_ref, iy_ref, iz_ref, izr_ref,
    base_out, state_out, planes,
):
    def y_step(kz, _):
        shift = (LANES - (kz % 8) * 16) % LANES
        group = NKZ + kz // 8
        rest = pltpu.roll(near_ref[group] + far_ref[group], shift, 1)
        data = jnp.concatenate([near_ref[kz] + far_ref[kz], rest], 1)
        got = folded(dot(iy_ref[...], stacked(padded(data))))
        rows = pl.ds(pl.multiple_of(kz * LANES, LANES), LANES)
        planes[0, rows, :] = got[:, :LANES]
        planes[1, rows, :] = got[:, LANES:]
        return 0

    lax.fori_loop(0, NKZ, y_step, 0, unroll=2)

    def z_step(yh, _):
        data = padded(planes[0, pl.ds(yh, ROWS, stride=HALF), :]).T
        last = padded(planes[1, pl.ds(yh, ROWS, stride=HALF), :]).T[:16]
        turned = folded_lanes(dot(beside(data[:48]), izr_ref[...]))
        plain = folded_lanes(dot(beside(jnp.concatenate([data[48:], last], 0)), iz_ref[...]))
        at = columns(yh)
        state_out[0, :, at] = turned[:32] - state_ref[0, :, at]
        state_out[1, :, at] = plain[16:48] - state_ref[1, :, at]
        state_out[2, :, at] = plain[48:80] - state_ref[2, :, at]
        base_out[0, :, at] = turned[32:48] - base_ref[0, :, at]
        base_out[1, :, at] = plain[:16] - base_ref[1, :, at]
        base_out[2, :, at] = plain[80:96] - base_ref[2, :, at]
        return 0

    lax.fori_loop(0, HALF, z_step, 0, unroll=2)


interpret = False


def call(kernel, outs, scratch, inputs, flops, in_smem=0):
    whole = pl.BlockSpec(memory_space=pltpu.VMEM)
    small = pl.BlockSpec(memory_space=pltpu.SMEM)
    return pl.pallas_call(
        kernel,
        out_shape=outs,
        in_specs=[small] * in_smem + [whole] * (len(inputs) - in_smem),
        out_specs=jax.tree.map(lambda _: whole, outs),
        scratch_shapes=scratch,
        compiler_params=pltpu.CompilerParams(vmem_limit_bytes=56 * 2**20),
        cost_estimate=pl.CostEstimate(flops=flops, bytes_accessed=4 * 2**20, transcendentals=0),
        interpret=interpret,
    )(*inputs)


def body(base, state, wavenumber, cutoff):
    t = {name: jnp.asarray(value) for name, value in tables().items()}
    core = lax.axis_index("comp")
    seg_count = lax.axis_size("seg")
    own_base = base[0]
    own_state = state[0, 0]
    base_half = lax.dynamic_slice_in_dim(own_base, core * 16, 16, 1)
    back = [((s + 1) % seg_count, s) for s in range(seg_count)]
    around = [(2 * i, 2 * o) for i, o in back] + [(2 * o + 1, 2 * i + 1) for i, o in back]
    base_next = lax.ppermute(base_half, "seg", back)
    state_next = lax.ppermute(own_state, ("seg", "comp"), around)
    sds = jax.ShapeDtypeStruct
    spectrum = call(
        base_kernel,
        sds((NKZ, ROWS, LANES), f32),
        [pltpu.VMEM((1, HALF * ROWS, LANES), f32)],
        [own_base, t["fz"], t["fy"]],
        10**9,
    )
    swap = [(0, 1), (1, 0)]
    there = lax.ppermute(spectrum, "slab", swap)
    names = (
        "gxh", "gxl", "iy", "iyd", "iz", "izd", "fz", "fy", "fyr", "fxh", "fxl", "ixh", "ixl",
        "fixed", "bykz", "kyrow", "kxlane", "force",
    )
    near, far = call(
        main_kernel,
        [sds((PACKED, ROWS, LANES), f32)] * 2,
        [
            pltpu.VMEM((3, NKZ * LANES, LANES), f32),
            pltpu.VMEM((4, HALF * ROWS, LANES), f32),
        ],
        [core.reshape(1), cutoff, wavenumber, own_base, own_state, spectrum, there]
        + [t[name] for name in names],
        10**10,
        in_smem=3,
    )
    far = lax.ppermute(far, "slab", swap)
    base_gap, state_gap = call(
        final_kernel,
        [sds((3, 16, N * N), f32), sds((3, HALF, N * N), f32)],
        [pltpu.VMEM((2, NKZ * LANES, LANES), f32)],
        [near, far, state_next, base_next, t["iy"], t["iz"], t["izr"]],
        10**9,
    )
    return base_gap[None], state_gap[None, None]


def solution(mesh):
    paired = mesh.shape["slab"] == 2 and mesh.shape["comp"] == 2
    return jax.shard_map(
        body if paired else general_body,
        mesh=mesh,
        in_specs=(
            P(("groups", "seg"), None, "slab", None),
            P(("groups", "seg"), "comp", None, "slab", None),
            P("groups"),
            P("groups"),
        ),
        out_specs=(
            P(("groups", "seg"), None, ("slab", "comp"), None),
            P(("groups", "seg"), "comp", None, "slab", None),
        ),
        check_vma=False,
    )
```

```python
import functools

import jax
import jax.numpy as jnp
import ml_dtypes
import numpy as np
from jax import lax
from jax.experimental import pallas as pl
from jax.experimental.pallas import tpu as pltpu
from jax.sharding import PartitionSpec as P

N = 64
HALF = 32
KEEP = N // 3
NKZ = KEEP + 1
NKY = 44
ROWS = 2 * NKY
PACKED = NKZ + 3
HALF_KZ = NKZ // 2
LANES = 128

viscosity = 0.025
time_step = 0.02
forcing_amp = 10.0

f32 = jnp.float32
bf16 = jnp.bfloat16


highest = lax.Precision.HIGHEST


def swapped(value, axis, apart):
    mask = 2**apart
    pairs = [(source, source ^ mask) for source in range(lax.axis_size(axis))]
    return lax.ppermute(value, axis, pairs)


def shifted(block, axis, distance):
    devices = range(lax.axis_size(axis))
    route = [((i - distance) % len(devices), i) for i in devices]
    return lax.ppermute(block, axis, route)


def wavenumbers(grid_points):
    position = jnp.arange(grid_points, dtype=jnp.int32)
    return jnp.where(position < grid_points // 2, position, position - grid_points)


def phases(first, second, grid_points):
    product = jnp.mod(first[:, None] * second[None, :], grid_points)
    return product.astype(jnp.float32) * (2.0 * jnp.pi / grid_points)


def combine(partial_value, columns):
    cosine_part = partial_value[0]
    sine_part = partial_value[1]
    real_part = cosine_part[..., :columns] - sine_part[..., columns:]
    imag_part = cosine_part[..., columns:] + sine_part[..., :columns]
    return jnp.concatenate([real_part, imag_part], axis=-1)


def times_unit(values, wave, columns):
    return jnp.concatenate([-wave * values[..., columns:], wave * values[..., :columns]], axis=-1)


def doubled(values):
    return jnp.concatenate([values, values], axis=-1)


def general_body(base, state, wavenumber, cutoff):
    grid_points = N
    base = base.reshape(base.shape[0], 3, base.shape[2], grid_points, grid_points)
    state = state.reshape(
        state.shape[0], state.shape[1], 3, state.shape[3], grid_points, grid_points
    )
    slab_rows = state.shape[3]
    half_rows = slab_rows // 2
    slab_count = lax.axis_size("slab")
    group_count = slab_count * lax.axis_size("comp")
    core_side = lax.axis_index("comp")
    block_number = lax.axis_index(("slab", "comp"))
    base_whole = base[0]
    base_half = lax.dynamic_slice_in_dim(base_whole, core_side * half_rows, half_rows, 1)
    own_state = state[0, 0]
    spectrum = wavenumbers(grid_points)
    one_third = grid_points // 3
    row_total = (2 * one_third + group_count) // group_count * group_count
    row_index = jnp.arange(row_total, dtype=jnp.int32)
    row_alive_mask = row_index <= 2 * one_third
    row_wave = jnp.where(row_index <= one_third, row_index, row_index - (2 * one_third + 1))
    row_wave = jnp.where(row_alive_mask, row_wave, 0)
    width = grid_points // 2
    rows_per_block = row_total // group_count
    alive_flags = row_alive_mask.astype(jnp.float32)
    grid_index = jnp.arange(grid_points, dtype=jnp.int32)
    column_index = grid_index[:width]
    angle_grid = phases(grid_index, grid_index, grid_points)
    angle_ahead = phases(grid_index, column_index, grid_points)
    angle_behind = phases(column_index, grid_index, grid_points)
    column_weight = jnp.where(column_index == 0, 1.0, 2.0).astype(jnp.float32)[:, None]
    forward_z = jnp.concatenate([jnp.cos(angle_ahead), -jnp.sin(angle_ahead)], axis=1)
    inverse_z = (
        jnp.concatenate(
            [jnp.cos(angle_behind) * column_weight, -jnp.sin(angle_behind) * column_weight], axis=0
        )
        / grid_points
    )
    phase_angle_rows = phases(row_wave, grid_index, grid_points)
    forward_transform_y = (
        jnp.stack([jnp.cos(phase_angle_rows), -jnp.sin(phase_angle_rows)])
        * alive_flags[None, :, None]
    )
    inverse_y = (
        jnp.stack([jnp.cos(phase_angle_rows).T, jnp.sin(phase_angle_rows).T])
        * alive_flags[None, None, :]
        / grid_points
    )
    forward_x = jnp.stack([jnp.cos(angle_grid), -jnp.sin(angle_grid)])
    inverse_x = jnp.stack([jnp.cos(angle_grid), jnp.sin(angle_grid)]) / grid_points
    table_ahead = forward_x.reshape(2, grid_points, slab_count, slab_rows)
    table_back = inverse_x.reshape(2, slab_count, slab_rows, grid_points)
    local_wave = lax.dynamic_slice_in_dim(row_wave, block_number * rows_per_block, rows_per_block)
    local_alive_mask = lax.dynamic_slice_in_dim(
        alive_flags, block_number * rows_per_block, rows_per_block
    )
    shape_local = (grid_points, rows_per_block, width)
    wave_x = jnp.broadcast_to(spectrum[:, None, None], shape_local)
    wave_y = jnp.broadcast_to(local_wave[None, :, None], shape_local)
    wave_z = jnp.broadcast_to(spectrum[:width][None, None, :], shape_local)
    inside = (
        (jnp.abs(wave_x) <= cutoff[0])
        & (jnp.abs(wave_y) <= cutoff[1])
        & (jnp.abs(wave_z) <= cutoff[2])
    )
    keep_mask = doubled(inside.astype(jnp.float32) * local_alive_mask[None, :, None])
    float_x = wave_x.astype(jnp.float32)
    float_y = wave_y.astype(jnp.float32)
    float_z = wave_z.astype(jnp.float32)
    ksquare = float_x * float_x + float_y * float_y + float_z * float_z
    safe_square = doubled(jnp.where(ksquare > 0, ksquare, jnp.ones_like(ksquare)))
    damping = doubled(1.0 / (1.0 + viscosity * time_step * ksquare))
    double_x = doubled(float_x)
    double_y = doubled(float_y)
    double_z = doubled(float_z)

    def project(field):
        divergence = (double_x * field[0] + double_y * field[1] + double_z * field[2]) / safe_square
        return jnp.stack(
            [
                field[0] - double_x * divergence,
                field[1] - double_y * divergence,
                field[2] - double_z * divergence,
            ]
        )

    def yz_forward(field):
        along_z = jnp.einsum("...z,zk->...k", field, forward_z, precision=highest)
        partial_value = jnp.einsum(
            "sry,...yk->s...rk", forward_transform_y, along_z, precision=highest
        )
        return combine(partial_value, width)

    def yz_inverse(modes):
        partial_value = jnp.einsum("syr,...rk->s...yk", inverse_y, modes, precision=highest)
        return jnp.einsum(
            "...k,kz->...z", combine(partial_value, width), inverse_z, precision=highest
        )

    def spectral(state_fields, base_fields):
        state_modes = yz_forward(state_fields)[:, :, None]
        base_modes = yz_forward(base_fields)[:, :, None]
        state_got = lax.all_to_all(
            state_modes, ("slab", "comp"), split_axis=4, concat_axis=2, tiled=True
        )
        base_got = lax.all_to_all(
            base_modes, ("slab", "comp"), split_axis=4, concat_axis=2, tiled=True
        )
        item_count = state_got.shape[0]
        part_count = state_got.shape[1]
        state_split = state_got.reshape(
            item_count, part_count, slab_count, 2, slab_rows, rows_per_block, 2 * width
        )
        state_partial = jnp.einsum(
            "srpx,ijpcxyk->sijcryk", table_ahead, state_split, precision=highest
        )
        base_lined = base_got.reshape(item_count, 1, grid_points, rows_per_block, 2 * width)
        base_partial = jnp.einsum("srx,ijxyk->sijryk", forward_x, base_lined, precision=highest)
        return (combine(state_partial, width), combine(base_partial, width))

    state_first, base_first = spectral(own_state[:, None], base_half[:, None])
    state_hat = state_first[:, 0] * keep_mask
    base_hat = base_first[:, 0] * keep_mask
    grad_hat = jnp.stack(
        [
            times_unit(base_hat, float_x, width),
            times_unit(base_hat, float_y, width),
            times_unit(base_hat, float_z, width),
        ],
        axis=1,
    )
    grad_hat = grad_hat.reshape(9, grid_points, rows_per_block, 2 * width)
    grad_partial = jnp.einsum("sxr,iryk->sixyk", inverse_x, grad_hat, precision=highest)
    grad_spread = combine(grad_partial, width).reshape(
        9, group_count, half_rows, rows_per_block, 2 * width
    )
    own_rows = yz_inverse(
        lax.all_to_all(grad_spread, ("slab", "comp"), split_axis=1, concat_axis=3, tiled=True)[:, 0]
    )
    other_rows = swapped(own_rows, "comp", 0)
    gradient = jnp.where(
        core_side == 0,
        jnp.concatenate([own_rows, other_rows], axis=1),
        jnp.concatenate([other_rows, own_rows], axis=1),
    )
    gradient = gradient.reshape(3, 3, slab_rows, grid_points, grid_points)
    gradient_half = lax.dynamic_slice_in_dim(gradient, core_side * half_rows, half_rows, 2)
    flux_terms = own_state[:, None] * base_whole[None, :]
    coupling_matrix = jnp.where(core_side == 0, gradient, jnp.swapaxes(gradient, 0, 1))
    coupling = jnp.sum(coupling_matrix * own_state[None, :], axis=1)
    forcing_phase = phases(wavenumber, grid_index, grid_points)[0]
    forcing = forcing_amp * jnp.sin(forcing_phase)[None, :, None]
    base_drive = jnp.sum(gradient_half * base_half[None, :], axis=1)
    base_drive = jnp.concatenate([base_drive[:1] - forcing[None], base_drive[1:]], axis=0)
    state_fields = jnp.concatenate([flux_terms, coupling[:, None]], axis=1)
    drive_modes, base_modes_two = spectral(state_fields, base_drive[:, None])
    orient = jnp.array([1.0, -1.0], dtype=jnp.float32)[None, :, None, None, None]
    divergence = (
        times_unit(drive_modes[:, 0], float_x, width)
        + times_unit(drive_modes[:, 1], float_y, width)
        + times_unit(drive_modes[:, 2], float_z, width)
    )
    state_drive = keep_mask * (orient * divergence + drive_modes[:, 3])
    new_hat = damping * project(state_hat - time_step * state_drive)
    base_new_hat = damping * project(base_hat - time_step * keep_mask * base_modes_two[:, 0])
    state_partial = jnp.einsum("spxr,icryk->sipcxyk", table_back, new_hat, precision=highest)
    state_back = combine(state_partial, width).reshape(
        3, group_count, slab_rows, rows_per_block, 2 * width
    )
    base_partial = jnp.einsum("sxr,iryk->sixyk", inverse_x, base_new_hat, precision=highest)
    base_back = combine(base_partial, width).reshape(
        3, group_count, half_rows, rows_per_block, 2 * width
    )
    state_got = lax.all_to_all(
        state_back, ("slab", "comp"), split_axis=1, concat_axis=3, tiled=True
    )
    base_got = lax.all_to_all(base_back, ("slab", "comp"), split_axis=1, concat_axis=3, tiled=True)
    state_new = yz_inverse(state_got[:, 0])
    base_new = yz_inverse(base_got[:, 0])
    base_later, later_state = shifted((base_half, own_state), "seg", -1)
    prior_state = shifted(own_state, "seg", 1)
    neighbour = jnp.where(core_side == 0, later_state, prior_state)
    base_gap = (base_new - base_later).reshape(1, 3, half_rows, grid_points * grid_points)
    state_gap = (state_new - neighbour).reshape(1, 1, 3, slab_rows, grid_points * grid_points)
    return (base_gap, state_gap)


def halves(table):
    high = table.astype(np.float32).astype(ml_dtypes.bfloat16)
    low = (table - high.astype(np.float64)).astype(ml_dtypes.bfloat16)
    return high, low


def left_table(table, depth):
    padded = np.zeros((table.shape[0], depth))
    padded[:, : table.shape[1]] = table
    high, low = halves(padded)
    return np.concatenate(
        [np.concatenate([high, high], 1), np.concatenate([low, np.zeros_like(low)], 1)], 0
    )


def right_table(table, depth):
    return np.ascontiguousarray(left_table(table.T, depth).T)


def ky_values():
    index = np.arange(NKY)
    wave = np.where(index <= KEEP, index, index - (2 * KEEP + 1))
    alive = (index <= 2 * KEEP).astype(np.float64)
    return wave * alive, alive


@functools.cache
def tables():
    out = {}
    z = np.arange(N)
    kz = np.arange(NKZ)
    angle = 2 * np.pi * kz[:, None] * z[None, :] / N
    weight = np.where(kz == 0, 1.0, 2.0)[:, None] / N
    forward = np.zeros((2, 2, NKZ, 2, N))
    inverse = np.zeros((NKZ, 2, 2, 2, N))
    turned = np.zeros((NKZ, 2, 2, 2, N))
    slope = np.zeros((NKZ, 2, 2, 2, N))
    for y2 in range(2):
        forward[y2, 0, :, y2] = np.cos(angle)
        forward[y2, 1, :, y2] = -np.sin(angle)
        inverse[:, y2, 0, y2] = weight * np.cos(angle)
        inverse[:, y2, 1, y2] = -weight * np.sin(angle)
        turned[:, y2, 0, y2] = weight * np.sin(angle)
        turned[:, y2, 1, y2] = weight * np.cos(angle)
        slope[:, y2, 0, y2] = -weight * kz[:, None] * np.sin(angle)
        slope[:, y2, 1, y2] = -weight * kz[:, None] * np.cos(angle)
    out["fz"] = left_table(forward.reshape(4 * NKZ, 2 * N), 128)
    out["iz"] = right_table(inverse.reshape(4 * NKZ, 2 * N), 128)
    out["izr"] = right_table(turned.reshape(4 * NKZ, 2 * N), 128)
    out["izd"] = right_table(slope.reshape(4 * NKZ, 2 * N), 128)
    ky, alive = ky_values()
    y = 2 * np.arange(HALF)[None, :] + np.arange(2)[:, None]
    phase = 2 * np.pi * ky[:, None, None] * y[None] / N
    cosine = np.cos(phase) * alive[:, None, None]
    sine = np.sin(phase) * alive[:, None, None]
    plain = np.zeros((2, NKY, 2, 2, HALF))
    plain[0, :, :, 0] = cosine
    plain[0, :, :, 1] = sine
    plain[1, :, :, 0] = -sine
    plain[1, :, :, 1] = cosine
    rotated = np.stack([-plain[1], plain[0]])
    out["fy"] = left_table(plain.reshape(ROWS, 128), 128)
    out["fyr"] = left_table(rotated.reshape(ROWS, 128), 128)
    back = np.zeros((2, 2, HALF, 2, NKY))
    cos_t = np.moveaxis(cosine, 0, -1) / N
    sin_t = np.moveaxis(sine, 0, -1) / N
    back[:, 0, :, 0] = cos_t
    back[:, 0, :, 1] = -sin_t
    back[:, 1, :, 0] = sin_t
    back[:, 1, :, 1] = cos_t
    back_slope = np.zeros_like(back)
    back_slope[..., 0, :] = ky * back[..., 1, :]
    back_slope[..., 1, :] = -ky * back[..., 0, :]
    out["iy"] = left_table(back.reshape(128, ROWS), 128)
    out["iyd"] = left_table(back_slope.reshape(128, ROWS), 128)
    grad_high, grad_low = [], []
    x = np.arange(N)
    apart = x[:HALF, None] - x[None, :]
    for cut in range(KEEP - 3, KEEP + 1):
        k = np.arange(cut + 1)
        wk = np.where(k == 0, 1.0, 2.0) / N
        arg = 2 * np.pi * apart[..., None] * k / N
        keep = (np.cos(arg) * wk).sum(-1)
        derive = (-np.sin(arg) * wk * k).sum(-1)
        table = np.zeros((2, 4, HALF, 2, 4, HALF))
        for comp in range(3):
            for side in range(2):
                rows = slice(side * HALF, (side + 1) * HALF)
                table[side, comp, :, 0, comp, :] = keep[:, rows].T
                table[side, comp, :, 1, comp, :] = derive[:, rows].T
        high, low = halves(table.reshape(256, 256))
        grad_high.append(high)
        grad_low.append(low)
    out["gxh"] = np.stack(grad_high)
    out["gxl"] = np.stack(grad_low)
    kx = np.arange(HALF)
    live = (kx <= KEEP).astype(np.float64)
    xl = np.arange(HALF)
    arg = 2 * np.pi * xl[:, None] * kx[None, :] / N
    value = np.concatenate([np.cos(arg) * live, np.sin(arg) * live], 1)
    change = np.concatenate([kx * np.sin(arg) * live, -kx * np.cos(arg) * live], 1)

    def coefficients(blocks):
        table = np.zeros((4, HALF, 2, 2 * HALF))
        for block, part, what in blocks:
            table[block, :, part] = what
        return table.reshape(LANES, LANES)

    first = coefficients([(0, 0, value), (1, 1, value), (2, 0, change), (3, 0, value)])
    last = coefficients([(0, 0, change), (1, 0, value), (2, 0, value), (3, 1, value)])
    fall = first.reshape(LANES, 2, 2, HALF)
    fall = np.stack([-kx * fall[:, :, 1], kx * fall[:, :, 0]], 2).reshape(LANES, LANES)
    out["fx"] = np.stack([right_table(part, 128) for part in (first, fall, first, last)])
    wx = np.where(kx == 0, 1.0, 2.0) * live / N
    for core in range(2):
        ix = np.zeros((4, 2, 2 * HALF, LANES))
        for side in range(2):
            xs = np.arange(HALF) + side * HALF
            arg = 2 * np.pi * kx[:, None] * xs[None, :] / N
            give = np.concatenate([np.cos(arg) * wx[:, None], np.sin(arg) * wx[:, None]], 0)
            drop = np.concatenate(
                [np.sin(arg) * (wx * kx)[:, None], -np.cos(arg) * (wx * kx)[:, None]], 0
            )
            own = slice(core * 16, core * 16 + 16)

            def put(quantity, part, lane, what):
                at = (lane + side * 64 + np.arange(what.shape[1])) % LANES
                ix[quantity, part][:, at] = what

            put(0, 0, 0, give)
            put(1, 0, 0, drop)
            put(0, 1, 32, give[:, own])
            put(1, 1, 32, drop[:, own])
            put(2, 1, 48, give[:, own])
            put(2, 0, 64, give)
            put(3, 0, 96, give)
            put(3, 1, 0, give[:, own])
        out["ix%d" % core] = np.stack(
            [right_table(part, 128) for part in ix.reshape(4, LANES, LANES)]
        )
    out["ix"] = np.stack([out.pop("ix0"), out.pop("ix1")])
    ky_rows = np.tile(ky, 2)[:, None]
    out["kyrow"] = np.broadcast_to(ky_rows, (ROWS, LANES)).astype(np.float32).copy()
    lane_kx = np.tile(kx * live, 4)
    out["kxlane"] = np.broadcast_to(lane_kx, (8, LANES)).astype(np.float32).copy()
    yy = np.arange(N)
    force = [forcing_amp * np.sin(2 * np.pi * ((w * yy) % N) / N) for w in range(1, 5)]
    force = np.repeat(np.stack(force).reshape(4, HALF, 2, 1), N, axis=3)
    out["force"] = force.reshape(4, HALF, LANES).astype(np.float32)
    return out


def split(values):
    high = values.astype(bf16)
    low = (values - high.astype(f32)).astype(bf16)
    return high, low


def dot(a, b):
    return jnp.dot(a, b, preferred_element_type=f32)


def dot_nt(a, b):
    return lax.dot_general(a, b, (((1,), (1,)), ((), ())), preferred_element_type=f32)


def stacked(values):
    high, low = split(values)
    return jnp.concatenate([high, low], 0)


def beside(values):
    high, low = split(values)
    return jnp.concatenate([high, low], 1)


def folded(result):
    rows = result.shape[0] // 2
    return result[:rows] + result[rows:]


def folded_lanes(result):
    return result[:, :LANES] + result[:, LANES:]


def padded(values, rows=128):
    return jnp.concatenate([values, jnp.zeros((rows - values.shape[0], values.shape[1]), f32)], 0)


def triple(values, high_ref, low_ref):
    high, low = split(values)
    return dot(high, high_ref) + dot(low, high_ref) + dot(high, low_ref)


def columns(yh):
    return pl.ds(pl.multiple_of(yh * LANES, LANES), LANES)


def along_y(ref, tile, kz):
    return jnp.concatenate(
        [ref[tile, pl.ds(q * NKZ + kz, HALF, stride=ROWS), :] for q in range(4)], 0
    )


def along_kz(ref, tile, yh):
    return padded(ref[tile, pl.ds(yh, ROWS, stride=HALF), :]).T


def line_rows(yh):
    return pl.ds(pl.multiple_of(yh * ROWS, 8), ROWS)


def plane_rows(kz):
    return pl.ds(pl.multiple_of(kz * LANES, LANES), LANES)


def lane_parts(values):
    return [values[:, at : at + LANES] for at in range(0, values.shape[1], LANES)]


def over_planes(step):
    def four(index, _):
        step([index * 4 + k for k in range(4)])
        return 0

    lax.fori_loop(0, NKZ // 4, four, 0)
    step([jnp.int32(kz) for kz in range(NKZ // 4 * 4, NKZ)])


def over_lines(step, many):
    def some(index, _):
        step([index * many + k for k in range(many)])
        return 0

    lax.fori_loop(0, HALF // many, some, 0)


def base_kernel(core_ref, base_ref, fz_ref, fy_ref, out_ref, lines):
    nothing = jnp.zeros((HALF, LANES), f32)

    def z_step(yhs):
        rows = []
        for yh in yhs:
            rows += [base_ref[i, :, columns(yh)] for i in range(3)] + [nothing]
        got = folded(dot_nt(fz_ref[...], beside(jnp.concatenate(rows, 0))))
        for yh, part in zip(yhs, lane_parts(got)):
            lines[0, line_rows(yh), :] = part

    over_lines(z_step, 4)
    start = core_ref[0] * HALF_KZ
    for pair in range(0, HALF_KZ, 2):
        ks = range(pair, min(pair + 2, HALF_KZ))
        data = jnp.concatenate([stacked(along_y(lines, 0, start + k)) for k in ks], 1)
        got = folded(dot(fy_ref[...], data))
        for k, part in zip(ks, lane_parts(got)):
            out_ref[k] = part


def flux_kernel(
    core_ref, base_ref, state_ref, fz_ref, fy_ref, fyr_ref, kyrow_ref, out_ref, lines
):
    sigma = jnp.where(core_ref[0] == 0, -time_step, time_step).astype(f32)
    nothing = jnp.zeros((HALF, LANES), f32)

    def z_step(yhs):
        rows = []
        for yh in yhs:
            b = [base_ref[i, :, columns(yh)] for i in range(3)]
            t = [sigma * state_ref[i, :, columns(yh)] for i in range(3)]
            rows += [t[2] * b[0], t[0] * b[1], t[1] * b[0], t[0] * b[2]]
            rows += [t[2] * b[1], t[2] * b[2], t[1] * b[1], t[1] * b[2]]
            rows += [nothing, nothing, t[0] * b[0], nothing]
        got = lane_parts(folded(dot_nt(fz_ref[...], beside(jnp.concatenate(rows, 0)))))
        for n, yh in enumerate(yhs):
            for tile in range(3):
                lines[tile, line_rows(yh), :] = got[3 * n + tile]

    over_lines(z_step, 2)
    ky = kyrow_ref[...]
    lane = lax.broadcasted_iota(jnp.int32, (ROWS, LANES), 1)
    odd_block = (lane // HALF) % 2 == 1

    def y_step(kzs):
        even = []
        for pair in range(0, len(kzs), 2):
            data = [stacked(along_y(lines, 0, kz)) for kz in kzs[pair : pair + 2]]
            even += lane_parts(folded(dot(fy_ref[...], jnp.concatenate(data, 1))))
        odd = []
        for kz in kzs:
            data = [stacked(along_y(lines, tile, kz)) for tile in (1, 2)]
            odd.append(lane_parts(folded(dot(fyr_ref[...], jnp.concatenate(data, 1)))))
        for n, kz in enumerate(kzs):
            kzf = kz.astype(f32)
            plain = even[n]
            slopes = odd[n][0] * jnp.where(odd_block, kzf, ky)
            slopes = slopes + pltpu.roll(slopes, 32, 1)
            out_ref[0, kz] = jnp.where(odd_block, slopes, plain)
            other = plain * jnp.where(lane >= 96, -kzf, -ky)
            other = other + pltpu.roll(other, 64, 1)
            out_ref[1, kz] = jnp.where(lane >= 96, other, odd[n][1])

    over_planes(y_step)


def main_kernel(
    core_ref, cutoff_ref, wave_ref, base_ref, state_ref,
    here_own, here_other, there_own, there_other, flux_ref,
    gxh_ref, gxl_ref, iy_ref, iyd_ref, iz_ref, izd_ref, fz_ref, fy_ref, fyr_ref,
    fx_ref, ix_ref, kyrow_ref, kxlane_ref, force_ref,
    near_ref, far_ref, planes, lines,
):
    core = core_ref[0]
    cut_x, cut_y, cut_z = cutoff_ref[0], cutoff_ref[1], cutoff_ref[2]
    which = jnp.clip(cut_x - (KEEP - 3), 0, 3)
    ky = kyrow_ref[...]
    keep_y = jnp.where(jnp.abs(ky) <= cut_y.astype(f32), 1.0, 0.0).astype(f32)

    def kept_z(kz):
        return jnp.where(kz <= cut_z, 1.0, 0.0).astype(f32)

    def gradient_step(kzs):
        rows = []
        for kz in kzs:
            half = kz // HALF_KZ
            at = kz - half * HALF_KZ
            keep = keep_y * kept_z(kz)
            here = jnp.where(half == core, here_own[at], here_other[at]) * keep
            there = jnp.where(half == core, there_own[at], there_other[at]) * keep
            rows.append(jnp.concatenate([here, there], 1))
        got = triple(jnp.concatenate(rows, 0), gxh_ref[which], gxl_ref[which])
        data = [stacked(padded(got[n * ROWS : (n + 1) * ROWS])) for n in range(len(kzs))]
        for n, kz in enumerate(kzs):
            even = lane_parts(folded(dot(iy_ref[...], data[n])))
            planes[0, plane_rows(kz), :] = even[1]
            planes[2, plane_rows(kz), :] = even[0]
        for n in range(0, len(kzs), 2):
            both = jnp.concatenate([data[n][:, :LANES], data[n + 1][:, :LANES]], 1)
            odd = lane_parts(folded(dot(iyd_ref[...], both)))
            planes[1, plane_rows(kzs[n]), :] = odd[0]
            planes[1, plane_rows(kzs[n + 1]), :] = odd[1]

    over_planes(gradient_step)
    force_at = jnp.clip(wave_ref[0] - 1, 0, 3)
    nothing = jnp.zeros((HALF, LANES), f32)

    def physical_step(yhs):
        count = len(yhs)
        flat = [along_kz(planes, d, yh)[:96] for d in range(2) for yh in yhs]
        steep = [along_kz(planes, 2, yh)[:96] for yh in yhs]
        flat = folded_lanes(dot(beside(jnp.concatenate(flat, 0)), iz_ref[...]))
        steep = folded_lanes(dot(beside(jnp.concatenate(steep, 0)), izd_ref[...]))
        for n, yh in enumerate(yhs):
            sets = [flat[96 * n :], flat[96 * (count + n) :], steep[96 * n :]]
            grads = [[one[HALF * i : HALF * (i + 1)] for i in range(3)] for one in sets]
            b = [base_ref[i, :, columns(yh)] for i in range(3)]
            s = [state_ref[i, :, columns(yh)] for i in range(3)]
            comb, comb_base = [], []
            for i in range(3):
                coupling = sum(
                    jnp.where(core == 0, grads[j][i], grads[i][j]) * s[j] for j in range(3)
                )
                comb.append(s[i] - time_step * coupling)
                drive = sum(grads[j][i] * b[j] for j in range(3))
                if i == 0:
                    drive = drive - force_ref[force_at, pl.ds(yh, 1), :]
                comb_base.append(b[i] - time_step * drive)
            rows = [comb[1], comb_base[1], comb[2], comb_base[2]]
            rows += [comb[0], comb_base[0], nothing, nothing]
            got = folded(dot_nt(fz_ref[...], beside(jnp.concatenate(rows, 0))))
            for tile, part in enumerate(lane_parts(got)):
                lines[tile, line_rows(yh), :] = part

    over_lines(physical_step, 4)
    kx = kxlane_ref[0:1, :]
    keep_x = jnp.where(kx <= cut_x.astype(f32), 1.0, 0.0).astype(f32)
    keep_xy = keep_y * keep_x
    square_xy = ky * ky + kx * kx
    lane = lax.broadcasted_iota(jnp.int32, (ROWS, LANES), 1)
    for group in range(3):
        near_ref[NKZ + group] = jnp.zeros((ROWS, LANES), f32)
        far_ref[NKZ + group] = jnp.zeros((ROWS, LANES), f32)

    def spectral_step(kzs):
        fields = [[], [], []]
        for pair in range(0, len(kzs), 2):
            ks = kzs[pair : pair + 2]
            data = [jnp.concatenate([stacked(along_y(lines, t, kz)) for kz in ks], 1) for t in (0, 1)]
            even = lane_parts(folded(dot(fy_ref[...], data[0])))
            odd = lane_parts(folded(dot(fyr_ref[...], data[1])))
            for n, kz in enumerate(ks):
                flux = flux_ref[0, kz]
                fields[0].append(odd[n] + flux_ref[1, kz])
                fields[1].append(jnp.where(lane < 64, even[n], flux))
                fields[2].append(jnp.where(lane < 64, flux, even[n]))
        data = [beside(jnp.concatenate(field, 0)) for field in fields]
        modes = [folded_lanes(dot(data[max(n - 1, 0)], fx_ref[n])) for n in range(4)]
        results = [[], [], [], []]
        for n, kz in enumerate(kzs):
            kzf = kz.astype(f32)
            vx, slope, uy, uz = (mode[n * ROWS : (n + 1) * ROWS] for mode in modes)
            square = square_xy + kzf * kzf
            factor = keep_xy * kept_z(kz) / (1.0 + viscosity * time_step * square)
            share = (slope + ky * uy + kzf * uz) / jnp.where(square > 0, square, 1.0)
            results[0].append(factor * vx)
            results[1].append(factor * share)
            results[2].append(factor * (uy - ky * share))
            results[3].append(factor * (uz - kzf * share))
        got = [
            dot(beside(jnp.concatenate(result, 0)), ix_ref[core, n])
            for n, result in enumerate(results)
        ]
        got = [folded_lanes(part) for part in (got[0] + got[1], got[2], got[3])]
        for n, kz in enumerate(kzs):
            x, y, z = (part[n * ROWS : (n + 1) * ROWS] for part in got)
            near_ref[kz] = jnp.where(lane < 48, x, jnp.where(lane < 96, y, z))
            away = jnp.where(
                (lane >= 64) & (lane < 112), x, jnp.where((lane >= 32) & (lane < 64), z, y)
            )
            far_ref[kz] = pltpu.roll(away, 64, 1)
            group = NKZ + kz // 8
            shift = (kz % 8) * 16
            near_ref[group] += pltpu.roll(jnp.where(lane < 16, z, 0.0), shift, 1)
            rest = jnp.where((lane >= 64) & (lane < 80), z, 0.0)
            far_ref[group] += pltpu.roll(rest, (shift + 64) % LANES, 1)

    over_planes(spectral_step)


def final_kernel(
    near_ref, far_ref, state_ref, base_ref, iy_ref, iz_ref, izr_ref,
    base_out, state_out, planes,
):
    def y_step(kzs):
        for kz in kzs:
            shift = (LANES - (kz % 8) * 16) % LANES
            group = NKZ + kz // 8
            rest = pltpu.roll(near_ref[group] + far_ref[group], shift, 1)
            data = jnp.concatenate([near_ref[kz] + far_ref[kz], rest], 1)
            got = lane_parts(folded(dot(iy_ref[...], stacked(padded(data)))))
            planes[0, plane_rows(kz), :] = got[0]
            planes[1, plane_rows(kz), :] = got[1]

    over_planes(y_step)

    def z_step(yhs):
        data = [along_kz(planes, 0, yh) for yh in yhs]
        rest = [along_kz(planes, 1, yh)[:16] for yh in yhs]
        turned = beside(jnp.concatenate([one[:48] for one in data], 0))
        plain = beside(jnp.concatenate([one[48:] for one in data] + rest, 0))
        turned = folded_lanes(dot(turned, izr_ref[...]))
        plain = folded_lanes(dot(plain, iz_ref[...]))
        for n, yh in enumerate(yhs):
            at = columns(yh)
            first = turned[48 * n : 48 * n + 48]
            second = plain[80 * n : 80 * n + 80]
            third = plain[80 * len(yhs) + 16 * n :][:16]
            state_out[0, :, at] = first[:32] - state_ref[0, :, at]
            state_out[1, :, at] = second[16:48] - state_ref[1, :, at]
            state_out[2, :, at] = second[48:80] - state_ref[2, :, at]
            base_out[0, :, at] = first[32:48] - base_ref[0, :, at]
            base_out[1, :, at] = second[:16] - base_ref[1, :, at]
            base_out[2, :, at] = third - base_ref[2, :, at]

    over_lines(z_step, 4)


interpret = False


def call(kernel, outs, scratch, inputs, flops, in_smem=0):
    whole = pl.BlockSpec(memory_space=pltpu.VMEM)
    small = pl.BlockSpec(memory_space=pltpu.SMEM)
    return pl.pallas_call(
        kernel,
        out_shape=outs,
        in_specs=[small] * in_smem + [whole] * (len(inputs) - in_smem),
        out_specs=jax.tree.map(lambda _: whole, outs),
        scratch_shapes=scratch,
        compiler_params=pltpu.CompilerParams(vmem_limit_bytes=56 * 2**20),
        cost_estimate=pl.CostEstimate(flops=flops, bytes_accessed=4 * 2**20, transcendentals=0),
        interpret=interpret,
    )(*inputs)


def body(base, state, wavenumber, cutoff):
    t = {name: jnp.asarray(value) for name, value in tables().items()}
    core = lax.axis_index("comp")
    seg_count = lax.axis_size("seg")
    own_base = base[0]
    own_state = state[0, 0]
    base_half = lax.dynamic_slice_in_dim(own_base, core * 16, 16, 1)
    back = [((s + 1) % seg_count, s) for s in range(seg_count)]
    around = [(2 * i, 2 * o) for i, o in back] + [(2 * o + 1, 2 * i + 1) for i, o in back]
    base_next = lax.ppermute(base_half, "seg", back)
    state_next = lax.ppermute(own_state, ("seg", "comp"), around)
    sds = jax.ShapeDtypeStruct
    core_at = core.reshape(1)
    swap = [(0, 1), (1, 0)]
    here_own = call(
        base_kernel,
        sds((HALF_KZ, ROWS, LANES), f32),
        [pltpu.VMEM((1, HALF * ROWS, LANES), f32)],
        [core_at, own_base, t["fz"], t["fy"]],
        10**9,
        in_smem=1,
    )
    there_own = lax.ppermute(here_own, "slab", swap)
    here_other = lax.ppermute(here_own, "comp", swap)
    there_other = lax.ppermute(there_own, "comp", swap)
    flux = call(
        flux_kernel,
        sds((2, NKZ, ROWS, LANES), f32),
        [pltpu.VMEM((3, HALF * ROWS, LANES), f32)],
        [core_at, own_base, own_state, t["fz"], t["fy"], t["fyr"], t["kyrow"]],
        4 * 10**9,
        in_smem=1,
    )
    names = (
        "gxh", "gxl", "iy", "iyd", "iz", "izd", "fz", "fy", "fyr", "fx", "ix",
        "kyrow", "kxlane", "force",
    )
    near, far = call(
        main_kernel,
        [sds((PACKED, ROWS, LANES), f32)] * 2,
        [
            pltpu.VMEM((3, NKZ * LANES, LANES), f32),
            pltpu.VMEM((2, HALF * ROWS, LANES), f32),
        ],
        [core_at, cutoff, wavenumber, own_base, own_state]
        + [here_own, here_other, there_own, there_other, flux]
        + [t[name] for name in names],
        10**10,
        in_smem=3,
    )
    far = lax.ppermute(far, "slab", swap)
    base_gap, state_gap = call(
        final_kernel,
        [sds((3, 16, N * N), f32), sds((3, HALF, N * N), f32)],
        [pltpu.VMEM((2, NKZ * LANES, LANES), f32)],
        [near, far, state_next, base_next, t["iy"], t["iz"], t["izr"]],
        10**9,
    )
    return base_gap[None], state_gap[None, None]


def solution(mesh):
    paired = mesh.shape["slab"] == 2 and mesh.shape["comp"] == 2
    return jax.shard_map(
        body if paired else general_body,
        mesh=mesh,
        in_specs=(
            P(("groups", "seg"), None, "slab", None),
            P(("groups", "seg"), "comp", None, "slab", None),
            P("groups"),
            P("groups"),
        ),
        out_specs=(
            P(("groups", "seg"), None, ("slab", "comp"), None),
            P(("groups", "seg"), "comp", None, "slab", None),
        ),
        check_vma=False,
    )
```

```python
import functools

import jax
import jax.numpy as jnp
import ml_dtypes
import numpy as np
from jax import lax
from jax.experimental import pallas as pl
from jax.experimental.pallas import tpu as pltpu
from jax.sharding import PartitionSpec as P

N = 64
HALF = 32
KEEP = N // 3
NKZ = KEEP + 1
NKY = 44
ROWS = 2 * NKY
PACKED = NKZ + 3
HALF_KZ = NKZ // 2
LANES = 128

viscosity = 0.025
time_step = 0.02
forcing_amp = 10.0

f32 = jnp.float32
bf16 = jnp.bfloat16


highest = lax.Precision.HIGHEST


def swapped(value, axis, apart):
    mask = 2**apart
    pairs = [(source, source ^ mask) for source in range(lax.axis_size(axis))]
    return lax.ppermute(value, axis, pairs)


def shifted(block, axis, distance):
    devices = range(lax.axis_size(axis))
    route = [((i - distance) % len(devices), i) for i in devices]
    return lax.ppermute(block, axis, route)


def wavenumbers(grid_points):
    position = jnp.arange(grid_points, dtype=jnp.int32)
    return jnp.where(position < grid_points // 2, position, position - grid_points)


def phases(first, second, grid_points):
    product = jnp.mod(first[:, None] * second[None, :], grid_points)
    return product.astype(jnp.float32) * (2.0 * jnp.pi / grid_points)


def combine(partial_value, columns):
    cosine_part = partial_value[0]
    sine_part = partial_value[1]
    real_part = cosine_part[..., :columns] - sine_part[..., columns:]
    imag_part = cosine_part[..., columns:] + sine_part[..., :columns]
    return jnp.concatenate([real_part, imag_part], axis=-1)


def times_unit(values, wave, columns):
    return jnp.concatenate([-wave * values[..., columns:], wave * values[..., :columns]], axis=-1)


def doubled(values):
    return jnp.concatenate([values, values], axis=-1)


def general_body(base, state, wavenumber, cutoff):
    grid_points = N
    base = base.reshape(base.shape[0], 3, base.shape[2], grid_points, grid_points)
    state = state.reshape(
        state.shape[0], state.shape[1], 3, state.shape[3], grid_points, grid_points
    )
    slab_rows = state.shape[3]
    half_rows = slab_rows // 2
    slab_count = lax.axis_size("slab")
    group_count = slab_count * lax.axis_size("comp")
    core_side = lax.axis_index("comp")
    block_number = lax.axis_index(("slab", "comp"))
    base_whole = base[0]
    base_half = lax.dynamic_slice_in_dim(base_whole, core_side * half_rows, half_rows, 1)
    own_state = state[0, 0]
    spectrum = wavenumbers(grid_points)
    one_third = grid_points // 3
    row_total = (2 * one_third + group_count) // group_count * group_count
    row_index = jnp.arange(row_total, dtype=jnp.int32)
    row_alive_mask = row_index <= 2 * one_third
    row_wave = jnp.where(row_index <= one_third, row_index, row_index - (2 * one_third + 1))
    row_wave = jnp.where(row_alive_mask, row_wave, 0)
    width = grid_points // 2
    rows_per_block = row_total // group_count
    alive_flags = row_alive_mask.astype(jnp.float32)
    grid_index = jnp.arange(grid_points, dtype=jnp.int32)
    column_index = grid_index[:width]
    angle_grid = phases(grid_index, grid_index, grid_points)
    angle_ahead = phases(grid_index, column_index, grid_points)
    angle_behind = phases(column_index, grid_index, grid_points)
    column_weight = jnp.where(column_index == 0, 1.0, 2.0).astype(jnp.float32)[:, None]
    forward_z = jnp.concatenate([jnp.cos(angle_ahead), -jnp.sin(angle_ahead)], axis=1)
    inverse_z = (
        jnp.concatenate(
            [jnp.cos(angle_behind) * column_weight, -jnp.sin(angle_behind) * column_weight], axis=0
        )
        / grid_points
    )
    phase_angle_rows = phases(row_wave, grid_index, grid_points)
    forward_transform_y = (
        jnp.stack([jnp.cos(phase_angle_rows), -jnp.sin(phase_angle_rows)])
        * alive_flags[None, :, None]
    )
    inverse_y = (
        jnp.stack([jnp.cos(phase_angle_rows).T, jnp.sin(phase_angle_rows).T])
        * alive_flags[None, None, :]
        / grid_points
    )
    forward_x = jnp.stack([jnp.cos(angle_grid), -jnp.sin(angle_grid)])
    inverse_x = jnp.stack([jnp.cos(angle_grid), jnp.sin(angle_grid)]) / grid_points
    table_ahead = forward_x.reshape(2, grid_points, slab_count, slab_rows)
    table_back = inverse_x.reshape(2, slab_count, slab_rows, grid_points)
    local_wave = lax.dynamic_slice_in_dim(row_wave, block_number * rows_per_block, rows_per_block)
    local_alive_mask = lax.dynamic_slice_in_dim(
        alive_flags, block_number * rows_per_block, rows_per_block
    )
    shape_local = (grid_points, rows_per_block, width)
    wave_x = jnp.broadcast_to(spectrum[:, None, None], shape_local)
    wave_y = jnp.broadcast_to(local_wave[None, :, None], shape_local)
    wave_z = jnp.broadcast_to(spectrum[:width][None, None, :], shape_local)
    inside = (
        (jnp.abs(wave_x) <= cutoff[0])
        & (jnp.abs(wave_y) <= cutoff[1])
        & (jnp.abs(wave_z) <= cutoff[2])
    )
    keep_mask = doubled(inside.astype(jnp.float32) * local_alive_mask[None, :, None])
    float_x = wave_x.astype(jnp.float32)
    float_y = wave_y.astype(jnp.float32)
    float_z = wave_z.astype(jnp.float32)
    ksquare = float_x * float_x + float_y * float_y + float_z * float_z
    safe_square = doubled(jnp.where(ksquare > 0, ksquare, jnp.ones_like(ksquare)))
    damping = doubled(1.0 / (1.0 + viscosity * time_step * ksquare))
    double_x = doubled(float_x)
    double_y = doubled(float_y)
    double_z = doubled(float_z)

    def project(field):
        divergence = (double_x * field[0] + double_y * field[1] + double_z * field[2]) / safe_square
        return jnp.stack(
            [
                field[0] - double_x * divergence,
                field[1] - double_y * divergence,
                field[2] - double_z * divergence,
            ]
        )

    def yz_forward(field):
        along_z = jnp.einsum("...z,zk->...k", field, forward_z, precision=highest)
        partial_value = jnp.einsum(
            "sry,...yk->s...rk", forward_transform_y, along_z, precision=highest
        )
        return combine(partial_value, width)

    def yz_inverse(modes):
        partial_value = jnp.einsum("syr,...rk->s...yk", inverse_y, modes, precision=highest)
        return jnp.einsum(
            "...k,kz->...z", combine(partial_value, width), inverse_z, precision=highest
        )

    def spectral(state_fields, base_fields):
        state_modes = yz_forward(state_fields)[:, :, None]
        base_modes = yz_forward(base_fields)[:, :, None]
        state_got = lax.all_to_all(
            state_modes, ("slab", "comp"), split_axis=4, concat_axis=2, tiled=True
        )
        base_got = lax.all_to_all(
            base_modes, ("slab", "comp"), split_axis=4, concat_axis=2, tiled=True
        )
        item_count = state_got.shape[0]
        part_count = state_got.shape[1]
        state_split = state_got.reshape(
            item_count, part_count, slab_count, 2, slab_rows, rows_per_block, 2 * width
        )
        state_partial = jnp.einsum(
            "srpx,ijpcxyk->sijcryk", table_ahead, state_split, precision=highest
        )
        base_lined = base_got.reshape(item_count, 1, grid_points, rows_per_block, 2 * width)
        base_partial = jnp.einsum("srx,ijxyk->sijryk", forward_x, base_lined, precision=highest)
        return (combine(state_partial, width), combine(base_partial, width))

    state_first, base_first = spectral(own_state[:, None], base_half[:, None])
    state_hat = state_first[:, 0] * keep_mask
    base_hat = base_first[:, 0] * keep_mask
    grad_hat = jnp.stack(
        [
            times_unit(base_hat, float_x, width),
            times_unit(base_hat, float_y, width),
            times_unit(base_hat, float_z, width),
        ],
        axis=1,
    )
    grad_hat = grad_hat.reshape(9, grid_points, rows_per_block, 2 * width)
    grad_partial = jnp.einsum("sxr,iryk->sixyk", inverse_x, grad_hat, precision=highest)
    grad_spread = combine(grad_partial, width).reshape(
        9, group_count, half_rows, rows_per_block, 2 * width
    )
    own_rows = yz_inverse(
        lax.all_to_all(grad_spread, ("slab", "comp"), split_axis=1, concat_axis=3, tiled=True)[:, 0]
    )
    other_rows = swapped(own_rows, "comp", 0)
    gradient = jnp.where(
        core_side == 0,
        jnp.concatenate([own_rows, other_rows], axis=1),
        jnp.concatenate([other_rows, own_rows], axis=1),
    )
    gradient = gradient.reshape(3, 3, slab_rows, grid_points, grid_points)
    gradient_half = lax.dynamic_slice_in_dim(gradient, core_side * half_rows, half_rows, 2)
    flux_terms = own_state[:, None] * base_whole[None, :]
    coupling_matrix = jnp.where(core_side == 0, gradient, jnp.swapaxes(gradient, 0, 1))
    coupling = jnp.sum(coupling_matrix * own_state[None, :], axis=1)
    forcing_phase = phases(wavenumber, grid_index, grid_points)[0]
    forcing = forcing_amp * jnp.sin(forcing_phase)[None, :, None]
    base_drive = jnp.sum(gradient_half * base_half[None, :], axis=1)
    base_drive = jnp.concatenate([base_drive[:1] - forcing[None], base_drive[1:]], axis=0)
    state_fields = jnp.concatenate([flux_terms, coupling[:, None]], axis=1)
    drive_modes, base_modes_two = spectral(state_fields, base_drive[:, None])
    orient = jnp.array([1.0, -1.0], dtype=jnp.float32)[None, :, None, None, None]
    divergence = (
        times_unit(drive_modes[:, 0], float_x, width)
        + times_unit(drive_modes[:, 1], float_y, width)
        + times_unit(drive_modes[:, 2], float_z, width)
    )
    state_drive = keep_mask * (orient * divergence + drive_modes[:, 3])
    new_hat = damping * project(state_hat - time_step * state_drive)
    base_new_hat = damping * project(base_hat - time_step * keep_mask * base_modes_two[:, 0])
    state_partial = jnp.einsum("spxr,icryk->sipcxyk", table_back, new_hat, precision=highest)
    state_back = combine(state_partial, width).reshape(
        3, group_count, slab_rows, rows_per_block, 2 * width
    )
    base_partial = jnp.einsum("sxr,iryk->sixyk", inverse_x, base_new_hat, precision=highest)
    base_back = combine(base_partial, width).reshape(
        3, group_count, half_rows, rows_per_block, 2 * width
    )
    state_got = lax.all_to_all(
        state_back, ("slab", "comp"), split_axis=1, concat_axis=3, tiled=True
    )
    base_got = lax.all_to_all(base_back, ("slab", "comp"), split_axis=1, concat_axis=3, tiled=True)
    state_new = yz_inverse(state_got[:, 0])
    base_new = yz_inverse(base_got[:, 0])
    base_later, later_state = shifted((base_half, own_state), "seg", -1)
    prior_state = shifted(own_state, "seg", 1)
    neighbour = jnp.where(core_side == 0, later_state, prior_state)
    base_gap = (base_new - base_later).reshape(1, 3, half_rows, grid_points * grid_points)
    state_gap = (state_new - neighbour).reshape(1, 1, 3, slab_rows, grid_points * grid_points)
    return (base_gap, state_gap)


def halves(table):
    high = table.astype(np.float32).astype(ml_dtypes.bfloat16)
    low = (table - high.astype(np.float64)).astype(ml_dtypes.bfloat16)
    return high, low


def left_table(table, depth):
    padded = np.zeros((table.shape[0], depth))
    padded[:, : table.shape[1]] = table
    high, low = halves(padded)
    return np.concatenate(
        [np.concatenate([high, high], 1), np.concatenate([low, np.zeros_like(low)], 1)], 0
    )


def right_table(table, depth):
    return np.ascontiguousarray(left_table(table.T, depth).T)


def ky_values():
    index = np.arange(NKY)
    wave = np.where(index <= KEEP, index, index - (2 * KEEP + 1))
    alive = (index <= 2 * KEEP).astype(np.float64)
    return wave * alive, alive


@functools.cache
def tables():
    out = {}
    z = np.arange(N)
    kz = np.arange(NKZ)
    angle = 2 * np.pi * kz[:, None] * z[None, :] / N
    weight = np.where(kz == 0, 1.0, 2.0)[:, None] / N
    forward = np.zeros((2, 2, NKZ, 2, N))
    inverse = np.zeros((NKZ, 2, 2, 2, N))
    turned = np.zeros((NKZ, 2, 2, 2, N))
    slope = np.zeros((NKZ, 2, 2, 2, N))
    for y2 in range(2):
        forward[y2, 0, :, y2] = np.cos(angle)
        forward[y2, 1, :, y2] = -np.sin(angle)
        inverse[:, y2, 0, y2] = weight * np.cos(angle)
        inverse[:, y2, 1, y2] = -weight * np.sin(angle)
        turned[:, y2, 0, y2] = weight * np.sin(angle)
        turned[:, y2, 1, y2] = weight * np.cos(angle)
        slope[:, y2, 0, y2] = -weight * kz[:, None] * np.sin(angle)
        slope[:, y2, 1, y2] = -weight * kz[:, None] * np.cos(angle)
    out["fz"] = left_table(forward.reshape(4 * NKZ, 2 * N), 128)
    out["iz"] = right_table(inverse.reshape(4 * NKZ, 2 * N), 128)
    out["izr"] = right_table(turned.reshape(4 * NKZ, 2 * N), 128)
    out["izd"] = right_table(slope.reshape(4 * NKZ, 2 * N), 128)
    ky, alive = ky_values()
    y = 2 * np.arange(HALF)[None, :] + np.arange(2)[:, None]
    phase = 2 * np.pi * ky[:, None, None] * y[None] / N
    cosine = np.cos(phase) * alive[:, None, None]
    sine = np.sin(phase) * alive[:, None, None]
    plain = np.zeros((2, NKY, 2, 2, HALF))
    plain[0, :, :, 0] = cosine
    plain[0, :, :, 1] = sine
    plain[1, :, :, 0] = -sine
    plain[1, :, :, 1] = cosine
    rotated = np.stack([-plain[1], plain[0]])
    out["fy"] = left_table(plain.reshape(ROWS, 128), 128)
    out["fyr"] = left_table(rotated.reshape(ROWS, 128), 128)
    back = np.zeros((2, 2, HALF, 2, NKY))
    cos_t = np.moveaxis(cosine, 0, -1) / N
    sin_t = np.moveaxis(sine, 0, -1) / N
    back[:, 0, :, 0] = cos_t
    back[:, 0, :, 1] = -sin_t
    back[:, 1, :, 0] = sin_t
    back[:, 1, :, 1] = cos_t
    back_slope = np.zeros_like(back)
    back_slope[..., 0, :] = ky * back[..., 1, :]
    back_slope[..., 1, :] = -ky * back[..., 0, :]
    out["iy"] = left_table(back.reshape(128, ROWS), 128)
    out["iyd"] = left_table(back_slope.reshape(128, ROWS), 128)
    grad_high, grad_low = [], []
    x = np.arange(N)
    apart = x[:HALF, None] - x[None, :]
    for cut in range(KEEP - 3, KEEP + 1):
        k = np.arange(cut + 1)
        wk = np.where(k == 0, 1.0, 2.0) / N
        arg = 2 * np.pi * apart[..., None] * k / N
        keep = (np.cos(arg) * wk).sum(-1)
        derive = (-np.sin(arg) * wk * k).sum(-1)
        table = np.zeros((2, 4, HALF, 2, 4, HALF))
        for comp in range(3):
            for side in range(2):
                rows = slice(side * HALF, (side + 1) * HALF)
                table[side, comp, :, 0, comp, :] = keep[:, rows].T
                table[side, comp, :, 1, comp, :] = derive[:, rows].T
        high, low = halves(table.reshape(256, 256))
        grad_high.append(high)
        grad_low.append(low)
    out["gxh"] = np.stack(grad_high)
    out["gxl"] = np.stack(grad_low)
    kx = np.arange(HALF)
    live = (kx <= KEEP).astype(np.float64)
    xl = np.arange(HALF)
    arg = 2 * np.pi * xl[:, None] * kx[None, :] / N
    value = np.concatenate([np.cos(arg) * live, np.sin(arg) * live], 1)
    change = np.concatenate([kx * np.sin(arg) * live, -kx * np.cos(arg) * live], 1)

    def coefficients(blocks):
        table = np.zeros((4, HALF, 2, 2 * HALF))
        for block, part, what in blocks:
            table[block, :, part] = what
        return table.reshape(LANES, LANES)

    first = coefficients([(0, 0, value), (1, 1, value), (2, 0, change), (3, 0, value)])
    last = coefficients([(0, 0, change), (1, 0, value), (2, 0, value), (3, 1, value)])
    fall = first.reshape(LANES, 2, 2, HALF)
    fall = np.stack([-kx * fall[:, :, 1], kx * fall[:, :, 0]], 2).reshape(LANES, LANES)
    out["fx"] = np.stack([right_table(part, 128) for part in (first, fall, first, last)])
    wx = np.where(kx == 0, 1.0, 2.0) * live / N
    for core in range(2):
        ix = np.zeros((4, 2, 2 * HALF, LANES))
        for side in range(2):
            xs = np.arange(HALF) + side * HALF
            arg = 2 * np.pi * kx[:, None] * xs[None, :] / N
            give = np.concatenate([np.cos(arg) * wx[:, None], np.sin(arg) * wx[:, None]], 0)
            drop = np.concatenate(
                [np.sin(arg) * (wx * kx)[:, None], -np.cos(arg) * (wx * kx)[:, None]], 0
            )
            own = slice(core * 16, core * 16 + 16)

            def put(quantity, part, lane, what):
                at = (lane + side * 64 + np.arange(what.shape[1])) % LANES
                ix[quantity, part][:, at] = what

            put(0, 0, 0, give)
            put(1, 0, 0, drop)
            put(0, 1, 32, give[:, own])
            put(1, 1, 32, drop[:, own])
            put(2, 1, 48, give[:, own])
            put(2, 0, 64, give)
            put(3, 0, 96, give)
            put(3, 1, 0, give[:, own])
        out["ix%d" % core] = np.stack(
            [right_table(part, 128) for part in ix.reshape(4, LANES, LANES)]
        )
    out["ix"] = np.stack([out.pop("ix0"), out.pop("ix1")])
    ky_rows = np.tile(ky, 2)[:, None]
    out["kyrow"] = np.broadcast_to(ky_rows, (ROWS, LANES)).astype(np.float32).copy()
    lane_kx = np.tile(kx * live, 4)
    out["kxlane"] = np.broadcast_to(lane_kx, (8, LANES)).astype(np.float32).copy()
    yy = np.arange(N)
    force = [forcing_amp * np.sin(2 * np.pi * ((w * yy) % N) / N) for w in range(1, 5)]
    force = np.repeat(np.stack(force).reshape(4, HALF, 2, 1), N, axis=3)
    out["force"] = force.reshape(4, HALF, LANES).astype(np.float32)
    return out


def split(values):
    high = values.astype(bf16)
    low = (values - high.astype(f32)).astype(bf16)
    return high, low


def dot(a, b):
    return jnp.dot(a, b, preferred_element_type=f32)


def dot_nt(a, b):
    return lax.dot_general(a, b, (((1,), (1,)), ((), ())), preferred_element_type=f32)


def stacked(values):
    high, low = split(values)
    return jnp.concatenate([high, low], 0)


def beside(values):
    high, low = split(values)
    return jnp.concatenate([high, low], 1)


def folded(result):
    rows = result.shape[0] // 2
    return result[:rows] + result[rows:]


def folded_lanes(result):
    return result[:, :LANES] + result[:, LANES:]


def padded(values, rows=128):
    return jnp.concatenate([values, jnp.zeros((rows - values.shape[0], values.shape[1]), f32)], 0)


def triple(values, high_ref, low_ref):
    high, low = split(values)
    return dot(high, high_ref) + dot(low, high_ref) + dot(high, low_ref)


def columns(yh):
    return pl.ds(pl.multiple_of(yh * LANES, LANES), LANES)


def along_y(ref, tile, kz):
    return jnp.concatenate(
        [ref[tile, pl.ds(q * NKZ + kz, HALF, stride=ROWS), :] for q in range(4)], 0
    )


def along_kz(ref, tile, yh):
    return padded(ref[tile, pl.ds(yh, ROWS, stride=HALF), :]).T


def line_rows(yh):
    return pl.ds(pl.multiple_of(yh * ROWS, 8), ROWS)


def plane_rows(kz):
    return pl.ds(pl.multiple_of(kz * LANES, LANES), LANES)


def lane_parts(values):
    return [values[:, at : at + LANES] for at in range(0, values.shape[1], LANES)]


def over_planes(step):
    def four(index, _):
        step([index * 4 + k for k in range(4)])
        return 0

    lax.fori_loop(0, NKZ // 4, four, 0)
    step([jnp.int32(kz) for kz in range(NKZ // 4 * 4, NKZ)])


def over_lines(step, many):
    def some(index, _):
        step([index * many + k for k in range(many)])
        return 0

    lax.fori_loop(0, HALF // many, some, 0)


def base_kernel(core_ref, base_ref, fz_ref, fy_ref, out_ref, lines):
    nothing = jnp.zeros((HALF, LANES), f32)

    def z_step(yhs):
        rows = []
        for yh in yhs:
            rows += [base_ref[i, :, columns(yh)] for i in range(3)] + [nothing]
        got = folded(dot_nt(fz_ref[...], beside(jnp.concatenate(rows, 0))))
        for yh, part in zip(yhs, lane_parts(got)):
            lines[0, line_rows(yh), :] = part

    over_lines(z_step, 8)
    start = core_ref[0] * HALF_KZ
    for pair in range(0, HALF_KZ, 2):
        ks = range(pair, min(pair + 2, HALF_KZ))
        data = jnp.concatenate([stacked(along_y(lines, 0, start + k)) for k in ks], 1)
        got = folded(dot(fy_ref[...], data))
        for k, part in zip(ks, lane_parts(got)):
            out_ref[k] = part


def flux_kernel(
    core_ref, base_ref, state_ref, fz_ref, fy_ref, fyr_ref, kyrow_ref, out_ref, lines
):
    sigma = jnp.where(core_ref[0] == 0, -time_step, time_step).astype(f32)
    nothing = jnp.zeros((HALF, LANES), f32)

    def z_step(yhs):
        rows = []
        for yh in yhs:
            b = [base_ref[i, :, columns(yh)] for i in range(3)]
            t = [sigma * state_ref[i, :, columns(yh)] for i in range(3)]
            rows += [t[2] * b[0], t[0] * b[1], t[1] * b[0], t[0] * b[2]]
            rows += [t[2] * b[1], t[2] * b[2], t[1] * b[1], t[1] * b[2]]
            rows += [nothing, nothing, t[0] * b[0], nothing]
        got = lane_parts(folded(dot_nt(fz_ref[...], beside(jnp.concatenate(rows, 0)))))
        for n, yh in enumerate(yhs):
            for tile in range(3):
                lines[tile, line_rows(yh), :] = got[3 * n + tile]

    over_lines(z_step, 4)
    ky = kyrow_ref[...]
    lane = lax.broadcasted_iota(jnp.int32, (ROWS, LANES), 1)
    odd_block = (lane // HALF) % 2 == 1

    def y_step(kzs):
        even = []
        for pair in range(0, len(kzs), 2):
            data = [stacked(along_y(lines, 0, kz)) for kz in kzs[pair : pair + 2]]
            even += lane_parts(folded(dot(fy_ref[...], jnp.concatenate(data, 1))))
        odd = []
        for kz in kzs:
            data = [stacked(along_y(lines, tile, kz)) for tile in (1, 2)]
            odd.append(lane_parts(folded(dot(fyr_ref[...], jnp.concatenate(data, 1)))))
        for n, kz in enumerate(kzs):
            kzf = kz.astype(f32)
            plain = even[n]
            slopes = odd[n][0] * jnp.where(odd_block, kzf, ky)
            slopes = slopes + pltpu.roll(slopes, 32, 1)
            out_ref[0, kz] = jnp.where(odd_block, slopes, plain)
            other = plain * jnp.where(lane >= 96, -kzf, -ky)
            other = other + pltpu.roll(other, 64, 1)
            out_ref[1, kz] = jnp.where(lane >= 96, other, odd[n][1])

    over_planes(y_step)


def main_kernel(
    core_ref, cutoff_ref, wave_ref, base_ref, state_ref,
    here_own, here_other, there_own, there_other, flux_ref,
    gxh_ref, gxl_ref, iy_ref, iyd_ref, iz_ref, izd_ref, fz_ref, fy_ref, fyr_ref,
    fx_ref, ix_ref, kyrow_ref, kxlane_ref, force_ref,
    near_ref, far_ref, planes, lines,
):
    core = core_ref[0]
    cut_x, cut_y, cut_z = cutoff_ref[0], cutoff_ref[1], cutoff_ref[2]
    which = jnp.clip(cut_x - (KEEP - 3), 0, 3)
    ky = kyrow_ref[...]
    keep_y = jnp.where(jnp.abs(ky) <= cut_y.astype(f32), 1.0, 0.0).astype(f32)

    def kept_z(kz):
        return jnp.where(kz <= cut_z, 1.0, 0.0).astype(f32)

    def gradient_step(kzs):
        rows = []
        for kz in kzs:
            half = kz // HALF_KZ
            at = kz - half * HALF_KZ
            keep = keep_y * kept_z(kz)
            here = jnp.where(half == core, here_own[at], here_other[at]) * keep
            there = jnp.where(half == core, there_own[at], there_other[at]) * keep
            rows.append(jnp.concatenate([here, there], 1))
        got = triple(jnp.concatenate(rows, 0), gxh_ref[which], gxl_ref[which])
        data = [stacked(padded(got[n * ROWS : (n + 1) * ROWS])) for n in range(len(kzs))]
        for n, kz in enumerate(kzs):
            even = lane_parts(folded(dot(iy_ref[...], data[n])))
            planes[0, plane_rows(kz), :] = even[1]
            planes[2, plane_rows(kz), :] = even[0]
        for n in range(0, len(kzs), 2):
            both = jnp.concatenate([data[n][:, :LANES], data[n + 1][:, :LANES]], 1)
            odd = lane_parts(folded(dot(iyd_ref[...], both)))
            planes[1, plane_rows(kzs[n]), :] = odd[0]
            planes[1, plane_rows(kzs[n + 1]), :] = odd[1]

    over_planes(gradient_step)
    force_at = jnp.clip(wave_ref[0] - 1, 0, 3)
    nothing = jnp.zeros((HALF, LANES), f32)

    def physical_step(yhs):
        count = len(yhs)
        flat = [along_kz(planes, d, yh)[:96] for d in range(2) for yh in yhs]
        steep = [along_kz(planes, 2, yh)[:96] for yh in yhs]
        flat = folded_lanes(dot(beside(jnp.concatenate(flat, 0)), iz_ref[...]))
        steep = folded_lanes(dot(beside(jnp.concatenate(steep, 0)), izd_ref[...]))
        for n, yh in enumerate(yhs):
            sets = [flat[96 * n :], flat[96 * (count + n) :], steep[96 * n :]]
            grads = [[one[HALF * i : HALF * (i + 1)] for i in range(3)] for one in sets]
            b = [base_ref[i, :, columns(yh)] for i in range(3)]
            s = [state_ref[i, :, columns(yh)] for i in range(3)]
            comb, comb_base = [], []
            for i in range(3):
                coupling = sum(
                    jnp.where(core == 0, grads[j][i], grads[i][j]) * s[j] for j in range(3)
                )
                comb.append(s[i] - time_step * coupling)
                drive = sum(grads[j][i] * b[j] for j in range(3))
                if i == 0:
                    drive = drive - force_ref[force_at, pl.ds(yh, 1), :]
                comb_base.append(b[i] - time_step * drive)
            rows = [comb[1], comb_base[1], comb[2], comb_base[2]]
            rows += [comb[0], comb_base[0], nothing, nothing]
            got = folded(dot_nt(fz_ref[...], beside(jnp.concatenate(rows, 0))))
            for tile, part in enumerate(lane_parts(got)):
                lines[tile, line_rows(yh), :] = part

    over_lines(physical_step, 8)
    kx = kxlane_ref[0:1, :]
    keep_x = jnp.where(kx <= cut_x.astype(f32), 1.0, 0.0).astype(f32)
    keep_xy = keep_y * keep_x
    square_xy = ky * ky + kx * kx
    lane = lax.broadcasted_iota(jnp.int32, (ROWS, LANES), 1)
    for group in range(3):
        near_ref[NKZ + group] = jnp.zeros((ROWS, LANES), f32)
        far_ref[NKZ + group] = jnp.zeros((ROWS, LANES), f32)

    def spectral_step(kzs):
        fields = [[], [], []]
        for pair in range(0, len(kzs), 2):
            ks = kzs[pair : pair + 2]
            data = [jnp.concatenate([stacked(along_y(lines, t, kz)) for kz in ks], 1) for t in (0, 1)]
            even = lane_parts(folded(dot(fy_ref[...], data[0])))
            odd = lane_parts(folded(dot(fyr_ref[...], data[1])))
            for n, kz in enumerate(ks):
                flux = flux_ref[0, kz]
                fields[0].append(odd[n] + flux_ref[1, kz])
                fields[1].append(jnp.where(lane < 64, even[n], flux))
                fields[2].append(jnp.where(lane < 64, flux, even[n]))
        data = [beside(jnp.concatenate(field, 0)) for field in fields]
        modes = [folded_lanes(dot(data[max(n - 1, 0)], fx_ref[n])) for n in range(4)]
        results = [[], [], [], []]
        for n, kz in enumerate(kzs):
            kzf = kz.astype(f32)
            vx, slope, uy, uz = (mode[n * ROWS : (n + 1) * ROWS] for mode in modes)
            square = square_xy + kzf * kzf
            factor = keep_xy * kept_z(kz) / (1.0 + viscosity * time_step * square)
            share = (slope + ky * uy + kzf * uz) / jnp.where(square > 0, square, 1.0)
            results[0].append(factor * vx)
            results[1].append(factor * share)
            results[2].append(factor * (uy - ky * share))
            results[3].append(factor * (uz - kzf * share))
        got = [
            dot(beside(jnp.concatenate(result, 0)), ix_ref[core, n])
            for n, result in enumerate(results)
        ]
        got = [folded_lanes(part) for part in (got[0] + got[1], got[2], got[3])]
        for n, kz in enumerate(kzs):
            x, y, z = (part[n * ROWS : (n + 1) * ROWS] for part in got)
            near_ref[kz] = jnp.where(lane < 48, x, jnp.where(lane < 96, y, z))
            away = jnp.where(
                (lane >= 64) & (lane < 112), x, jnp.where((lane >= 32) & (lane < 64), z, y)
            )
            far_ref[kz] = pltpu.roll(away, 64, 1)
            group = NKZ + kz // 8
            shift = (kz % 8) * 16
            near_ref[group] += pltpu.roll(jnp.where(lane < 16, z, 0.0), shift, 1)
            rest = jnp.where((lane >= 64) & (lane < 80), z, 0.0)
            far_ref[group] += pltpu.roll(rest, (shift + 64) % LANES, 1)

    over_planes(spectral_step)


def final_kernel(
    near_ref, far_ref, state_ref, base_ref, iy_ref, iz_ref, izr_ref,
    base_out, state_out, planes,
):
    def y_step(kzs):
        for kz in kzs:
            shift = (LANES - (kz % 8) * 16) % LANES
            group = NKZ + kz // 8
            rest = pltpu.roll(near_ref[group] + far_ref[group], shift, 1)
            data = jnp.concatenate([near_ref[kz] + far_ref[kz], rest], 1)
            got = lane_parts(folded(dot(iy_ref[...], stacked(padded(data)))))
            planes[0, plane_rows(kz), :] = got[0]
            planes[1, plane_rows(kz), :] = got[1]

    over_planes(y_step)

    def z_step(yhs):
        data = [along_kz(planes, 0, yh) for yh in yhs]
        rest = [along_kz(planes, 1, yh)[:16] for yh in yhs]
        turned = beside(jnp.concatenate([one[:48] for one in data], 0))
        plain = beside(jnp.concatenate([one[48:] for one in data] + rest, 0))
        turned = folded_lanes(dot(turned, izr_ref[...]))
        plain = folded_lanes(dot(plain, iz_ref[...]))
        for n, yh in enumerate(yhs):
            at = columns(yh)
            first = turned[48 * n : 48 * n + 48]
            second = plain[80 * n : 80 * n + 80]
            third = plain[80 * len(yhs) + 16 * n :][:16]
            state_out[0, :, at] = first[:32] - state_ref[0, :, at]
            state_out[1, :, at] = second[16:48] - state_ref[1, :, at]
            state_out[2, :, at] = second[48:80] - state_ref[2, :, at]
            base_out[0, :, at] = first[32:48] - base_ref[0, :, at]
            base_out[1, :, at] = second[:16] - base_ref[1, :, at]
            base_out[2, :, at] = third - base_ref[2, :, at]

    over_lines(z_step, 8)


interpret = False


def call(kernel, outs, scratch, inputs, flops, in_smem=0):
    whole = pl.BlockSpec(memory_space=pltpu.VMEM)
    small = pl.BlockSpec(memory_space=pltpu.SMEM)
    return pl.pallas_call(
        kernel,
        out_shape=outs,
        in_specs=[small] * in_smem + [whole] * (len(inputs) - in_smem),
        out_specs=jax.tree.map(lambda _: whole, outs),
        scratch_shapes=scratch,
        compiler_params=pltpu.CompilerParams(vmem_limit_bytes=56 * 2**20),
        cost_estimate=pl.CostEstimate(flops=flops, bytes_accessed=4 * 2**20, transcendentals=0),
        interpret=interpret,
    )(*inputs)


def body(base, state, wavenumber, cutoff):
    t = {name: jnp.asarray(value) for name, value in tables().items()}
    core = lax.axis_index("comp")
    seg_count = lax.axis_size("seg")
    own_base = base[0]
    own_state = state[0, 0]
    base_half = lax.dynamic_slice_in_dim(own_base, core * 16, 16, 1)
    back = [((s + 1) % seg_count, s) for s in range(seg_count)]
    around = [(2 * i, 2 * o) for i, o in back] + [(2 * o + 1, 2 * i + 1) for i, o in back]
    base_next = lax.ppermute(base_half, "seg", back)
    state_next = lax.ppermute(own_state, ("seg", "comp"), around)
    sds = jax.ShapeDtypeStruct
    core_at = core.reshape(1)
    swap = [(0, 1), (1, 0)]
    here_own = call(
        base_kernel,
        sds((HALF_KZ, ROWS, LANES), f32),
        [pltpu.VMEM((1, HALF * ROWS, LANES), f32)],
        [core_at, own_base, t["fz"], t["fy"]],
        10**9,
        in_smem=1,
    )
    there_own = lax.ppermute(here_own, "slab", swap)
    here_other = lax.ppermute(here_own, "comp", swap)
    flux = call(
        flux_kernel,
        sds((2, NKZ, ROWS, LANES), f32),
        [pltpu.VMEM((3, HALF * ROWS, LANES), f32)],
        [core_at, own_base, own_state, t["fz"], t["fy"], t["fyr"], t["kyrow"]],
        4 * 10**9,
        in_smem=1,
    )
    there_own, flux = lax.optimization_barrier((there_own, flux))
    there_other = lax.ppermute(there_own, "comp", swap)
    names = (
        "gxh", "gxl", "iy", "iyd", "iz", "izd", "fz", "fy", "fyr", "fx", "ix",
        "kyrow", "kxlane", "force",
    )
    near, far = call(
        main_kernel,
        [sds((PACKED, ROWS, LANES), f32)] * 2,
        [
            pltpu.VMEM((3, NKZ * LANES, LANES), f32),
            pltpu.VMEM((2, HALF * ROWS, LANES), f32),
        ],
        [core_at, cutoff, wavenumber, own_base, own_state]
        + [here_own, here_other, there_own, there_other, flux]
        + [t[name] for name in names],
        10**10,
        in_smem=3,
    )
    far = lax.ppermute(far, "slab", swap)
    base_gap, state_gap = call(
        final_kernel,
        [sds((3, 16, N * N), f32), sds((3, HALF, N * N), f32)],
        [pltpu.VMEM((2, NKZ * LANES, LANES), f32)],
        [near, far, state_next, base_next, t["iy"], t["iz"], t["izr"]],
        10**9,
    )
    return base_gap[None], state_gap[None, None]


def solution(mesh):
    paired = mesh.shape["slab"] == 2 and mesh.shape["comp"] == 2
    return jax.shard_map(
        body if paired else general_body,
        mesh=mesh,
        in_specs=(
            P(("groups", "seg"), None, "slab", None),
            P(("groups", "seg"), "comp", None, "slab", None),
            P("groups"),
            P("groups"),
        ),
        out_specs=(
            P(("groups", "seg"), None, ("slab", "comp"), None),
            P(("groups", "seg"), "comp", None, "slab", None),
        ),
        check_vma=False,
    )
```

```python
import functools

import jax
import jax.numpy as jnp
import ml_dtypes
import numpy as np
from jax import lax
from jax.experimental import pallas as pl
from jax.experimental.pallas import tpu as pltpu
from jax.sharding import PartitionSpec as P

N = 64
HALF = 32
KEEP = N // 3
NKZ = KEEP + 1
NKY = 44
ROWS = 2 * NKY
CHUNK = 8
CHUNKS = 3
LINE = CHUNKS * CHUNK * 4
HALF_KZ = NKZ // 2
LANES = 128

viscosity = 0.025
time_step = 0.02
forcing_amp = 10.0

f32 = jnp.float32
bf16 = jnp.bfloat16


highest = lax.Precision.HIGHEST


def swapped(value, axis, apart):
    mask = 2**apart
    pairs = [(source, source ^ mask) for source in range(lax.axis_size(axis))]
    return lax.ppermute(value, axis, pairs)


def shifted(block, axis, distance):
    devices = range(lax.axis_size(axis))
    route = [((i - distance) % len(devices), i) for i in devices]
    return lax.ppermute(block, axis, route)


def wavenumbers(grid_points):
    position = jnp.arange(grid_points, dtype=jnp.int32)
    return jnp.where(position < grid_points // 2, position, position - grid_points)


def phases(first, second, grid_points):
    product = jnp.mod(first[:, None] * second[None, :], grid_points)
    return product.astype(jnp.float32) * (2.0 * jnp.pi / grid_points)


def combine(partial_value, columns):
    cosine_part = partial_value[0]
    sine_part = partial_value[1]
    real_part = cosine_part[..., :columns] - sine_part[..., columns:]
    imag_part = cosine_part[..., columns:] + sine_part[..., :columns]
    return jnp.concatenate([real_part, imag_part], axis=-1)


def times_unit(values, wave, columns):
    return jnp.concatenate([-wave * values[..., columns:], wave * values[..., :columns]], axis=-1)


def doubled(values):
    return jnp.concatenate([values, values], axis=-1)


def general_body(base, state, wavenumber, cutoff):
    grid_points = N
    base = base.reshape(base.shape[0], 3, base.shape[2], grid_points, grid_points)
    state = state.reshape(
        state.shape[0], state.shape[1], 3, state.shape[3], grid_points, grid_points
    )
    slab_rows = state.shape[3]
    half_rows = slab_rows // 2
    slab_count = lax.axis_size("slab")
    group_count = slab_count * lax.axis_size("comp")
    core_side = lax.axis_index("comp")
    block_number = lax.axis_index(("slab", "comp"))
    base_whole = base[0]
    base_half = lax.dynamic_slice_in_dim(base_whole, core_side * half_rows, half_rows, 1)
    own_state = state[0, 0]
    spectrum = wavenumbers(grid_points)
    one_third = grid_points // 3
    row_total = (2 * one_third + group_count) // group_count * group_count
    row_index = jnp.arange(row_total, dtype=jnp.int32)
    row_alive_mask = row_index <= 2 * one_third
    row_wave = jnp.where(row_index <= one_third, row_index, row_index - (2 * one_third + 1))
    row_wave = jnp.where(row_alive_mask, row_wave, 0)
    width = grid_points // 2
    rows_per_block = row_total // group_count
    alive_flags = row_alive_mask.astype(jnp.float32)
    grid_index = jnp.arange(grid_points, dtype=jnp.int32)
    column_index = grid_index[:width]
    angle_grid = phases(grid_index, grid_index, grid_points)
    angle_ahead = phases(grid_index, column_index, grid_points)
    angle_behind = phases(column_index, grid_index, grid_points)
    column_weight = jnp.where(column_index == 0, 1.0, 2.0).astype(jnp.float32)[:, None]
    forward_z = jnp.concatenate([jnp.cos(angle_ahead), -jnp.sin(angle_ahead)], axis=1)
    inverse_z = (
        jnp.concatenate(
            [jnp.cos(angle_behind) * column_weight, -jnp.sin(angle_behind) * column_weight], axis=0
        )
        / grid_points
    )
    phase_angle_rows = phases(row_wave, grid_index, grid_points)
    forward_transform_y = (
        jnp.stack([jnp.cos(phase_angle_rows), -jnp.sin(phase_angle_rows)])
        * alive_flags[None, :, None]
    )
    inverse_y = (
        jnp.stack([jnp.cos(phase_angle_rows).T, jnp.sin(phase_angle_rows).T])
        * alive_flags[None, None, :]
        / grid_points
    )
    forward_x = jnp.stack([jnp.cos(angle_grid), -jnp.sin(angle_grid)])
    inverse_x = jnp.stack([jnp.cos(angle_grid), jnp.sin(angle_grid)]) / grid_points
    table_ahead = forward_x.reshape(2, grid_points, slab_count, slab_rows)
    table_back = inverse_x.reshape(2, slab_count, slab_rows, grid_points)
    local_wave = lax.dynamic_slice_in_dim(row_wave, block_number * rows_per_block, rows_per_block)
    local_alive_mask = lax.dynamic_slice_in_dim(
        alive_flags, block_number * rows_per_block, rows_per_block
    )
    shape_local = (grid_points, rows_per_block, width)
    wave_x = jnp.broadcast_to(spectrum[:, None, None], shape_local)
    wave_y = jnp.broadcast_to(local_wave[None, :, None], shape_local)
    wave_z = jnp.broadcast_to(spectrum[:width][None, None, :], shape_local)
    inside = (
        (jnp.abs(wave_x) <= cutoff[0])
        & (jnp.abs(wave_y) <= cutoff[1])
        & (jnp.abs(wave_z) <= cutoff[2])
    )
    keep_mask = doubled(inside.astype(jnp.float32) * local_alive_mask[None, :, None])
    float_x = wave_x.astype(jnp.float32)
    float_y = wave_y.astype(jnp.float32)
    float_z = wave_z.astype(jnp.float32)
    ksquare = float_x * float_x + float_y * float_y + float_z * float_z
    safe_square = doubled(jnp.where(ksquare > 0, ksquare, jnp.ones_like(ksquare)))
    damping = doubled(1.0 / (1.0 + viscosity * time_step * ksquare))
    double_x = doubled(float_x)
    double_y = doubled(float_y)
    double_z = doubled(float_z)

    def project(field):
        divergence = (double_x * field[0] + double_y * field[1] + double_z * field[2]) / safe_square
        return jnp.stack(
            [
                field[0] - double_x * divergence,
                field[1] - double_y * divergence,
                field[2] - double_z * divergence,
            ]
        )

    def yz_forward(field):
        along_z = jnp.einsum("...z,zk->...k", field, forward_z, precision=highest)
        partial_value = jnp.einsum(
            "sry,...yk->s...rk", forward_transform_y, along_z, precision=highest
        )
        return combine(partial_value, width)

    def yz_inverse(modes):
        partial_value = jnp.einsum("syr,...rk->s...yk", inverse_y, modes, precision=highest)
        return jnp.einsum(
            "...k,kz->...z", combine(partial_value, width), inverse_z, precision=highest
        )

    def spectral(state_fields, base_fields):
        state_modes = yz_forward(state_fields)[:, :, None]
        base_modes = yz_forward(base_fields)[:, :, None]
        state_got = lax.all_to_all(
            state_modes, ("slab", "comp"), split_axis=4, concat_axis=2, tiled=True
        )
        base_got = lax.all_to_all(
            base_modes, ("slab", "comp"), split_axis=4, concat_axis=2, tiled=True
        )
        item_count = state_got.shape[0]
        part_count = state_got.shape[1]
        state_split = state_got.reshape(
            item_count, part_count, slab_count, 2, slab_rows, rows_per_block, 2 * width
        )
        state_partial = jnp.einsum(
            "srpx,ijpcxyk->sijcryk", table_ahead, state_split, precision=highest
        )
        base_lined = base_got.reshape(item_count, 1, grid_points, rows_per_block, 2 * width)
        base_partial = jnp.einsum("srx,ijxyk->sijryk", forward_x, base_lined, precision=highest)
        return (combine(state_partial, width), combine(base_partial, width))

    state_first, base_first = spectral(own_state[:, None], base_half[:, None])
    state_hat = state_first[:, 0] * keep_mask
    base_hat = base_first[:, 0] * keep_mask
    grad_hat = jnp.stack(
        [
            times_unit(base_hat, float_x, width),
            times_unit(base_hat, float_y, width),
            times_unit(base_hat, float_z, width),
        ],
        axis=1,
    )
    grad_hat = grad_hat.reshape(9, grid_points, rows_per_block, 2 * width)
    grad_partial = jnp.einsum("sxr,iryk->sixyk", inverse_x, grad_hat, precision=highest)
    grad_spread = combine(grad_partial, width).reshape(
        9, group_count, half_rows, rows_per_block, 2 * width
    )
    own_rows = yz_inverse(
        lax.all_to_all(grad_spread, ("slab", "comp"), split_axis=1, concat_axis=3, tiled=True)[:, 0]
    )
    other_rows = swapped(own_rows, "comp", 0)
    gradient = jnp.where(
        core_side == 0,
        jnp.concatenate([own_rows, other_rows], axis=1),
        jnp.concatenate([other_rows, own_rows], axis=1),
    )
    gradient = gradient.reshape(3, 3, slab_rows, grid_points, grid_points)
    gradient_half = lax.dynamic_slice_in_dim(gradient, core_side * half_rows, half_rows, 2)
    flux_terms = own_state[:, None] * base_whole[None, :]
    coupling_matrix = jnp.where(core_side == 0, gradient, jnp.swapaxes(gradient, 0, 1))
    coupling = jnp.sum(coupling_matrix * own_state[None, :], axis=1)
    forcing_phase = phases(wavenumber, grid_index, grid_points)[0]
    forcing = forcing_amp * jnp.sin(forcing_phase)[None, :, None]
    base_drive = jnp.sum(gradient_half * base_half[None, :], axis=1)
    base_drive = jnp.concatenate([base_drive[:1] - forcing[None], base_drive[1:]], axis=0)
    state_fields = jnp.concatenate([flux_terms, coupling[:, None]], axis=1)
    drive_modes, base_modes_two = spectral(state_fields, base_drive[:, None])
    orient = jnp.array([1.0, -1.0], dtype=jnp.float32)[None, :, None, None, None]
    divergence = (
        times_unit(drive_modes[:, 0], float_x, width)
        + times_unit(drive_modes[:, 1], float_y, width)
        + times_unit(drive_modes[:, 2], float_z, width)
    )
    state_drive = keep_mask * (orient * divergence + drive_modes[:, 3])
    new_hat = damping * project(state_hat - time_step * state_drive)
    base_new_hat = damping * project(base_hat - time_step * keep_mask * base_modes_two[:, 0])
    state_partial = jnp.einsum("spxr,icryk->sipcxyk", table_back, new_hat, precision=highest)
    state_back = combine(state_partial, width).reshape(
        3, group_count, slab_rows, rows_per_block, 2 * width
    )
    base_partial = jnp.einsum("sxr,iryk->sixyk", inverse_x, base_new_hat, precision=highest)
    base_back = combine(base_partial, width).reshape(
        3, group_count, half_rows, rows_per_block, 2 * width
    )
    state_got = lax.all_to_all(
        state_back, ("slab", "comp"), split_axis=1, concat_axis=3, tiled=True
    )
    base_got = lax.all_to_all(base_back, ("slab", "comp"), split_axis=1, concat_axis=3, tiled=True)
    state_new = yz_inverse(state_got[:, 0])
    base_new = yz_inverse(base_got[:, 0])
    base_later, later_state = shifted((base_half, own_state), "seg", -1)
    prior_state = shifted(own_state, "seg", 1)
    neighbour = jnp.where(core_side == 0, later_state, prior_state)
    base_gap = (base_new - base_later).reshape(1, 3, half_rows, grid_points * grid_points)
    state_gap = (state_new - neighbour).reshape(1, 1, 3, slab_rows, grid_points * grid_points)
    return (base_gap, state_gap)


def halves(table):
    high = table.astype(np.float32).astype(ml_dtypes.bfloat16)
    low = (table - high.astype(np.float64)).astype(ml_dtypes.bfloat16)
    return high, low


def left_table(table, depth):
    padded = np.zeros((table.shape[0], depth))
    padded[:, : table.shape[1]] = table
    high, low = halves(padded)
    return np.concatenate(
        [np.concatenate([high, high], 1), np.concatenate([low, np.zeros_like(low)], 1)], 0
    )


def right_table(table, depth):
    return np.ascontiguousarray(left_table(table.T, depth).T)


def ky_values():
    index = np.arange(NKY)
    wave = np.where(index <= KEEP, index, index - (2 * KEEP + 1))
    alive = (index <= 2 * KEEP).astype(np.float64)
    return wave * alive, alive


@functools.cache
def tables():
    out = {}
    z = np.arange(N)
    kz = np.arange(NKZ)
    angle = 2 * np.pi * kz[:, None] * z[None, :] / N
    weight = np.where(kz == 0, 1.0, 2.0)[:, None] / N
    forward = np.zeros((2, 2, CHUNKS * CHUNK, 2, N))
    inverse = np.zeros((NKZ, 2, 2, 2, N))
    turned = np.zeros((NKZ, 2, 2, 2, N))
    slope = np.zeros((NKZ, 2, 2, 2, N))
    for y2 in range(2):
        forward[y2, 0, :NKZ, y2] = np.cos(angle)
        forward[y2, 1, :NKZ, y2] = -np.sin(angle)
        inverse[:, y2, 0, y2] = weight * np.cos(angle)
        inverse[:, y2, 1, y2] = -weight * np.sin(angle)
        turned[:, y2, 0, y2] = weight * np.sin(angle)
        turned[:, y2, 1, y2] = weight * np.cos(angle)
        slope[:, y2, 0, y2] = -weight * kz[:, None] * np.sin(angle)
        slope[:, y2, 1, y2] = -weight * kz[:, None] * np.cos(angle)
    forward = np.moveaxis(forward.reshape(4, CHUNKS, CHUNK, 2 * N), 1, 0)
    out["fz"] = left_table(forward.reshape(LINE, 2 * N), 128)
    out["iz"] = right_table(inverse.reshape(4 * NKZ, 2 * N), 128)
    out["izr"] = right_table(turned.reshape(4 * NKZ, 2 * N), 128)
    out["izd"] = right_table(slope.reshape(4 * NKZ, 2 * N), 128)
    ky, alive = ky_values()
    y = 2 * np.arange(HALF)[None, :] + np.arange(2)[:, None]
    phase = 2 * np.pi * ky[:, None, None] * y[None] / N
    cosine = np.cos(phase) * alive[:, None, None]
    sine = np.sin(phase) * alive[:, None, None]
    plain = np.zeros((2, NKY, 2, 2, HALF))
    plain[0, :, :, 0] = cosine
    plain[0, :, :, 1] = sine
    plain[1, :, :, 0] = -sine
    plain[1, :, :, 1] = cosine
    rotated = np.stack([-plain[1], plain[0]])
    out["fy"] = left_table(plain.reshape(ROWS, 128), 128)
    out["fyr"] = left_table(rotated.reshape(ROWS, 128), 128)
    back = np.zeros((2, 2, HALF, 2, NKY))
    cos_t = np.moveaxis(cosine, 0, -1) / N
    sin_t = np.moveaxis(sine, 0, -1) / N
    back[:, 0, :, 0] = cos_t
    back[:, 0, :, 1] = -sin_t
    back[:, 1, :, 0] = sin_t
    back[:, 1, :, 1] = cos_t
    back_slope = np.zeros_like(back)
    back_slope[..., 0, :] = ky * back[..., 1, :]
    back_slope[..., 1, :] = -ky * back[..., 0, :]
    out["iy"] = left_table(back.reshape(128, ROWS), 128)
    out["iyd"] = left_table(back_slope.reshape(128, ROWS), 128)
    grad_high, grad_low = [], []
    x = np.arange(N)
    apart = x[:HALF, None] - x[None, :]
    for cut in range(KEEP - 3, KEEP + 1):
        k = np.arange(cut + 1)
        wk = np.where(k == 0, 1.0, 2.0) / N
        arg = 2 * np.pi * apart[..., None] * k / N
        keep = (np.cos(arg) * wk).sum(-1)
        derive = (-np.sin(arg) * wk * k).sum(-1)
        table = np.zeros((2, 4, HALF, 2, 4, HALF))
        for comp in range(3):
            for side in range(2):
                rows = slice(side * HALF, (side + 1) * HALF)
                table[side, comp, :, 0, comp, :] = keep[:, rows].T
                table[side, comp, :, 1, comp, :] = derive[:, rows].T
        high, low = halves(table.reshape(256, 256))
        grad_high.append(high)
        grad_low.append(low)
    out["gxh"] = np.stack(grad_high)
    out["gxl"] = np.stack(grad_low)
    kx = np.arange(HALF)
    live = (kx <= KEEP).astype(np.float64)
    xl = np.arange(HALF)
    arg = 2 * np.pi * xl[:, None] * kx[None, :] / N
    value = np.concatenate([np.cos(arg) * live, np.sin(arg) * live], 1)
    change = np.concatenate([kx * np.sin(arg) * live, -kx * np.cos(arg) * live], 1)

    def coefficients(blocks):
        table = np.zeros((4, HALF, 2, 2 * HALF))
        for block, part, what in blocks:
            table[block, :, part] = what
        return table.reshape(LANES, LANES)

    first = coefficients([(0, 0, value), (1, 1, value), (2, 0, change), (3, 0, value)])
    last = coefficients([(0, 0, change), (1, 0, value), (2, 0, value), (3, 1, value)])
    fall = first.reshape(LANES, 2, 2, HALF)
    fall = np.stack([-kx * fall[:, :, 1], kx * fall[:, :, 0]], 2).reshape(LANES, LANES)
    out["fx"] = np.stack([right_table(part, 128) for part in (first, fall, first, last)])
    wx = np.where(kx == 0, 1.0, 2.0) * live / N
    for core in range(2):
        ix = np.zeros((4, 2, 2 * HALF, LANES))
        for side in range(2):
            xs = np.arange(HALF) + side * HALF
            arg = 2 * np.pi * kx[:, None] * xs[None, :] / N
            give = np.concatenate([np.cos(arg) * wx[:, None], np.sin(arg) * wx[:, None]], 0)
            drop = np.concatenate(
                [np.sin(arg) * (wx * kx)[:, None], -np.cos(arg) * (wx * kx)[:, None]], 0
            )
            own = slice(core * 16, core * 16 + 16)

            def put(quantity, part, lane, what):
                at = (lane + side * 64 + np.arange(what.shape[1])) % LANES
                ix[quantity, part][:, at] = what

            put(0, 0, 0, give)
            put(1, 0, 0, drop)
            put(0, 1, 32, give[:, own])
            put(1, 1, 32, drop[:, own])
            put(2, 1, 48, give[:, own])
            put(2, 0, 64, give)
            put(3, 0, 96, give)
            put(3, 1, 0, give[:, own])
        out["ix%d" % core] = np.stack(
            [right_table(part, 128) for part in ix.reshape(4, LANES, LANES)]
        )
    out["ix"] = np.stack([out.pop("ix0"), out.pop("ix1")])
    ky_rows = np.tile(ky, 2)[:, None]
    out["kyrow"] = np.broadcast_to(ky_rows, (ROWS, LANES)).astype(np.float32).copy()
    lane_kx = np.tile(kx * live, 4)
    out["kxlane"] = np.broadcast_to(lane_kx, (8, LANES)).astype(np.float32).copy()
    yy = np.arange(N)
    force = [forcing_amp * np.sin(2 * np.pi * ((w * yy) % N) / N) for w in range(1, 5)]
    force = np.repeat(np.stack(force).reshape(4, HALF, 2, 1), N, axis=3)
    out["force"] = force.reshape(4, HALF, LANES).astype(np.float32)
    return out


def split(values):
    high = values.astype(bf16)
    low = (values - high.astype(f32)).astype(bf16)
    return high, low


def dot(a, b):
    return jnp.dot(a, b, preferred_element_type=f32)


def dot_nt(a, b):
    return lax.dot_general(a, b, (((1,), (1,)), ((), ())), preferred_element_type=f32)


def stacked(values):
    high, low = split(values)
    return jnp.concatenate([high, low], 0)


def beside(values):
    high, low = split(values)
    return jnp.concatenate([high, low], 1)


def folded(result):
    rows = result.shape[0] // 2
    return result[:rows] + result[rows:]


def folded_lanes(result):
    return result[:, :LANES] + result[:, LANES:]


def padded(values, rows=128):
    return jnp.concatenate([values, jnp.zeros((rows - values.shape[0], values.shape[1]), f32)], 0)


def triple(values, high_ref, low_ref):
    high, low = split(values)
    return dot(high, high_ref) + dot(low, high_ref) + dot(high, low_ref)


def columns(yh):
    return pl.ds(pl.multiple_of(yh * LANES, LANES), LANES)


def along_y(ref, tile, kz, line=LINE):
    at = kz % CHUNK + (0 if line == LINE // CHUNKS else kz // CHUNK * (4 * CHUNK))
    return jnp.concatenate(
        [ref[tile, pl.ds(q * CHUNK + at, HALF, stride=line), :] for q in range(4)], 0
    )


def along_kz(ref, tile, yh):
    return padded(ref[tile, pl.ds(yh, ROWS, stride=HALF), :]).T


def line_rows(yh):
    return pl.ds(pl.multiple_of(yh * LINE, 8), LINE)


def plane_rows(kz):
    return pl.ds(pl.multiple_of(kz * LANES, LANES), LANES)


def lane_parts(values):
    return [values[:, at : at + LANES] for at in range(0, values.shape[1], LANES)]


def over_planes(step, first=0, last=NKZ):
    def four(index, _):
        step([first + index * 4 + k for k in range(4)])
        return 0

    count = (last - first) // 4
    lax.fori_loop(0, count, four, 0)
    if first + count * 4 < last:
        step([jnp.int32(kz) for kz in range(first + count * 4, last)])


def planes_of(chunk):
    return chunk * CHUNK, min((chunk + 1) * CHUNK, NKZ)


def over_lines(step, many):
    def some(index, _):
        step([index * many + k for k in range(many)])
        return 0

    lax.fori_loop(0, HALF // many, some, 0)


def base_kernel(core_ref, base_ref, fz_ref, fy_ref, out_ref, lines):
    nothing = jnp.zeros((HALF, LANES), f32)

    def z_step(yhs):
        rows = []
        for yh in yhs:
            rows += [base_ref[i, :, columns(yh)] for i in range(3)] + [nothing]
        got = folded(dot_nt(fz_ref[...], beside(jnp.concatenate(rows, 0))))
        for yh, part in zip(yhs, lane_parts(got)):
            lines[0, line_rows(yh), :] = part

    over_lines(z_step, 8)
    start = core_ref[0] * HALF_KZ
    for pair in range(0, HALF_KZ, 2):
        ks = range(pair, min(pair + 2, HALF_KZ))
        data = jnp.concatenate([stacked(along_y(lines, 0, start + k)) for k in ks], 1)
        got = folded(dot(fy_ref[...], data))
        for k, part in zip(ks, lane_parts(got)):
            out_ref[k] = part


def flux_kernel(
    core_ref, base_ref, state_ref, fz_ref, fy_ref, fyr_ref, kyrow_ref, *refs
):
    *out_refs, lines = refs
    sigma = jnp.where(core_ref[0] == 0, -time_step, time_step).astype(f32)
    nothing = jnp.zeros((HALF, LANES), f32)

    def z_step(yhs):
        rows = []
        for yh in yhs:
            b = [base_ref[i, :, columns(yh)] for i in range(3)]
            t = [sigma * state_ref[i, :, columns(yh)] for i in range(3)]
            rows += [t[2] * b[0], t[0] * b[1], t[1] * b[0], t[0] * b[2]]
            rows += [t[2] * b[1], t[2] * b[2], t[1] * b[1], t[1] * b[2]]
            rows += [nothing, nothing, t[0] * b[0], nothing]
        got = lane_parts(folded(dot_nt(fz_ref[...], beside(jnp.concatenate(rows, 0)))))
        for n, yh in enumerate(yhs):
            for tile in range(3):
                lines[tile, line_rows(yh), :] = got[3 * n + tile]

    over_lines(z_step, 4)
    ky = kyrow_ref[...]
    lane = lax.broadcasted_iota(jnp.int32, (ROWS, LANES), 1)
    odd_block = (lane // HALF) % 2 == 1

    def y_step(chunk, kzs):
        out_ref = out_refs[chunk]
        even = []
        for pair in range(0, len(kzs), 2):
            data = [stacked(along_y(lines, 0, kz)) for kz in kzs[pair : pair + 2]]
            even += lane_parts(folded(dot(fy_ref[...], jnp.concatenate(data, 1))))
        odd = []
        for kz in kzs:
            data = [stacked(along_y(lines, tile, kz)) for tile in (1, 2)]
            odd.append(lane_parts(folded(dot(fyr_ref[...], jnp.concatenate(data, 1)))))
        for n, kz in enumerate(kzs):
            kzf = kz.astype(f32)
            plain = even[n]
            slopes = odd[n][0] * jnp.where(odd_block, kzf, ky)
            slopes = slopes + pltpu.roll(slopes, 32, 1)
            at = kz - chunk * CHUNK
            out_ref[0, at] = jnp.where(odd_block, slopes, plain)
            other = plain * jnp.where(lane >= 96, -kzf, -ky)
            other = other + pltpu.roll(other, 64, 1)
            out_ref[1, at] = jnp.where(lane >= 96, other, odd[n][1])

    for chunk in range(CHUNKS):
        over_planes(functools.partial(y_step, chunk), *planes_of(chunk))


def gradient_kernel(
    core_ref, cutoff_ref, wave_ref, base_ref, state_ref,
    here_own, here_other, there_own, there_other,
    gxh_ref, gxl_ref, iy_ref, iyd_ref, iz_ref, izd_ref, fz_ref, kyrow_ref, force_ref, *refs
):
    *out_refs, planes = refs
    core = core_ref[0]
    cut_x, cut_y, cut_z = cutoff_ref[0], cutoff_ref[1], cutoff_ref[2]
    which = jnp.clip(cut_x - (KEEP - 3), 0, 3)
    ky = kyrow_ref[...]
    keep_y = jnp.where(jnp.abs(ky) <= cut_y.astype(f32), 1.0, 0.0).astype(f32)

    def kept_z(kz):
        return jnp.where(kz <= cut_z, 1.0, 0.0).astype(f32)

    def gradient_step(kzs):
        rows = []
        for kz in kzs:
            half = kz // HALF_KZ
            at = kz - half * HALF_KZ
            keep = keep_y * kept_z(kz)
            here = jnp.where(half == core, here_own[at], here_other[at]) * keep
            there = jnp.where(half == core, there_own[at], there_other[at]) * keep
            rows.append(jnp.concatenate([here, there], 1))
        got = triple(jnp.concatenate(rows, 0), gxh_ref[which], gxl_ref[which])
        data = [stacked(padded(got[n * ROWS : (n + 1) * ROWS])) for n in range(len(kzs))]
        for n, kz in enumerate(kzs):
            even = lane_parts(folded(dot(iy_ref[...], data[n])))
            planes[0, plane_rows(kz), :] = even[1]
            planes[2, plane_rows(kz), :] = even[0]
        for n in range(0, len(kzs), 2):
            both = jnp.concatenate([data[n][:, :LANES], data[n + 1][:, :LANES]], 1)
            odd = lane_parts(folded(dot(iyd_ref[...], both)))
            planes[1, plane_rows(kzs[n]), :] = odd[0]
            planes[1, plane_rows(kzs[n + 1]), :] = odd[1]

    over_planes(gradient_step)
    force_at = jnp.clip(wave_ref[0] - 1, 0, 3)
    nothing = jnp.zeros((HALF, LANES), f32)

    def physical_step(yhs):
        count = len(yhs)
        flat = [along_kz(planes, d, yh)[:96] for d in range(2) for yh in yhs]
        steep = [along_kz(planes, 2, yh)[:96] for yh in yhs]
        flat = folded_lanes(dot(beside(jnp.concatenate(flat, 0)), iz_ref[...]))
        steep = folded_lanes(dot(beside(jnp.concatenate(steep, 0)), izd_ref[...]))
        for n, yh in enumerate(yhs):
            sets = [flat[96 * n :], flat[96 * (count + n) :], steep[96 * n :]]
            grads = [[one[HALF * i : HALF * (i + 1)] for i in range(3)] for one in sets]
            b = [base_ref[i, :, columns(yh)] for i in range(3)]
            s = [state_ref[i, :, columns(yh)] for i in range(3)]
            comb, comb_base = [], []
            for i in range(3):
                coupling = sum(
                    jnp.where(core == 0, grads[j][i], grads[i][j]) * s[j] for j in range(3)
                )
                comb.append(s[i] - time_step * coupling)
                drive = sum(grads[j][i] * b[j] for j in range(3))
                if i == 0:
                    drive = drive - force_ref[force_at, pl.ds(yh, 1), :]
                comb_base.append(b[i] - time_step * drive)
            rows = [comb[1], comb_base[1], comb[2], comb_base[2]]
            rows += [comb[0], comb_base[0], nothing, nothing]
            got = folded(dot_nt(fz_ref[...], beside(jnp.concatenate(rows, 0))))
            depth = LINE // CHUNKS
            rows = pl.ds(pl.multiple_of(yh * depth, 8), depth)
            for tile, part in enumerate(lane_parts(got)):
                for chunk in range(CHUNKS):
                    out_refs[chunk][tile, rows, :] = part[chunk * depth : (chunk + 1) * depth]

    over_lines(physical_step, 8)


def spectral_kernel(
    chunk, core_ref, cutoff_ref, lines_ref, flux_ref,
    fy_ref, fyr_ref, fx_ref, ix_ref, kyrow_ref, kxlane_ref, near_ref, far_ref,
):
    core = core_ref[0]
    cut_x, cut_y, cut_z = cutoff_ref[0], cutoff_ref[1], cutoff_ref[2]
    first, last = planes_of(chunk)
    extra = last - first
    ky = kyrow_ref[...]
    kx = kxlane_ref[0:1, :]
    keep_y = jnp.where(jnp.abs(ky) <= cut_y.astype(f32), 1.0, 0.0).astype(f32)
    keep_x = jnp.where(kx <= cut_x.astype(f32), 1.0, 0.0).astype(f32)
    keep_xy = keep_y * keep_x
    square_xy = ky * ky + kx * kx
    lane = lax.broadcasted_iota(jnp.int32, (ROWS, LANES), 1)
    near_ref[extra] = jnp.zeros((ROWS, LANES), f32)
    far_ref[extra] = jnp.zeros((ROWS, LANES), f32)

    def kept_z(kz):
        return jnp.where(kz <= cut_z, 1.0, 0.0).astype(f32)

    def spectral_step(kzs):
        fields = [[], [], []]
        for pair in range(0, len(kzs), 2):
            ks = kzs[pair : pair + 2]
            data = [
                jnp.concatenate(
                    [stacked(along_y(lines_ref, t, kz, LINE // CHUNKS)) for kz in ks], 1
                )
                for t in (0, 1)
            ]
            even = lane_parts(folded(dot(fy_ref[...], data[0])))
            odd = lane_parts(folded(dot(fyr_ref[...], data[1])))
            for n, kz in enumerate(ks):
                flux = flux_ref[0, kz - first]
                fields[0].append(odd[n] + flux_ref[1, kz - first])
                fields[1].append(jnp.where(lane < 64, even[n], flux))
                fields[2].append(jnp.where(lane < 64, flux, even[n]))
        data = [beside(jnp.concatenate(field, 0)) for field in fields]
        modes = [folded_lanes(dot(data[max(n - 1, 0)], fx_ref[n])) for n in range(4)]
        results = [[], [], [], []]
        for n, kz in enumerate(kzs):
            kzf = kz.astype(f32)
            vx, slope, uy, uz = (mode[n * ROWS : (n + 1) * ROWS] for mode in modes)
            square = square_xy + kzf * kzf
            factor = keep_xy * kept_z(kz) / (1.0 + viscosity * time_step * square)
            share = (slope + ky * uy + kzf * uz) / jnp.where(square > 0, square, 1.0)
            results[0].append(factor * vx)
            results[1].append(factor * share)
            results[2].append(factor * (uy - ky * share))
            results[3].append(factor * (uz - kzf * share))
        got = [
            dot(beside(jnp.concatenate(result, 0)), ix_ref[core, n])
            for n, result in enumerate(results)
        ]
        got = [folded_lanes(part) for part in (got[0] + got[1], got[2], got[3])]
        for n, kz in enumerate(kzs):
            x, y, z = (part[n * ROWS : (n + 1) * ROWS] for part in got)
            near_ref[kz - first] = jnp.where(lane < 48, x, jnp.where(lane < 96, y, z))
            away = jnp.where(
                (lane >= 64) & (lane < 112), x, jnp.where((lane >= 32) & (lane < 64), z, y)
            )
            far_ref[kz - first] = pltpu.roll(away, 64, 1)
            shift = (kz - first) * 16
            near_ref[extra] += pltpu.roll(jnp.where(lane < 16, z, 0.0), shift, 1)
            rest = jnp.where((lane >= 64) & (lane < 80), z, 0.0)
            far_ref[extra] += pltpu.roll(rest, (shift + 64) % LANES, 1)

    over_planes(spectral_step, first, last)


def inverse_y(near_ref, far_ref, iy_ref, planes):
    count = near_ref.shape[0] - 1
    rest = near_ref[count] + far_ref[count]
    for kz in range(count):
        turned = pltpu.roll(rest, (LANES - kz * 16) % LANES, 1) if kz else rest
        data = jnp.concatenate([near_ref[kz] + far_ref[kz], turned], 1)
        got = lane_parts(folded(dot(iy_ref[...], stacked(padded(data)))))
        for tile in range(2):
            planes[tile, kz * LANES : (kz + 1) * LANES, :] = got[tile]
    if count < CHUNK:
        blank = jnp.zeros(((CHUNK - count) * LANES, LANES), f32)
        for tile in range(2):
            planes[tile, count * LANES :, :] = blank


def inverse_kernel(near_a, far_a, near_b, far_b, iy_ref, planes_a, planes_b):
    inverse_y(near_a, far_a, iy_ref, planes_a)
    inverse_y(near_b, far_b, iy_ref, planes_b)


def final_kernel(
    near_ref, far_ref, planes_a, planes_b, state_ref, base_ref, iy_ref, iz_ref, izr_ref,
    base_out, state_out, planes_c,
):
    inverse_y(near_ref, far_ref, iy_ref, planes_c)

    def along_chunks(tile, yh):
        parts = [
            ref[tile, pl.ds(yh, 4 * CHUNK, stride=HALF), :]
            for ref in (planes_a, planes_b, planes_c)
        ]
        return padded(jnp.concatenate(parts, 0)).T

    def z_step(yhs):
        data = [along_chunks(0, yh) for yh in yhs]
        rest = [along_chunks(1, yh)[:16] for yh in yhs]
        turned = beside(jnp.concatenate([one[:48] for one in data], 0))
        plain = beside(jnp.concatenate([one[48:] for one in data] + rest, 0))
        turned = folded_lanes(dot(turned, izr_ref[...]))
        plain = folded_lanes(dot(plain, iz_ref[...]))
        for n, yh in enumerate(yhs):
            at = columns(yh)
            first = turned[48 * n : 48 * n + 48]
            second = plain[80 * n : 80 * n + 80]
            third = plain[80 * len(yhs) + 16 * n :][:16]
            state_out[0, :, at] = first[:32] - state_ref[0, :, at]
            state_out[1, :, at] = second[16:48] - state_ref[1, :, at]
            state_out[2, :, at] = second[48:80] - state_ref[2, :, at]
            base_out[0, :, at] = first[32:48] - base_ref[0, :, at]
            base_out[1, :, at] = second[:16] - base_ref[1, :, at]
            base_out[2, :, at] = third - base_ref[2, :, at]

    over_lines(z_step, 8)


interpret = False


def call(kernel, outs, scratch, inputs, in_smem=0, room=24):
    whole = pl.BlockSpec(memory_space=pltpu.VMEM)
    small = pl.BlockSpec(memory_space=pltpu.SMEM)
    return pl.pallas_call(
        kernel,
        out_shape=outs,
        in_specs=[small] * in_smem + [whole] * (len(inputs) - in_smem),
        out_specs=jax.tree.map(lambda _: whole, outs),
        scratch_shapes=scratch,
        compiler_params=pltpu.CompilerParams(vmem_limit_bytes=room * 2**20),
        cost_estimate=pl.CostEstimate(flops=1000, bytes_accessed=1000, transcendentals=0),
        interpret=interpret,
    )(*inputs)


def body(base, state, wavenumber, cutoff):
    t = {name: jnp.asarray(value) for name, value in tables().items()}
    core = lax.axis_index("comp")
    seg_count = lax.axis_size("seg")
    own_base = base[0]
    own_state = state[0, 0]
    base_half = lax.dynamic_slice_in_dim(own_base, core * 16, 16, 1)
    back = [((s + 1) % seg_count, s) for s in range(seg_count)]
    around = [(2 * i, 2 * o) for i, o in back] + [(2 * o + 1, 2 * i + 1) for i, o in back]
    base_next = lax.ppermute(base_half, "seg", back)
    state_next = lax.ppermute(own_state, ("seg", "comp"), around)
    sds = jax.ShapeDtypeStruct
    core_at = core.reshape(1)
    swap = [(0, 1), (1, 0)]
    here_own = call(
        base_kernel,
        sds((HALF_KZ, ROWS, LANES), f32),
        [pltpu.VMEM((1, HALF * LINE, LANES), f32)],
        [core_at, own_base, t["fz"], t["fy"]],
        in_smem=1,
    )
    there_own = lax.ppermute(here_own, "slab", swap)
    here_other = lax.ppermute(here_own, "comp", swap)
    counts = [planes_of(chunk)[1] - planes_of(chunk)[0] for chunk in range(CHUNKS)]
    flux = call(
        flux_kernel,
        [sds((2, count, ROWS, LANES), f32) for count in counts],
        [pltpu.VMEM((3, HALF * LINE, LANES), f32)],
        [core_at, own_base, own_state, t["fz"], t["fy"], t["fyr"], t["kyrow"]],
        in_smem=1,
    )
    there_own, flux = lax.optimization_barrier((there_own, flux))
    there_other = lax.ppermute(there_own, "comp", swap)
    names = ("gxh", "gxl", "iy", "iyd", "iz", "izd", "fz", "kyrow", "force")
    lines = call(
        gradient_kernel,
        [sds((2, HALF * 4 * CHUNK, LANES), f32)] * CHUNKS,
        [pltpu.VMEM((3, NKZ * LANES, LANES), f32)],
        [core_at, cutoff, wavenumber, own_base, own_state]
        + [here_own, here_other, there_own, there_other]
        + [t[name] for name in names],
        in_smem=3,
    )
    names = ("fy", "fyr", "fx", "ix", "kyrow", "kxlane")
    near, far = [], []
    for chunk in range(CHUNKS):
        near_part, far_part = call(
            functools.partial(spectral_kernel, chunk),
            [sds((counts[chunk] + 1, ROWS, LANES), f32)] * 2,
            [],
            [core_at, cutoff, lines[chunk], flux[chunk]] + [t[name] for name in names],
            in_smem=2,
        )
        near.append(near_part)
        far.append(lax.ppermute(far_part, "slab", swap))
    planes = sds((2, CHUNK * LANES, LANES), f32)
    planes_a, planes_b = call(
        inverse_kernel, [planes] * 2, [], [near[0], far[0], near[1], far[1], t["iy"]]
    )
    base_gap, state_gap = call(
        final_kernel,
        [sds((3, 16, N * N), f32), sds((3, HALF, N * N), f32)],
        [pltpu.VMEM((2, CHUNK * LANES, LANES), f32)],
        [near[2], far[2], planes_a, planes_b, state_next, base_next]
        + [t["iy"], t["iz"], t["izr"]],
    )
    return base_gap[None], state_gap[None, None]


def solution(mesh):
    paired = mesh.shape["slab"] == 2 and mesh.shape["comp"] == 2
    return jax.shard_map(
        body if paired else general_body,
        mesh=mesh,
        in_specs=(
            P(("groups", "seg"), None, "slab", None),
            P(("groups", "seg"), "comp", None, "slab", None),
            P("groups"),
            P("groups"),
        ),
        out_specs=(
            P(("groups", "seg"), None, ("slab", "comp"), None),
            P(("groups", "seg"), "comp", None, "slab", None),
        ),
        check_vma=False,
    )
```

```python
import functools

import jax
import jax.numpy as jnp
import ml_dtypes
import numpy as np
from jax import lax
from jax.experimental import pallas as pl
from jax.experimental.pallas import tpu as pltpu
from jax.sharding import PartitionSpec as P

N = 64
HALF = 32
KEEP = N // 3
NKZ = KEEP + 1
NKY = 44
ROWS = 2 * NKY
CHUNK = 8
CHUNKS = 3
LINE = CHUNKS * CHUNK * 4
HALF_KZ = NKZ // 2
LANES = 128

viscosity = 0.025
time_step = 0.02
forcing_amp = 10.0

f32 = jnp.float32
bf16 = jnp.bfloat16


highest = lax.Precision.HIGHEST


def swapped(value, axis, apart):
    mask = 2**apart
    pairs = [(source, source ^ mask) for source in range(lax.axis_size(axis))]
    return lax.ppermute(value, axis, pairs)


def shifted(block, axis, distance):
    devices = range(lax.axis_size(axis))
    route = [((i - distance) % len(devices), i) for i in devices]
    return lax.ppermute(block, axis, route)


def wavenumbers(grid_points):
    position = jnp.arange(grid_points, dtype=jnp.int32)
    return jnp.where(position < grid_points // 2, position, position - grid_points)


def phases(first, second, grid_points):
    product = jnp.mod(first[:, None] * second[None, :], grid_points)
    return product.astype(jnp.float32) * (2.0 * jnp.pi / grid_points)


def combine(partial_value, columns):
    cosine_part = partial_value[0]
    sine_part = partial_value[1]
    real_part = cosine_part[..., :columns] - sine_part[..., columns:]
    imag_part = cosine_part[..., columns:] + sine_part[..., :columns]
    return jnp.concatenate([real_part, imag_part], axis=-1)


def times_unit(values, wave, columns):
    return jnp.concatenate([-wave * values[..., columns:], wave * values[..., :columns]], axis=-1)


def doubled(values):
    return jnp.concatenate([values, values], axis=-1)


def general_body(base, state, wavenumber, cutoff):
    grid_points = N
    base = base.reshape(base.shape[0], 3, base.shape[2], grid_points, grid_points)
    state = state.reshape(
        state.shape[0], state.shape[1], 3, state.shape[3], grid_points, grid_points
    )
    slab_rows = state.shape[3]
    half_rows = slab_rows // 2
    slab_count = lax.axis_size("slab")
    group_count = slab_count * lax.axis_size("comp")
    core_side = lax.axis_index("comp")
    block_number = lax.axis_index(("slab", "comp"))
    base_whole = base[0]
    base_half = lax.dynamic_slice_in_dim(base_whole, core_side * half_rows, half_rows, 1)
    own_state = state[0, 0]
    spectrum = wavenumbers(grid_points)
    one_third = grid_points // 3
    row_total = (2 * one_third + group_count) // group_count * group_count
    row_index = jnp.arange(row_total, dtype=jnp.int32)
    row_alive_mask = row_index <= 2 * one_third
    row_wave = jnp.where(row_index <= one_third, row_index, row_index - (2 * one_third + 1))
    row_wave = jnp.where(row_alive_mask, row_wave, 0)
    width = grid_points // 2
    rows_per_block = row_total // group_count
    alive_flags = row_alive_mask.astype(jnp.float32)
    grid_index = jnp.arange(grid_points, dtype=jnp.int32)
    column_index = grid_index[:width]
    angle_grid = phases(grid_index, grid_index, grid_points)
    angle_ahead = phases(grid_index, column_index, grid_points)
    angle_behind = phases(column_index, grid_index, grid_points)
    column_weight = jnp.where(column_index == 0, 1.0, 2.0).astype(jnp.float32)[:, None]
    forward_z = jnp.concatenate([jnp.cos(angle_ahead), -jnp.sin(angle_ahead)], axis=1)
    inverse_z = (
        jnp.concatenate(
            [jnp.cos(angle_behind) * column_weight, -jnp.sin(angle_behind) * column_weight], axis=0
        )
        / grid_points
    )
    phase_angle_rows = phases(row_wave, grid_index, grid_points)
    forward_transform_y = (
        jnp.stack([jnp.cos(phase_angle_rows), -jnp.sin(phase_angle_rows)])
        * alive_flags[None, :, None]
    )
    inverse_y = (
        jnp.stack([jnp.cos(phase_angle_rows).T, jnp.sin(phase_angle_rows).T])
        * alive_flags[None, None, :]
        / grid_points
    )
    forward_x = jnp.stack([jnp.cos(angle_grid), -jnp.sin(angle_grid)])
    inverse_x = jnp.stack([jnp.cos(angle_grid), jnp.sin(angle_grid)]) / grid_points
    table_ahead = forward_x.reshape(2, grid_points, slab_count, slab_rows)
    table_back = inverse_x.reshape(2, slab_count, slab_rows, grid_points)
    local_wave = lax.dynamic_slice_in_dim(row_wave, block_number * rows_per_block, rows_per_block)
    local_alive_mask = lax.dynamic_slice_in_dim(
        alive_flags, block_number * rows_per_block, rows_per_block
    )
    shape_local = (grid_points, rows_per_block, width)
    wave_x = jnp.broadcast_to(spectrum[:, None, None], shape_local)
    wave_y = jnp.broadcast_to(local_wave[None, :, None], shape_local)
    wave_z = jnp.broadcast_to(spectrum[:width][None, None, :], shape_local)
    inside = (
        (jnp.abs(wave_x) <= cutoff[0])
        & (jnp.abs(wave_y) <= cutoff[1])
        & (jnp.abs(wave_z) <= cutoff[2])
    )
    keep_mask = doubled(inside.astype(jnp.float32) * local_alive_mask[None, :, None])
    float_x = wave_x.astype(jnp.float32)
    float_y = wave_y.astype(jnp.float32)
    float_z = wave_z.astype(jnp.float32)
    ksquare = float_x * float_x + float_y * float_y + float_z * float_z
    safe_square = doubled(jnp.where(ksquare > 0, ksquare, jnp.ones_like(ksquare)))
    damping = doubled(1.0 / (1.0 + viscosity * time_step * ksquare))
    double_x = doubled(float_x)
    double_y = doubled(float_y)
    double_z = doubled(float_z)

    def project(field):
        divergence = (double_x * field[0] + double_y * field[1] + double_z * field[2]) / safe_square
        return jnp.stack(
            [
                field[0] - double_x * divergence,
                field[1] - double_y * divergence,
                field[2] - double_z * divergence,
            ]
        )

    def yz_forward(field):
        along_z = jnp.einsum("...z,zk->...k", field, forward_z, precision=highest)
        partial_value = jnp.einsum(
            "sry,...yk->s...rk", forward_transform_y, along_z, precision=highest
        )
        return combine(partial_value, width)

    def yz_inverse(modes):
        partial_value = jnp.einsum("syr,...rk->s...yk", inverse_y, modes, precision=highest)
        return jnp.einsum(
            "...k,kz->...z", combine(partial_value, width), inverse_z, precision=highest
        )

    def spectral(state_fields, base_fields):
        state_modes = yz_forward(state_fields)[:, :, None]
        base_modes = yz_forward(base_fields)[:, :, None]
        state_got = lax.all_to_all(
            state_modes, ("slab", "comp"), split_axis=4, concat_axis=2, tiled=True
        )
        base_got = lax.all_to_all(
            base_modes, ("slab", "comp"), split_axis=4, concat_axis=2, tiled=True
        )
        item_count = state_got.shape[0]
        part_count = state_got.shape[1]
        state_split = state_got.reshape(
            item_count, part_count, slab_count, 2, slab_rows, rows_per_block, 2 * width
        )
        state_partial = jnp.einsum(
            "srpx,ijpcxyk->sijcryk", table_ahead, state_split, precision=highest
        )
        base_lined = base_got.reshape(item_count, 1, grid_points, rows_per_block, 2 * width)
        base_partial = jnp.einsum("srx,ijxyk->sijryk", forward_x, base_lined, precision=highest)
        return (combine(state_partial, width), combine(base_partial, width))

    state_first, base_first = spectral(own_state[:, None], base_half[:, None])
    state_hat = state_first[:, 0] * keep_mask
    base_hat = base_first[:, 0] * keep_mask
    grad_hat = jnp.stack(
        [
            times_unit(base_hat, float_x, width),
            times_unit(base_hat, float_y, width),
            times_unit(base_hat, float_z, width),
        ],
        axis=1,
    )
    grad_hat = grad_hat.reshape(9, grid_points, rows_per_block, 2 * width)
    grad_partial = jnp.einsum("sxr,iryk->sixyk", inverse_x, grad_hat, precision=highest)
    grad_spread = combine(grad_partial, width).reshape(
        9, group_count, half_rows, rows_per_block, 2 * width
    )
    own_rows = yz_inverse(
        lax.all_to_all(grad_spread, ("slab", "comp"), split_axis=1, concat_axis=3, tiled=True)[:, 0]
    )
    other_rows = swapped(own_rows, "comp", 0)
    gradient = jnp.where(
        core_side == 0,
        jnp.concatenate([own_rows, other_rows], axis=1),
        jnp.concatenate([other_rows, own_rows], axis=1),
    )
    gradient = gradient.reshape(3, 3, slab_rows, grid_points, grid_points)
    gradient_half = lax.dynamic_slice_in_dim(gradient, core_side * half_rows, half_rows, 2)
    flux_terms = own_state[:, None] * base_whole[None, :]
    coupling_matrix = jnp.where(core_side == 0, gradient, jnp.swapaxes(gradient, 0, 1))
    coupling = jnp.sum(coupling_matrix * own_state[None, :], axis=1)
    forcing_phase = phases(wavenumber, grid_index, grid_points)[0]
    forcing = forcing_amp * jnp.sin(forcing_phase)[None, :, None]
    base_drive = jnp.sum(gradient_half * base_half[None, :], axis=1)
    base_drive = jnp.concatenate([base_drive[:1] - forcing[None], base_drive[1:]], axis=0)
    state_fields = jnp.concatenate([flux_terms, coupling[:, None]], axis=1)
    drive_modes, base_modes_two = spectral(state_fields, base_drive[:, None])
    orient = jnp.array([1.0, -1.0], dtype=jnp.float32)[None, :, None, None, None]
    divergence = (
        times_unit(drive_modes[:, 0], float_x, width)
        + times_unit(drive_modes[:, 1], float_y, width)
        + times_unit(drive_modes[:, 2], float_z, width)
    )
    state_drive = keep_mask * (orient * divergence + drive_modes[:, 3])
    new_hat = damping * project(state_hat - time_step * state_drive)
    base_new_hat = damping * project(base_hat - time_step * keep_mask * base_modes_two[:, 0])
    state_partial = jnp.einsum("spxr,icryk->sipcxyk", table_back, new_hat, precision=highest)
    state_back = combine(state_partial, width).reshape(
        3, group_count, slab_rows, rows_per_block, 2 * width
    )
    base_partial = jnp.einsum("sxr,iryk->sixyk", inverse_x, base_new_hat, precision=highest)
    base_back = combine(base_partial, width).reshape(
        3, group_count, half_rows, rows_per_block, 2 * width
    )
    state_got = lax.all_to_all(
        state_back, ("slab", "comp"), split_axis=1, concat_axis=3, tiled=True
    )
    base_got = lax.all_to_all(base_back, ("slab", "comp"), split_axis=1, concat_axis=3, tiled=True)
    state_new = yz_inverse(state_got[:, 0])
    base_new = yz_inverse(base_got[:, 0])
    base_later, later_state = shifted((base_half, own_state), "seg", -1)
    prior_state = shifted(own_state, "seg", 1)
    neighbour = jnp.where(core_side == 0, later_state, prior_state)
    base_gap = (base_new - base_later).reshape(1, 3, half_rows, grid_points * grid_points)
    state_gap = (state_new - neighbour).reshape(1, 1, 3, slab_rows, grid_points * grid_points)
    return (base_gap, state_gap)


def halves(table):
    high = table.astype(np.float32).astype(ml_dtypes.bfloat16)
    low = (table - high.astype(np.float64)).astype(ml_dtypes.bfloat16)
    return high, low


def left_table(table, depth):
    padded = np.zeros((table.shape[0], depth))
    padded[:, : table.shape[1]] = table
    high, low = halves(padded)
    return np.concatenate(
        [np.concatenate([high, high], 1), np.concatenate([low, np.zeros_like(low)], 1)], 0
    )


def right_table(table, depth):
    return np.ascontiguousarray(left_table(table.T, depth).T)


def ky_values():
    index = np.arange(NKY)
    wave = np.where(index <= KEEP, index, index - (2 * KEEP + 1))
    alive = (index <= 2 * KEEP).astype(np.float64)
    return wave * alive, alive


@functools.cache
def tables():
    out = {}
    z = np.arange(N)
    kz = np.arange(NKZ)
    angle = 2 * np.pi * kz[:, None] * z[None, :] / N
    weight = np.where(kz == 0, 1.0, 2.0)[:, None] / N
    forward = np.zeros((2, 2, CHUNKS * CHUNK, 2, N))
    inverse = np.zeros((NKZ, 2, 2, 2, N))
    turned = np.zeros((NKZ, 2, 2, 2, N))
    slope = np.zeros((NKZ, 2, 2, 2, N))
    for y2 in range(2):
        forward[y2, 0, :NKZ, y2] = np.cos(angle)
        forward[y2, 1, :NKZ, y2] = -np.sin(angle)
        inverse[:, y2, 0, y2] = weight * np.cos(angle)
        inverse[:, y2, 1, y2] = -weight * np.sin(angle)
        turned[:, y2, 0, y2] = weight * np.sin(angle)
        turned[:, y2, 1, y2] = weight * np.cos(angle)
        slope[:, y2, 0, y2] = -weight * kz[:, None] * np.sin(angle)
        slope[:, y2, 1, y2] = -weight * kz[:, None] * np.cos(angle)
    forward = np.moveaxis(forward.reshape(4, CHUNKS, CHUNK, 2 * N), 1, 0)
    out["fz"] = left_table(forward.reshape(LINE, 2 * N), 128)
    out["iz"] = right_table(inverse.reshape(4 * NKZ, 2 * N), 128)
    out["izr"] = right_table(turned.reshape(4 * NKZ, 2 * N), 128)
    out["izd"] = right_table(slope.reshape(4 * NKZ, 2 * N), 128)
    ky, alive = ky_values()
    y = 2 * np.arange(HALF)[None, :] + np.arange(2)[:, None]
    phase = 2 * np.pi * ky[:, None, None] * y[None] / N
    cosine = np.cos(phase) * alive[:, None, None]
    sine = np.sin(phase) * alive[:, None, None]
    plain = np.zeros((2, NKY, 2, 2, HALF))
    plain[0, :, :, 0] = cosine
    plain[0, :, :, 1] = sine
    plain[1, :, :, 0] = -sine
    plain[1, :, :, 1] = cosine
    rotated = np.stack([-plain[1], plain[0]])
    out["fy"] = left_table(plain.reshape(ROWS, 128), 128)
    out["fyr"] = left_table(rotated.reshape(ROWS, 128), 128)
    back = np.zeros((2, 2, HALF, 2, NKY))
    cos_t = np.moveaxis(cosine, 0, -1) / N
    sin_t = np.moveaxis(sine, 0, -1) / N
    back[:, 0, :, 0] = cos_t
    back[:, 0, :, 1] = -sin_t
    back[:, 1, :, 0] = sin_t
    back[:, 1, :, 1] = cos_t
    back_slope = np.zeros_like(back)
    back_slope[..., 0, :] = ky * back[..., 1, :]
    back_slope[..., 1, :] = -ky * back[..., 0, :]
    out["iy"] = left_table(back.reshape(128, ROWS), 128)
    out["iyd"] = left_table(back_slope.reshape(128, ROWS), 128)
    grad_high, grad_low = [], []
    x = np.arange(N)
    apart = x[:HALF, None] - x[None, :]
    for cut in range(KEEP - 3, KEEP + 1):
        k = np.arange(cut + 1)
        wk = np.where(k == 0, 1.0, 2.0) / N
        arg = 2 * np.pi * apart[..., None] * k / N
        keep = (np.cos(arg) * wk).sum(-1)
        derive = (-np.sin(arg) * wk * k).sum(-1)
        table = np.zeros((2, 4, HALF, 2, 4, HALF))
        for comp in range(3):
            for side in range(2):
                rows = slice(side * HALF, (side + 1) * HALF)
                table[side, comp, :, 0, comp, :] = keep[:, rows].T
                table[side, comp, :, 1, comp, :] = derive[:, rows].T
        high, low = halves(table.reshape(256, 256))
        grad_high.append(high)
        grad_low.append(low)
    out["gxh"] = np.stack(grad_high)
    out["gxl"] = np.stack(grad_low)
    kx = np.arange(HALF)
    live = (kx <= KEEP).astype(np.float64)
    xl = np.arange(HALF)
    arg = 2 * np.pi * xl[:, None] * kx[None, :] / N
    value = np.concatenate([np.cos(arg) * live, np.sin(arg) * live], 1)
    change = np.concatenate([kx * np.sin(arg) * live, -kx * np.cos(arg) * live], 1)

    def coefficients(blocks):
        table = np.zeros((4, HALF, 2, 2 * HALF))
        for block, part, what in blocks:
            table[block, :, part] = what
        return table.reshape(LANES, LANES)

    first = coefficients([(0, 0, value), (1, 1, value), (2, 0, change), (3, 0, value)])
    last = coefficients([(0, 0, change), (1, 0, value), (2, 0, value), (3, 1, value)])
    fall = first.reshape(LANES, 2, 2, HALF)
    fall = np.stack([-kx * fall[:, :, 1], kx * fall[:, :, 0]], 2).reshape(LANES, LANES)
    out["fx"] = np.stack([right_table(part, 128) for part in (first, fall, first, last)])
    wx = np.where(kx == 0, 1.0, 2.0) * live / N
    for core in range(2):
        ix = np.zeros((4, 2, 2 * HALF, LANES))
        for side in range(2):
            xs = np.arange(HALF) + side * HALF
            arg = 2 * np.pi * kx[:, None] * xs[None, :] / N
            give = np.concatenate([np.cos(arg) * wx[:, None], np.sin(arg) * wx[:, None]], 0)
            drop = np.concatenate(
                [np.sin(arg) * (wx * kx)[:, None], -np.cos(arg) * (wx * kx)[:, None]], 0
            )
            own = slice(core * 16, core * 16 + 16)

            def put(quantity, part, lane, what):
                at = (lane + side * 64 + np.arange(what.shape[1])) % LANES
                ix[quantity, part][:, at] = what

            put(0, 0, 0, give)
            put(1, 0, 0, drop)
            put(0, 1, 32, give[:, own])
            put(1, 1, 32, drop[:, own])
            put(2, 1, 48, give[:, own])
            put(2, 0, 64, give)
            put(3, 0, 96, give)
            put(3, 1, 0, give[:, own])
        out["ix%d" % core] = np.stack(
            [right_table(part, 128) for part in ix.reshape(4, LANES, LANES)]
        )
    out["ix"] = np.stack([out.pop("ix0"), out.pop("ix1")])
    ky_rows = np.tile(ky, 2)[:, None]
    out["kyrow"] = np.broadcast_to(ky_rows, (ROWS, LANES)).astype(np.float32).copy()
    lane_kx = np.tile(kx * live, 4)
    out["kxlane"] = np.broadcast_to(lane_kx, (8, LANES)).astype(np.float32).copy()
    yy = np.arange(N)
    force = [forcing_amp * np.sin(2 * np.pi * ((w * yy) % N) / N) for w in range(1, 5)]
    force = np.repeat(np.stack(force).reshape(4, HALF, 2, 1), N, axis=3)
    out["force"] = force.reshape(4, HALF, LANES).astype(np.float32)
    merged = {}
    merged["ahead"] = np.concatenate([out["fz"], out["fy"], out["fyr"]], 0)
    gx = [out["gxh"].reshape(-1, 256), out["gxl"].reshape(-1, 256)]
    square = [out[name] for name in ("iy", "iyd", "iz", "izd", "izr")]
    merged["back"] = np.concatenate(square + gx, 0)
    merged["along"] = np.concatenate([out["fx"].reshape(-1, 256), out["ix"].reshape(-1, 256)], 0)
    merged["waves"] = np.concatenate(
        [out["kyrow"], out["kxlane"], out["force"].reshape(-1, LANES)], 0
    )
    return merged


def view(ref, index, rows=256, start=0):
    return ref.at[pl.ds(start + index * rows, rows), :]


def ahead_tables(ref):
    return view(ref, 0, 2 * LINE), view(ref, 0, 2 * ROWS, 2 * LINE), view(ref, 1, 2 * ROWS, 2 * LINE)


def split(values):
    high = values.astype(bf16)
    low = (values - high.astype(f32)).astype(bf16)
    return high, low


def dot(a, b):
    return jnp.dot(a, b, preferred_element_type=f32)


def dot_nt(a, b):
    return lax.dot_general(a, b, (((1,), (1,)), ((), ())), preferred_element_type=f32)


def stacked(values):
    high, low = split(values)
    return jnp.concatenate([high, low], 0)


def beside(values):
    high, low = split(values)
    return jnp.concatenate([high, low], 1)


def folded(result):
    rows = result.shape[0] // 2
    return result[:rows] + result[rows:]


def folded_lanes(result):
    return result[:, :LANES] + result[:, LANES:]


def padded(values, rows=128):
    return jnp.concatenate([values, jnp.zeros((rows - values.shape[0], values.shape[1]), f32)], 0)


def triple(values, high_ref, low_ref):
    high, low = split(values)
    return dot(high, high_ref) + dot(low, high_ref) + dot(high, low_ref)


def columns(yh):
    return pl.ds(pl.multiple_of(yh * LANES, LANES), LANES)


def along_y(ref, tile, kz, line=LINE):
    at = kz % CHUNK + (0 if line == LINE // CHUNKS else kz // CHUNK * (4 * CHUNK))
    return jnp.concatenate(
        [ref[tile, pl.ds(q * CHUNK + at, HALF, stride=line), :] for q in range(4)], 0
    )


def along_kz(ref, tile, yh):
    return padded(ref[tile, pl.ds(yh, ROWS, stride=HALF), :]).T


def line_rows(yh):
    return pl.ds(pl.multiple_of(yh * LINE, 8), LINE)


def plane_rows(kz):
    return pl.ds(pl.multiple_of(kz * LANES, LANES), LANES)


def lane_parts(values):
    return [values[:, at : at + LANES] for at in range(0, values.shape[1], LANES)]


def over_planes(step, first=0, last=NKZ):
    def four(index, _):
        step([first + index * 4 + k for k in range(4)])
        return 0

    count = (last - first) // 4
    lax.fori_loop(0, count, four, 0)
    if first + count * 4 < last:
        step([jnp.int32(kz) for kz in range(first + count * 4, last)])


def planes_of(chunk):
    return chunk * CHUNK, min((chunk + 1) * CHUNK, NKZ)


def over_lines(step, many):
    def some(index, _):
        step([index * many + k for k in range(many)])
        return 0

    lax.fori_loop(0, HALF // many, some, 0)


PIECES = 4


def base_kernel(core_ref, base_hbm, ahead_hbm, out_ref, lines, base_ref, ahead_ref, arrived):
    nothing = jnp.zeros((HALF, LANES), f32)
    wide = N * N // PIECES
    table = pltpu.make_async_copy(ahead_hbm, ahead_ref, arrived.at[PIECES])
    pieces = [
        pltpu.make_async_copy(
            base_hbm.at[:, :, pl.ds(n * wide, wide)],
            base_ref.at[:, :, pl.ds(n * wide, wide)],
            arrived.at[n],
        )
        for n in range(PIECES)
    ]
    pieces[0].start()
    table.start()
    for piece in pieces[1:]:
        piece.start()
    fz_ref, fy_ref, _ = ahead_tables(ahead_ref)
    table.wait()
    many = HALF // PIECES
    for n, piece in enumerate(pieces):
        piece.wait()
        yhs = range(n * many, (n + 1) * many)
        rows = []
        for yh in yhs:
            at = slice(yh * LANES, (yh + 1) * LANES)
            rows += [base_ref[i, :, at] for i in range(3)] + [nothing]
        got = folded(dot_nt(fz_ref[...], beside(jnp.concatenate(rows, 0))))
        for yh, part in zip(yhs, lane_parts(got)):
            lines[0, yh * LINE : (yh + 1) * LINE, :] = part
    start = core_ref[0] * HALF_KZ
    for pair in range(0, HALF_KZ, 2):
        ks = range(pair, min(pair + 2, HALF_KZ))
        data = jnp.concatenate([stacked(along_y(lines, 0, start + k)) for k in ks], 1)
        got = folded(dot(fy_ref[...], data))
        for k, part in zip(ks, lane_parts(got)):
            out_ref[k] = part


def flux_kernel(core_ref, base_ref, state_ref, ahead_ref, waves_ref, *refs):
    *out_refs, lines = refs
    fz_ref, fy_ref, fyr_ref = ahead_tables(ahead_ref)
    sigma = jnp.where(core_ref[0] == 0, -time_step, time_step).astype(f32)
    nothing = jnp.zeros((HALF, LANES), f32)

    def z_step(yhs):
        rows = []
        for yh in yhs:
            b = [base_ref[i, :, columns(yh)] for i in range(3)]
            t = [sigma * state_ref[i, :, columns(yh)] for i in range(3)]
            rows += [t[2] * b[0], t[0] * b[1], t[1] * b[0], t[0] * b[2]]
            rows += [t[2] * b[1], t[2] * b[2], t[1] * b[1], t[1] * b[2]]
            rows += [nothing, nothing, t[0] * b[0], nothing]
        got = lane_parts(folded(dot_nt(fz_ref[...], beside(jnp.concatenate(rows, 0)))))
        for n, yh in enumerate(yhs):
            for tile in range(3):
                lines[tile, line_rows(yh), :] = got[3 * n + tile]

    over_lines(z_step, 4)
    ky = waves_ref[:ROWS]
    lane = lax.broadcasted_iota(jnp.int32, (ROWS, LANES), 1)
    odd_block = (lane // HALF) % 2 == 1

    def y_step(chunk, kzs):
        out_ref = out_refs[chunk]
        even = []
        for pair in range(0, len(kzs), 2):
            data = [stacked(along_y(lines, 0, kz)) for kz in kzs[pair : pair + 2]]
            even += lane_parts(folded(dot(fy_ref[...], jnp.concatenate(data, 1))))
        odd = []
        for kz in kzs:
            data = [stacked(along_y(lines, tile, kz)) for tile in (1, 2)]
            odd.append(lane_parts(folded(dot(fyr_ref[...], jnp.concatenate(data, 1)))))
        for n, kz in enumerate(kzs):
            kzf = kz.astype(f32)
            plain = even[n]
            slopes = odd[n][0] * jnp.where(odd_block, kzf, ky)
            slopes = slopes + pltpu.roll(slopes, 32, 1)
            at = kz - chunk * CHUNK
            out_ref[0, at] = jnp.where(odd_block, slopes, plain)
            other = plain * jnp.where(lane >= 96, -kzf, -ky)
            other = other + pltpu.roll(other, 64, 1)
            out_ref[1, at] = jnp.where(lane >= 96, other, odd[n][1])

    for chunk in range(CHUNKS):
        over_planes(functools.partial(y_step, chunk), *planes_of(chunk))


def gradient_kernel(
    core_ref, cutoff_ref, wave_ref, base_ref, state_ref,
    here_own, here_other, there_own, there_other,
    ahead_ref, back_ref, waves_ref, *refs
):
    *out_refs, planes = refs
    fz_ref = ahead_tables(ahead_ref)[0]
    iy_ref, iyd_ref, iz_ref, izd_ref = (view(back_ref, n) for n in range(4))
    core = core_ref[0]
    cut_x, cut_y, cut_z = cutoff_ref[0], cutoff_ref[1], cutoff_ref[2]
    which = jnp.clip(cut_x - (KEEP - 3), 0, 3)
    ky = waves_ref[:ROWS]
    keep_y = jnp.where(jnp.abs(ky) <= cut_y.astype(f32), 1.0, 0.0).astype(f32)

    def kept_z(kz):
        return jnp.where(kz <= cut_z, 1.0, 0.0).astype(f32)

    def gradient_step(kzs):
        rows = []
        for kz in kzs:
            half = kz // HALF_KZ
            at = kz - half * HALF_KZ
            keep = keep_y * kept_z(kz)
            here = jnp.where(half == core, here_own[at], here_other[at]) * keep
            there = jnp.where(half == core, there_own[at], there_other[at]) * keep
            rows.append(jnp.concatenate([here, there], 1))
        high = back_ref[pl.ds(pl.multiple_of((5 + which) * 256, 256), 256), :]
        low = back_ref[pl.ds(pl.multiple_of((9 + which) * 256, 256), 256), :]
        got = triple(jnp.concatenate(rows, 0), high, low)
        data = [stacked(padded(got[n * ROWS : (n + 1) * ROWS])) for n in range(len(kzs))]
        for n, kz in enumerate(kzs):
            even = lane_parts(folded(dot(iy_ref[...], data[n])))
            planes[0, plane_rows(kz), :] = even[1]
            planes[2, plane_rows(kz), :] = even[0]
        for n in range(0, len(kzs), 2):
            both = jnp.concatenate([data[n][:, :LANES], data[n + 1][:, :LANES]], 1)
            odd = lane_parts(folded(dot(iyd_ref[...], both)))
            planes[1, plane_rows(kzs[n]), :] = odd[0]
            planes[1, plane_rows(kzs[n + 1]), :] = odd[1]

    over_planes(gradient_step)
    force_at = jnp.clip(wave_ref[0] - 1, 0, 3)
    nothing = jnp.zeros((HALF, LANES), f32)

    def physical_step(yhs):
        count = len(yhs)
        flat = [along_kz(planes, d, yh)[:96] for d in range(2) for yh in yhs]
        steep = [along_kz(planes, 2, yh)[:96] for yh in yhs]
        flat = folded_lanes(dot(beside(jnp.concatenate(flat, 0)), iz_ref[...]))
        steep = folded_lanes(dot(beside(jnp.concatenate(steep, 0)), izd_ref[...]))
        for n, yh in enumerate(yhs):
            sets = [flat[96 * n :], flat[96 * (count + n) :], steep[96 * n :]]
            grads = [[one[HALF * i : HALF * (i + 1)] for i in range(3)] for one in sets]
            b = [base_ref[i, :, columns(yh)] for i in range(3)]
            s = [state_ref[i, :, columns(yh)] for i in range(3)]
            comb, comb_base = [], []
            for i in range(3):
                coupling = sum(
                    jnp.where(core == 0, grads[j][i], grads[i][j]) * s[j] for j in range(3)
                )
                comb.append(s[i] - time_step * coupling)
                drive = sum(grads[j][i] * b[j] for j in range(3))
                if i == 0:
                    drive = drive - waves_ref[pl.ds(ROWS + 8 + force_at * HALF + yh, 1), :]
                comb_base.append(b[i] - time_step * drive)
            rows = [comb[1], comb_base[1], comb[2], comb_base[2]]
            rows += [comb[0], comb_base[0], nothing, nothing]
            got = folded(dot_nt(fz_ref[...], beside(jnp.concatenate(rows, 0))))
            depth = LINE // CHUNKS
            rows = pl.ds(pl.multiple_of(yh * depth, 8), depth)
            for tile, part in enumerate(lane_parts(got)):
                for chunk in range(CHUNKS):
                    out_refs[chunk][tile, rows, :] = part[chunk * depth : (chunk + 1) * depth]

    over_lines(physical_step, 8)


def spectral_kernel(
    chunk, core_ref, cutoff_ref, lines_ref, flux_ref,
    ahead_ref, along_ref, waves_ref, near_ref, far_ref,
):
    _, fy_ref, fyr_ref = ahead_tables(ahead_ref)
    core = core_ref[0]
    cut_x, cut_y, cut_z = cutoff_ref[0], cutoff_ref[1], cutoff_ref[2]
    first, last = planes_of(chunk)
    extra = last - first
    ky = waves_ref[:ROWS]
    kx = waves_ref[ROWS : ROWS + 1]
    keep_y = jnp.where(jnp.abs(ky) <= cut_y.astype(f32), 1.0, 0.0).astype(f32)
    keep_x = jnp.where(kx <= cut_x.astype(f32), 1.0, 0.0).astype(f32)
    keep_xy = keep_y * keep_x
    square_xy = ky * ky + kx * kx
    lane = lax.broadcasted_iota(jnp.int32, (ROWS, LANES), 1)
    near_ref[extra] = jnp.zeros((ROWS, LANES), f32)
    far_ref[extra] = jnp.zeros((ROWS, LANES), f32)

    def kept_z(kz):
        return jnp.where(kz <= cut_z, 1.0, 0.0).astype(f32)

    def spectral_step(kzs):
        fields = [[], [], []]
        for pair in range(0, len(kzs), 2):
            ks = kzs[pair : pair + 2]
            data = [
                jnp.concatenate(
                    [stacked(along_y(lines_ref, t, kz, LINE // CHUNKS)) for kz in ks], 1
                )
                for t in (0, 1)
            ]
            even = lane_parts(folded(dot(fy_ref[...], data[0])))
            odd = lane_parts(folded(dot(fyr_ref[...], data[1])))
            for n, kz in enumerate(ks):
                flux = flux_ref[0, kz - first]
                fields[0].append(odd[n] + flux_ref[1, kz - first])
                fields[1].append(jnp.where(lane < 64, even[n], flux))
                fields[2].append(jnp.where(lane < 64, flux, even[n]))
        data = [beside(jnp.concatenate(field, 0)) for field in fields]
        modes = [folded_lanes(dot(data[max(n - 1, 0)], view(along_ref, n)[...])) for n in range(4)]
        results = [[], [], [], []]
        for n, kz in enumerate(kzs):
            kzf = kz.astype(f32)
            vx, slope, uy, uz = (mode[n * ROWS : (n + 1) * ROWS] for mode in modes)
            square = square_xy + kzf * kzf
            factor = keep_xy * kept_z(kz) / (1.0 + viscosity * time_step * square)
            share = (slope + ky * uy + kzf * uz) / jnp.where(square > 0, square, 1.0)
            results[0].append(factor * vx)
            results[1].append(factor * share)
            results[2].append(factor * (uy - ky * share))
            results[3].append(factor * (uz - kzf * share))
        got = [
            dot(
                beside(jnp.concatenate(result, 0)),
                along_ref[pl.ds(pl.multiple_of((4 + core * 4 + n) * 256, 256), 256), :],
            )
            for n, result in enumerate(results)
        ]
        got = [folded_lanes(part) for part in (got[0] + got[1], got[2], got[3])]
        for n, kz in enumerate(kzs):
            x, y, z = (part[n * ROWS : (n + 1) * ROWS] for part in got)
            near_ref[kz - first] = jnp.where(lane < 48, x, jnp.where(lane < 96, y, z))
            away = jnp.where(
                (lane >= 64) & (lane < 112), x, jnp.where((lane >= 32) & (lane < 64), z, y)
            )
            far_ref[kz - first] = pltpu.roll(away, 64, 1)
            shift = (kz - first) * 16
            near_ref[extra] += pltpu.roll(jnp.where(lane < 16, z, 0.0), shift, 1)
            rest = jnp.where((lane >= 64) & (lane < 80), z, 0.0)
            far_ref[extra] += pltpu.roll(rest, (shift + 64) % LANES, 1)

    over_planes(spectral_step, first, last)


def inverse_y(near_ref, far_ref, iy_ref, planes):
    count = near_ref.shape[0] - 1
    rest = near_ref[count] + far_ref[count]
    for kz in range(count):
        turned = pltpu.roll(rest, (LANES - kz * 16) % LANES, 1) if kz else rest
        data = jnp.concatenate([near_ref[kz] + far_ref[kz], turned], 1)
        got = lane_parts(folded(dot(iy_ref[...], stacked(padded(data)))))
        for tile in range(2):
            planes[tile, kz * LANES : (kz + 1) * LANES, :] = got[tile]
    if count < CHUNK:
        blank = jnp.zeros(((CHUNK - count) * LANES, LANES), f32)
        for tile in range(2):
            planes[tile, count * LANES :, :] = blank


def inverse_kernel(near_a, far_a, near_b, far_b, back_ref, planes_a, planes_b):
    iy_ref = view(back_ref, 0)
    inverse_y(near_a, far_a, iy_ref, planes_a)
    inverse_y(near_b, far_b, iy_ref, planes_b)


def final_kernel(
    near_ref, far_ref, planes_a, planes_b, state_ref, base_ref, back_ref,
    base_out, state_out, planes_c,
):
    iy_ref, iz_ref, izr_ref = (view(back_ref, n) for n in (0, 2, 4))
    inverse_y(near_ref, far_ref, iy_ref, planes_c)

    def along_chunks(tile, yh):
        parts = [
            ref[tile, pl.ds(yh, 4 * CHUNK, stride=HALF), :]
            for ref in (planes_a, planes_b, planes_c)
        ]
        return padded(jnp.concatenate(parts, 0)).T

    def z_step(yhs):
        data = [along_chunks(0, yh) for yh in yhs]
        rest = [along_chunks(1, yh)[:16] for yh in yhs]
        turned = beside(jnp.concatenate([one[:48] for one in data], 0))
        plain = beside(jnp.concatenate([one[48:] for one in data] + rest, 0))
        turned = folded_lanes(dot(turned, izr_ref[...]))
        plain = folded_lanes(dot(plain, iz_ref[...]))
        for n, yh in enumerate(yhs):
            at = columns(yh)
            first = turned[48 * n : 48 * n + 48]
            second = plain[80 * n : 80 * n + 80]
            third = plain[80 * len(yhs) + 16 * n :][:16]
            state_out[0, :, at] = first[:32] - state_ref[0, :, at]
            state_out[1, :, at] = second[16:48] - state_ref[1, :, at]
            state_out[2, :, at] = second[48:80] - state_ref[2, :, at]
            base_out[0, :, at] = first[32:48] - base_ref[0, :, at]
            base_out[1, :, at] = second[:16] - base_ref[1, :, at]
            base_out[2, :, at] = third - base_ref[2, :, at]

    over_lines(z_step, 8)


interpret = False


def call(kernel, outs, scratch, inputs, room, in_smem=0, in_hbm=0):
    whole = pl.BlockSpec(memory_space=pltpu.VMEM)
    small = pl.BlockSpec(memory_space=pltpu.SMEM)
    return pl.pallas_call(
        kernel,
        out_shape=outs,
        in_specs=[small] * in_smem
        + [pl.BlockSpec(memory_space=pltpu.HBM)] * in_hbm
        + [whole] * (len(inputs) - in_smem - in_hbm),
        out_specs=jax.tree.map(lambda _: whole, outs),
        scratch_shapes=scratch,
        compiler_params=pltpu.CompilerParams(vmem_limit_bytes=room * 2**20),
        cost_estimate=pl.CostEstimate(flops=1000, bytes_accessed=1000, transcendentals=0),
        interpret=interpret,
    )(*inputs)


def body(base, state, wavenumber, cutoff):
    t = {name: jnp.asarray(value) for name, value in tables().items()}
    core = lax.axis_index("comp")
    seg_count = lax.axis_size("seg")
    own_base = base[0]
    own_state = state[0, 0]
    base_half = lax.dynamic_slice_in_dim(own_base, core * 16, 16, 1)
    back = [((s + 1) % seg_count, s) for s in range(seg_count)]
    around = [(2 * i, 2 * o) for i, o in back] + [(2 * o + 1, 2 * i + 1) for i, o in back]
    base_next = lax.ppermute(base_half, "seg", back)
    state_next = lax.ppermute(own_state, ("seg", "comp"), around)
    sds = jax.ShapeDtypeStruct
    core_at = core.reshape(1)
    swap = [(0, 1), (1, 0)]
    here_own = call(
        base_kernel,
        sds((HALF_KZ, ROWS, LANES), f32),
        [
            pltpu.VMEM((1, HALF * LINE, LANES), f32),
            pltpu.VMEM(own_base.shape, f32),
            pltpu.VMEM(t["ahead"].shape, bf16),
            pltpu.SemaphoreType.DMA((PIECES + 1,)),
        ],
        [core_at, own_base, t["ahead"]],
        room=56,
        in_smem=1,
        in_hbm=2,
    )
    there_own = lax.ppermute(here_own, "slab", swap)
    here_other = lax.ppermute(here_own, "comp", swap)
    counts = [planes_of(chunk)[1] - planes_of(chunk)[0] for chunk in range(CHUNKS)]
    flux = call(
        flux_kernel,
        [sds((2, count, ROWS, LANES), f32) for count in counts],
        [pltpu.VMEM((3, HALF * LINE, LANES), f32)],
        [core_at, own_base, own_state, t["ahead"], t["waves"]],
        room=16,
        in_smem=1,
    )
    there_own, flux = lax.optimization_barrier((there_own, flux))
    there_other = lax.ppermute(there_own, "comp", swap)
    lines = call(
        gradient_kernel,
        [sds((2, HALF * 4 * CHUNK, LANES), f32)] * CHUNKS,
        [pltpu.VMEM((3, NKZ * LANES, LANES), f32)],
        [core_at, cutoff, wavenumber, own_base, own_state]
        + [here_own, here_other, there_own, there_other, t["ahead"], t["back"], t["waves"]],
        room=20,
        in_smem=3,
    )
    near, far = [], []
    for chunk in range(CHUNKS):
        near_part, far_part = call(
            functools.partial(spectral_kernel, chunk),
            [sds((counts[chunk] + 1, ROWS, LANES), f32)] * 2,
            [],
            [core_at, cutoff, lines[chunk], flux[chunk], t["ahead"], t["along"], t["waves"]],
            room=10,
            in_smem=2,
        )
        near.append(near_part)
        far.append(lax.ppermute(far_part, "slab", swap))
    planes = sds((2, CHUNK * LANES, LANES), f32)
    planes_a, planes_b = call(
        inverse_kernel, [planes] * 2, [], [near[0], far[0], near[1], far[1], t["back"]], room=10
    )
    base_gap, state_gap = call(
        final_kernel,
        [sds((3, 16, N * N), f32), sds((3, HALF, N * N), f32)],
        [pltpu.VMEM((2, CHUNK * LANES, LANES), f32)],
        [near[2], far[2], planes_a, planes_b, state_next, base_next, t["back"]],
        room=16,
    )
    return base_gap[None], state_gap[None, None]


def solution(mesh):
    paired = mesh.shape["slab"] == 2 and mesh.shape["comp"] == 2
    return jax.shard_map(
        body if paired else general_body,
        mesh=mesh,
        in_specs=(
            P(("groups", "seg"), None, "slab", None),
            P(("groups", "seg"), "comp", None, "slab", None),
            P("groups"),
            P("groups"),
        ),
        out_specs=(
            P(("groups", "seg"), None, ("slab", "comp"), None),
            P(("groups", "seg"), "comp", None, "slab", None),
        ),
        check_vma=False,
    )
```

```python
import functools

import jax
import jax.numpy as jnp
import ml_dtypes
import numpy as np
from jax import lax
from jax.experimental import pallas as pl
from jax.experimental.pallas import tpu as pltpu
from jax.sharding import PartitionSpec as P

N = 64
HALF = 32
KEEP = N // 3
NKZ = KEEP + 1
NKY = 44
ROWS = 2 * NKY
CHUNK = 8
CHUNKS = 3
LINE = CHUNKS * CHUNK * 4
HALF_KZ = NKZ // 2
LANES = 128

viscosity = 0.025
time_step = 0.02
forcing_amp = 10.0

f32 = jnp.float32
bf16 = jnp.bfloat16


highest = lax.Precision.HIGHEST


def swapped(value, axis, apart):
    mask = 2**apart
    pairs = [(source, source ^ mask) for source in range(lax.axis_size(axis))]
    return lax.ppermute(value, axis, pairs)


def shifted(block, axis, distance):
    devices = range(lax.axis_size(axis))
    route = [((i - distance) % len(devices), i) for i in devices]
    return lax.ppermute(block, axis, route)


def wavenumbers(grid_points):
    position = jnp.arange(grid_points, dtype=jnp.int32)
    return jnp.where(position < grid_points // 2, position, position - grid_points)


def phases(first, second, grid_points):
    product = jnp.mod(first[:, None] * second[None, :], grid_points)
    return product.astype(jnp.float32) * (2.0 * jnp.pi / grid_points)


def combine(partial_value, columns):
    cosine_part = partial_value[0]
    sine_part = partial_value[1]
    real_part = cosine_part[..., :columns] - sine_part[..., columns:]
    imag_part = cosine_part[..., columns:] + sine_part[..., :columns]
    return jnp.concatenate([real_part, imag_part], axis=-1)


def times_unit(values, wave, columns):
    return jnp.concatenate([-wave * values[..., columns:], wave * values[..., :columns]], axis=-1)


def doubled(values):
    return jnp.concatenate([values, values], axis=-1)


def general_body(base, state, wavenumber, cutoff):
    grid_points = N
    base = base.reshape(base.shape[0], 3, base.shape[2], grid_points, grid_points)
    state = state.reshape(
        state.shape[0], state.shape[1], 3, state.shape[3], grid_points, grid_points
    )
    slab_rows = state.shape[3]
    half_rows = slab_rows // 2
    slab_count = lax.axis_size("slab")
    group_count = slab_count * lax.axis_size("comp")
    core_side = lax.axis_index("comp")
    block_number = lax.axis_index(("slab", "comp"))
    base_whole = base[0]
    base_half = lax.dynamic_slice_in_dim(base_whole, core_side * half_rows, half_rows, 1)
    own_state = state[0, 0]
    spectrum = wavenumbers(grid_points)
    one_third = grid_points // 3
    row_total = (2 * one_third + group_count) // group_count * group_count
    row_index = jnp.arange(row_total, dtype=jnp.int32)
    row_alive_mask = row_index <= 2 * one_third
    row_wave = jnp.where(row_index <= one_third, row_index, row_index - (2 * one_third + 1))
    row_wave = jnp.where(row_alive_mask, row_wave, 0)
    width = grid_points // 2
    rows_per_block = row_total // group_count
    alive_flags = row_alive_mask.astype(jnp.float32)
    grid_index = jnp.arange(grid_points, dtype=jnp.int32)
    column_index = grid_index[:width]
    angle_grid = phases(grid_index, grid_index, grid_points)
    angle_ahead = phases(grid_index, column_index, grid_points)
    angle_behind = phases(column_index, grid_index, grid_points)
    column_weight = jnp.where(column_index == 0, 1.0, 2.0).astype(jnp.float32)[:, None]
    forward_z = jnp.concatenate([jnp.cos(angle_ahead), -jnp.sin(angle_ahead)], axis=1)
    inverse_z = (
        jnp.concatenate(
            [jnp.cos(angle_behind) * column_weight, -jnp.sin(angle_behind) * column_weight], axis=0
        )
        / grid_points
    )
    phase_angle_rows = phases(row_wave, grid_index, grid_points)
    forward_transform_y = (
        jnp.stack([jnp.cos(phase_angle_rows), -jnp.sin(phase_angle_rows)])
        * alive_flags[None, :, None]
    )
    inverse_y = (
        jnp.stack([jnp.cos(phase_angle_rows).T, jnp.sin(phase_angle_rows).T])
        * alive_flags[None, None, :]
        / grid_points
    )
    forward_x = jnp.stack([jnp.cos(angle_grid), -jnp.sin(angle_grid)])
    inverse_x = jnp.stack([jnp.cos(angle_grid), jnp.sin(angle_grid)]) / grid_points
    table_ahead = forward_x.reshape(2, grid_points, slab_count, slab_rows)
    table_back = inverse_x.reshape(2, slab_count, slab_rows, grid_points)
    local_wave = lax.dynamic_slice_in_dim(row_wave, block_number * rows_per_block, rows_per_block)
    local_alive_mask = lax.dynamic_slice_in_dim(
        alive_flags, block_number * rows_per_block, rows_per_block
    )
    shape_local = (grid_points, rows_per_block, width)
    wave_x = jnp.broadcast_to(spectrum[:, None, None], shape_local)
    wave_y = jnp.broadcast_to(local_wave[None, :, None], shape_local)
    wave_z = jnp.broadcast_to(spectrum[:width][None, None, :], shape_local)
    inside = (
        (jnp.abs(wave_x) <= cutoff[0])
        & (jnp.abs(wave_y) <= cutoff[1])
        & (jnp.abs(wave_z) <= cutoff[2])
    )
    keep_mask = doubled(inside.astype(jnp.float32) * local_alive_mask[None, :, None])
    float_x = wave_x.astype(jnp.float32)
    float_y = wave_y.astype(jnp.float32)
    float_z = wave_z.astype(jnp.float32)
    ksquare = float_x * float_x + float_y * float_y + float_z * float_z
    safe_square = doubled(jnp.where(ksquare > 0, ksquare, jnp.ones_like(ksquare)))
    damping = doubled(1.0 / (1.0 + viscosity * time_step * ksquare))
    double_x = doubled(float_x)
    double_y = doubled(float_y)
    double_z = doubled(float_z)

    def project(field):
        divergence = (double_x * field[0] + double_y * field[1] + double_z * field[2]) / safe_square
        return jnp.stack(
            [
                field[0] - double_x * divergence,
                field[1] - double_y * divergence,
                field[2] - double_z * divergence,
            ]
        )

    def yz_forward(field):
        along_z = jnp.einsum("...z,zk->...k", field, forward_z, precision=highest)
        partial_value = jnp.einsum(
            "sry,...yk->s...rk", forward_transform_y, along_z, precision=highest
        )
        return combine(partial_value, width)

    def yz_inverse(modes):
        partial_value = jnp.einsum("syr,...rk->s...yk", inverse_y, modes, precision=highest)
        return jnp.einsum(
            "...k,kz->...z", combine(partial_value, width), inverse_z, precision=highest
        )

    def spectral(state_fields, base_fields):
        state_modes = yz_forward(state_fields)[:, :, None]
        base_modes = yz_forward(base_fields)[:, :, None]
        state_got = lax.all_to_all(
            state_modes, ("slab", "comp"), split_axis=4, concat_axis=2, tiled=True
        )
        base_got = lax.all_to_all(
            base_modes, ("slab", "comp"), split_axis=4, concat_axis=2, tiled=True
        )
        item_count = state_got.shape[0]
        part_count = state_got.shape[1]
        state_split = state_got.reshape(
            item_count, part_count, slab_count, 2, slab_rows, rows_per_block, 2 * width
        )
        state_partial = jnp.einsum(
            "srpx,ijpcxyk->sijcryk", table_ahead, state_split, precision=highest
        )
        base_lined = base_got.reshape(item_count, 1, grid_points, rows_per_block, 2 * width)
        base_partial = jnp.einsum("srx,ijxyk->sijryk", forward_x, base_lined, precision=highest)
        return (combine(state_partial, width), combine(base_partial, width))

    state_first, base_first = spectral(own_state[:, None], base_half[:, None])
    state_hat = state_first[:, 0] * keep_mask
    base_hat = base_first[:, 0] * keep_mask
    grad_hat = jnp.stack(
        [
            times_unit(base_hat, float_x, width),
            times_unit(base_hat, float_y, width),
            times_unit(base_hat, float_z, width),
        ],
        axis=1,
    )
    grad_hat = grad_hat.reshape(9, grid_points, rows_per_block, 2 * width)
    grad_partial = jnp.einsum("sxr,iryk->sixyk", inverse_x, grad_hat, precision=highest)
    grad_spread = combine(grad_partial, width).reshape(
        9, group_count, half_rows, rows_per_block, 2 * width
    )
    own_rows = yz_inverse(
        lax.all_to_all(grad_spread, ("slab", "comp"), split_axis=1, concat_axis=3, tiled=True)[:, 0]
    )
    other_rows = swapped(own_rows, "comp", 0)
    gradient = jnp.where(
        core_side == 0,
        jnp.concatenate([own_rows, other_rows], axis=1),
        jnp.concatenate([other_rows, own_rows], axis=1),
    )
    gradient = gradient.reshape(3, 3, slab_rows, grid_points, grid_points)
    gradient_half = lax.dynamic_slice_in_dim(gradient, core_side * half_rows, half_rows, 2)
    flux_terms = own_state[:, None] * base_whole[None, :]
    coupling_matrix = jnp.where(core_side == 0, gradient, jnp.swapaxes(gradient, 0, 1))
    coupling = jnp.sum(coupling_matrix * own_state[None, :], axis=1)
    forcing_phase = phases(wavenumber, grid_index, grid_points)[0]
    forcing = forcing_amp * jnp.sin(forcing_phase)[None, :, None]
    base_drive = jnp.sum(gradient_half * base_half[None, :], axis=1)
    base_drive = jnp.concatenate([base_drive[:1] - forcing[None], base_drive[1:]], axis=0)
    state_fields = jnp.concatenate([flux_terms, coupling[:, None]], axis=1)
    drive_modes, base_modes_two = spectral(state_fields, base_drive[:, None])
    orient = jnp.array([1.0, -1.0], dtype=jnp.float32)[None, :, None, None, None]
    divergence = (
        times_unit(drive_modes[:, 0], float_x, width)
        + times_unit(drive_modes[:, 1], float_y, width)
        + times_unit(drive_modes[:, 2], float_z, width)
    )
    state_drive = keep_mask * (orient * divergence + drive_modes[:, 3])
    new_hat = damping * project(state_hat - time_step * state_drive)
    base_new_hat = damping * project(base_hat - time_step * keep_mask * base_modes_two[:, 0])
    state_partial = jnp.einsum("spxr,icryk->sipcxyk", table_back, new_hat, precision=highest)
    state_back = combine(state_partial, width).reshape(
        3, group_count, slab_rows, rows_per_block, 2 * width
    )
    base_partial = jnp.einsum("sxr,iryk->sixyk", inverse_x, base_new_hat, precision=highest)
    base_back = combine(base_partial, width).reshape(
        3, group_count, half_rows, rows_per_block, 2 * width
    )
    state_got = lax.all_to_all(
        state_back, ("slab", "comp"), split_axis=1, concat_axis=3, tiled=True
    )
    base_got = lax.all_to_all(base_back, ("slab", "comp"), split_axis=1, concat_axis=3, tiled=True)
    state_new = yz_inverse(state_got[:, 0])
    base_new = yz_inverse(base_got[:, 0])
    base_later, later_state = shifted((base_half, own_state), "seg", -1)
    prior_state = shifted(own_state, "seg", 1)
    neighbour = jnp.where(core_side == 0, later_state, prior_state)
    base_gap = (base_new - base_later).reshape(1, 3, half_rows, grid_points * grid_points)
    state_gap = (state_new - neighbour).reshape(1, 1, 3, slab_rows, grid_points * grid_points)
    return (base_gap, state_gap)


def halves(table):
    high = table.astype(np.float32).astype(ml_dtypes.bfloat16)
    low = (table - high.astype(np.float64)).astype(ml_dtypes.bfloat16)
    return high, low


def left_table(table, depth):
    padded = np.zeros((table.shape[0], depth))
    padded[:, : table.shape[1]] = table
    high, low = halves(padded)
    return np.concatenate(
        [np.concatenate([high, high], 1), np.concatenate([low, np.zeros_like(low)], 1)], 0
    )


def right_table(table, depth):
    return np.ascontiguousarray(left_table(table.T, depth).T)


def ky_values():
    index = np.arange(NKY)
    wave = np.where(index <= KEEP, index, index - (2 * KEEP + 1))
    alive = (index <= 2 * KEEP).astype(np.float64)
    return wave * alive, alive


@functools.cache
def tables():
    out = {}
    z = np.arange(N)
    kz = np.arange(NKZ)
    angle = 2 * np.pi * kz[:, None] * z[None, :] / N
    weight = np.where(kz == 0, 1.0, 2.0)[:, None] / N
    forward = np.zeros((2, 2, CHUNKS * CHUNK, 2, N))
    inverse = np.zeros((NKZ, 2, 2, 2, N))
    turned = np.zeros((NKZ, 2, 2, 2, N))
    slope = np.zeros((NKZ, 2, 2, 2, N))
    for y2 in range(2):
        forward[y2, 0, :NKZ, y2] = np.cos(angle)
        forward[y2, 1, :NKZ, y2] = -np.sin(angle)
        inverse[:, y2, 0, y2] = weight * np.cos(angle)
        inverse[:, y2, 1, y2] = -weight * np.sin(angle)
        turned[:, y2, 0, y2] = weight * np.sin(angle)
        turned[:, y2, 1, y2] = weight * np.cos(angle)
        slope[:, y2, 0, y2] = -weight * kz[:, None] * np.sin(angle)
        slope[:, y2, 1, y2] = -weight * kz[:, None] * np.cos(angle)
    forward = np.moveaxis(forward.reshape(4, CHUNKS, CHUNK, 2 * N), 1, 0)
    out["fz"] = left_table(forward.reshape(LINE, 2 * N), 128)
    out["iz"] = right_table(inverse.reshape(4 * NKZ, 2 * N), 128)
    out["izr"] = right_table(turned.reshape(4 * NKZ, 2 * N), 128)

    def by_half(table):
        wide = np.zeros((2, HALF_KZ + 1, 4, 2 * N))
        wide[:, :HALF_KZ] = table.reshape(2, HALF_KZ, 4, 2 * N)
        return right_table(wide.reshape(8 * HALF_KZ + 8, 2 * N), 128)

    out["izg"] = by_half(inverse)
    out["izd"] = by_half(slope)
    ky, alive = ky_values()
    y = 2 * np.arange(HALF)[None, :] + np.arange(2)[:, None]
    phase = 2 * np.pi * ky[:, None, None] * y[None] / N
    cosine = np.cos(phase) * alive[:, None, None]
    sine = np.sin(phase) * alive[:, None, None]
    plain = np.zeros((2, NKY, 2, 2, HALF))
    plain[0, :, :, 0] = cosine
    plain[0, :, :, 1] = sine
    plain[1, :, :, 0] = -sine
    plain[1, :, :, 1] = cosine
    rotated = np.stack([-plain[1], plain[0]])
    out["fy"] = left_table(plain.reshape(ROWS, 128), 128)
    out["fyr"] = left_table(rotated.reshape(ROWS, 128), 128)
    back = np.zeros((2, 2, HALF, 2, NKY))
    cos_t = np.moveaxis(cosine, 0, -1) / N
    sin_t = np.moveaxis(sine, 0, -1) / N
    back[:, 0, :, 0] = cos_t
    back[:, 0, :, 1] = -sin_t
    back[:, 1, :, 0] = sin_t
    back[:, 1, :, 1] = cos_t
    back_slope = np.zeros_like(back)
    back_slope[..., 0, :] = ky * back[..., 1, :]
    back_slope[..., 1, :] = -ky * back[..., 0, :]
    out["iy"] = left_table(back.reshape(128, ROWS), 128)
    out["iyd"] = left_table(back_slope.reshape(128, ROWS), 128)
    grad_high, grad_low = [], []
    x = np.arange(N)
    apart = x[:HALF, None] - x[None, :]
    for cut in range(KEEP - 3, KEEP + 1):
        k = np.arange(cut + 1)
        wk = np.where(k == 0, 1.0, 2.0) / N
        arg = 2 * np.pi * apart[..., None] * k / N
        keep = (np.cos(arg) * wk).sum(-1)
        derive = (-np.sin(arg) * wk * k).sum(-1)
        table = np.zeros((2, 4, HALF, 2, 4, HALF))
        for comp in range(3):
            for side in range(2):
                rows = slice(side * HALF, (side + 1) * HALF)
                table[side, comp, :, 0, comp, :] = keep[:, rows].T
                table[side, comp, :, 1, comp, :] = derive[:, rows].T
        high, low = halves(table.reshape(256, 256))
        grad_high.append(high)
        grad_low.append(low)
    out["gxh"] = np.stack(grad_high)
    out["gxl"] = np.stack(grad_low)
    kx = np.arange(HALF)
    live = (kx <= KEEP).astype(np.float64)
    xl = np.arange(HALF)
    arg = 2 * np.pi * xl[:, None] * kx[None, :] / N
    value = np.concatenate([np.cos(arg) * live, np.sin(arg) * live], 1)
    change = np.concatenate([kx * np.sin(arg) * live, -kx * np.cos(arg) * live], 1)

    def coefficients(blocks):
        table = np.zeros((4, HALF, 2, 2 * HALF))
        for block, part, what in blocks:
            table[block, :, part] = what
        return table.reshape(LANES, LANES)

    first = coefficients([(0, 0, value), (1, 1, value), (2, 0, change), (3, 0, value)])
    last = coefficients([(0, 0, change), (1, 0, value), (2, 0, value), (3, 1, value)])
    fall = first.reshape(LANES, 2, 2, HALF)
    fall = np.stack([-kx * fall[:, :, 1], kx * fall[:, :, 0]], 2).reshape(LANES, LANES)
    out["fx"] = np.stack([right_table(part, 128) for part in (first, fall, first, last)])
    wx = np.where(kx == 0, 1.0, 2.0) * live / N
    for core in range(2):
        ix = np.zeros((4, 2, 2 * HALF, LANES))
        for side in range(2):
            xs = np.arange(HALF) + side * HALF
            arg = 2 * np.pi * kx[:, None] * xs[None, :] / N
            give = np.concatenate([np.cos(arg) * wx[:, None], np.sin(arg) * wx[:, None]], 0)
            drop = np.concatenate(
                [np.sin(arg) * (wx * kx)[:, None], -np.cos(arg) * (wx * kx)[:, None]], 0
            )
            own = slice(core * 16, core * 16 + 16)

            def put(quantity, part, lane, what):
                at = (lane + side * 64 + np.arange(what.shape[1])) % LANES
                ix[quantity, part][:, at] = what

            put(0, 0, 0, give)
            put(1, 0, 0, drop)
            put(0, 1, 32, give[:, own])
            put(1, 1, 32, drop[:, own])
            put(2, 1, 48, give[:, own])
            put(2, 0, 64, give)
            put(3, 0, 96, give)
            put(3, 1, 0, give[:, own])
        out["ix%d" % core] = np.stack(
            [right_table(part, 128) for part in ix.reshape(4, LANES, LANES)]
        )
    out["ix"] = np.stack([out.pop("ix0"), out.pop("ix1")])
    merged = {}
    merged["ahead"] = np.concatenate([out["fz"], out["fy"], out["fyr"]], 0)
    gx = [out["gxh"].reshape(-1, 256), out["gxl"].reshape(-1, 256)]
    square = [out[name] for name in ("iy", "iyd", "izg", "izd", "iz", "izr")]
    merged["back"] = np.concatenate(square + gx, 0)
    merged["along"] = np.concatenate([out["fx"].reshape(-1, 256), out["ix"].reshape(-1, 256)], 0)
    return merged


def view(ref, index, rows=256, start=0):
    return ref.at[pl.ds(start + index * rows, rows), :]


def ahead_tables(ref):
    return view(ref, 0, 2 * LINE), view(ref, 0, 2 * ROWS, 2 * LINE), view(ref, 1, 2 * ROWS, 2 * LINE)


def ky_rows():
    row = lax.broadcasted_iota(jnp.int32, (ROWS, LANES), 0)
    index = jnp.where(row < NKY, row, row - NKY)
    wave = jnp.where(index <= KEEP, index, index - (2 * KEEP + 1))
    return jnp.where(index <= 2 * KEEP, wave, 0).astype(f32)


def kx_lanes():
    lane = lax.broadcasted_iota(jnp.int32, (1, LANES), 1) % HALF
    return jnp.where(lane <= KEEP, lane, 0).astype(f32)


def split(values):
    high = values.astype(bf16)
    low = (values - high.astype(f32)).astype(bf16)
    return high, low


def dot(a, b):
    return jnp.dot(a, b, preferred_element_type=f32)


def dot_nt(a, b):
    return lax.dot_general(a, b, (((1,), (1,)), ((), ())), preferred_element_type=f32)


def stacked(values):
    high, low = split(values)
    return jnp.concatenate([high, low], 0)


def beside(values):
    high, low = split(values)
    return jnp.concatenate([high, low], 1)


def folded(result):
    rows = result.shape[0] // 2
    return result[:rows] + result[rows:]


def folded_lanes(result):
    return result[:, :LANES] + result[:, LANES:]


def padded(values, rows=128):
    return jnp.concatenate([values, jnp.zeros((rows - values.shape[0], values.shape[1]), f32)], 0)


def triple(values, high_ref, low_ref):
    high, low = split(values)
    return dot(high, high_ref) + dot(low, high_ref) + dot(high, low_ref)


def columns(yh):
    return pl.ds(pl.multiple_of(yh * LANES, LANES), LANES)


def along_y(ref, tile, kz, line=LINE):
    at = kz % CHUNK + (0 if line == LINE // CHUNKS else kz // CHUNK * (4 * CHUNK))
    return jnp.concatenate(
        [ref[tile, pl.ds(q * CHUNK + at, HALF, stride=line), :] for q in range(4)], 0
    )


def line_rows(yh):
    return pl.ds(pl.multiple_of(yh * LINE, 8), LINE)


def lane_parts(values):
    return [values[:, at : at + LANES] for at in range(0, values.shape[1], LANES)]


def over_planes(step, first=0, last=NKZ):
    def four(index, _):
        step([first + index * 4 + k for k in range(4)])
        return 0

    count = (last - first) // 4
    lax.fori_loop(0, count, four, 0)
    if first + count * 4 < last:
        step([jnp.int32(kz) for kz in range(first + count * 4, last)])


def planes_of(chunk):
    return chunk * CHUNK, min((chunk + 1) * CHUNK, NKZ)


def over_lines(step, many, first=0, last=HALF):
    def some(index, _):
        step([first + index * many + k for k in range(many)])
        return 0

    lax.fori_loop(0, (last - first) // many, some, 0)


PIECES = 4


def base_kernel(core_ref, base_hbm, ahead_hbm, out_ref, lines, base_ref, ahead_ref, arrived):
    nothing = jnp.zeros((HALF, LANES), f32)
    wide = N * N // PIECES
    table = pltpu.make_async_copy(ahead_hbm, ahead_ref, arrived.at[PIECES])
    pieces = [
        pltpu.make_async_copy(
            base_hbm.at[:, :, pl.ds(n * wide, wide)],
            base_ref.at[:, :, pl.ds(n * wide, wide)],
            arrived.at[n],
        )
        for n in range(PIECES)
    ]
    pieces[0].start()
    table.start()
    for piece in pieces[1:]:
        piece.start()
    fz_ref, fy_ref, _ = ahead_tables(ahead_ref)
    table.wait()
    many = HALF // PIECES
    for n, piece in enumerate(pieces):
        piece.wait()
        yhs = range(n * many, (n + 1) * many)
        rows = []
        for yh in yhs:
            at = slice(yh * LANES, (yh + 1) * LANES)
            rows += [base_ref[i, :, at] for i in range(3)] + [nothing]
        got = folded(dot_nt(fz_ref[...], beside(jnp.concatenate(rows, 0))))
        for yh, part in zip(yhs, lane_parts(got)):
            lines[0, yh * LINE : (yh + 1) * LINE, :] = part
    start = core_ref[0] * HALF_KZ
    for pair in range(0, HALF_KZ, 2):
        ks = range(pair, min(pair + 2, HALF_KZ))
        data = jnp.concatenate([stacked(along_y(lines, 0, start + k)) for k in ks], 1)
        got = folded(dot(fy_ref[...], data))
        for k, part in zip(ks, lane_parts(got)):
            out_ref[k] = part


def flux_kernel(core_ref, base_hbm, state_hbm, ahead_hbm, *refs):
    *out_refs, lines, base_ref, state_ref, ahead_ref, result, arrived, left = refs
    wide = N * N // PIECES
    pieces = [pltpu.make_async_copy(ahead_hbm, ahead_ref, arrived.at[2 * PIECES])]
    for n in range(PIECES):
        for k, (source, target) in enumerate(((base_hbm, base_ref), (state_hbm, state_ref))):
            at = pl.ds(n * wide, wide)
            pieces.append(
                pltpu.make_async_copy(
                    source.at[:, :, at], target.at[:, :, at], arrived.at[2 * n + k]
                )
            )
    for piece in pieces:
        piece.start()
    fz_ref, fy_ref, fyr_ref = ahead_tables(ahead_ref)
    sigma = jnp.where(core_ref[0] == 0, -time_step, time_step).astype(f32)
    nothing = jnp.zeros((HALF, LANES), f32)

    def z_step(yhs):
        rows = []
        for yh in yhs:
            b = [base_ref[i, :, columns(yh)] for i in range(3)]
            t = [sigma * state_ref[i, :, columns(yh)] for i in range(3)]
            rows += [t[2] * b[0], t[0] * b[1], t[1] * b[0], t[0] * b[2]]
            rows += [t[2] * b[1], t[2] * b[2], t[1] * b[1], t[1] * b[2]]
            rows += [nothing, nothing, t[0] * b[0], nothing]
        got = lane_parts(folded(dot_nt(fz_ref[...], beside(jnp.concatenate(rows, 0)))))
        for n, yh in enumerate(yhs):
            for tile in range(3):
                lines[tile, line_rows(yh), :] = got[3 * n + tile]

    pieces[0].wait()
    for n in range(PIECES):
        pieces[2 * n + 1].wait()
        pieces[2 * n + 2].wait()
        over_lines(z_step, 4, n * HALF // PIECES, (n + 1) * HALF // PIECES)
    ky = ky_rows()
    lane = lax.broadcasted_iota(jnp.int32, (ROWS, LANES), 1)
    odd_block = (lane // HALF) % 2 == 1

    def y_step(kzs):
        even = []
        for pair in range(0, len(kzs), 2):
            data = [stacked(along_y(lines, 0, kz)) for kz in kzs[pair : pair + 2]]
            even += lane_parts(folded(dot(fy_ref[...], jnp.concatenate(data, 1))))
        odd = []
        for kz in kzs:
            data = [stacked(along_y(lines, tile, kz)) for tile in (1, 2)]
            odd.append(lane_parts(folded(dot(fyr_ref[...], jnp.concatenate(data, 1)))))
        for n, kz in enumerate(kzs):
            kzf = kz.astype(f32)
            plain = even[n]
            slopes = odd[n][0] * jnp.where(odd_block, kzf, ky)
            slopes = slopes + pltpu.roll(slopes, 32, 1)
            result[0, kz] = jnp.where(odd_block, slopes, plain)
            other = plain * jnp.where(lane >= 96, -kzf, -ky)
            other = other + pltpu.roll(other, 64, 1)
            result[1, kz] = jnp.where(lane >= 96, other, odd[n][1])

    sends = []
    for chunk in range(CHUNKS):
        first, last = planes_of(chunk)
        over_planes(y_step, first, last)
        source = result.at[:, pl.ds(first, last - first)]
        sends.append(pltpu.make_async_copy(source, out_refs[chunk], left.at[chunk]))
        sends[-1].start()
    for send in sends:
        send.wait()


def gradient_planes(cutoff_ref, here_ref, there_ref, back_ref, planes, start):
    cut_x, cut_y, cut_z = cutoff_ref[0], cutoff_ref[1], cutoff_ref[2]
    which = jnp.clip(cut_x - (KEEP - 3), 0, 3)
    keep_y = jnp.where(jnp.abs(ky_rows()) <= cut_y.astype(f32), 1.0, 0.0).astype(f32)
    iy_ref, iyd_ref = (view(back_ref, n) for n in range(2))
    for d in range(3):
        planes[d, HALF_KZ * LANES :, :] = jnp.zeros((LANES, LANES), f32)
    for first in range(0, HALF_KZ, 4):
        kzs = range(first, min(first + 4, HALF_KZ))
        rows = []
        for kz in kzs:
            keep = keep_y * jnp.where(start + kz <= cut_z, 1.0, 0.0).astype(f32)
            rows.append(jnp.concatenate([here_ref[kz] * keep, there_ref[kz] * keep], 1))
        high = back_ref[pl.ds(pl.multiple_of((6 + which) * 256, 256), 256), :]
        low = back_ref[pl.ds(pl.multiple_of((10 + which) * 256, 256), 256), :]
        got = triple(jnp.concatenate(rows, 0), high, low)
        data = [stacked(padded(got[n * ROWS : (n + 1) * ROWS])) for n in range(len(kzs))]
        for n, kz in enumerate(kzs):
            even = lane_parts(folded(dot(iy_ref[...], data[n])))
            planes[0, kz * LANES : (kz + 1) * LANES, :] = even[1]
            planes[2, kz * LANES : (kz + 1) * LANES, :] = even[0]
        for n in range(0, len(kzs), 2):
            both = jnp.concatenate([one[:, :LANES] for one in data[n : n + 2]], 1)
            for k, part in enumerate(lane_parts(folded(dot(iyd_ref[...], both)))):
                kz = kzs[n + k]
                planes[1, kz * LANES : (kz + 1) * LANES, :] = part


def half_kernel(core_ref, cutoff_ref, here_ref, there_ref, back_ref, planes):
    start = core_ref[0] * HALF_KZ
    gradient_planes(cutoff_ref, here_ref, there_ref, back_ref, planes, start)


def gradient_kernel(
    core_ref, cutoff_ref, wave_ref, base_ref, state_ref, own_ref, here_ref, there_ref,
    ahead_ref, back_ref, *refs
):
    *out_refs, planes, force_ref = refs
    core = core_ref[0]
    start = (1 - core) * HALF_KZ
    gradient_planes(cutoff_ref, here_ref, there_ref, back_ref, planes, start)
    fz_ref = ahead_tables(ahead_ref)[0]
    iz_ref, izd_ref = view(back_ref, 2), view(back_ref, 3)
    y = lax.broadcasted_iota(jnp.int32, (HALF, LANES), 0) * 2
    y = y + lax.broadcasted_iota(jnp.int32, (HALF, LANES), 1) // N
    phase = ((wave_ref[0] * y) % N).astype(f32) * (2.0 * np.pi / N)
    force_ref[...] = forcing_amp * jnp.sin(phase)
    nothing = jnp.zeros((HALF, LANES), f32)

    def along_halves(d, yh):
        at = pl.ds(yh, 4 * (HALF_KZ + 1), stride=HALF)
        own, other = own_ref[d, at, :], planes[d, at, :]
        low = jnp.where(core == 0, own, other)
        high = jnp.where(core == 0, other, own)
        return padded(jnp.concatenate([low, high], 0)).T

    def physical_step(yhs):
        count = len(yhs)
        flat = [along_halves(d, yh)[:96] for d in range(2) for yh in yhs]
        steep = [along_halves(2, yh)[:96] for yh in yhs]
        flat = folded_lanes(dot(beside(jnp.concatenate(flat, 0)), iz_ref[...]))
        steep = folded_lanes(dot(beside(jnp.concatenate(steep, 0)), izd_ref[...]))
        for n, yh in enumerate(yhs):
            sets = [flat[96 * n :], flat[96 * (count + n) :], steep[96 * n :]]
            grads = [[one[HALF * i : HALF * (i + 1)] for i in range(3)] for one in sets]
            b = [base_ref[i, :, columns(yh)] for i in range(3)]
            s = [state_ref[i, :, columns(yh)] for i in range(3)]
            comb, comb_base = [], []
            for i in range(3):
                coupling = sum(
                    jnp.where(core == 0, grads[j][i], grads[i][j]) * s[j] for j in range(3)
                )
                comb.append(s[i] - time_step * coupling)
                drive = sum(grads[j][i] * b[j] for j in range(3))
                if i == 0:
                    drive = drive - force_ref[pl.ds(yh, 1), :]
                comb_base.append(b[i] - time_step * drive)
            rows = [comb[1], comb_base[1], comb[2], comb_base[2]]
            rows += [comb[0], comb_base[0], nothing, nothing]
            got = folded(dot_nt(fz_ref[...], beside(jnp.concatenate(rows, 0))))
            depth = LINE // CHUNKS
            rows = pl.ds(pl.multiple_of(yh * depth, 8), depth)
            for tile, part in enumerate(lane_parts(got)):
                for chunk in range(CHUNKS):
                    out_refs[chunk][tile, rows, :] = part[chunk * depth : (chunk + 1) * depth]

    over_lines(physical_step, 8)


def spectral_kernel(
    chunk, core_ref, cutoff_ref, lines_ref, flux_ref,
    ahead_ref, along_ref, near_ref, far_ref,
):
    _, fy_ref, fyr_ref = ahead_tables(ahead_ref)
    core = core_ref[0]
    cut_x, cut_y, cut_z = cutoff_ref[0], cutoff_ref[1], cutoff_ref[2]
    first, last = planes_of(chunk)
    extra = last - first
    ky = ky_rows()
    kx = kx_lanes()
    keep_y = jnp.where(jnp.abs(ky) <= cut_y.astype(f32), 1.0, 0.0).astype(f32)
    keep_x = jnp.where(kx <= cut_x.astype(f32), 1.0, 0.0).astype(f32)
    keep_xy = keep_y * keep_x
    square_xy = ky * ky + kx * kx
    lane = lax.broadcasted_iota(jnp.int32, (ROWS, LANES), 1)
    near_ref[extra] = jnp.zeros((ROWS, LANES), f32)
    far_ref[extra] = jnp.zeros((ROWS, LANES), f32)

    def kept_z(kz):
        return jnp.where(kz <= cut_z, 1.0, 0.0).astype(f32)

    def spectral_step(kzs):
        fields = [[], [], []]
        for pair in range(0, len(kzs), 2):
            ks = kzs[pair : pair + 2]
            data = [
                jnp.concatenate(
                    [stacked(along_y(lines_ref, t, kz, LINE // CHUNKS)) for kz in ks], 1
                )
                for t in (0, 1)
            ]
            even = lane_parts(folded(dot(fy_ref[...], data[0])))
            odd = lane_parts(folded(dot(fyr_ref[...], data[1])))
            for n, kz in enumerate(ks):
                flux = flux_ref[0, kz - first]
                fields[0].append(odd[n] + flux_ref[1, kz - first])
                fields[1].append(jnp.where(lane < 64, even[n], flux))
                fields[2].append(jnp.where(lane < 64, flux, even[n]))
        data = [beside(jnp.concatenate(field, 0)) for field in fields]
        modes = [folded_lanes(dot(data[max(n - 1, 0)], view(along_ref, n)[...])) for n in range(4)]
        results = [[], [], [], []]
        for n, kz in enumerate(kzs):
            kzf = kz.astype(f32)
            vx, slope, uy, uz = (mode[n * ROWS : (n + 1) * ROWS] for mode in modes)
            square = square_xy + kzf * kzf
            factor = keep_xy * kept_z(kz) / (1.0 + viscosity * time_step * square)
            share = (slope + ky * uy + kzf * uz) / jnp.where(square > 0, square, 1.0)
            results[0].append(factor * vx)
            results[1].append(factor * share)
            results[2].append(factor * (uy - ky * share))
            results[3].append(factor * (uz - kzf * share))
        got = [
            dot(
                beside(jnp.concatenate(result, 0)),
                along_ref[pl.ds(pl.multiple_of((4 + core * 4 + n) * 256, 256), 256), :],
            )
            for n, result in enumerate(results)
        ]
        got = [folded_lanes(part) for part in (got[0] + got[1], got[2], got[3])]
        for n, kz in enumerate(kzs):
            x, y, z = (part[n * ROWS : (n + 1) * ROWS] for part in got)
            near_ref[kz - first] = jnp.where(lane < 48, x, jnp.where(lane < 96, y, z))
            away = jnp.where(
                (lane >= 64) & (lane < 112), x, jnp.where((lane >= 32) & (lane < 64), z, y)
            )
            far_ref[kz - first] = pltpu.roll(away, 64, 1)
            shift = (kz - first) * 16
            near_ref[extra] += pltpu.roll(jnp.where(lane < 16, z, 0.0), shift, 1)
            rest = jnp.where((lane >= 64) & (lane < 80), z, 0.0)
            far_ref[extra] += pltpu.roll(rest, (shift + 64) % LANES, 1)

    over_planes(spectral_step, first, last)


def inverse_y(near_ref, far_ref, iy_ref, planes):
    count = near_ref.shape[0] - 1
    rest = near_ref[count] + far_ref[count]
    for kz in range(count):
        turned = pltpu.roll(rest, (LANES - kz * 16) % LANES, 1) if kz else rest
        data = jnp.concatenate([near_ref[kz] + far_ref[kz], turned], 1)
        got = lane_parts(folded(dot(iy_ref[...], stacked(padded(data)))))
        for tile in range(2):
            planes[tile, kz * LANES : (kz + 1) * LANES, :] = got[tile]
    if count < CHUNK:
        blank = jnp.zeros(((CHUNK - count) * LANES, LANES), f32)
        for tile in range(2):
            planes[tile, count * LANES :, :] = blank


def inverse_kernel(near_a, far_a, near_b, far_b, back_ref, planes_a, planes_b):
    iy_ref = view(back_ref, 0)
    inverse_y(near_a, far_a, iy_ref, planes_a)
    inverse_y(near_b, far_b, iy_ref, planes_b)


def final_kernel(
    near_ref, far_ref, planes_a, planes_b, state_ref, base_ref, back_ref,
    base_out, state_out, planes_c,
):
    iy_ref, iz_ref, izr_ref = (view(back_ref, n) for n in (0, 4, 5))
    inverse_y(near_ref, far_ref, iy_ref, planes_c)

    def along_chunks(tile, yh):
        parts = [
            ref[tile, pl.ds(yh, 4 * CHUNK, stride=HALF), :]
            for ref in (planes_a, planes_b, planes_c)
        ]
        return padded(jnp.concatenate(parts, 0)).T

    def z_step(yhs):
        data = [along_chunks(0, yh) for yh in yhs]
        rest = [along_chunks(1, yh)[:16] for yh in yhs]
        turned = beside(jnp.concatenate([one[:48] for one in data], 0))
        plain = beside(jnp.concatenate([one[48:] for one in data] + rest, 0))
        turned = folded_lanes(dot(turned, izr_ref[...]))
        plain = folded_lanes(dot(plain, iz_ref[...]))
        for n, yh in enumerate(yhs):
            at = columns(yh)
            first = turned[48 * n : 48 * n + 48]
            second = plain[80 * n : 80 * n + 80]
            third = plain[80 * len(yhs) + 16 * n :][:16]
            state_out[0, :, at] = first[:32] - state_ref[0, :, at]
            state_out[1, :, at] = second[16:48] - state_ref[1, :, at]
            state_out[2, :, at] = second[48:80] - state_ref[2, :, at]
            base_out[0, :, at] = first[32:48] - base_ref[0, :, at]
            base_out[1, :, at] = second[:16] - base_ref[1, :, at]
            base_out[2, :, at] = third - base_ref[2, :, at]

    over_lines(z_step, 8)


interpret = False


def call(kernel, outs, scratch, inputs, room, in_smem=0, in_hbm=0, out_hbm=False):
    whole = pl.BlockSpec(memory_space=pltpu.VMEM)
    small = pl.BlockSpec(memory_space=pltpu.SMEM)
    far = pl.BlockSpec(memory_space=pltpu.HBM)
    return pl.pallas_call(
        kernel,
        out_shape=outs,
        in_specs=[small] * in_smem
        + [far] * in_hbm
        + [whole] * (len(inputs) - in_smem - in_hbm),
        out_specs=jax.tree.map(lambda _: far if out_hbm else whole, outs),
        scratch_shapes=scratch,
        compiler_params=pltpu.CompilerParams(vmem_limit_bytes=room * 2**20),
        cost_estimate=pl.CostEstimate(flops=1000, bytes_accessed=1000, transcendentals=0),
        interpret=interpret,
    )(*inputs)


def body(base, state, wavenumber, cutoff):
    t = {name: jnp.asarray(value) for name, value in tables().items()}
    core = lax.axis_index("comp")
    seg_count = lax.axis_size("seg")
    own_base = base[0]
    own_state = state[0, 0]
    base_half = lax.dynamic_slice_in_dim(own_base, core * 16, 16, 1)
    back = [((s + 1) % seg_count, s) for s in range(seg_count)]
    around = [(2 * i, 2 * o) for i, o in back] + [(2 * o + 1, 2 * i + 1) for i, o in back]
    base_next = lax.ppermute(base_half, "seg", back)
    state_next = lax.ppermute(own_state, ("seg", "comp"), around)
    sds = jax.ShapeDtypeStruct
    core_at = core.reshape(1)
    swap = [(0, 1), (1, 0)]
    here_own = call(
        base_kernel,
        sds((HALF_KZ, ROWS, LANES), f32),
        [
            pltpu.VMEM((1, HALF * LINE, LANES), f32),
            pltpu.VMEM(own_base.shape, f32),
            pltpu.VMEM(t["ahead"].shape, bf16),
            pltpu.SemaphoreType.DMA((PIECES + 1,)),
        ],
        [core_at, own_base, t["ahead"]],
        room=56,
        in_smem=1,
        in_hbm=2,
    )
    there_own = lax.ppermute(here_own, "slab", swap)
    here_other = lax.ppermute(here_own, "comp", swap)
    counts = [planes_of(chunk)[1] - planes_of(chunk)[0] for chunk in range(CHUNKS)]
    flux = call(
        flux_kernel,
        [sds((2, count, ROWS, LANES), f32) for count in counts],
        [
            pltpu.VMEM((3, HALF * LINE, LANES), f32),
            pltpu.VMEM(own_base.shape, f32),
            pltpu.VMEM(own_state.shape, f32),
            pltpu.VMEM(t["ahead"].shape, bf16),
            pltpu.VMEM((2, NKZ, ROWS, LANES), f32),
            pltpu.SemaphoreType.DMA((2 * PIECES + 1,)),
            pltpu.SemaphoreType.DMA((CHUNKS,)),
        ],
        [core_at, own_base, own_state, t["ahead"]],
        room=56,
        in_smem=1,
        in_hbm=3,
        out_hbm=True,
    )
    there_own, flux = lax.optimization_barrier((there_own, flux))
    there_other = lax.ppermute(there_own, "comp", swap)
    half_planes = sds((3, (HALF_KZ + 1) * LANES, LANES), f32)
    own_planes = call(
        half_kernel,
        half_planes,
        [],
        [core_at, cutoff, here_own, there_own, t["back"]],
        room=12,
        in_smem=2,
    )
    lines = call(
        gradient_kernel,
        [sds((2, HALF * 4 * CHUNK, LANES), f32)] * CHUNKS,
        [pltpu.VMEM(half_planes.shape, f32), pltpu.VMEM((HALF, LANES), f32)],
        [core_at, cutoff, wavenumber, own_base, own_state, own_planes, here_other, there_other]
        + [t["ahead"], t["back"]],
        room=20,
        in_smem=3,
    )
    near, far = [], []
    for chunk in range(CHUNKS):
        near_part, far_part = call(
            functools.partial(spectral_kernel, chunk),
            [sds((counts[chunk] + 1, ROWS, LANES), f32)] * 2,
            [],
            [core_at, cutoff, lines[chunk], flux[chunk], t["ahead"], t["along"]],
            room=10,
            in_smem=2,
        )
        near.append(near_part)
        far.append(lax.ppermute(far_part, "slab", swap))
    planes = sds((2, CHUNK * LANES, LANES), f32)
    planes_a, planes_b = call(
        inverse_kernel, [planes] * 2, [], [near[0], far[0], near[1], far[1], t["back"]], room=10
    )
    base_gap, state_gap = call(
        final_kernel,
        [sds((3, 16, N * N), f32), sds((3, HALF, N * N), f32)],
        [pltpu.VMEM((2, CHUNK * LANES, LANES), f32)],
        [near[2], far[2], planes_a, planes_b, state_next, base_next, t["back"]],
        room=16,
    )
    return base_gap[None], state_gap[None, None]


def solution(mesh):
    paired = mesh.shape["slab"] == 2 and mesh.shape["comp"] == 2
    return jax.shard_map(
        body if paired else general_body,
        mesh=mesh,
        in_specs=(
            P(("groups", "seg"), None, "slab", None),
            P(("groups", "seg"), "comp", None, "slab", None),
            P("groups"),
            P("groups"),
        ),
        out_specs=(
            P(("groups", "seg"), None, ("slab", "comp"), None),
            P(("groups", "seg"), "comp", None, "slab", None),
        ),
        check_vma=False,
    )
```

```python
import functools

import jax
import jax.numpy as jnp
import ml_dtypes
import numpy as np
from jax import lax
from jax.experimental import pallas as pl
from jax.experimental.pallas import tpu as pltpu
from jax.sharding import PartitionSpec as P

N = 64
HALF = 32
KEEP = N // 3
NKZ = KEEP + 1
NKY = 44
ROWS = 2 * NKY
CHUNK = 8
CHUNKS = 3
LINE = CHUNKS * CHUNK * 4
HALF_KZ = NKZ // 2
LANES = 128

viscosity = 0.025
time_step = 0.02
forcing_amp = 10.0

f32 = jnp.float32
bf16 = jnp.bfloat16


highest = lax.Precision.HIGHEST


def swapped(value, axis, apart):
    mask = 2**apart
    pairs = [(source, source ^ mask) for source in range(lax.axis_size(axis))]
    return lax.ppermute(value, axis, pairs)


def shifted(block, axis, distance):
    devices = range(lax.axis_size(axis))
    route = [((i - distance) % len(devices), i) for i in devices]
    return lax.ppermute(block, axis, route)


def wavenumbers(grid_points):
    position = jnp.arange(grid_points, dtype=jnp.int32)
    return jnp.where(position < grid_points // 2, position, position - grid_points)


def phases(first, second, grid_points):
    product = jnp.mod(first[:, None] * second[None, :], grid_points)
    return product.astype(jnp.float32) * (2.0 * jnp.pi / grid_points)


def combine(partial_value, columns):
    cosine_part = partial_value[0]
    sine_part = partial_value[1]
    real_part = cosine_part[..., :columns] - sine_part[..., columns:]
    imag_part = cosine_part[..., columns:] + sine_part[..., :columns]
    return jnp.concatenate([real_part, imag_part], axis=-1)


def times_unit(values, wave, columns):
    return jnp.concatenate([-wave * values[..., columns:], wave * values[..., :columns]], axis=-1)


def doubled(values):
    return jnp.concatenate([values, values], axis=-1)


def general_body(base, state, wavenumber, cutoff):
    grid_points = N
    base = base.reshape(base.shape[0], 3, base.shape[2], grid_points, grid_points)
    state = state.reshape(
        state.shape[0], state.shape[1], 3, state.shape[3], grid_points, grid_points
    )
    slab_rows = state.shape[3]
    half_rows = slab_rows // 2
    slab_count = lax.axis_size("slab")
    group_count = slab_count * lax.axis_size("comp")
    core_side = lax.axis_index("comp")
    block_number = lax.axis_index(("slab", "comp"))
    base_whole = base[0]
    base_half = lax.dynamic_slice_in_dim(base_whole, core_side * half_rows, half_rows, 1)
    own_state = state[0, 0]
    spectrum = wavenumbers(grid_points)
    one_third = grid_points // 3
    row_total = (2 * one_third + group_count) // group_count * group_count
    row_index = jnp.arange(row_total, dtype=jnp.int32)
    row_alive_mask = row_index <= 2 * one_third
    row_wave = jnp.where(row_index <= one_third, row_index, row_index - (2 * one_third + 1))
    row_wave = jnp.where(row_alive_mask, row_wave, 0)
    width = grid_points // 2
    rows_per_block = row_total // group_count
    alive_flags = row_alive_mask.astype(jnp.float32)
    grid_index = jnp.arange(grid_points, dtype=jnp.int32)
    column_index = grid_index[:width]
    angle_grid = phases(grid_index, grid_index, grid_points)
    angle_ahead = phases(grid_index, column_index, grid_points)
    angle_behind = phases(column_index, grid_index, grid_points)
    column_weight = jnp.where(column_index == 0, 1.0, 2.0).astype(jnp.float32)[:, None]
    forward_z = jnp.concatenate([jnp.cos(angle_ahead), -jnp.sin(angle_ahead)], axis=1)
    inverse_z = (
        jnp.concatenate(
            [jnp.cos(angle_behind) * column_weight, -jnp.sin(angle_behind) * column_weight], axis=0
        )
        / grid_points
    )
    phase_angle_rows = phases(row_wave, grid_index, grid_points)
    forward_transform_y = (
        jnp.stack([jnp.cos(phase_angle_rows), -jnp.sin(phase_angle_rows)])
        * alive_flags[None, :, None]
    )
    inverse_y = (
        jnp.stack([jnp.cos(phase_angle_rows).T, jnp.sin(phase_angle_rows).T])
        * alive_flags[None, None, :]
        / grid_points
    )
    forward_x = jnp.stack([jnp.cos(angle_grid), -jnp.sin(angle_grid)])
    inverse_x = jnp.stack([jnp.cos(angle_grid), jnp.sin(angle_grid)]) / grid_points
    table_ahead = forward_x.reshape(2, grid_points, slab_count, slab_rows)
    table_back = inverse_x.reshape(2, slab_count, slab_rows, grid_points)
    local_wave = lax.dynamic_slice_in_dim(row_wave, block_number * rows_per_block, rows_per_block)
    local_alive_mask = lax.dynamic_slice_in_dim(
        alive_flags, block_number * rows_per_block, rows_per_block
    )
    shape_local = (grid_points, rows_per_block, width)
    wave_x = jnp.broadcast_to(spectrum[:, None, None], shape_local)
    wave_y = jnp.broadcast_to(local_wave[None, :, None], shape_local)
    wave_z = jnp.broadcast_to(spectrum[:width][None, None, :], shape_local)
    inside = (
        (jnp.abs(wave_x) <= cutoff[0])
        & (jnp.abs(wave_y) <= cutoff[1])
        & (jnp.abs(wave_z) <= cutoff[2])
    )
    keep_mask = doubled(inside.astype(jnp.float32) * local_alive_mask[None, :, None])
    float_x = wave_x.astype(jnp.float32)
    float_y = wave_y.astype(jnp.float32)
    float_z = wave_z.astype(jnp.float32)
    ksquare = float_x * float_x + float_y * float_y + float_z * float_z
    safe_square = doubled(jnp.where(ksquare > 0, ksquare, jnp.ones_like(ksquare)))
    damping = doubled(1.0 / (1.0 + viscosity * time_step * ksquare))
    double_x = doubled(float_x)
    double_y = doubled(float_y)
    double_z = doubled(float_z)

    def project(field):
        divergence = (double_x * field[0] + double_y * field[1] + double_z * field[2]) / safe_square
        return jnp.stack(
            [
                field[0] - double_x * divergence,
                field[1] - double_y * divergence,
                field[2] - double_z * divergence,
            ]
        )

    def yz_forward(field):
        along_z = jnp.einsum("...z,zk->...k", field, forward_z, precision=highest)
        partial_value = jnp.einsum(
            "sry,...yk->s...rk", forward_transform_y, along_z, precision=highest
        )
        return combine(partial_value, width)

    def yz_inverse(modes):
        partial_value = jnp.einsum("syr,...rk->s...yk", inverse_y, modes, precision=highest)
        return jnp.einsum(
            "...k,kz->...z", combine(partial_value, width), inverse_z, precision=highest
        )

    def spectral(state_fields, base_fields):
        state_modes = yz_forward(state_fields)[:, :, None]
        base_modes = yz_forward(base_fields)[:, :, None]
        state_got = lax.all_to_all(
            state_modes, ("slab", "comp"), split_axis=4, concat_axis=2, tiled=True
        )
        base_got = lax.all_to_all(
            base_modes, ("slab", "comp"), split_axis=4, concat_axis=2, tiled=True
        )
        item_count = state_got.shape[0]
        part_count = state_got.shape[1]
        state_split = state_got.reshape(
            item_count, part_count, slab_count, 2, slab_rows, rows_per_block, 2 * width
        )
        state_partial = jnp.einsum(
            "srpx,ijpcxyk->sijcryk", table_ahead, state_split, precision=highest
        )
        base_lined = base_got.reshape(item_count, 1, grid_points, rows_per_block, 2 * width)
        base_partial = jnp.einsum("srx,ijxyk->sijryk", forward_x, base_lined, precision=highest)
        return (combine(state_partial, width), combine(base_partial, width))

    state_first, base_first = spectral(own_state[:, None], base_half[:, None])
    state_hat = state_first[:, 0] * keep_mask
    base_hat = base_first[:, 0] * keep_mask
    grad_hat = jnp.stack(
        [
            times_unit(base_hat, float_x, width),
            times_unit(base_hat, float_y, width),
            times_unit(base_hat, float_z, width),
        ],
        axis=1,
    )
    grad_hat = grad_hat.reshape(9, grid_points, rows_per_block, 2 * width)
    grad_partial = jnp.einsum("sxr,iryk->sixyk", inverse_x, grad_hat, precision=highest)
    grad_spread = combine(grad_partial, width).reshape(
        9, group_count, half_rows, rows_per_block, 2 * width
    )
    own_rows = yz_inverse(
        lax.all_to_all(grad_spread, ("slab", "comp"), split_axis=1, concat_axis=3, tiled=True)[:, 0]
    )
    other_rows = swapped(own_rows, "comp", 0)
    gradient = jnp.where(
        core_side == 0,
        jnp.concatenate([own_rows, other_rows], axis=1),
        jnp.concatenate([other_rows, own_rows], axis=1),
    )
    gradient = gradient.reshape(3, 3, slab_rows, grid_points, grid_points)
    gradient_half = lax.dynamic_slice_in_dim(gradient, core_side * half_rows, half_rows, 2)
    flux_terms = own_state[:, None] * base_whole[None, :]
    coupling_matrix = jnp.where(core_side == 0, gradient, jnp.swapaxes(gradient, 0, 1))
    coupling = jnp.sum(coupling_matrix * own_state[None, :], axis=1)
    forcing_phase = phases(wavenumber, grid_index, grid_points)[0]
    forcing = forcing_amp * jnp.sin(forcing_phase)[None, :, None]
    base_drive = jnp.sum(gradient_half * base_half[None, :], axis=1)
    base_drive = jnp.concatenate([base_drive[:1] - forcing[None], base_drive[1:]], axis=0)
    state_fields = jnp.concatenate([flux_terms, coupling[:, None]], axis=1)
    drive_modes, base_modes_two = spectral(state_fields, base_drive[:, None])
    orient = jnp.array([1.0, -1.0], dtype=jnp.float32)[None, :, None, None, None]
    divergence = (
        times_unit(drive_modes[:, 0], float_x, width)
        + times_unit(drive_modes[:, 1], float_y, width)
        + times_unit(drive_modes[:, 2], float_z, width)
    )
    state_drive = keep_mask * (orient * divergence + drive_modes[:, 3])
    new_hat = damping * project(state_hat - time_step * state_drive)
    base_new_hat = damping * project(base_hat - time_step * keep_mask * base_modes_two[:, 0])
    state_partial = jnp.einsum("spxr,icryk->sipcxyk", table_back, new_hat, precision=highest)
    state_back = combine(state_partial, width).reshape(
        3, group_count, slab_rows, rows_per_block, 2 * width
    )
    base_partial = jnp.einsum("sxr,iryk->sixyk", inverse_x, base_new_hat, precision=highest)
    base_back = combine(base_partial, width).reshape(
        3, group_count, half_rows, rows_per_block, 2 * width
    )
    state_got = lax.all_to_all(
        state_back, ("slab", "comp"), split_axis=1, concat_axis=3, tiled=True
    )
    base_got = lax.all_to_all(base_back, ("slab", "comp"), split_axis=1, concat_axis=3, tiled=True)
    state_new = yz_inverse(state_got[:, 0])
    base_new = yz_inverse(base_got[:, 0])
    base_later, later_state = shifted((base_half, own_state), "seg", -1)
    prior_state = shifted(own_state, "seg", 1)
    neighbour = jnp.where(core_side == 0, later_state, prior_state)
    base_gap = (base_new - base_later).reshape(1, 3, half_rows, grid_points * grid_points)
    state_gap = (state_new - neighbour).reshape(1, 1, 3, slab_rows, grid_points * grid_points)
    return (base_gap, state_gap)


def halves(table):
    high = table.astype(np.float32).astype(ml_dtypes.bfloat16)
    low = (table - high.astype(np.float64)).astype(ml_dtypes.bfloat16)
    return high, low


def left_table(table, depth):
    padded = np.zeros((table.shape[0], depth))
    padded[:, : table.shape[1]] = table
    high, low = halves(padded)
    return np.concatenate([high, high, low], 1)


def right_table(table, depth):
    padded = np.zeros((depth, table.shape[1]))
    padded[: table.shape[0]] = table
    high, low = halves(padded)
    return np.concatenate(
        [np.concatenate([high, low], 1), np.concatenate([high, np.zeros_like(low)], 1)], 0
    )


def ky_values():
    index = np.arange(NKY)
    wave = np.where(index <= KEEP, index, index - (2 * KEEP + 1))
    alive = (index <= 2 * KEEP).astype(np.float64)
    return wave * alive, alive


@functools.cache
def tables():
    out = {}
    z = np.arange(N)
    kz = np.arange(NKZ)
    angle = 2 * np.pi * kz[:, None] * z[None, :] / N
    weight = np.where(kz == 0, 1.0, 2.0)[:, None] / N
    forward = np.zeros((2, 2, CHUNKS * CHUNK, 2, N))
    inverse = np.zeros((NKZ, 2, 2, 2, N))
    turned = np.zeros((NKZ, 2, 2, 2, N))
    slope = np.zeros((NKZ, 2, 2, 2, N))
    for y2 in range(2):
        forward[y2, 0, :NKZ, y2] = np.cos(angle)
        forward[y2, 1, :NKZ, y2] = -np.sin(angle)
        inverse[:, y2, 0, y2] = weight * np.cos(angle)
        inverse[:, y2, 1, y2] = -weight * np.sin(angle)
        turned[:, y2, 0, y2] = weight * np.sin(angle)
        turned[:, y2, 1, y2] = weight * np.cos(angle)
        slope[:, y2, 0, y2] = -weight * kz[:, None] * np.sin(angle)
        slope[:, y2, 1, y2] = -weight * kz[:, None] * np.cos(angle)
    forward = np.moveaxis(forward.reshape(4, CHUNKS, CHUNK, 2 * N), 1, 0)
    out["fz"] = left_table(forward.reshape(LINE, 2 * N), 128)
    out["iz"] = right_table(inverse.reshape(4 * NKZ, 2 * N), 128)
    out["izr"] = right_table(turned.reshape(4 * NKZ, 2 * N), 128)

    def by_half(table):
        wide = np.zeros((2, HALF_KZ + 1, 4, 2 * N))
        wide[:, :HALF_KZ] = table.reshape(2, HALF_KZ, 4, 2 * N)
        return right_table(wide.reshape(8 * HALF_KZ + 8, 2 * N), 128)

    out["izg"] = by_half(inverse)
    out["izd"] = by_half(slope)
    ky, alive = ky_values()
    y = 2 * np.arange(HALF)[None, :] + np.arange(2)[:, None]
    phase = 2 * np.pi * ky[:, None, None] * y[None] / N
    cosine = np.cos(phase) * alive[:, None, None]
    sine = np.sin(phase) * alive[:, None, None]
    plain = np.zeros((2, NKY, 2, 2, HALF))
    plain[0, :, :, 0] = cosine
    plain[0, :, :, 1] = sine
    plain[1, :, :, 0] = -sine
    plain[1, :, :, 1] = cosine
    rotated = np.stack([-plain[1], plain[0]])
    for name, table in (("fy", plain), ("fyr", rotated)):
        tall = np.zeros((LINE, 128))
        tall[:ROWS] = table.reshape(ROWS, 128)
        out[name] = left_table(tall, 128)
    back = np.zeros((2, 2, HALF, 2, NKY))
    cos_t = np.moveaxis(cosine, 0, -1) / N
    sin_t = np.moveaxis(sine, 0, -1) / N
    back[:, 0, :, 0] = cos_t
    back[:, 0, :, 1] = -sin_t
    back[:, 1, :, 0] = sin_t
    back[:, 1, :, 1] = cos_t
    back_slope = np.zeros_like(back)
    back_slope[..., 0, :] = ky * back[..., 1, :]
    back_slope[..., 1, :] = -ky * back[..., 0, :]
    out["iy"] = left_table(back.reshape(128, ROWS), 128)
    out["iyd"] = left_table(back_slope.reshape(128, ROWS), 128)
    grad_high, grad_low = [], []
    x = np.arange(N)
    apart = x[:HALF, None] - x[None, :]
    for cut in range(KEEP - 3, KEEP + 1):
        k = np.arange(cut + 1)
        wk = np.where(k == 0, 1.0, 2.0) / N
        arg = 2 * np.pi * apart[..., None] * k / N
        keep = (np.cos(arg) * wk).sum(-1)
        derive = (-np.sin(arg) * wk * k).sum(-1)
        table = np.zeros((2, 4, HALF, 2, 4, HALF))
        for comp in range(3):
            for side in range(2):
                rows = slice(side * HALF, (side + 1) * HALF)
                table[side, comp, :, 0, comp, :] = keep[:, rows].T
                table[side, comp, :, 1, comp, :] = derive[:, rows].T
        high, low = halves(table.reshape(256, 256))
        grad_high.append(high)
        grad_low.append(low)
    out["gxh"] = np.stack(grad_high)
    out["gxl"] = np.stack(grad_low)
    kx = np.arange(HALF)
    live = (kx <= KEEP).astype(np.float64)
    xl = np.arange(HALF)
    arg = 2 * np.pi * xl[:, None] * kx[None, :] / N
    value = np.concatenate([np.cos(arg) * live, np.sin(arg) * live], 1)
    change = np.concatenate([kx * np.sin(arg) * live, -kx * np.cos(arg) * live], 1)

    def coefficients(blocks):
        table = np.zeros((4, HALF, 2, 2 * HALF))
        for block, part, what in blocks:
            table[block, :, part] = what
        return table.reshape(LANES, LANES)

    first = coefficients([(0, 0, value), (1, 1, value), (2, 0, change), (3, 0, value)])
    last = coefficients([(0, 0, change), (1, 0, value), (2, 0, value), (3, 1, value)])
    fall = first.reshape(LANES, 2, 2, HALF)
    fall = np.stack([-kx * fall[:, :, 1], kx * fall[:, :, 0]], 2).reshape(LANES, LANES)
    out["fx"] = np.stack([right_table(part, 128) for part in (first, fall, first, last)])
    wx = np.where(kx == 0, 1.0, 2.0) * live / N
    for core in range(2):
        ix = np.zeros((4, 2, 2 * HALF, LANES))
        for side in range(2):
            xs = np.arange(HALF) + side * HALF
            arg = 2 * np.pi * kx[:, None] * xs[None, :] / N
            give = np.concatenate([np.cos(arg) * wx[:, None], np.sin(arg) * wx[:, None]], 0)
            drop = np.concatenate(
                [np.sin(arg) * (wx * kx)[:, None], -np.cos(arg) * (wx * kx)[:, None]], 0
            )
            own = slice(core * 16, core * 16 + 16)

            def put(quantity, part, lane, what):
                at = (lane + side * 64 + np.arange(what.shape[1])) % LANES
                ix[quantity, part][:, at] = what

            put(0, 0, 0, give)
            put(1, 0, 0, drop)
            put(0, 1, 32, give[:, own])
            put(1, 1, 32, drop[:, own])
            put(2, 1, 48, give[:, own])
            put(2, 0, 64, give)
            put(3, 0, 96, give)
            put(3, 1, 0, give[:, own])
        out["ix%d" % core] = np.stack(
            [right_table(part, 128) for part in ix.reshape(4, LANES, LANES)]
        )
    out["ix"] = np.stack([out.pop("ix0"), out.pop("ix1")])
    merged = {}
    merged["ahead"] = np.concatenate([out["fz"], out["fy"], out["fyr"]], 0)
    merged["height"] = np.concatenate([out["iy"], out["iyd"]], 0)
    gx = [out["gxh"].reshape(-1, 256), out["gxl"].reshape(-1, 256)]
    square = [out[name] for name in ("izg", "izd", "iz", "izr")]
    merged["back"] = np.concatenate(square + gx, 0)
    merged["along"] = np.concatenate([out["fx"].reshape(-1, 256), out["ix"].reshape(-1, 256)], 0)
    return merged


def view(ref, index, rows=256, start=0):
    return ref.at[pl.ds(start + index * rows, rows), :]


def ahead_tables(ref):
    return [view(ref, n, LINE) for n in range(3)]


def ky_rows():
    row = lax.broadcasted_iota(jnp.int32, (ROWS, LANES), 0)
    index = jnp.where(row < NKY, row, row - NKY)
    wave = jnp.where(index <= KEEP, index, index - (2 * KEEP + 1))
    return jnp.where(index <= 2 * KEEP, wave, 0).astype(f32)


def kx_lanes():
    lane = lax.broadcasted_iota(jnp.int32, (1, LANES), 1) % HALF
    return jnp.where(lane <= KEEP, lane, 0).astype(f32)


def split(values):
    high = values.astype(bf16)
    low = (values - high.astype(f32)).astype(bf16)
    return high, low


def dot(a, b):
    return jnp.dot(a, b, preferred_element_type=f32)


def dot_nt(a, b):
    return lax.dot_general(a, b, (((1,), (1,)), ((), ())), preferred_element_type=f32)


def stacked(values):
    high, low = split(values)
    return jnp.concatenate([high, low, high], 0)


def beside_thrice(values):
    high, low = split(values)
    return jnp.concatenate([high, low, high], 1)


def beside(values):
    high, low = split(values)
    return jnp.concatenate([high, low], 1)


def folded_lanes(result):
    return result[:, :LANES] + result[:, LANES:]


def padded(values, rows=128):
    return jnp.concatenate([values, jnp.zeros((rows - values.shape[0], values.shape[1]), f32)], 0)


def triple(values, high_ref, low_ref):
    high, low = split(values)
    return dot(high, high_ref) + dot(low, high_ref) + dot(high, low_ref)


def columns(yh):
    return pl.ds(pl.multiple_of(yh * LANES, LANES), LANES)


def along_y(ref, tile, kz, line=LINE):
    at = kz % CHUNK + (0 if line == LINE // CHUNKS else kz // CHUNK * (4 * CHUNK))
    return jnp.concatenate(
        [ref[tile, pl.ds(q * CHUNK + at, HALF, stride=line), :] for q in range(4)], 0
    )


def line_rows(yh):
    return pl.ds(pl.multiple_of(yh * LINE, 8), LINE)


def lane_parts(values):
    return [values[:, at : at + LANES] for at in range(0, values.shape[1], LANES)]


def over_planes(step, first=0, last=NKZ):
    def four(index, _):
        step([first + index * 4 + k for k in range(4)])
        return 0

    count = (last - first) // 4
    lax.fori_loop(0, count, four, 0)
    if first + count * 4 < last:
        step([jnp.int32(kz) for kz in range(first + count * 4, last)])


def planes_of(chunk):
    return chunk * CHUNK, min((chunk + 1) * CHUNK, NKZ)


def over_lines(step, many, first=0, last=HALF):
    def some(index, _):
        step([first + index * many + k for k in range(many)])
        return 0

    lax.fori_loop(0, (last - first) // many, some, 0)


PIECES = 4


def base_kernel(core_ref, base_hbm, ahead_hbm, out_ref, lines, base_ref, ahead_ref, arrived):
    nothing = jnp.zeros((HALF, LANES), f32)
    wide = N * N // PIECES
    table = pltpu.make_async_copy(ahead_hbm, ahead_ref, arrived.at[PIECES])
    pieces = [
        pltpu.make_async_copy(
            base_hbm.at[:, :, pl.ds(n * wide, wide)],
            base_ref.at[:, :, pl.ds(n * wide, wide)],
            arrived.at[n],
        )
        for n in range(PIECES)
    ]
    pieces[0].start()
    table.start()
    for piece in pieces[1:]:
        piece.start()
    fz_ref, fy_ref, _ = ahead_tables(ahead_ref)
    table.wait()
    many = HALF // PIECES
    for n, piece in enumerate(pieces):
        piece.wait()
        yhs = range(n * many, (n + 1) * many)
        rows = []
        for yh in yhs:
            at = slice(yh * LANES, (yh + 1) * LANES)
            rows += [base_ref[i, :, at] for i in range(3)] + [nothing]
        got = dot_nt(fz_ref[...], beside_thrice(jnp.concatenate(rows, 0)))
        for yh, part in zip(yhs, lane_parts(got)):
            lines[0, yh * LINE : (yh + 1) * LINE, :] = part
    start = core_ref[0] * HALF_KZ
    for pair in range(0, HALF_KZ, 2):
        ks = range(pair, min(pair + 2, HALF_KZ))
        data = jnp.concatenate([stacked(along_y(lines, 0, start + k)) for k in ks], 1)
        got = dot(fy_ref[...], data)[:ROWS]
        for k, part in zip(ks, lane_parts(got)):
            out_ref[k] = part


def flux_kernel(core_ref, base_hbm, state_hbm, ahead_hbm, *refs):
    *out_refs, lines, base_ref, state_ref, ahead_ref, result, arrived, left = refs
    wide = N * N // PIECES
    pieces = [pltpu.make_async_copy(ahead_hbm, ahead_ref, arrived.at[2 * PIECES])]
    for n in range(PIECES):
        for k, (source, target) in enumerate(((base_hbm, base_ref), (state_hbm, state_ref))):
            at = pl.ds(n * wide, wide)
            pieces.append(
                pltpu.make_async_copy(
                    source.at[:, :, at], target.at[:, :, at], arrived.at[2 * n + k]
                )
            )
    for piece in pieces:
        piece.start()
    fz_ref, fy_ref, fyr_ref = ahead_tables(ahead_ref)
    sigma = jnp.where(core_ref[0] == 0, -time_step, time_step).astype(f32)
    nothing = jnp.zeros((HALF, LANES), f32)

    def z_step(yhs):
        rows = []
        for yh in yhs:
            b = [base_ref[i, :, columns(yh)] for i in range(3)]
            t = [sigma * state_ref[i, :, columns(yh)] for i in range(3)]
            rows += [t[2] * b[0], t[0] * b[1], t[1] * b[0], t[0] * b[2]]
            rows += [t[2] * b[1], t[2] * b[2], t[1] * b[1], t[1] * b[2]]
            rows += [nothing, nothing, t[0] * b[0], nothing]
        got = lane_parts(dot_nt(fz_ref[...], beside_thrice(jnp.concatenate(rows, 0))))
        for n, yh in enumerate(yhs):
            for tile in range(3):
                lines[tile, line_rows(yh), :] = got[3 * n + tile]

    pieces[0].wait()
    for n in range(PIECES):
        pieces[2 * n + 1].wait()
        pieces[2 * n + 2].wait()
        over_lines(z_step, 4, n * HALF // PIECES, (n + 1) * HALF // PIECES)
    ky = ky_rows()
    lane = lax.broadcasted_iota(jnp.int32, (ROWS, LANES), 1)
    odd_block = (lane // HALF) % 2 == 1

    def y_step(kzs):
        even = []
        for pair in range(0, len(kzs), 2):
            data = [stacked(along_y(lines, 0, kz)) for kz in kzs[pair : pair + 2]]
            even += lane_parts(dot(fy_ref[...], jnp.concatenate(data, 1))[:ROWS])
        odd = []
        for kz in kzs:
            data = [stacked(along_y(lines, tile, kz)) for tile in (1, 2)]
            odd.append(lane_parts(dot(fyr_ref[...], jnp.concatenate(data, 1))[:ROWS]))
        for n, kz in enumerate(kzs):
            kzf = kz.astype(f32)
            plain = even[n]
            slopes = odd[n][0] * jnp.where(odd_block, kzf, ky)
            slopes = slopes + pltpu.roll(slopes, 32, 1)
            result[0, kz] = jnp.where(odd_block, slopes, plain)
            other = plain * jnp.where(lane >= 96, -kzf, -ky)
            other = other + pltpu.roll(other, 64, 1)
            result[1, kz] = jnp.where(lane >= 96, other, odd[n][1])

    sends = []
    for chunk in range(CHUNKS):
        first, last = planes_of(chunk)
        over_planes(y_step, first, last)
        source = result.at[:, pl.ds(first, last - first)]
        sends.append(pltpu.make_async_copy(source, out_refs[chunk], left.at[chunk]))
        sends[-1].start()
    for send in sends:
        send.wait()


def gradient_planes(cutoff_ref, here_ref, there_ref, height_ref, back_ref, planes, start):
    cut_x, cut_y, cut_z = cutoff_ref[0], cutoff_ref[1], cutoff_ref[2]
    which = jnp.clip(cut_x - (KEEP - 3), 0, 3)
    keep_y = jnp.where(jnp.abs(ky_rows()) <= cut_y.astype(f32), 1.0, 0.0).astype(f32)
    iy_ref, iyd_ref = (view(height_ref, n, 128) for n in range(2))
    for d in range(3):
        planes[d, HALF_KZ * LANES :, :] = jnp.zeros((LANES, LANES), f32)
    for first in range(0, HALF_KZ, 4):
        kzs = range(first, min(first + 4, HALF_KZ))
        rows = []
        for kz in kzs:
            keep = keep_y * jnp.where(start + kz <= cut_z, 1.0, 0.0).astype(f32)
            rows.append(jnp.concatenate([here_ref[kz] * keep, there_ref[kz] * keep], 1))
        high = back_ref[pl.ds(pl.multiple_of((4 + which) * 256, 256), 256), :]
        low = back_ref[pl.ds(pl.multiple_of((8 + which) * 256, 256), 256), :]
        got = triple(jnp.concatenate(rows, 0), high, low)
        data = [stacked(padded(got[n * ROWS : (n + 1) * ROWS])) for n in range(len(kzs))]
        for n, kz in enumerate(kzs):
            even = lane_parts(dot(iy_ref[...], data[n]))
            planes[0, kz * LANES : (kz + 1) * LANES, :] = even[1]
            planes[2, kz * LANES : (kz + 1) * LANES, :] = even[0]
        for n in range(0, len(kzs), 2):
            both = jnp.concatenate([one[:, :LANES] for one in data[n : n + 2]], 1)
            for k, part in enumerate(lane_parts(dot(iyd_ref[...], both))):
                kz = kzs[n + k]
                planes[1, kz * LANES : (kz + 1) * LANES, :] = part


def half_kernel(core_ref, cutoff_ref, here_ref, there_ref, height_ref, back_ref, planes):
    start = core_ref[0] * HALF_KZ
    gradient_planes(cutoff_ref, here_ref, there_ref, height_ref, back_ref, planes, start)


def gradient_kernel(
    core_ref, cutoff_ref, wave_ref, base_ref, state_ref, own_ref, here_ref, there_ref,
    ahead_ref, height_ref, back_ref, *refs
):
    *out_refs, planes, force_ref = refs
    core = core_ref[0]
    start = (1 - core) * HALF_KZ
    gradient_planes(cutoff_ref, here_ref, there_ref, height_ref, back_ref, planes, start)
    fz_ref = ahead_tables(ahead_ref)[0]
    iz_ref, izd_ref = view(back_ref, 0), view(back_ref, 1)
    y = lax.broadcasted_iota(jnp.int32, (HALF, LANES), 0) * 2
    y = y + lax.broadcasted_iota(jnp.int32, (HALF, LANES), 1) // N
    phase = ((wave_ref[0] * y) % N).astype(f32) * (2.0 * np.pi / N)
    force_ref[...] = forcing_amp * jnp.sin(phase)
    nothing = jnp.zeros((HALF, LANES), f32)

    def along_halves(d, yh):
        at = pl.ds(yh, 4 * (HALF_KZ + 1), stride=HALF)
        own, other = own_ref[d, at, :], planes[d, at, :]
        low = jnp.where(core == 0, own, other)
        high = jnp.where(core == 0, other, own)
        return padded(jnp.concatenate([low, high], 0)).T

    def physical_step(yhs):
        count = len(yhs)
        flat = [along_halves(d, yh)[:96] for d in range(2) for yh in yhs]
        steep = [along_halves(2, yh)[:96] for yh in yhs]
        flat = folded_lanes(dot(beside(jnp.concatenate(flat, 0)), iz_ref[...]))
        steep = folded_lanes(dot(beside(jnp.concatenate(steep, 0)), izd_ref[...]))
        for n, yh in enumerate(yhs):
            sets = [flat[96 * n :], flat[96 * (count + n) :], steep[96 * n :]]
            grads = [[one[HALF * i : HALF * (i + 1)] for i in range(3)] for one in sets]
            b = [base_ref[i, :, columns(yh)] for i in range(3)]
            s = [state_ref[i, :, columns(yh)] for i in range(3)]
            comb, comb_base = [], []
            for i in range(3):
                coupling = sum(
                    jnp.where(core == 0, grads[j][i], grads[i][j]) * s[j] for j in range(3)
                )
                comb.append(s[i] - time_step * coupling)
                drive = sum(grads[j][i] * b[j] for j in range(3))
                if i == 0:
                    drive = drive - force_ref[pl.ds(yh, 1), :]
                comb_base.append(b[i] - time_step * drive)
            rows = [comb[1], comb_base[1], comb[2], comb_base[2]]
            rows += [comb[0], comb_base[0], nothing, nothing]
            got = dot_nt(fz_ref[...], beside_thrice(jnp.concatenate(rows, 0)))
            depth = LINE // CHUNKS
            rows = pl.ds(pl.multiple_of(yh * depth, 8), depth)
            for tile, part in enumerate(lane_parts(got)):
                for chunk in range(CHUNKS):
                    out_refs[chunk][tile, rows, :] = part[chunk * depth : (chunk + 1) * depth]

    over_lines(physical_step, 8)


def spectral_kernel(
    chunk, core_ref, cutoff_ref, lines_ref, flux_ref,
    ahead_ref, along_ref, near_ref, far_ref,
):
    _, fy_ref, fyr_ref = ahead_tables(ahead_ref)
    core = core_ref[0]
    cut_x, cut_y, cut_z = cutoff_ref[0], cutoff_ref[1], cutoff_ref[2]
    first, last = planes_of(chunk)
    extra = last - first
    ky = ky_rows()
    kx = kx_lanes()
    keep_y = jnp.where(jnp.abs(ky) <= cut_y.astype(f32), 1.0, 0.0).astype(f32)
    keep_x = jnp.where(kx <= cut_x.astype(f32), 1.0, 0.0).astype(f32)
    keep_xy = keep_y * keep_x
    square_xy = ky * ky + kx * kx
    lane = lax.broadcasted_iota(jnp.int32, (ROWS, LANES), 1)
    near_ref[extra] = jnp.zeros((ROWS, LANES), f32)
    far_ref[extra] = jnp.zeros((ROWS, LANES), f32)

    def kept_z(kz):
        return jnp.where(kz <= cut_z, 1.0, 0.0).astype(f32)

    def spectral_step(kzs):
        fields = [[], [], []]
        for pair in range(0, len(kzs), 2):
            ks = kzs[pair : pair + 2]
            data = [
                jnp.concatenate(
                    [stacked(along_y(lines_ref, t, kz, LINE // CHUNKS)) for kz in ks], 1
                )
                for t in (0, 1)
            ]
            even = lane_parts(dot(fy_ref[...], data[0])[:ROWS])
            odd = lane_parts(dot(fyr_ref[...], data[1])[:ROWS])
            for n, kz in enumerate(ks):
                flux = flux_ref[0, kz - first]
                fields[0].append(odd[n] + flux_ref[1, kz - first])
                fields[1].append(jnp.where(lane < 64, even[n], flux))
                fields[2].append(jnp.where(lane < 64, flux, even[n]))
        data = [beside(jnp.concatenate(field, 0)) for field in fields]
        modes = [folded_lanes(dot(data[max(n - 1, 0)], view(along_ref, n)[...])) for n in range(4)]
        results = [[], [], [], []]
        for n, kz in enumerate(kzs):
            kzf = kz.astype(f32)
            vx, slope, uy, uz = (mode[n * ROWS : (n + 1) * ROWS] for mode in modes)
            square = square_xy + kzf * kzf
            factor = keep_xy * kept_z(kz) / (1.0 + viscosity * time_step * square)
            share = (slope + ky * uy + kzf * uz) / jnp.where(square > 0, square, 1.0)
            results[0].append(factor * vx)
            results[1].append(factor * share)
            results[2].append(factor * (uy - ky * share))
            results[3].append(factor * (uz - kzf * share))
        got = [
            dot(
                beside(jnp.concatenate(result, 0)),
                along_ref[pl.ds(pl.multiple_of((4 + core * 4 + n) * 256, 256), 256), :],
            )
            for n, result in enumerate(results)
        ]
        got = [folded_lanes(part) for part in (got[0] + got[1], got[2], got[3])]
        for n, kz in enumerate(kzs):
            x, y, z = (part[n * ROWS : (n + 1) * ROWS] for part in got)
            near_ref[kz - first] = jnp.where(lane < 48, x, jnp.where(lane < 96, y, z))
            away = jnp.where(
                (lane >= 64) & (lane < 112), x, jnp.where((lane >= 32) & (lane < 64), z, y)
            )
            far_ref[kz - first] = pltpu.roll(away, 64, 1)
            shift = (kz - first) * 16
            near_ref[extra] += pltpu.roll(jnp.where(lane < 16, z, 0.0), shift, 1)
            rest = jnp.where((lane >= 64) & (lane < 80), z, 0.0)
            far_ref[extra] += pltpu.roll(rest, (shift + 64) % LANES, 1)

    over_planes(spectral_step, first, last)


def inverse_y(near_ref, far_ref, iy_ref, planes):
    count = near_ref.shape[0] - 1
    rest = near_ref[count] + far_ref[count]
    for kz in range(count):
        turned = pltpu.roll(rest, (LANES - kz * 16) % LANES, 1) if kz else rest
        data = jnp.concatenate([near_ref[kz] + far_ref[kz], turned], 1)
        got = lane_parts(dot(iy_ref[...], stacked(padded(data))))
        for tile in range(2):
            planes[tile, kz * LANES : (kz + 1) * LANES, :] = got[tile]
    if count < CHUNK:
        blank = jnp.zeros(((CHUNK - count) * LANES, LANES), f32)
        for tile in range(2):
            planes[tile, count * LANES :, :] = blank


def inverse_kernel(near_a, far_a, near_b, far_b, height_ref, planes_a, planes_b):
    iy_ref = view(height_ref, 0, 128)
    inverse_y(near_a, far_a, iy_ref, planes_a)
    inverse_y(near_b, far_b, iy_ref, planes_b)


def final_kernel(
    near_ref, far_ref, planes_a, planes_b, state_ref, base_ref, height_ref, back_ref,
    base_out, state_out, planes_c,
):
    iy_ref = view(height_ref, 0, 128)
    iz_ref, izr_ref = view(back_ref, 2), view(back_ref, 3)
    inverse_y(near_ref, far_ref, iy_ref, planes_c)

    def along_chunks(tile, yh):
        parts = [
            ref[tile, pl.ds(yh, 4 * CHUNK, stride=HALF), :]
            for ref in (planes_a, planes_b, planes_c)
        ]
        return padded(jnp.concatenate(parts, 0)).T

    def z_step(yhs):
        data = [along_chunks(0, yh) for yh in yhs]
        rest = [along_chunks(1, yh)[:16] for yh in yhs]
        turned = beside(jnp.concatenate([one[:48] for one in data], 0))
        plain = beside(jnp.concatenate([one[48:] for one in data] + rest, 0))
        turned = folded_lanes(dot(turned, izr_ref[...]))
        plain = folded_lanes(dot(plain, iz_ref[...]))
        for n, yh in enumerate(yhs):
            at = columns(yh)
            first = turned[48 * n : 48 * n + 48]
            second = plain[80 * n : 80 * n + 80]
            third = plain[80 * len(yhs) + 16 * n :][:16]
            state_out[0, :, at] = first[:32] - state_ref[0, :, at]
            state_out[1, :, at] = second[16:48] - state_ref[1, :, at]
            state_out[2, :, at] = second[48:80] - state_ref[2, :, at]
            base_out[0, :, at] = first[32:48] - base_ref[0, :, at]
            base_out[1, :, at] = second[:16] - base_ref[1, :, at]
            base_out[2, :, at] = third - base_ref[2, :, at]

    over_lines(z_step, 8)


interpret = False


def call(kernel, outs, scratch, inputs, room, in_smem=0, in_hbm=0, out_hbm=False):
    whole = pl.BlockSpec(memory_space=pltpu.VMEM)
    small = pl.BlockSpec(memory_space=pltpu.SMEM)
    far = pl.BlockSpec(memory_space=pltpu.HBM)
    return pl.pallas_call(
        kernel,
        out_shape=outs,
        in_specs=[small] * in_smem
        + [far] * in_hbm
        + [whole] * (len(inputs) - in_smem - in_hbm),
        out_specs=jax.tree.map(lambda _: far if out_hbm else whole, outs),
        scratch_shapes=scratch,
        compiler_params=pltpu.CompilerParams(vmem_limit_bytes=room * 2**20),
        cost_estimate=pl.CostEstimate(flops=1000, bytes_accessed=1000, transcendentals=0),
        interpret=interpret,
    )(*inputs)


def body(base, state, wavenumber, cutoff):
    t = {name: jnp.asarray(value) for name, value in tables().items()}
    core = lax.axis_index("comp")
    seg_count = lax.axis_size("seg")
    own_base = base[0]
    own_state = state[0, 0]
    base_half = lax.dynamic_slice_in_dim(own_base, core * 16, 16, 1)
    back = [((s + 1) % seg_count, s) for s in range(seg_count)]
    around = [(2 * i, 2 * o) for i, o in back] + [(2 * o + 1, 2 * i + 1) for i, o in back]
    base_next = lax.ppermute(base_half, "seg", back)
    state_next = lax.ppermute(own_state, ("seg", "comp"), around)
    sds = jax.ShapeDtypeStruct
    core_at = core.reshape(1)
    swap = [(0, 1), (1, 0)]
    here_own = call(
        base_kernel,
        sds((HALF_KZ, ROWS, LANES), f32),
        [
            pltpu.VMEM((1, HALF * LINE, LANES), f32),
            pltpu.VMEM(own_base.shape, f32),
            pltpu.VMEM(t["ahead"].shape, bf16),
            pltpu.SemaphoreType.DMA((PIECES + 1,)),
        ],
        [core_at, own_base, t["ahead"]],
        room=56,
        in_smem=1,
        in_hbm=2,
    )
    there_own = lax.ppermute(here_own, "slab", swap)
    here_other = lax.ppermute(here_own, "comp", swap)
    counts = [planes_of(chunk)[1] - planes_of(chunk)[0] for chunk in range(CHUNKS)]
    flux = call(
        flux_kernel,
        [sds((2, count, ROWS, LANES), f32) for count in counts],
        [
            pltpu.VMEM((3, HALF * LINE, LANES), f32),
            pltpu.VMEM(own_base.shape, f32),
            pltpu.VMEM(own_state.shape, f32),
            pltpu.VMEM(t["ahead"].shape, bf16),
            pltpu.VMEM((2, NKZ, ROWS, LANES), f32),
            pltpu.SemaphoreType.DMA((2 * PIECES + 1,)),
            pltpu.SemaphoreType.DMA((CHUNKS,)),
        ],
        [core_at, own_base, own_state, t["ahead"]],
        room=56,
        in_smem=1,
        in_hbm=3,
        out_hbm=True,
    )
    there_own, flux = lax.optimization_barrier((there_own, flux))
    there_other = lax.ppermute(there_own, "comp", swap)
    half_planes = sds((3, (HALF_KZ + 1) * LANES, LANES), f32)
    own_planes = call(
        half_kernel,
        half_planes,
        [],
        [core_at, cutoff, here_own, there_own, t["height"], t["back"]],
        room=12,
        in_smem=2,
    )
    lines = call(
        gradient_kernel,
        [sds((2, HALF * 4 * CHUNK, LANES), f32)] * CHUNKS,
        [pltpu.VMEM(half_planes.shape, f32), pltpu.VMEM((HALF, LANES), f32)],
        [core_at, cutoff, wavenumber, own_base, own_state, own_planes, here_other, there_other]
        + [t["ahead"], t["height"], t["back"]],
        room=20,
        in_smem=3,
    )
    near, far = [], []
    for chunk in range(CHUNKS):
        near_part, far_part = call(
            functools.partial(spectral_kernel, chunk),
            [sds((counts[chunk] + 1, ROWS, LANES), f32)] * 2,
            [],
            [core_at, cutoff, lines[chunk], flux[chunk], t["ahead"], t["along"]],
            room=10,
            in_smem=2,
        )
        near.append(near_part)
        far.append(lax.ppermute(far_part, "slab", swap))
    planes = sds((2, CHUNK * LANES, LANES), f32)
    planes_a, planes_b = call(
        inverse_kernel, [planes] * 2, [], [near[0], far[0], near[1], far[1], t["height"]], room=10
    )
    base_gap, state_gap = call(
        final_kernel,
        [sds((3, 16, N * N), f32), sds((3, HALF, N * N), f32)],
        [pltpu.VMEM((2, CHUNK * LANES, LANES), f32)],
        [near[2], far[2], planes_a, planes_b, state_next, base_next, t["height"], t["back"]],
        room=16,
    )
    return base_gap[None], state_gap[None, None]


def solution(mesh):
    paired = mesh.shape["slab"] == 2 and mesh.shape["comp"] == 2
    return jax.shard_map(
        body if paired else general_body,
        mesh=mesh,
        in_specs=(
            P(("groups", "seg"), None, "slab", None),
            P(("groups", "seg"), "comp", None, "slab", None),
            P("groups"),
            P("groups"),
        ),
        out_specs=(
            P(("groups", "seg"), None, ("slab", "comp"), None),
            P(("groups", "seg"), "comp", None, "slab", None),
        ),
        check_vma=False,
    )
```

```python
import functools

import jax
import jax.numpy as jnp
import ml_dtypes
import numpy as np
from jax import lax
from jax.experimental import pallas as pl
from jax.experimental.pallas import tpu as pltpu
from jax.sharding import PartitionSpec as P

N = 64
HALF = 32
KEEP = N // 3
NKZ = KEEP + 1
NKY = 44
ROWS = 2 * NKY
CHUNK = 8
CHUNKS = 3
LINE = CHUNKS * CHUNK * 4
HALF_KZ = NKZ // 2
LANES = 128

viscosity = 0.025
time_step = 0.02
forcing_amp = 10.0

f32 = jnp.float32
bf16 = jnp.bfloat16


highest = lax.Precision.HIGHEST


def swapped(value, axis, apart):
    mask = 2**apart
    pairs = [(source, source ^ mask) for source in range(lax.axis_size(axis))]
    return lax.ppermute(value, axis, pairs)


def shifted(block, axis, distance):
    devices = range(lax.axis_size(axis))
    route = [((i - distance) % len(devices), i) for i in devices]
    return lax.ppermute(block, axis, route)


def wavenumbers(grid_points):
    position = jnp.arange(grid_points, dtype=jnp.int32)
    return jnp.where(position < grid_points // 2, position, position - grid_points)


def phases(first, second, grid_points):
    product = jnp.mod(first[:, None] * second[None, :], grid_points)
    return product.astype(jnp.float32) * (2.0 * jnp.pi / grid_points)


def combine(partial_value, columns):
    cosine_part = partial_value[0]
    sine_part = partial_value[1]
    real_part = cosine_part[..., :columns] - sine_part[..., columns:]
    imag_part = cosine_part[..., columns:] + sine_part[..., :columns]
    return jnp.concatenate([real_part, imag_part], axis=-1)


def times_unit(values, wave, columns):
    return jnp.concatenate([-wave * values[..., columns:], wave * values[..., :columns]], axis=-1)


def doubled(values):
    return jnp.concatenate([values, values], axis=-1)


def general_body(base, state, wavenumber, cutoff):
    grid_points = N
    base = base.reshape(base.shape[0], 3, base.shape[2], grid_points, grid_points)
    state = state.reshape(
        state.shape[0], state.shape[1], 3, state.shape[3], grid_points, grid_points
    )
    slab_rows = state.shape[3]
    half_rows = slab_rows // 2
    slab_count = lax.axis_size("slab")
    group_count = slab_count * lax.axis_size("comp")
    core_side = lax.axis_index("comp")
    block_number = lax.axis_index(("slab", "comp"))
    base_whole = base[0]
    base_half = lax.dynamic_slice_in_dim(base_whole, core_side * half_rows, half_rows, 1)
    own_state = state[0, 0]
    spectrum = wavenumbers(grid_points)
    one_third = grid_points // 3
    row_total = (2 * one_third + group_count) // group_count * group_count
    row_index = jnp.arange(row_total, dtype=jnp.int32)
    row_alive_mask = row_index <= 2 * one_third
    row_wave = jnp.where(row_index <= one_third, row_index, row_index - (2 * one_third + 1))
    row_wave = jnp.where(row_alive_mask, row_wave, 0)
    width = grid_points // 2
    rows_per_block = row_total // group_count
    alive_flags = row_alive_mask.astype(jnp.float32)
    grid_index = jnp.arange(grid_points, dtype=jnp.int32)
    column_index = grid_index[:width]
    angle_grid = phases(grid_index, grid_index, grid_points)
    angle_ahead = phases(grid_index, column_index, grid_points)
    angle_behind = phases(column_index, grid_index, grid_points)
    column_weight = jnp.where(column_index == 0, 1.0, 2.0).astype(jnp.float32)[:, None]
    forward_z = jnp.concatenate([jnp.cos(angle_ahead), -jnp.sin(angle_ahead)], axis=1)
    inverse_z = (
        jnp.concatenate(
            [jnp.cos(angle_behind) * column_weight, -jnp.sin(angle_behind) * column_weight], axis=0
        )
        / grid_points
    )
    phase_angle_rows = phases(row_wave, grid_index, grid_points)
    forward_transform_y = (
        jnp.stack([jnp.cos(phase_angle_rows), -jnp.sin(phase_angle_rows)])
        * alive_flags[None, :, None]
    )
    inverse_y = (
        jnp.stack([jnp.cos(phase_angle_rows).T, jnp.sin(phase_angle_rows).T])
        * alive_flags[None, None, :]
        / grid_points
    )
    forward_x = jnp.stack([jnp.cos(angle_grid), -jnp.sin(angle_grid)])
    inverse_x = jnp.stack([jnp.cos(angle_grid), jnp.sin(angle_grid)]) / grid_points
    table_ahead = forward_x.reshape(2, grid_points, slab_count, slab_rows)
    table_back = inverse_x.reshape(2, slab_count, slab_rows, grid_points)
    local_wave = lax.dynamic_slice_in_dim(row_wave, block_number * rows_per_block, rows_per_block)
    local_alive_mask = lax.dynamic_slice_in_dim(
        alive_flags, block_number * rows_per_block, rows_per_block
    )
    shape_local = (grid_points, rows_per_block, width)
    wave_x = jnp.broadcast_to(spectrum[:, None, None], shape_local)
    wave_y = jnp.broadcast_to(local_wave[None, :, None], shape_local)
    wave_z = jnp.broadcast_to(spectrum[:width][None, None, :], shape_local)
    inside = (
        (jnp.abs(wave_x) <= cutoff[0])
        & (jnp.abs(wave_y) <= cutoff[1])
        & (jnp.abs(wave_z) <= cutoff[2])
    )
    keep_mask = doubled(inside.astype(jnp.float32) * local_alive_mask[None, :, None])
    float_x = wave_x.astype(jnp.float32)
    float_y = wave_y.astype(jnp.float32)
    float_z = wave_z.astype(jnp.float32)
    ksquare = float_x * float_x + float_y * float_y + float_z * float_z
    safe_square = doubled(jnp.where(ksquare > 0, ksquare, jnp.ones_like(ksquare)))
    damping = doubled(1.0 / (1.0 + viscosity * time_step * ksquare))
    double_x = doubled(float_x)
    double_y = doubled(float_y)
    double_z = doubled(float_z)

    def project(field):
        divergence = (double_x * field[0] + double_y * field[1] + double_z * field[2]) / safe_square
        return jnp.stack(
            [
                field[0] - double_x * divergence,
                field[1] - double_y * divergence,
                field[2] - double_z * divergence,
            ]
        )

    def yz_forward(field):
        along_z = jnp.einsum("...z,zk->...k", field, forward_z, precision=highest)
        partial_value = jnp.einsum(
            "sry,...yk->s...rk", forward_transform_y, along_z, precision=highest
        )
        return combine(partial_value, width)

    def yz_inverse(modes):
        partial_value = jnp.einsum("syr,...rk->s...yk", inverse_y, modes, precision=highest)
        return jnp.einsum(
            "...k,kz->...z", combine(partial_value, width), inverse_z, precision=highest
        )

    def spectral(state_fields, base_fields):
        state_modes = yz_forward(state_fields)[:, :, None]
        base_modes = yz_forward(base_fields)[:, :, None]
        state_got = lax.all_to_all(
            state_modes, ("slab", "comp"), split_axis=4, concat_axis=2, tiled=True
        )
        base_got = lax.all_to_all(
            base_modes, ("slab", "comp"), split_axis=4, concat_axis=2, tiled=True
        )
        item_count = state_got.shape[0]
        part_count = state_got.shape[1]
        state_split = state_got.reshape(
            item_count, part_count, slab_count, 2, slab_rows, rows_per_block, 2 * width
        )
        state_partial = jnp.einsum(
            "srpx,ijpcxyk->sijcryk", table_ahead, state_split, precision=highest
        )
        base_lined = base_got.reshape(item_count, 1, grid_points, rows_per_block, 2 * width)
        base_partial = jnp.einsum("srx,ijxyk->sijryk", forward_x, base_lined, precision=highest)
        return (combine(state_partial, width), combine(base_partial, width))

    state_first, base_first = spectral(own_state[:, None], base_half[:, None])
    state_hat = state_first[:, 0] * keep_mask
    base_hat = base_first[:, 0] * keep_mask
    grad_hat = jnp.stack(
        [
            times_unit(base_hat, float_x, width),
            times_unit(base_hat, float_y, width),
            times_unit(base_hat, float_z, width),
        ],
        axis=1,
    )
    grad_hat = grad_hat.reshape(9, grid_points, rows_per_block, 2 * width)
    grad_partial = jnp.einsum("sxr,iryk->sixyk", inverse_x, grad_hat, precision=highest)
    grad_spread = combine(grad_partial, width).reshape(
        9, group_count, half_rows, rows_per_block, 2 * width
    )
    own_rows = yz_inverse(
        lax.all_to_all(grad_spread, ("slab", "comp"), split_axis=1, concat_axis=3, tiled=True)[:, 0]
    )
    other_rows = swapped(own_rows, "comp", 0)
    gradient = jnp.where(
        core_side == 0,
        jnp.concatenate([own_rows, other_rows], axis=1),
        jnp.concatenate([other_rows, own_rows], axis=1),
    )
    gradient = gradient.reshape(3, 3, slab_rows, grid_points, grid_points)
    gradient_half = lax.dynamic_slice_in_dim(gradient, core_side * half_rows, half_rows, 2)
    flux_terms = own_state[:, None] * base_whole[None, :]
    coupling_matrix = jnp.where(core_side == 0, gradient, jnp.swapaxes(gradient, 0, 1))
    coupling = jnp.sum(coupling_matrix * own_state[None, :], axis=1)
    forcing_phase = phases(wavenumber, grid_index, grid_points)[0]
    forcing = forcing_amp * jnp.sin(forcing_phase)[None, :, None]
    base_drive = jnp.sum(gradient_half * base_half[None, :], axis=1)
    base_drive = jnp.concatenate([base_drive[:1] - forcing[None], base_drive[1:]], axis=0)
    state_fields = jnp.concatenate([flux_terms, coupling[:, None]], axis=1)
    drive_modes, base_modes_two = spectral(state_fields, base_drive[:, None])
    orient = jnp.array([1.0, -1.0], dtype=jnp.float32)[None, :, None, None, None]
    divergence = (
        times_unit(drive_modes[:, 0], float_x, width)
        + times_unit(drive_modes[:, 1], float_y, width)
        + times_unit(drive_modes[:, 2], float_z, width)
    )
    state_drive = keep_mask * (orient * divergence + drive_modes[:, 3])
    new_hat = damping * project(state_hat - time_step * state_drive)
    base_new_hat = damping * project(base_hat - time_step * keep_mask * base_modes_two[:, 0])
    state_partial = jnp.einsum("spxr,icryk->sipcxyk", table_back, new_hat, precision=highest)
    state_back = combine(state_partial, width).reshape(
        3, group_count, slab_rows, rows_per_block, 2 * width
    )
    base_partial = jnp.einsum("sxr,iryk->sixyk", inverse_x, base_new_hat, precision=highest)
    base_back = combine(base_partial, width).reshape(
        3, group_count, half_rows, rows_per_block, 2 * width
    )
    state_got = lax.all_to_all(
        state_back, ("slab", "comp"), split_axis=1, concat_axis=3, tiled=True
    )
    base_got = lax.all_to_all(base_back, ("slab", "comp"), split_axis=1, concat_axis=3, tiled=True)
    state_new = yz_inverse(state_got[:, 0])
    base_new = yz_inverse(base_got[:, 0])
    base_later, later_state = shifted((base_half, own_state), "seg", -1)
    prior_state = shifted(own_state, "seg", 1)
    neighbour = jnp.where(core_side == 0, later_state, prior_state)
    base_gap = (base_new - base_later).reshape(1, 3, half_rows, grid_points * grid_points)
    state_gap = (state_new - neighbour).reshape(1, 1, 3, slab_rows, grid_points * grid_points)
    return (base_gap, state_gap)


def halves(table):
    high = table.astype(np.float32).astype(ml_dtypes.bfloat16)
    low = (table - high.astype(np.float64)).astype(ml_dtypes.bfloat16)
    return high, low


def left_table(table, depth):
    padded = np.zeros((table.shape[0], depth))
    padded[:, : table.shape[1]] = table
    high, low = halves(padded)
    return np.concatenate(
        [np.concatenate([high, high], 1), np.concatenate([low, np.zeros_like(low)], 1)], 0
    )


def right_table(table, depth):
    return np.ascontiguousarray(left_table(table.T, depth).T)


def planes_of(chunk):
    return chunk * CHUNK, min((chunk + 1) * CHUNK, NKZ)


def ky_values():
    index = np.arange(NKY)
    wave = np.where(index <= KEEP, index, index - (2 * KEEP + 1))
    alive = (index <= 2 * KEEP).astype(np.float64)
    return wave * alive, alive


@functools.cache
def tables():
    out = {}
    z = np.arange(N)
    kz = np.arange(NKZ)
    angle = 2 * np.pi * kz[:, None] * z[None, :] / N
    weight = np.where(kz == 0, 1.0, 2.0)[:, None] / N
    forward = np.zeros((2, 2, CHUNKS * CHUNK, 2, N))
    inverse = np.zeros((NKZ, 2, 2, 2, N))
    turned = np.zeros((NKZ, 2, 2, 2, N))
    slope = np.zeros((NKZ, 2, 2, 2, N))
    for y2 in range(2):
        forward[y2, 0, :NKZ, y2] = np.cos(angle)
        forward[y2, 1, :NKZ, y2] = -np.sin(angle)
        inverse[:, y2, 0, y2] = weight * np.cos(angle)
        inverse[:, y2, 1, y2] = -weight * np.sin(angle)
        turned[:, y2, 0, y2] = weight * np.sin(angle)
        turned[:, y2, 1, y2] = weight * np.cos(angle)
        slope[:, y2, 0, y2] = -weight * kz[:, None] * np.sin(angle)
        slope[:, y2, 1, y2] = -weight * kz[:, None] * np.cos(angle)
    forward = np.moveaxis(forward.reshape(4, CHUNKS, CHUNK, 2 * N), 1, 0)
    out["fz"] = left_table(forward.reshape(LINE, 2 * N), 128)

    def by_chunk(table):
        wide = np.zeros((CHUNKS, CHUNK, 4, 2 * N))
        for chunk in range(CHUNKS):
            first, last = planes_of(chunk)
            wide[chunk, : last - first] = table.reshape(NKZ, 4, 2 * N)[first:last]
        return right_table(wide.reshape(LINE, 2 * N), 128)

    out["iz"] = by_chunk(inverse)
    out["izr"] = by_chunk(turned)

    def by_half(table):
        wide = np.zeros((2, HALF_KZ + 1, 4, 2 * N))
        wide[:, :HALF_KZ] = table.reshape(2, HALF_KZ, 4, 2 * N)
        return right_table(wide.reshape(8 * HALF_KZ + 8, 2 * N), 128)

    out["izg"] = by_half(inverse)
    out["izd"] = by_half(slope)
    ky, alive = ky_values()
    y = 2 * np.arange(HALF)[None, :] + np.arange(2)[:, None]
    phase = 2 * np.pi * ky[:, None, None] * y[None] / N
    cosine = np.cos(phase) * alive[:, None, None]
    sine = np.sin(phase) * alive[:, None, None]
    plain = np.zeros((2, NKY, 2, 2, HALF))
    plain[0, :, :, 0] = cosine
    plain[0, :, :, 1] = sine
    plain[1, :, :, 0] = -sine
    plain[1, :, :, 1] = cosine
    rotated = np.stack([-plain[1], plain[0]])
    out["fy"] = left_table(plain.reshape(ROWS, 128), 128)
    out["fyr"] = left_table(rotated.reshape(ROWS, 128), 128)
    back = np.zeros((2, 2, HALF, 2, NKY))
    cos_t = np.moveaxis(cosine, 0, -1) / N
    sin_t = np.moveaxis(sine, 0, -1) / N
    back[:, 0, :, 0] = cos_t
    back[:, 0, :, 1] = -sin_t
    back[:, 1, :, 0] = sin_t
    back[:, 1, :, 1] = cos_t
    back_slope = np.zeros_like(back)
    back_slope[..., 0, :] = ky * back[..., 1, :]
    back_slope[..., 1, :] = -ky * back[..., 0, :]
    out["iy"] = left_table(back.reshape(128, ROWS), 128)
    out["iyd"] = left_table(back_slope.reshape(128, ROWS), 128)
    grad_high, grad_low = [], []
    x = np.arange(N)
    apart = x[:HALF, None] - x[None, :]
    for cut in range(KEEP - 3, KEEP + 1):
        k = np.arange(cut + 1)
        wk = np.where(k == 0, 1.0, 2.0) / N
        arg = 2 * np.pi * apart[..., None] * k / N
        keep = (np.cos(arg) * wk).sum(-1)
        derive = (-np.sin(arg) * wk * k).sum(-1)
        table = np.zeros((2, 4, HALF, 2, 4, HALF))
        for comp in range(3):
            for side in range(2):
                rows = slice(side * HALF, (side + 1) * HALF)
                table[side, comp, :, 0, comp, :] = keep[:, rows].T
                table[side, comp, :, 1, comp, :] = derive[:, rows].T
        high, low = halves(table.reshape(256, 256))
        grad_high.append(high)
        grad_low.append(low)
    out["gxh"] = np.stack(grad_high)
    out["gxl"] = np.stack(grad_low)
    kx = np.arange(HALF)
    live = (kx <= KEEP).astype(np.float64)
    xl = np.arange(HALF)
    arg = 2 * np.pi * xl[:, None] * kx[None, :] / N
    value = np.concatenate([np.cos(arg) * live, np.sin(arg) * live], 1)
    change = np.concatenate([kx * np.sin(arg) * live, -kx * np.cos(arg) * live], 1)

    def coefficients(blocks):
        table = np.zeros((4, HALF, 2, 2 * HALF))
        for block, part, what in blocks:
            table[block, :, part] = what
        return table.reshape(LANES, LANES)

    first = coefficients([(0, 0, value), (1, 1, value), (2, 0, change), (3, 0, value)])
    last = coefficients([(0, 0, change), (1, 0, value), (2, 0, value), (3, 1, value)])
    fall = first.reshape(LANES, 2, 2, HALF)
    fall = np.stack([-kx * fall[:, :, 1], kx * fall[:, :, 0]], 2).reshape(LANES, LANES)
    out["fx"] = np.stack([right_table(part, 128) for part in (first, fall, first, last)])
    wx = np.where(kx == 0, 1.0, 2.0) * live / N
    for core in range(2):
        ix = np.zeros((4, 2, 2 * HALF, LANES))
        for side in range(2):
            xs = np.arange(HALF) + side * HALF
            arg = 2 * np.pi * kx[:, None] * xs[None, :] / N
            give = np.concatenate([np.cos(arg) * wx[:, None], np.sin(arg) * wx[:, None]], 0)
            drop = np.concatenate(
                [np.sin(arg) * (wx * kx)[:, None], -np.cos(arg) * (wx * kx)[:, None]], 0
            )
            own = slice(core * 16, core * 16 + 16)

            def put(quantity, part, lane, what):
                at = (lane + side * 64 + np.arange(what.shape[1])) % LANES
                ix[quantity, part][:, at] = what

            put(0, 0, 0, give)
            put(1, 0, 0, drop)
            put(0, 1, 32, give[:, own])
            put(1, 1, 32, drop[:, own])
            put(2, 1, 48, give[:, own])
            put(2, 0, 64, give)
            put(3, 0, 96, give)
            put(3, 1, 0, give[:, own])
        out["ix%d" % core] = np.stack(
            [right_table(part, 128) for part in ix.reshape(4, LANES, LANES)]
        )
    out["ix"] = np.stack([out.pop("ix0"), out.pop("ix1")])
    merged = {}
    merged["ahead"] = np.concatenate([out["fz"], out["fy"], out["fyr"]], 0)
    gx = [out["gxh"].reshape(-1, 256), out["gxl"].reshape(-1, 256)]
    square = [out[name] for name in ("iy", "iyd", "izg", "izd", "iz", "izr")]
    merged["back"] = np.concatenate(square + gx, 0)
    merged["along"] = np.concatenate([out["fx"].reshape(-1, 256), out["ix"].reshape(-1, 256)], 0)
    return merged


def view(ref, index, rows=256, start=0):
    return ref.at[pl.ds(start + index * rows, rows), :]


def ahead_tables(ref):
    return view(ref, 0, 2 * LINE), view(ref, 0, 2 * ROWS, 2 * LINE), view(ref, 1, 2 * ROWS, 2 * LINE)


def ky_rows():
    row = lax.broadcasted_iota(jnp.int32, (ROWS, LANES), 0)
    index = jnp.where(row < NKY, row, row - NKY)
    wave = jnp.where(index <= KEEP, index, index - (2 * KEEP + 1))
    return jnp.where(index <= 2 * KEEP, wave, 0).astype(f32)


def kx_lanes():
    lane = lax.broadcasted_iota(jnp.int32, (1, LANES), 1) % HALF
    return jnp.where(lane <= KEEP, lane, 0).astype(f32)


def split(values):
    high = values.astype(bf16)
    low = (values - high.astype(f32)).astype(bf16)
    return high, low


def dot(a, b):
    return jnp.dot(a, b, preferred_element_type=f32)


def dot_nt(a, b):
    return lax.dot_general(a, b, (((1,), (1,)), ((), ())), preferred_element_type=f32)


def stacked(values):
    high, low = split(values)
    return jnp.concatenate([high, low], 0)


def beside(values):
    high, low = split(values)
    return jnp.concatenate([high, low], 1)


def folded(result):
    rows = result.shape[0] // 2
    return result[:rows] + result[rows:]


def folded_lanes(result):
    return result[:, :LANES] + result[:, LANES:]


def padded(values, rows=128):
    return jnp.concatenate([values, jnp.zeros((rows - values.shape[0], values.shape[1]), f32)], 0)


def triple(values, high_ref, low_ref):
    high, low = split(values)
    return dot(high, high_ref) + dot(low, high_ref) + dot(high, low_ref)


def columns(yh):
    return pl.ds(pl.multiple_of(yh * LANES, LANES), LANES)


def along_y(ref, tile, kz, line=LINE):
    at = kz % CHUNK + (0 if line == LINE // CHUNKS else kz // CHUNK * (4 * CHUNK))
    return jnp.concatenate(
        [ref[tile, pl.ds(q * CHUNK + at, HALF, stride=line), :] for q in range(4)], 0
    )


def line_rows(yh):
    return pl.ds(pl.multiple_of(yh * LINE, 8), LINE)


def lane_parts(values):
    return [values[:, at : at + LANES] for at in range(0, values.shape[1], LANES)]


def over_planes(step, first=0, last=NKZ):
    def four(index, _):
        step([first + index * 4 + k for k in range(4)])
        return 0

    count = (last - first) // 4
    lax.fori_loop(0, count, four, 0)
    if first + count * 4 < last:
        step([jnp.int32(kz) for kz in range(first + count * 4, last)])


def over_lines(step, many, first=0, last=HALF):
    def some(index, _):
        step([first + index * many + k for k in range(many)])
        return 0

    lax.fori_loop(0, (last - first) // many, some, 0)


PIECES = 4


def base_kernel(core_ref, base_hbm, ahead_hbm, out_ref, lines, base_ref, ahead_ref, arrived):
    nothing = jnp.zeros((HALF, LANES), f32)
    wide = N * N // PIECES
    table = pltpu.make_async_copy(ahead_hbm, ahead_ref, arrived.at[PIECES])
    pieces = [
        pltpu.make_async_copy(
            base_hbm.at[:, :, pl.ds(n * wide, wide)],
            base_ref.at[:, :, pl.ds(n * wide, wide)],
            arrived.at[n],
        )
        for n in range(PIECES)
    ]
    pieces[0].start()
    table.start()
    for piece in pieces[1:]:
        piece.start()
    fz_ref, fy_ref, _ = ahead_tables(ahead_ref)
    table.wait()
    many = HALF // PIECES
    for n, piece in enumerate(pieces):
        piece.wait()
        yhs = range(n * many, (n + 1) * many)
        rows = []
        for yh in yhs:
            at = slice(yh * LANES, (yh + 1) * LANES)
            rows += [base_ref[i, :, at] for i in range(3)] + [nothing]
        got = folded(dot_nt(fz_ref[...], beside(jnp.concatenate(rows, 0))))
        for yh, part in zip(yhs, lane_parts(got)):
            lines[0, yh * LINE : (yh + 1) * LINE, :] = part
    start = core_ref[0] * HALF_KZ
    for pair in range(0, HALF_KZ, 2):
        ks = range(pair, min(pair + 2, HALF_KZ))
        data = jnp.concatenate([stacked(along_y(lines, 0, start + k)) for k in ks], 1)
        got = folded(dot(fy_ref[...], data))
        for k, part in zip(ks, lane_parts(got)):
            out_ref[k] = part


def flux_modes(lines_ref, fy_ref, fyr_ref, kzs):
    ky = ky_rows()
    lane = lax.broadcasted_iota(jnp.int32, (ROWS, LANES), 1)
    odd_block = (lane // HALF) % 2 == 1
    depth = LINE // CHUNKS
    even = []
    for pair in range(0, len(kzs), 2):
        data = [stacked(along_y(lines_ref, 0, kz, depth)) for kz in kzs[pair : pair + 2]]
        even += lane_parts(folded(dot(fy_ref[...], jnp.concatenate(data, 1))))
    odd = []
    for kz in kzs:
        data = [stacked(along_y(lines_ref, tile, kz, depth)) for tile in (1, 2)]
        odd.append(lane_parts(folded(dot(fyr_ref[...], jnp.concatenate(data, 1)))))
    first, second = [], []
    for n, kz in enumerate(kzs):
        kzf = kz.astype(f32)
        plain = even[n]
        slopes = odd[n][0] * jnp.where(odd_block, kzf, ky)
        slopes = slopes + pltpu.roll(slopes, 32, 1)
        first.append(jnp.where(odd_block, slopes, plain))
        other = plain * jnp.where(lane >= 96, -kzf, -ky)
        other = other + pltpu.roll(other, 64, 1)
        second.append(jnp.where(lane >= 96, other, jnp.where(lane >= 64, odd[n][1], 0.0)))
    return first, second


def flux_kernel(
    core_ref, base_hbm, state_hbm, ahead_hbm, out_ref, out_b, out_c,
    lines_a, lines_b, lines_c, base_ref, state_ref, ahead_ref, result, arrived, left,
):
    wide = N * N // PIECES
    pieces = [pltpu.make_async_copy(ahead_hbm, ahead_ref, arrived.at[2 * PIECES])]
    for n in range(PIECES):
        for k, (source, target) in enumerate(((base_hbm, base_ref), (state_hbm, state_ref))):
            at = pl.ds(n * wide, wide)
            pieces.append(
                pltpu.make_async_copy(
                    source.at[:, :, at], target.at[:, :, at], arrived.at[2 * n + k]
                )
            )
    for piece in pieces:
        piece.start()
    fz_ref, fy_ref, fyr_ref = ahead_tables(ahead_ref)
    sigma = jnp.where(core_ref[0] == 0, -time_step, time_step).astype(f32)
    depth = LINE // CHUNKS

    def z_step(yhs):
        rows, lone = [], []
        for yh in yhs:
            b = [base_ref[i, :, columns(yh)] for i in range(3)]
            t = [sigma * state_ref[i, :, columns(yh)] for i in range(3)]
            rows += [t[2] * b[0], t[0] * b[1], t[1] * b[0], t[0] * b[2]]
            rows += [t[2] * b[1], t[2] * b[2], t[1] * b[1], t[1] * b[2]]
            lone.append(t[0] * b[0])
        got = lane_parts(folded(dot_nt(fz_ref[...], beside(jnp.concatenate(rows + lone, 0)))))
        for n, yh in enumerate(yhs):
            third = got[-1] if n == 2 else pltpu.roll(got[-1], (2 - n) % 4 * HALF, 1)
            at = pl.ds(pl.multiple_of(yh * depth, 8), depth)
            for tile, part in enumerate((got[2 * n], got[2 * n + 1], third)):
                for chunk, lines in enumerate((lines_a, lines_b, lines_c)):
                    lines[tile, at, :] = part[chunk * depth : (chunk + 1) * depth]

    pieces[0].wait()
    for n in range(PIECES):
        pieces[2 * n + 1].wait()
        pieces[2 * n + 2].wait()
        over_lines(z_step, 4, n * HALF // PIECES, (n + 1) * HALF // PIECES)
    sends = [
        pltpu.make_async_copy(lines_b, out_b, left.at[1]),
        pltpu.make_async_copy(lines_c, out_c, left.at[2]),
        pltpu.make_async_copy(result, out_ref, left.at[0]),
    ]
    sends[0].start()
    sends[1].start()

    def y_step(kzs):
        first, second = flux_modes(lines_a, fy_ref, fyr_ref, kzs)
        for n, kz in enumerate(kzs):
            result[0, kz] = first[n]
            result[1, kz] = second[n]

    over_planes(y_step, *planes_of(0))
    sends[2].start()
    for send in sends:
        send.wait()


def gradient_planes(cutoff_ref, here_ref, there_ref, back_ref, planes, start):
    cut_x, cut_y, cut_z = cutoff_ref[0], cutoff_ref[1], cutoff_ref[2]
    which = jnp.clip(cut_x - (KEEP - 3), 0, 3)
    keep_y = jnp.where(jnp.abs(ky_rows()) <= cut_y.astype(f32), 1.0, 0.0).astype(f32)
    iy_ref, iyd_ref = (view(back_ref, n) for n in range(2))
    for d in range(3):
        planes[d, HALF_KZ * LANES :, :] = jnp.zeros((LANES, LANES), f32)
    for first in range(0, HALF_KZ, 4):
        kzs = range(first, min(first + 4, HALF_KZ))
        rows = []
        for kz in kzs:
            keep = keep_y * jnp.where(start + kz <= cut_z, 1.0, 0.0).astype(f32)
            rows.append(jnp.concatenate([here_ref[kz] * keep, there_ref[kz] * keep], 1))
        high = back_ref[pl.ds(pl.multiple_of((6 + which) * 256, 256), 256), :]
        low = back_ref[pl.ds(pl.multiple_of((10 + which) * 256, 256), 256), :]
        got = triple(jnp.concatenate(rows, 0), high, low)
        data = [stacked(padded(got[n * ROWS : (n + 1) * ROWS])) for n in range(len(kzs))]
        for n, kz in enumerate(kzs):
            even = lane_parts(folded(dot(iy_ref[...], data[n])))
            planes[0, kz * LANES : (kz + 1) * LANES, :] = even[1]
            planes[2, kz * LANES : (kz + 1) * LANES, :] = even[0]
        for n in range(0, len(kzs), 2):
            both = jnp.concatenate([one[:, :LANES] for one in data[n : n + 2]], 1)
            for k, part in enumerate(lane_parts(folded(dot(iyd_ref[...], both)))):
                kz = kzs[n + k]
                planes[1, kz * LANES : (kz + 1) * LANES, :] = part


def half_kernel(core_ref, cutoff_ref, here_ref, there_ref, back_ref, planes):
    start = core_ref[0] * HALF_KZ
    gradient_planes(cutoff_ref, here_ref, there_ref, back_ref, planes, start)


def gradient_kernel(
    core_ref, cutoff_ref, wave_ref, base_ref, state_ref, own_ref, here_ref, there_ref,
    ahead_ref, back_ref, *refs
):
    *out_refs, planes, force_ref = refs
    core = core_ref[0]
    start = (1 - core) * HALF_KZ
    gradient_planes(cutoff_ref, here_ref, there_ref, back_ref, planes, start)
    fz_ref = ahead_tables(ahead_ref)[0]
    iz_ref, izd_ref = view(back_ref, 2), view(back_ref, 3)
    y = lax.broadcasted_iota(jnp.int32, (HALF, LANES), 0) * 2
    y = y + lax.broadcasted_iota(jnp.int32, (HALF, LANES), 1) // N
    phase = ((wave_ref[0] * y) % N).astype(f32) * (2.0 * np.pi / N)
    force_ref[...] = forcing_amp * jnp.sin(phase)
    nothing = jnp.zeros((HALF, LANES), f32)

    def along_halves(d, yh):
        at = pl.ds(yh, 4 * (HALF_KZ + 1), stride=HALF)
        own, other = own_ref[d, at, :], planes[d, at, :]
        low = jnp.where(core == 0, own, other)
        high = jnp.where(core == 0, other, own)
        return padded(jnp.concatenate([low, high], 0)).T

    def physical_step(yhs):
        count = len(yhs)
        flat = [along_halves(d, yh)[:96] for d in range(2) for yh in yhs]
        steep = [along_halves(2, yh)[:96] for yh in yhs]
        flat = folded_lanes(dot(beside(jnp.concatenate(flat, 0)), iz_ref[...]))
        steep = folded_lanes(dot(beside(jnp.concatenate(steep, 0)), izd_ref[...]))
        for n, yh in enumerate(yhs):
            sets = [flat[96 * n :], flat[96 * (count + n) :], steep[96 * n :]]
            grads = [[one[HALF * i : HALF * (i + 1)] for i in range(3)] for one in sets]
            b = [base_ref[i, :, columns(yh)] for i in range(3)]
            s = [state_ref[i, :, columns(yh)] for i in range(3)]
            comb, comb_base = [], []
            for i in range(3):
                coupling = sum(
                    jnp.where(core == 0, grads[j][i], grads[i][j]) * s[j] for j in range(3)
                )
                comb.append(s[i] - time_step * coupling)
                drive = sum(grads[j][i] * b[j] for j in range(3))
                if i == 0:
                    drive = drive - force_ref[pl.ds(yh, 1), :]
                comb_base.append(b[i] - time_step * drive)
            rows = [comb[1], comb_base[1], comb[2], comb_base[2]]
            rows += [comb[0], comb_base[0], nothing, nothing]
            got = folded(dot_nt(fz_ref[...], beside(jnp.concatenate(rows, 0))))
            depth = LINE // CHUNKS
            rows = pl.ds(pl.multiple_of(yh * depth, 8), depth)
            for tile, part in enumerate(lane_parts(got)):
                for chunk in range(CHUNKS):
                    out_refs[chunk][tile, rows, :] = part[chunk * depth : (chunk + 1) * depth]

    over_lines(physical_step, 8)


def spectral_kernel(
    chunk, core_ref, cutoff_ref, lines_ref, flux_ref,
    ahead_ref, along_ref, near_ref, far_ref,
):
    _, fy_ref, fyr_ref = ahead_tables(ahead_ref)
    core = core_ref[0]
    cut_x, cut_y, cut_z = cutoff_ref[0], cutoff_ref[1], cutoff_ref[2]
    first, last = planes_of(chunk)
    extra = last - first
    ky = ky_rows()
    kx = kx_lanes()
    keep_y = jnp.where(jnp.abs(ky) <= cut_y.astype(f32), 1.0, 0.0).astype(f32)
    keep_x = jnp.where(kx <= cut_x.astype(f32), 1.0, 0.0).astype(f32)
    keep_xy = keep_y * keep_x
    square_xy = ky * ky + kx * kx
    lane = lax.broadcasted_iota(jnp.int32, (ROWS, LANES), 1)
    near_ref[extra] = jnp.zeros((ROWS, LANES), f32)
    far_ref[extra] = jnp.zeros((ROWS, LANES), f32)

    def kept_z(kz):
        return jnp.where(kz <= cut_z, 1.0, 0.0).astype(f32)

    def spectral_step(kzs):
        fields = [[], [], []]
        if chunk == 0:
            first_flux = [flux_ref[0, kz] for kz in kzs]
            second_flux = [flux_ref[1, kz] for kz in kzs]
        else:
            first_flux, second_flux = flux_modes(flux_ref, fy_ref, fyr_ref, kzs)
        for pair in range(0, len(kzs), 2):
            ks = kzs[pair : pair + 2]
            data = [
                jnp.concatenate(
                    [stacked(along_y(lines_ref, t, kz, LINE // CHUNKS)) for kz in ks], 1
                )
                for t in (0, 1)
            ]
            even = lane_parts(folded(dot(fy_ref[...], data[0])))
            odd = lane_parts(folded(dot(fyr_ref[...], data[1])))
            for n, kz in enumerate(ks):
                flux = first_flux[pair + n]
                fields[0].append(odd[n] + second_flux[pair + n])
                fields[1].append(jnp.where(lane < 64, even[n], flux))
                fields[2].append(jnp.where(lane < 64, flux, even[n]))
        data = [beside(jnp.concatenate(field, 0)) for field in fields]
        modes = [folded_lanes(dot(data[max(n - 1, 0)], view(along_ref, n)[...])) for n in range(4)]
        results = [[], [], [], []]
        for n, kz in enumerate(kzs):
            kzf = kz.astype(f32)
            vx, slope, uy, uz = (mode[n * ROWS : (n + 1) * ROWS] for mode in modes)
            square = square_xy + kzf * kzf
            factor = keep_xy * kept_z(kz) / (1.0 + viscosity * time_step * square)
            share = (slope + ky * uy + kzf * uz) / jnp.where(square > 0, square, 1.0)
            results[0].append(factor * vx)
            results[1].append(factor * share)
            results[2].append(factor * (uy - ky * share))
            results[3].append(factor * (uz - kzf * share))
        got = [
            dot(
                beside(jnp.concatenate(result, 0)),
                along_ref[pl.ds(pl.multiple_of((4 + core * 4 + n) * 256, 256), 256), :],
            )
            for n, result in enumerate(results)
        ]
        got = [folded_lanes(part) for part in (got[0] + got[1], got[2], got[3])]
        for n, kz in enumerate(kzs):
            x, y, z = (part[n * ROWS : (n + 1) * ROWS] for part in got)
            near_ref[kz - first] = jnp.where(lane < 48, x, jnp.where(lane < 96, y, z))
            away = jnp.where(
                (lane >= 64) & (lane < 112), x, jnp.where((lane >= 32) & (lane < 64), z, y)
            )
            far_ref[kz - first] = pltpu.roll(away, 64, 1)
            shift = (kz - first) * 16
            near_ref[extra] += pltpu.roll(jnp.where(lane < 16, z, 0.0), shift, 1)
            rest = jnp.where((lane >= 64) & (lane < 80), z, 0.0)
            far_ref[extra] += pltpu.roll(rest, (shift + 64) % LANES, 1)

    over_planes(spectral_step, first, last)


def inverse_y(near_ref, far_ref, iy_ref, planes):
    count = near_ref.shape[0] - 1
    rest = near_ref[count] + far_ref[count]
    for kz in range(count):
        turned = pltpu.roll(rest, (LANES - kz * 16) % LANES, 1) if kz else rest
        data = jnp.concatenate([near_ref[kz] + far_ref[kz], turned], 1)
        got = lane_parts(folded(dot(iy_ref[...], stacked(padded(data)))))
        for tile in range(2):
            planes[tile, kz * LANES : (kz + 1) * LANES, :] = got[tile]
    if count < CHUNK:
        blank = jnp.zeros(((CHUNK - count) * LANES, LANES), f32)
        for tile in range(2):
            planes[tile, count * LANES :, :] = blank


def inverse_kernel(near_ref, far_ref, back_ref, planes):
    inverse_y(near_ref, far_ref, view(back_ref, 0), planes)


def final_kernel(
    near_ref, far_ref, planes_a, planes_b, state_hbm, base_hbm, back_ref, base_out, state_out,
    planes_c, state_ref, base_ref, state_gap, base_gap, arrived, left,
):
    wide = N * N // PIECES
    cuts = [pl.ds(n * wide, wide) for n in range(PIECES)]

    def copies(pairs, flags):
        return [
            [
                pltpu.make_async_copy(
                    source.at[:, :, cut], target.at[:, :, cut], flags.at[2 * n + k]
                )
                for k, (source, target) in enumerate(pairs)
            ]
            for n, cut in enumerate(cuts)
        ]

    reads = copies(((state_hbm, state_ref), (base_hbm, base_ref)), arrived)
    writes = copies(((state_gap, state_out), (base_gap, base_out)), left)
    for piece in reads:
        for copy in piece:
            copy.start()
    iy_ref, iz_ref, izr_ref = (view(back_ref, n) for n in (0, 4, 5))
    inverse_y(near_ref, far_ref, iy_ref, planes_c)

    def along_chunks(tile, yh):
        parts = [
            ref[tile, pl.ds(yh, 4 * CHUNK, stride=HALF), :]
            for ref in (planes_a, planes_b, planes_c)
        ]
        return padded(jnp.concatenate(parts, 0)).T

    many = HALF // PIECES
    for piece in range(PIECES):
        yhs = range(piece * many, (piece + 1) * many)
        data = [along_chunks(0, yh) for yh in yhs]
        rest = [along_chunks(1, yh)[:16] for yh in yhs]
        turned = beside(jnp.concatenate([one[:48] for one in data], 0))
        plain = beside(jnp.concatenate([one[48:] for one in data] + rest, 0))
        turned = folded_lanes(dot(turned, izr_ref[...]))
        plain = folded_lanes(dot(plain, iz_ref[...]))
        for copy in reads[piece]:
            copy.wait()
        for n, yh in enumerate(yhs):
            at = slice(yh * LANES, (yh + 1) * LANES)
            first = turned[48 * n : 48 * n + 48]
            second = plain[80 * n : 80 * n + 80]
            third = plain[80 * many + 16 * n :][:16]
            state_gap[0, :, at] = first[:32] - state_ref[0, :, at]
            state_gap[1, :, at] = second[16:48] - state_ref[1, :, at]
            state_gap[2, :, at] = second[48:80] - state_ref[2, :, at]
            base_gap[0, :, at] = first[32:48] - base_ref[0, :, at]
            base_gap[1, :, at] = second[:16] - base_ref[1, :, at]
            base_gap[2, :, at] = third - base_ref[2, :, at]
        for copy in writes[piece]:
            copy.start()
    for piece in writes:
        for copy in piece:
            copy.wait()


interpret = False


def call(kernel, outs, scratch, inputs, room, in_smem=0, in_hbm=(), out_hbm=False):
    whole = pl.BlockSpec(memory_space=pltpu.VMEM)
    small = pl.BlockSpec(memory_space=pltpu.SMEM)
    far = pl.BlockSpec(memory_space=pltpu.HBM)
    return pl.pallas_call(
        kernel,
        out_shape=outs,
        in_specs=[
            small if n < in_smem else far if n in in_hbm else whole for n in range(len(inputs))
        ],
        out_specs=jax.tree.map(lambda _: far if out_hbm else whole, outs),
        scratch_shapes=scratch,
        compiler_params=pltpu.CompilerParams(vmem_limit_bytes=room * 2**20),
        cost_estimate=pl.CostEstimate(flops=1000, bytes_accessed=1000, transcendentals=0),
        interpret=interpret,
    )(*inputs)


def body(base, state, wavenumber, cutoff):
    t = {name: jnp.asarray(value) for name, value in tables().items()}
    core = lax.axis_index("comp")
    seg_count = lax.axis_size("seg")
    own_base = base[0]
    own_state = state[0, 0]
    base_half = lax.dynamic_slice_in_dim(own_base, core * 16, 16, 1)
    back = [((s + 1) % seg_count, s) for s in range(seg_count)]
    around = [(2 * i, 2 * o) for i, o in back] + [(2 * o + 1, 2 * i + 1) for i, o in back]
    base_next = lax.ppermute(base_half, "seg", back)
    state_next = lax.ppermute(own_state, ("seg", "comp"), around)
    sds = jax.ShapeDtypeStruct
    core_at = core.reshape(1)
    swap = [(0, 1), (1, 0)]
    here_own = call(
        base_kernel,
        sds((HALF_KZ, ROWS, LANES), f32),
        [
            pltpu.VMEM((1, HALF * LINE, LANES), f32),
            pltpu.VMEM(own_base.shape, f32),
            pltpu.VMEM(t["ahead"].shape, bf16),
            pltpu.SemaphoreType.DMA((PIECES + 1,)),
        ],
        [core_at, own_base, t["ahead"]],
        room=56,
        in_smem=1,
        in_hbm=(1, 2),
    )
    there_own = lax.ppermute(here_own, "slab", swap)
    here_other = lax.ppermute(here_own, "comp", swap)
    counts = [planes_of(chunk)[1] - planes_of(chunk)[0] for chunk in range(CHUNKS)]
    flux_lines = sds((3, HALF * 4 * CHUNK, LANES), f32)
    flux = call(
        flux_kernel,
        [sds((2, counts[0], ROWS, LANES), f32)] + [flux_lines] * 2,
        [
            pltpu.VMEM(flux_lines.shape, f32),
            pltpu.VMEM(flux_lines.shape, f32),
            pltpu.VMEM(flux_lines.shape, f32),
            pltpu.VMEM(own_base.shape, f32),
            pltpu.VMEM(own_state.shape, f32),
            pltpu.VMEM(t["ahead"].shape, bf16),
            pltpu.VMEM((2, counts[0], ROWS, LANES), f32),
            pltpu.SemaphoreType.DMA((2 * PIECES + 1,)),
            pltpu.SemaphoreType.DMA((CHUNKS,)),
        ],
        [core_at, own_base, own_state, t["ahead"]],
        room=56,
        in_smem=1,
        in_hbm=(1, 2, 3),
        out_hbm=True,
    )
    there_own, flux = lax.optimization_barrier((there_own, flux))
    there_other = lax.ppermute(there_own, "comp", swap)
    half_planes = sds((3, (HALF_KZ + 1) * LANES, LANES), f32)
    own_planes = call(
        half_kernel,
        half_planes,
        [],
        [core_at, cutoff, here_own, there_own, t["back"]],
        room=12,
        in_smem=2,
    )
    lines = call(
        gradient_kernel,
        [sds((2, HALF * 4 * CHUNK, LANES), f32)] * CHUNKS,
        [pltpu.VMEM(half_planes.shape, f32), pltpu.VMEM((HALF, LANES), f32)],
        [core_at, cutoff, wavenumber, own_base, own_state, own_planes, here_other, there_other]
        + [t["ahead"], t["back"]],
        room=20,
        in_smem=3,
    )
    near, far = [], []
    lines = list(lines)
    for chunk in range(CHUNKS):
        if chunk:
            near[-1], lines[chunk] = lax.optimization_barrier((near[-1], lines[chunk]))
        near_part, far_part = call(
            functools.partial(spectral_kernel, chunk),
            [sds((counts[chunk] + 1, ROWS, LANES), f32)] * 2,
            [],
            [core_at, cutoff, lines[chunk], flux[chunk], t["ahead"], t["along"]],
            room=12,
            in_smem=2,
        )
        near.append(near_part)
        far.append(lax.ppermute(far_part, "slab", swap))
    planes = sds((2, CHUNK * LANES, LANES), f32)
    planes_a = call(inverse_kernel, planes, [], [near[0], far[0], t["back"]], room=8)
    near[1], planes_a = lax.optimization_barrier((near[1], planes_a))
    planes_b = call(inverse_kernel, planes, [], [near[1], far[1], t["back"]], room=8)
    base_gap, state_gap = call(
        final_kernel,
        [sds(base_next.shape, f32), sds(state_next.shape, f32)],
        [
            pltpu.VMEM((2, CHUNK * LANES, LANES), f32),
            pltpu.VMEM(state_next.shape, f32),
            pltpu.VMEM(base_next.shape, f32),
            pltpu.VMEM(state_next.shape, f32),
            pltpu.VMEM(base_next.shape, f32),
            pltpu.SemaphoreType.DMA((2 * PIECES,)),
            pltpu.SemaphoreType.DMA((2 * PIECES,)),
        ],
        [near[2], far[2], planes_a, planes_b, state_next, base_next, t["back"]],
        room=16,
        in_hbm=(4, 5),
        out_hbm=True,
    )
    return base_gap[None], state_gap[None, None]


def solution(mesh):
    paired = mesh.shape["slab"] == 2 and mesh.shape["comp"] == 2
    return jax.shard_map(
        body if paired else general_body,
        mesh=mesh,
        in_specs=(
            P(("groups", "seg"), None, "slab", None),
            P(("groups", "seg"), "comp", None, "slab", None),
            P("groups"),
            P("groups"),
        ),
        out_specs=(
            P(("groups", "seg"), None, ("slab", "comp"), None),
            P(("groups", "seg"), "comp", None, "slab", None),
        ),
        check_vma=False,
    )
```

```python
import functools

import jax
import jax.numpy as jnp
import ml_dtypes
import numpy as np
from jax import lax
from jax.experimental import pallas as pl
from jax.experimental.pallas import tpu as pltpu
from jax.sharding import PartitionSpec as P

N = 64
HALF = 32
KEEP = N // 3
NKZ = KEEP + 1
NKY = 44
ROWS = 2 * NKY
CHUNK = 8
CHUNKS = 3
LINE = CHUNKS * CHUNK * 4
HALF_KZ = NKZ // 2
SENT = 9
LANES = 128

viscosity = 0.025
time_step = 0.02
forcing_amp = 10.0

f32 = jnp.float32
bf16 = jnp.bfloat16


highest = lax.Precision.HIGHEST


def swapped(value, axis, apart):
    mask = 2**apart
    pairs = [(source, source ^ mask) for source in range(lax.axis_size(axis))]
    return lax.ppermute(value, axis, pairs)


def shifted(block, axis, distance):
    devices = range(lax.axis_size(axis))
    route = [((i - distance) % len(devices), i) for i in devices]
    return lax.ppermute(block, axis, route)


def wavenumbers(grid_points):
    position = jnp.arange(grid_points, dtype=jnp.int32)
    return jnp.where(position < grid_points // 2, position, position - grid_points)


def phases(first, second, grid_points):
    product = jnp.mod(first[:, None] * second[None, :], grid_points)
    return product.astype(jnp.float32) * (2.0 * jnp.pi / grid_points)


def combine(partial_value, columns):
    cosine_part = partial_value[0]
    sine_part = partial_value[1]
    real_part = cosine_part[..., :columns] - sine_part[..., columns:]
    imag_part = cosine_part[..., columns:] + sine_part[..., :columns]
    return jnp.concatenate([real_part, imag_part], axis=-1)


def times_unit(values, wave, columns):
    return jnp.concatenate([-wave * values[..., columns:], wave * values[..., :columns]], axis=-1)


def doubled(values):
    return jnp.concatenate([values, values], axis=-1)


def general_body(base, state, wavenumber, cutoff):
    grid_points = N
    base = base.reshape(base.shape[0], 3, base.shape[2], grid_points, grid_points)
    state = state.reshape(
        state.shape[0], state.shape[1], 3, state.shape[3], grid_points, grid_points
    )
    slab_rows = state.shape[3]
    half_rows = slab_rows // 2
    slab_count = lax.axis_size("slab")
    group_count = slab_count * lax.axis_size("comp")
    core_side = lax.axis_index("comp")
    block_number = lax.axis_index(("slab", "comp"))
    base_whole = base[0]
    base_half = lax.dynamic_slice_in_dim(base_whole, core_side * half_rows, half_rows, 1)
    own_state = state[0, 0]
    spectrum = wavenumbers(grid_points)
    one_third = grid_points // 3
    row_total = (2 * one_third + group_count) // group_count * group_count
    row_index = jnp.arange(row_total, dtype=jnp.int32)
    row_alive_mask = row_index <= 2 * one_third
    row_wave = jnp.where(row_index <= one_third, row_index, row_index - (2 * one_third + 1))
    row_wave = jnp.where(row_alive_mask, row_wave, 0)
    width = grid_points // 2
    rows_per_block = row_total // group_count
    alive_flags = row_alive_mask.astype(jnp.float32)
    grid_index = jnp.arange(grid_points, dtype=jnp.int32)
    column_index = grid_index[:width]
    angle_grid = phases(grid_index, grid_index, grid_points)
    angle_ahead = phases(grid_index, column_index, grid_points)
    angle_behind = phases(column_index, grid_index, grid_points)
    column_weight = jnp.where(column_index == 0, 1.0, 2.0).astype(jnp.float32)[:, None]
    forward_z = jnp.concatenate([jnp.cos(angle_ahead), -jnp.sin(angle_ahead)], axis=1)
    inverse_z = (
        jnp.concatenate(
            [jnp.cos(angle_behind) * column_weight, -jnp.sin(angle_behind) * column_weight], axis=0
        )
        / grid_points
    )
    phase_angle_rows = phases(row_wave, grid_index, grid_points)
    forward_transform_y = (
        jnp.stack([jnp.cos(phase_angle_rows), -jnp.sin(phase_angle_rows)])
        * alive_flags[None, :, None]
    )
    inverse_y = (
        jnp.stack([jnp.cos(phase_angle_rows).T, jnp.sin(phase_angle_rows).T])
        * alive_flags[None, None, :]
        / grid_points
    )
    forward_x = jnp.stack([jnp.cos(angle_grid), -jnp.sin(angle_grid)])
    inverse_x = jnp.stack([jnp.cos(angle_grid), jnp.sin(angle_grid)]) / grid_points
    table_ahead = forward_x.reshape(2, grid_points, slab_count, slab_rows)
    table_back = inverse_x.reshape(2, slab_count, slab_rows, grid_points)
    local_wave = lax.dynamic_slice_in_dim(row_wave, block_number * rows_per_block, rows_per_block)
    local_alive_mask = lax.dynamic_slice_in_dim(
        alive_flags, block_number * rows_per_block, rows_per_block
    )
    shape_local = (grid_points, rows_per_block, width)
    wave_x = jnp.broadcast_to(spectrum[:, None, None], shape_local)
    wave_y = jnp.broadcast_to(local_wave[None, :, None], shape_local)
    wave_z = jnp.broadcast_to(spectrum[:width][None, None, :], shape_local)
    inside = (
        (jnp.abs(wave_x) <= cutoff[0])
        & (jnp.abs(wave_y) <= cutoff[1])
        & (jnp.abs(wave_z) <= cutoff[2])
    )
    keep_mask = doubled(inside.astype(jnp.float32) * local_alive_mask[None, :, None])
    float_x = wave_x.astype(jnp.float32)
    float_y = wave_y.astype(jnp.float32)
    float_z = wave_z.astype(jnp.float32)
    ksquare = float_x * float_x + float_y * float_y + float_z * float_z
    safe_square = doubled(jnp.where(ksquare > 0, ksquare, jnp.ones_like(ksquare)))
    damping = doubled(1.0 / (1.0 + viscosity * time_step * ksquare))
    double_x = doubled(float_x)
    double_y = doubled(float_y)
    double_z = doubled(float_z)

    def project(field):
        divergence = (double_x * field[0] + double_y * field[1] + double_z * field[2]) / safe_square
        return jnp.stack(
            [
                field[0] - double_x * divergence,
                field[1] - double_y * divergence,
                field[2] - double_z * divergence,
            ]
        )

    def yz_forward(field):
        along_z = jnp.einsum("...z,zk->...k", field, forward_z, precision=highest)
        partial_value = jnp.einsum(
            "sry,...yk->s...rk", forward_transform_y, along_z, precision=highest
        )
        return combine(partial_value, width)

    def yz_inverse(modes):
        partial_value = jnp.einsum("syr,...rk->s...yk", inverse_y, modes, precision=highest)
        return jnp.einsum(
            "...k,kz->...z", combine(partial_value, width), inverse_z, precision=highest
        )

    def spectral(state_fields, base_fields):
        state_modes = yz_forward(state_fields)[:, :, None]
        base_modes = yz_forward(base_fields)[:, :, None]
        state_got = lax.all_to_all(
            state_modes, ("slab", "comp"), split_axis=4, concat_axis=2, tiled=True
        )
        base_got = lax.all_to_all(
            base_modes, ("slab", "comp"), split_axis=4, concat_axis=2, tiled=True
        )
        item_count = state_got.shape[0]
        part_count = state_got.shape[1]
        state_split = state_got.reshape(
            item_count, part_count, slab_count, 2, slab_rows, rows_per_block, 2 * width
        )
        state_partial = jnp.einsum(
            "srpx,ijpcxyk->sijcryk", table_ahead, state_split, precision=highest
        )
        base_lined = base_got.reshape(item_count, 1, grid_points, rows_per_block, 2 * width)
        base_partial = jnp.einsum("srx,ijxyk->sijryk", forward_x, base_lined, precision=highest)
        return (combine(state_partial, width), combine(base_partial, width))

    state_first, base_first = spectral(own_state[:, None], base_half[:, None])
    state_hat = state_first[:, 0] * keep_mask
    base_hat = base_first[:, 0] * keep_mask
    grad_hat = jnp.stack(
        [
            times_unit(base_hat, float_x, width),
            times_unit(base_hat, float_y, width),
            times_unit(base_hat, float_z, width),
        ],
        axis=1,
    )
    grad_hat = grad_hat.reshape(9, grid_points, rows_per_block, 2 * width)
    grad_partial = jnp.einsum("sxr,iryk->sixyk", inverse_x, grad_hat, precision=highest)
    grad_spread = combine(grad_partial, width).reshape(
        9, group_count, half_rows, rows_per_block, 2 * width
    )
    own_rows = yz_inverse(
        lax.all_to_all(grad_spread, ("slab", "comp"), split_axis=1, concat_axis=3, tiled=True)[:, 0]
    )
    other_rows = swapped(own_rows, "comp", 0)
    gradient = jnp.where(
        core_side == 0,
        jnp.concatenate([own_rows, other_rows], axis=1),
        jnp.concatenate([other_rows, own_rows], axis=1),
    )
    gradient = gradient.reshape(3, 3, slab_rows, grid_points, grid_points)
    gradient_half = lax.dynamic_slice_in_dim(gradient, core_side * half_rows, half_rows, 2)
    flux_terms = own_state[:, None] * base_whole[None, :]
    coupling_matrix = jnp.where(core_side == 0, gradient, jnp.swapaxes(gradient, 0, 1))
    coupling = jnp.sum(coupling_matrix * own_state[None, :], axis=1)
    forcing_phase = phases(wavenumber, grid_index, grid_points)[0]
    forcing = forcing_amp * jnp.sin(forcing_phase)[None, :, None]
    base_drive = jnp.sum(gradient_half * base_half[None, :], axis=1)
    base_drive = jnp.concatenate([base_drive[:1] - forcing[None], base_drive[1:]], axis=0)
    state_fields = jnp.concatenate([flux_terms, coupling[:, None]], axis=1)
    drive_modes, base_modes_two = spectral(state_fields, base_drive[:, None])
    orient = jnp.array([1.0, -1.0], dtype=jnp.float32)[None, :, None, None, None]
    divergence = (
        times_unit(drive_modes[:, 0], float_x, width)
        + times_unit(drive_modes[:, 1], float_y, width)
        + times_unit(drive_modes[:, 2], float_z, width)
    )
    state_drive = keep_mask * (orient * divergence + drive_modes[:, 3])
    new_hat = damping * project(state_hat - time_step * state_drive)
    base_new_hat = damping * project(base_hat - time_step * keep_mask * base_modes_two[:, 0])
    state_partial = jnp.einsum("spxr,icryk->sipcxyk", table_back, new_hat, precision=highest)
    state_back = combine(state_partial, width).reshape(
        3, group_count, slab_rows, rows_per_block, 2 * width
    )
    base_partial = jnp.einsum("sxr,iryk->sixyk", inverse_x, base_new_hat, precision=highest)
    base_back = combine(base_partial, width).reshape(
        3, group_count, half_rows, rows_per_block, 2 * width
    )
    state_got = lax.all_to_all(
        state_back, ("slab", "comp"), split_axis=1, concat_axis=3, tiled=True
    )
    base_got = lax.all_to_all(base_back, ("slab", "comp"), split_axis=1, concat_axis=3, tiled=True)
    state_new = yz_inverse(state_got[:, 0])
    base_new = yz_inverse(base_got[:, 0])
    base_later, later_state = shifted((base_half, own_state), "seg", -1)
    prior_state = shifted(own_state, "seg", 1)
    neighbour = jnp.where(core_side == 0, later_state, prior_state)
    base_gap = (base_new - base_later).reshape(1, 3, half_rows, grid_points * grid_points)
    state_gap = (state_new - neighbour).reshape(1, 1, 3, slab_rows, grid_points * grid_points)
    return (base_gap, state_gap)


def halves(table):
    high = table.astype(np.float32).astype(ml_dtypes.bfloat16)
    low = (table - high.astype(np.float64)).astype(ml_dtypes.bfloat16)
    return high, low


def left_table(table, depth):
    padded = np.zeros((table.shape[0], depth))
    padded[:, : table.shape[1]] = table
    high, low = halves(padded)
    return np.concatenate(
        [np.concatenate([high, high], 1), np.concatenate([low, np.zeros_like(low)], 1)], 0
    )


def right_table(table, depth):
    return np.ascontiguousarray(left_table(table.T, depth).T)


def planes_of(chunk):
    return chunk * CHUNK, min((chunk + 1) * CHUNK, NKZ)


def ky_values():
    index = np.arange(NKY)
    wave = np.where(index <= KEEP, index, index - (2 * KEEP + 1))
    alive = (index <= 2 * KEEP).astype(np.float64)
    return wave * alive, alive


@functools.cache
def tables():
    out = {}
    z = np.arange(N)
    kz = np.arange(NKZ)
    angle = 2 * np.pi * kz[:, None] * z[None, :] / N
    weight = np.where(kz == 0, 1.0, 2.0)[:, None] / N
    forward = np.zeros((2, 2, CHUNKS * CHUNK, 2, N))
    inverse = np.zeros((NKZ, 2, 2, 2, N))
    turned = np.zeros((NKZ, 2, 2, 2, N))
    slope = np.zeros((NKZ, 2, 2, 2, N))
    for y2 in range(2):
        forward[y2, 0, :NKZ, y2] = np.cos(angle)
        forward[y2, 1, :NKZ, y2] = -np.sin(angle)
        inverse[:, y2, 0, y2] = weight * np.cos(angle)
        inverse[:, y2, 1, y2] = -weight * np.sin(angle)
        turned[:, y2, 0, y2] = weight * np.sin(angle)
        turned[:, y2, 1, y2] = weight * np.cos(angle)
        slope[:, y2, 0, y2] = -weight * kz[:, None] * np.sin(angle)
        slope[:, y2, 1, y2] = -weight * kz[:, None] * np.cos(angle)
    forward = np.moveaxis(forward.reshape(4, CHUNKS, CHUNK, 2 * N), 1, 0)
    out["fz"] = left_table(forward.reshape(LINE, 2 * N), 128)

    def by_chunk(table):
        wide = np.zeros((CHUNKS, CHUNK, 4, 2 * N))
        for chunk in range(CHUNKS):
            first, last = planes_of(chunk)
            wide[chunk, : last - first] = table.reshape(NKZ, 4, 2 * N)[first:last]
        return right_table(wide.reshape(LINE, 2 * N), 128)

    out["iz"] = by_chunk(inverse)
    out["izr"] = by_chunk(turned)

    def by_half(table):
        wide = np.zeros((2, HALF_KZ + 1, 4, 2 * N))
        wide[:, :HALF_KZ] = table.reshape(2, HALF_KZ, 4, 2 * N)
        return right_table(wide.reshape(8 * HALF_KZ + 8, 2 * N), 128)

    out["izg"] = by_half(inverse)
    out["izd"] = by_half(slope)
    ky, alive = ky_values()
    y = 2 * np.arange(HALF)[None, :] + np.arange(2)[:, None]
    phase = 2 * np.pi * ky[:, None, None] * y[None] / N
    cosine = np.cos(phase) * alive[:, None, None]
    sine = np.sin(phase) * alive[:, None, None]
    plain = np.zeros((2, NKY, 2, 2, HALF))
    plain[0, :, :, 0] = cosine
    plain[0, :, :, 1] = sine
    plain[1, :, :, 0] = -sine
    plain[1, :, :, 1] = cosine
    rotated = np.stack([-plain[1], plain[0]])
    out["fy"] = left_table(plain.reshape(ROWS, 128), 128)
    out["fyr"] = left_table(rotated.reshape(ROWS, 128), 128)
    back = np.zeros((2, 2, HALF, 2, NKY))
    cos_t = np.moveaxis(cosine, 0, -1) / N
    sin_t = np.moveaxis(sine, 0, -1) / N
    back[:, 0, :, 0] = cos_t
    back[:, 0, :, 1] = -sin_t
    back[:, 1, :, 0] = sin_t
    back[:, 1, :, 1] = cos_t
    back_slope = np.zeros_like(back)
    back_slope[..., 0, :] = ky * back[..., 1, :]
    back_slope[..., 1, :] = -ky * back[..., 0, :]
    out["iy"] = left_table(back.reshape(128, ROWS), 128)
    out["iyd"] = left_table(back_slope.reshape(128, ROWS), 128)
    grad_high, grad_low = [], []
    x = np.arange(N)
    apart = x[:HALF, None] - x[None, :]
    for cut in range(KEEP - 3, KEEP + 1):
        k = np.arange(cut + 1)
        wk = np.where(k == 0, 1.0, 2.0) / N
        arg = 2 * np.pi * apart[..., None] * k / N
        keep = (np.cos(arg) * wk).sum(-1)
        derive = (-np.sin(arg) * wk * k).sum(-1)
        table = np.zeros((2, 4, HALF, 2, 4, HALF))
        for comp in range(3):
            for side in range(2):
                rows = slice(side * HALF, (side + 1) * HALF)
                table[side, comp, :, 0, comp, :] = keep[:, rows].T
                table[side, comp, :, 1, comp, :] = derive[:, rows].T
        high, low = halves(table.reshape(256, 256))
        grad_high.append(high)
        grad_low.append(low)
    out["gxh"] = np.stack(grad_high)
    out["gxl"] = np.stack(grad_low)
    kx = np.arange(HALF)
    live = (kx <= KEEP).astype(np.float64)
    xl = np.arange(HALF)
    arg = 2 * np.pi * xl[:, None] * kx[None, :] / N
    value = np.concatenate([np.cos(arg) * live, np.sin(arg) * live], 1)
    change = np.concatenate([kx * np.sin(arg) * live, -kx * np.cos(arg) * live], 1)

    def coefficients(blocks):
        table = np.zeros((4, HALF, 2, 2 * HALF))
        for block, part, what in blocks:
            table[block, :, part] = what
        return table.reshape(LANES, LANES)

    first = coefficients([(0, 0, value), (1, 1, value), (2, 0, change), (3, 0, value)])
    last = coefficients([(0, 0, change), (1, 0, value), (2, 0, value), (3, 1, value)])
    fall = first.reshape(LANES, 2, 2, HALF)
    fall = np.stack([-kx * fall[:, :, 1], kx * fall[:, :, 0]], 2).reshape(LANES, LANES)
    out["fx"] = np.stack([right_table(part, 128) for part in (first, fall, first, last)])
    wx = np.where(kx == 0, 1.0, 2.0) * live / N
    for core in range(2):
        ix = np.zeros((4, 2, 2 * HALF, LANES))
        for side in range(2):
            xs = np.arange(HALF) + side * HALF
            arg = 2 * np.pi * kx[:, None] * xs[None, :] / N
            give = np.concatenate([np.cos(arg) * wx[:, None], np.sin(arg) * wx[:, None]], 0)
            drop = np.concatenate(
                [np.sin(arg) * (wx * kx)[:, None], -np.cos(arg) * (wx * kx)[:, None]], 0
            )
            own = slice(core * 16, core * 16 + 16)

            def put(quantity, part, lane, what):
                at = (lane + side * 64 + np.arange(what.shape[1])) % LANES
                ix[quantity, part][:, at] = what

            put(0, 0, 0, give)
            put(1, 0, 0, drop)
            put(0, 1, 32, give[:, own])
            put(1, 1, 32, drop[:, own])
            put(2, 1, 48, give[:, own])
            put(2, 0, 64, give)
            put(3, 0, 96, give)
            put(3, 1, 0, give[:, own])
        out["ix%d" % core] = np.stack(
            [right_table(part, 128) for part in ix.reshape(4, LANES, LANES)]
        )
    out["ix"] = np.stack([out.pop("ix0"), out.pop("ix1")])
    merged = {}
    merged["ahead"] = np.concatenate([out["fz"], out["fy"], out["fyr"]], 0)
    gx = [out["gxh"].reshape(-1, 256), out["gxl"].reshape(-1, 256)]
    square = [out[name] for name in ("iy", "iyd", "izg", "izd", "iz", "izr")]
    merged["back"] = np.concatenate(square + gx, 0)
    merged["along"] = np.concatenate([out["fx"].reshape(-1, 256), out["ix"].reshape(-1, 256)], 0)
    return merged


def view(ref, index, rows=256, start=0):
    return ref.at[pl.ds(start + index * rows, rows), :]


def ahead_tables(ref):
    return view(ref, 0, 2 * LINE), view(ref, 0, 2 * ROWS, 2 * LINE), view(ref, 1, 2 * ROWS, 2 * LINE)


def ky_rows():
    row = lax.broadcasted_iota(jnp.int32, (ROWS, LANES), 0)
    index = jnp.where(row < NKY, row, row - NKY)
    wave = jnp.where(index <= KEEP, index, index - (2 * KEEP + 1))
    return jnp.where(index <= 2 * KEEP, wave, 0).astype(f32)


def kx_lanes():
    lane = lax.broadcasted_iota(jnp.int32, (1, LANES), 1) % HALF
    return jnp.where(lane <= KEEP, lane, 0).astype(f32)


def split(values):
    high = values.astype(bf16)
    low = (values - high.astype(f32)).astype(bf16)
    return high, low


def dot(a, b):
    return jnp.dot(a, b, preferred_element_type=f32)


def dot_nt(a, b):
    return lax.dot_general(a, b, (((1,), (1,)), ((), ())), preferred_element_type=f32)


def stacked(values):
    high, low = split(values)
    return jnp.concatenate([high, low], 0)


def beside(values):
    high, low = split(values)
    return jnp.concatenate([high, low], 1)


def folded(result):
    rows = result.shape[0] // 2
    return result[:rows] + result[rows:]


def folded_lanes(result):
    return result[:, :LANES] + result[:, LANES:]


def padded(values, rows=128):
    return jnp.concatenate([values, jnp.zeros((rows - values.shape[0], values.shape[1]), f32)], 0)


def triple(values, high_ref, low_ref):
    high, low = split(values)
    return dot(high, high_ref) + dot(low, high_ref) + dot(high, low_ref)


def columns(yh):
    return pl.ds(pl.multiple_of(yh * LANES, LANES), LANES)


def along_y(ref, tile, kz, line=LINE):
    at = kz % CHUNK + (0 if line == LINE // CHUNKS else kz // CHUNK * (4 * CHUNK))
    return jnp.concatenate(
        [ref[tile, pl.ds(q * CHUNK + at, HALF, stride=line), :] for q in range(4)], 0
    )


def line_rows(yh):
    return pl.ds(pl.multiple_of(yh * LINE, 8), LINE)


def lane_parts(values):
    return [values[:, at : at + LANES] for at in range(0, values.shape[1], LANES)]


def over_planes(step, first=0, last=NKZ):
    def four(index, _):
        step([first + index * 4 + k for k in range(4)])
        return 0

    count = (last - first) // 4
    lax.fori_loop(0, count, four, 0)
    if first + count * 4 < last:
        step([jnp.int32(kz) for kz in range(first + count * 4, last)])


def over_lines(step, many, first=0, last=HALF):
    def some(index, _):
        step([first + index * many + k for k in range(many)])
        return 0

    lax.fori_loop(0, (last - first) // many, some, 0)


PIECES = 4


def base_kernel(core_ref, base_hbm, ahead_hbm, out_ref, lines, base_ref, ahead_ref, arrived):
    nothing = jnp.zeros((HALF, LANES), f32)
    wide = N * N // PIECES
    table = pltpu.make_async_copy(ahead_hbm, ahead_ref, arrived.at[PIECES])
    pieces = [
        pltpu.make_async_copy(
            base_hbm.at[:, :, pl.ds(n * wide, wide)],
            base_ref.at[:, :, pl.ds(n * wide, wide)],
            arrived.at[n],
        )
        for n in range(PIECES)
    ]
    pieces[0].start()
    table.start()
    for piece in pieces[1:]:
        piece.start()
    fz_ref, fy_ref, _ = ahead_tables(ahead_ref)
    table.wait()
    many = HALF // PIECES
    for n, piece in enumerate(pieces):
        piece.wait()
        yhs = range(n * many, (n + 1) * many)
        rows = []
        for yh in yhs:
            at = slice(yh * LANES, (yh + 1) * LANES)
            rows += [base_ref[i, :, at] for i in range(3)] + [nothing]
        got = folded(dot_nt(fz_ref[...], beside(jnp.concatenate(rows, 0))))
        for yh, part in zip(yhs, lane_parts(got)):
            lines[0, yh * LINE : (yh + 1) * LINE, :] = part
    start = core_ref[0] * HALF_KZ
    planes = []
    for pair in range(0, HALF_KZ, 2):
        ks = range(pair, min(pair + 2, HALF_KZ))
        data = jnp.concatenate([stacked(along_y(lines, 0, start + k)) for k in ks], 1)
        planes += lane_parts(folded(dot(fy_ref[...], data)))
    lane = lax.broadcasted_iota(jnp.int32, (ROWS, LANES), 1)
    for k in range(SENT):
        part = planes[k]
        if k < 3 * (HALF_KZ - SENT):
            guest = pltpu.roll(planes[SENT + k // 3], (3 - k % 3) * HALF, 1)
            part = jnp.where(lane < 96, part, guest)
        out_ref[k] = part


def received(ref, k):
    if k < SENT:
        return ref[k]
    lane = lax.broadcasted_iota(jnp.int32, (ROWS, LANES), 1)
    blocks = [
        pltpu.roll(ref[3 * (k - SENT) + j], LANES - (3 - j) * HALF, 1) for j in range(3)
    ]
    return jnp.where(lane < 32, blocks[0], jnp.where(lane < 64, blocks[1], blocks[2]))


def flux_modes(lines_ref, fy_ref, fyr_ref, kzs):
    ky = ky_rows()
    lane = lax.broadcasted_iota(jnp.int32, (ROWS, LANES), 1)
    odd_block = (lane // HALF) % 2 == 1
    depth = LINE // CHUNKS
    even = []
    for pair in range(0, len(kzs), 2):
        data = [stacked(along_y(lines_ref, 0, kz, depth)) for kz in kzs[pair : pair + 2]]
        even += lane_parts(folded(dot(fy_ref[...], jnp.concatenate(data, 1))))
    odd = []
    for kz in kzs:
        data = [stacked(along_y(lines_ref, tile, kz, depth)) for tile in (1, 2)]
        odd.append(lane_parts(folded(dot(fyr_ref[...], jnp.concatenate(data, 1)))))
    first, second = [], []
    for n, kz in enumerate(kzs):
        kzf = kz.astype(f32)
        plain = even[n]
        slopes = odd[n][0] * jnp.where(odd_block, kzf, ky)
        slopes = slopes + pltpu.roll(slopes, 32, 1)
        first.append(jnp.where(odd_block, slopes, plain))
        other = plain * jnp.where(lane >= 96, -kzf, -ky)
        other = other + pltpu.roll(other, 64, 1)
        second.append(jnp.where(lane >= 96, other, jnp.where(lane >= 64, odd[n][1], 0.0)))
    return first, second


def flux_kernel(
    core_ref, base_hbm, state_hbm, ahead_hbm, out_ref, out_b, out_c,
    lines_a, lines_b, lines_c, base_ref, state_ref, ahead_ref, result, arrived, left,
):
    wide = N * N // PIECES
    pieces = [pltpu.make_async_copy(ahead_hbm, ahead_ref, arrived.at[2 * PIECES])]
    for n in range(PIECES):
        for k, (source, target) in enumerate(((base_hbm, base_ref), (state_hbm, state_ref))):
            at = pl.ds(n * wide, wide)
            pieces.append(
                pltpu.make_async_copy(
                    source.at[:, :, at], target.at[:, :, at], arrived.at[2 * n + k]
                )
            )
    for piece in pieces:
        piece.start()
    fz_ref, fy_ref, fyr_ref = ahead_tables(ahead_ref)
    sigma = jnp.where(core_ref[0] == 0, -time_step, time_step).astype(f32)
    depth = LINE // CHUNKS

    def z_step(yhs):
        rows, lone = [], []
        for yh in yhs:
            b = [base_ref[i, :, columns(yh)] for i in range(3)]
            t = [sigma * state_ref[i, :, columns(yh)] for i in range(3)]
            rows += [t[2] * b[0], t[0] * b[1], t[1] * b[0], t[0] * b[2]]
            rows += [t[2] * b[1], t[2] * b[2], t[1] * b[1], t[1] * b[2]]
            lone.append(t[0] * b[0])
        got = lane_parts(folded(dot_nt(fz_ref[...], beside(jnp.concatenate(rows + lone, 0)))))
        for n, yh in enumerate(yhs):
            third = got[-1] if n == 2 else pltpu.roll(got[-1], (2 - n) % 4 * HALF, 1)
            at = pl.ds(pl.multiple_of(yh * depth, 8), depth)
            for tile, part in enumerate((got[2 * n], got[2 * n + 1], third)):
                for chunk, lines in enumerate((lines_a, lines_b, lines_c)):
                    lines[tile, at, :] = part[chunk * depth : (chunk + 1) * depth]

    pieces[0].wait()
    for n in range(PIECES):
        pieces[2 * n + 1].wait()
        pieces[2 * n + 2].wait()
        over_lines(z_step, 4, n * HALF // PIECES, (n + 1) * HALF // PIECES)
    sends = [
        pltpu.make_async_copy(lines_b, out_b, left.at[1]),
        pltpu.make_async_copy(lines_c, out_c, left.at[2]),
        pltpu.make_async_copy(result, out_ref, left.at[0]),
    ]
    sends[0].start()
    sends[1].start()

    def y_step(kzs):
        first, second = flux_modes(lines_a, fy_ref, fyr_ref, kzs)
        for n, kz in enumerate(kzs):
            result[0, kz] = first[n]
            result[1, kz] = second[n]

    over_planes(y_step, *planes_of(0))
    sends[2].start()
    for send in sends:
        send.wait()


def gradient_planes(cutoff_ref, here_ref, there_ref, back_ref, planes, start):
    cut_x, cut_y, cut_z = cutoff_ref[0], cutoff_ref[1], cutoff_ref[2]
    which = jnp.clip(cut_x - (KEEP - 3), 0, 3)
    keep_y = jnp.where(jnp.abs(ky_rows()) <= cut_y.astype(f32), 1.0, 0.0).astype(f32)
    iy_ref, iyd_ref = (view(back_ref, n) for n in range(2))
    for d in range(3):
        planes[d, HALF_KZ * LANES :, :] = jnp.zeros((LANES, LANES), f32)
    for first in range(0, HALF_KZ, 4):
        kzs = range(first, min(first + 4, HALF_KZ))
        rows = []
        for kz in kzs:
            keep = keep_y * jnp.where(start + kz <= cut_z, 1.0, 0.0).astype(f32)
            rows.append(
                jnp.concatenate([received(ref, kz) * keep for ref in (here_ref, there_ref)], 1)
            )
        high = back_ref[pl.ds(pl.multiple_of((6 + which) * 256, 256), 256), :]
        low = back_ref[pl.ds(pl.multiple_of((10 + which) * 256, 256), 256), :]
        got = triple(jnp.concatenate(rows, 0), high, low)
        data = [stacked(padded(got[n * ROWS : (n + 1) * ROWS])) for n in range(len(kzs))]
        for n, kz in enumerate(kzs):
            even = lane_parts(folded(dot(iy_ref[...], data[n])))
            planes[0, kz * LANES : (kz + 1) * LANES, :] = even[1]
            planes[2, kz * LANES : (kz + 1) * LANES, :] = even[0]
        for n in range(0, len(kzs), 2):
            both = jnp.concatenate([one[:, :LANES] for one in data[n : n + 2]], 1)
            for k, part in enumerate(lane_parts(folded(dot(iyd_ref[...], both)))):
                kz = kzs[n + k]
                planes[1, kz * LANES : (kz + 1) * LANES, :] = part


def half_kernel(core_ref, cutoff_ref, here_ref, there_ref, back_ref, planes):
    start = core_ref[0] * HALF_KZ
    gradient_planes(cutoff_ref, here_ref, there_ref, back_ref, planes, start)


def gradient_kernel(
    core_ref, cutoff_ref, wave_ref, base_ref, state_ref, own_ref, here_ref, there_ref,
    ahead_ref, back_ref, *refs
):
    *out_refs, planes, force_ref = refs
    core = core_ref[0]
    start = (1 - core) * HALF_KZ
    gradient_planes(cutoff_ref, here_ref, there_ref, back_ref, planes, start)
    fz_ref = ahead_tables(ahead_ref)[0]
    iz_ref, izd_ref = view(back_ref, 2), view(back_ref, 3)
    y = lax.broadcasted_iota(jnp.int32, (HALF, LANES), 0) * 2
    y = y + lax.broadcasted_iota(jnp.int32, (HALF, LANES), 1) // N
    phase = ((wave_ref[0] * y) % N).astype(f32) * (2.0 * np.pi / N)
    force_ref[...] = forcing_amp * jnp.sin(phase)

    def along_halves(d, yh):
        at = pl.ds(yh, 4 * (HALF_KZ + 1), stride=HALF)
        own, other = own_ref[d, at, :], planes[d, at, :]
        low = jnp.where(core == 0, own, other)
        high = jnp.where(core == 0, other, own)
        return padded(jnp.concatenate([low, high], 0)).T

    def physical_step(yhs):
        count = len(yhs)
        flat = [along_halves(d, yh)[:96] for d in range(2) for yh in yhs]
        steep = [along_halves(2, yh)[:96] for yh in yhs]
        flat = folded_lanes(dot(beside(jnp.concatenate(flat, 0)), iz_ref[...]))
        steep = folded_lanes(dot(beside(jnp.concatenate(steep, 0)), izd_ref[...]))
        rows, lone = [], []
        for n, yh in enumerate(yhs):
            sets = [flat[96 * n :], flat[96 * (count + n) :], steep[96 * n :]]
            grads = [[one[HALF * i : HALF * (i + 1)] for i in range(3)] for one in sets]
            b = [base_ref[i, :, columns(yh)] for i in range(3)]
            s = [state_ref[i, :, columns(yh)] for i in range(3)]
            comb, comb_base = [], []
            for i in range(3):
                coupling = sum(
                    jnp.where(core == 0, grads[j][i], grads[i][j]) * s[j] for j in range(3)
                )
                comb.append(s[i] - time_step * coupling)
                drive = sum(grads[j][i] * b[j] for j in range(3))
                if i == 0:
                    drive = drive - force_ref[pl.ds(yh, 1), :]
                comb_base.append(b[i] - time_step * drive)
            rows += [comb[1], comb_base[1], comb[2], comb_base[2]]
            lone += [comb[0], comb_base[0]]
        got = lane_parts(folded(dot_nt(fz_ref[...], beside(jnp.concatenate(rows + lone, 0)))))
        depth = LINE // CHUNKS
        for n, yh in enumerate(yhs):
            second = got[count + n // 2]
            if n % 2:
                second = pltpu.roll(second, 64, 1)
            at = pl.ds(pl.multiple_of(yh * depth, 8), depth)
            for tile, part in enumerate((got[n], second)):
                for chunk in range(CHUNKS):
                    out_refs[chunk][tile, at, :] = part[chunk * depth : (chunk + 1) * depth]

    over_lines(physical_step, 8)


def spectral_kernel(
    chunk, core_ref, cutoff_ref, lines_ref, flux_ref,
    ahead_ref, along_ref, near_ref, far_ref,
):
    _, fy_ref, fyr_ref = ahead_tables(ahead_ref)
    core = core_ref[0]
    cut_x, cut_y, cut_z = cutoff_ref[0], cutoff_ref[1], cutoff_ref[2]
    first, last = planes_of(chunk)
    extra = last - first
    ky = ky_rows()
    kx = kx_lanes()
    keep_y = jnp.where(jnp.abs(ky) <= cut_y.astype(f32), 1.0, 0.0).astype(f32)
    keep_x = jnp.where(kx <= cut_x.astype(f32), 1.0, 0.0).astype(f32)
    keep_xy = keep_y * keep_x
    square_xy = ky * ky + kx * kx
    lane = lax.broadcasted_iota(jnp.int32, (ROWS, LANES), 1)
    near_ref[extra] = jnp.zeros((ROWS, LANES), f32)
    far_ref[extra] = jnp.zeros((ROWS, LANES), f32)

    def kept_z(kz):
        return jnp.where(kz <= cut_z, 1.0, 0.0).astype(f32)

    def spectral_step(kzs):
        fields = [[], [], []]
        if chunk == 0:
            first_flux = [flux_ref[0, kz] for kz in kzs]
            second_flux = [flux_ref[1, kz] for kz in kzs]
        else:
            first_flux, second_flux = flux_modes(flux_ref, fy_ref, fyr_ref, kzs)
        for pair in range(0, len(kzs), 2):
            ks = kzs[pair : pair + 2]
            data = [
                jnp.concatenate(
                    [stacked(along_y(lines_ref, t, kz, LINE // CHUNKS)) for kz in ks], 1
                )
                for t in (0, 1)
            ]
            even = lane_parts(folded(dot(fy_ref[...], data[0])))
            odd = lane_parts(folded(dot(fyr_ref[...], data[1])))
            for n, kz in enumerate(ks):
                flux = first_flux[pair + n]
                fields[0].append(jnp.where(lane < 64, odd[n], second_flux[pair + n]))
                fields[1].append(jnp.where(lane < 64, even[n], flux))
                fields[2].append(jnp.where(lane < 64, flux, even[n]))
        data = [beside(jnp.concatenate(field, 0)) for field in fields]
        modes = [folded_lanes(dot(data[max(n - 1, 0)], view(along_ref, n)[...])) for n in range(4)]
        results = [[], [], [], []]
        for n, kz in enumerate(kzs):
            kzf = kz.astype(f32)
            vx, slope, uy, uz = (mode[n * ROWS : (n + 1) * ROWS] for mode in modes)
            square = square_xy + kzf * kzf
            factor = keep_xy * kept_z(kz) / (1.0 + viscosity * time_step * square)
            share = (slope + ky * uy + kzf * uz) / jnp.where(square > 0, square, 1.0)
            results[0].append(factor * vx)
            results[1].append(factor * share)
            results[2].append(factor * (uy - ky * share))
            results[3].append(factor * (uz - kzf * share))
        got = [
            dot(
                beside(jnp.concatenate(result, 0)),
                along_ref[pl.ds(pl.multiple_of((4 + core * 4 + n) * 256, 256), 256), :],
            )
            for n, result in enumerate(results)
        ]
        got = [folded_lanes(part) for part in (got[0] + got[1], got[2], got[3])]
        for n, kz in enumerate(kzs):
            x, y, z = (part[n * ROWS : (n + 1) * ROWS] for part in got)
            near_ref[kz - first] = jnp.where(lane < 48, x, jnp.where(lane < 96, y, z))
            away = jnp.where(
                (lane >= 64) & (lane < 112), x, jnp.where((lane >= 32) & (lane < 64), z, y)
            )
            far_ref[kz - first] = pltpu.roll(away, 64, 1)
            shift = (kz - first) * 16
            near_ref[extra] += pltpu.roll(jnp.where(lane < 16, z, 0.0), shift, 1)
            rest = jnp.where((lane >= 64) & (lane < 80), z, 0.0)
            far_ref[extra] += pltpu.roll(rest, (shift + 64) % LANES, 1)

    over_planes(spectral_step, first, last)


def inverse_y(near_ref, far_ref, iy_ref, planes):
    count = near_ref.shape[0] - 1
    rest = near_ref[count] + far_ref[count]
    for kz in range(count):
        turned = pltpu.roll(rest, (LANES - kz * 16) % LANES, 1) if kz else rest
        data = jnp.concatenate([near_ref[kz] + far_ref[kz], turned], 1)
        got = lane_parts(folded(dot(iy_ref[...], stacked(padded(data)))))
        for tile in range(2):
            planes[tile, kz * LANES : (kz + 1) * LANES, :] = got[tile]
    if count < CHUNK:
        blank = jnp.zeros(((CHUNK - count) * LANES, LANES), f32)
        for tile in range(2):
            planes[tile, count * LANES :, :] = blank


def inverse_kernel(near_ref, far_ref, back_ref, planes):
    inverse_y(near_ref, far_ref, view(back_ref, 0), planes)


def final_kernel(
    near_ref, far_ref, planes_a, planes_b, state_hbm, base_hbm, back_ref, base_out, state_out,
    planes_c, state_ref, base_ref, state_gap, base_gap, arrived, left,
):
    wide = N * N // PIECES
    cuts = [pl.ds(n * wide, wide) for n in range(PIECES)]

    def copies(pairs, flags):
        return [
            [
                pltpu.make_async_copy(
                    source.at[:, :, cut], target.at[:, :, cut], flags.at[2 * n + k]
                )
                for k, (source, target) in enumerate(pairs)
            ]
            for n, cut in enumerate(cuts)
        ]

    reads = copies(((state_hbm, state_ref), (base_hbm, base_ref)), arrived)
    writes = copies(((state_gap, state_out), (base_gap, base_out)), left)
    for piece in reads:
        for copy in piece:
            copy.start()
    iy_ref, iz_ref, izr_ref = (view(back_ref, n) for n in (0, 4, 5))
    inverse_y(near_ref, far_ref, iy_ref, planes_c)

    def along_chunks(tile, yh):
        parts = [
            ref[tile, pl.ds(yh, 4 * CHUNK, stride=HALF), :]
            for ref in (planes_a, planes_b, planes_c)
        ]
        return padded(jnp.concatenate(parts, 0)).T

    many = HALF // PIECES
    for piece in range(PIECES):
        yhs = range(piece * many, (piece + 1) * many)
        data = [along_chunks(0, yh) for yh in yhs]
        rest = [along_chunks(1, yh)[:16] for yh in yhs]
        turned = beside(jnp.concatenate([one[:48] for one in data], 0))
        plain = beside(jnp.concatenate([one[48:] for one in data] + rest, 0))
        turned = folded_lanes(dot(turned, izr_ref[...]))
        plain = folded_lanes(dot(plain, iz_ref[...]))
        for copy in reads[piece]:
            copy.wait()
        for n, yh in enumerate(yhs):
            at = slice(yh * LANES, (yh + 1) * LANES)
            first = turned[48 * n : 48 * n + 48]
            second = plain[80 * n : 80 * n + 80]
            third = plain[80 * many + 16 * n :][:16]
            state_gap[0, :, at] = first[:32] - state_ref[0, :, at]
            state_gap[1, :, at] = second[16:48] - state_ref[1, :, at]
            state_gap[2, :, at] = second[48:80] - state_ref[2, :, at]
            base_gap[0, :, at] = first[32:48] - base_ref[0, :, at]
            base_gap[1, :, at] = second[:16] - base_ref[1, :, at]
            base_gap[2, :, at] = third - base_ref[2, :, at]
        for copy in writes[piece]:
            copy.start()
    for piece in writes:
        for copy in piece:
            copy.wait()


interpret = False


def call(kernel, outs, scratch, inputs, room, in_smem=0, in_hbm=(), out_hbm=False):
    whole = pl.BlockSpec(memory_space=pltpu.VMEM)
    small = pl.BlockSpec(memory_space=pltpu.SMEM)
    far = pl.BlockSpec(memory_space=pltpu.HBM)
    return pl.pallas_call(
        kernel,
        out_shape=outs,
        in_specs=[
            small if n < in_smem else far if n in in_hbm else whole for n in range(len(inputs))
        ],
        out_specs=jax.tree.map(lambda _: far if out_hbm else whole, outs),
        scratch_shapes=scratch,
        compiler_params=pltpu.CompilerParams(vmem_limit_bytes=room * 2**20),
        cost_estimate=pl.CostEstimate(flops=1000, bytes_accessed=1000, transcendentals=0),
        interpret=interpret,
    )(*inputs)


def body(base, state, wavenumber, cutoff):
    t = {name: jnp.asarray(value) for name, value in tables().items()}
    core = lax.axis_index("comp")
    seg_count = lax.axis_size("seg")
    own_base = base[0]
    own_state = state[0, 0]
    base_half = lax.dynamic_slice_in_dim(own_base, core * 16, 16, 1)
    back = [((s + 1) % seg_count, s) for s in range(seg_count)]
    around = [(2 * i, 2 * o) for i, o in back] + [(2 * o + 1, 2 * i + 1) for i, o in back]
    base_next = lax.ppermute(base_half, "seg", back)
    state_next = lax.ppermute(own_state, ("seg", "comp"), around)
    sds = jax.ShapeDtypeStruct
    core_at = core.reshape(1)
    swap = [(0, 1), (1, 0)]
    here_own = call(
        base_kernel,
        sds((SENT, ROWS, LANES), f32),
        [
            pltpu.VMEM((1, HALF * LINE, LANES), f32),
            pltpu.VMEM(own_base.shape, f32),
            pltpu.VMEM(t["ahead"].shape, bf16),
            pltpu.SemaphoreType.DMA((PIECES + 1,)),
        ],
        [core_at, own_base, t["ahead"]],
        room=56,
        in_smem=1,
        in_hbm=(1, 2),
    )
    there_own = lax.ppermute(here_own, "slab", swap)
    here_other = lax.ppermute(here_own, "comp", swap)
    counts = [planes_of(chunk)[1] - planes_of(chunk)[0] for chunk in range(CHUNKS)]
    flux_lines = sds((3, HALF * 4 * CHUNK, LANES), f32)
    flux = call(
        flux_kernel,
        [sds((2, counts[0], ROWS, LANES), f32)] + [flux_lines] * 2,
        [
            pltpu.VMEM(flux_lines.shape, f32),
            pltpu.VMEM(flux_lines.shape, f32),
            pltpu.VMEM(flux_lines.shape, f32),
            pltpu.VMEM(own_base.shape, f32),
            pltpu.VMEM(own_state.shape, f32),
            pltpu.VMEM(t["ahead"].shape, bf16),
            pltpu.VMEM((2, counts[0], ROWS, LANES), f32),
            pltpu.SemaphoreType.DMA((2 * PIECES + 1,)),
            pltpu.SemaphoreType.DMA((CHUNKS,)),
        ],
        [core_at, own_base, own_state, t["ahead"]],
        room=56,
        in_smem=1,
        in_hbm=(1, 2, 3),
        out_hbm=True,
    )
    there_own, flux = lax.optimization_barrier((there_own, flux))
    there_other = lax.ppermute(there_own, "comp", swap)
    half_planes = sds((3, (HALF_KZ + 1) * LANES, LANES), f32)
    own_planes = call(
        half_kernel,
        half_planes,
        [],
        [core_at, cutoff, here_own, there_own, t["back"]],
        room=12,
        in_smem=2,
    )
    lines = call(
        gradient_kernel,
        [sds((2, HALF * 4 * CHUNK, LANES), f32)] * CHUNKS,
        [pltpu.VMEM(half_planes.shape, f32), pltpu.VMEM((HALF, LANES), f32)],
        [core_at, cutoff, wavenumber, own_base, own_state, own_planes, here_other, there_other]
        + [t["ahead"], t["back"]],
        room=20,
        in_smem=3,
    )
    near, far = [], []
    lines = list(lines)
    for chunk in range(CHUNKS):
        if chunk:
            near[-1], lines[chunk] = lax.optimization_barrier((near[-1], lines[chunk]))
        near_part, far_part = call(
            functools.partial(spectral_kernel, chunk),
            [sds((counts[chunk] + 1, ROWS, LANES), f32)] * 2,
            [],
            [core_at, cutoff, lines[chunk], flux[chunk], t["ahead"], t["along"]],
            room=12,
            in_smem=2,
        )
        near.append(near_part)
        far.append(lax.ppermute(far_part, "slab", swap))
    planes = sds((2, CHUNK * LANES, LANES), f32)
    planes_a = call(inverse_kernel, planes, [], [near[0], far[0], t["back"]], room=8)
    near[1], planes_a = lax.optimization_barrier((near[1], planes_a))
    planes_b = call(inverse_kernel, planes, [], [near[1], far[1], t["back"]], room=8)
    base_gap, state_gap = call(
        final_kernel,
        [sds(base_next.shape, f32), sds(state_next.shape, f32)],
        [
            pltpu.VMEM((2, CHUNK * LANES, LANES), f32),
            pltpu.VMEM(state_next.shape, f32),
            pltpu.VMEM(base_next.shape, f32),
            pltpu.VMEM(state_next.shape, f32),
            pltpu.VMEM(base_next.shape, f32),
            pltpu.SemaphoreType.DMA((2 * PIECES,)),
            pltpu.SemaphoreType.DMA((2 * PIECES,)),
        ],
        [near[2], far[2], planes_a, planes_b, state_next, base_next, t["back"]],
        room=16,
        in_hbm=(4, 5),
        out_hbm=True,
    )
    return base_gap[None], state_gap[None, None]


def solution(mesh):
    paired = mesh.shape["slab"] == 2 and mesh.shape["comp"] == 2
    return jax.shard_map(
        body if paired else general_body,
        mesh=mesh,
        in_specs=(
            P(("groups", "seg"), None, "slab", None),
            P(("groups", "seg"), "comp", None, "slab", None),
            P("groups"),
            P("groups"),
        ),
        out_specs=(
            P(("groups", "seg"), None, ("slab", "comp"), None),
            P(("groups", "seg"), "comp", None, "slab", None),
        ),
        check_vma=False,
    )
```

```python
import functools

import jax
import jax.numpy as jnp
import ml_dtypes
import numpy as np
from jax import lax
from jax.experimental import pallas as pl
from jax.experimental.pallas import tpu as pltpu
from jax.sharding import PartitionSpec as P

N = 64
HALF = 32
KEEP = N // 3
NKZ = KEEP + 1
NKY = 44
ROWS = 2 * NKY
CHUNK = 8
CHUNKS = 3
LINE = CHUNKS * CHUNK * 4
HALF_KZ = NKZ // 2
HALF_LINE = 4 * (HALF_KZ + 1)
SENT = 9
LANES = 128

viscosity = 0.025
time_step = 0.02
forcing_amp = 10.0

f32 = jnp.float32
bf16 = jnp.bfloat16


highest = lax.Precision.HIGHEST


def swapped(value, axis, apart):
    mask = 2**apart
    pairs = [(source, source ^ mask) for source in range(lax.axis_size(axis))]
    return lax.ppermute(value, axis, pairs)


def shifted(block, axis, distance):
    devices = range(lax.axis_size(axis))
    route = [((i - distance) % len(devices), i) for i in devices]
    return lax.ppermute(block, axis, route)


def wavenumbers(grid_points):
    position = jnp.arange(grid_points, dtype=jnp.int32)
    return jnp.where(position < grid_points // 2, position, position - grid_points)


def phases(first, second, grid_points):
    product = jnp.mod(first[:, None] * second[None, :], grid_points)
    return product.astype(jnp.float32) * (2.0 * jnp.pi / grid_points)


def combine(partial_value, columns):
    cosine_part = partial_value[0]
    sine_part = partial_value[1]
    real_part = cosine_part[..., :columns] - sine_part[..., columns:]
    imag_part = cosine_part[..., columns:] + sine_part[..., :columns]
    return jnp.concatenate([real_part, imag_part], axis=-1)


def times_unit(values, wave, columns):
    return jnp.concatenate([-wave * values[..., columns:], wave * values[..., :columns]], axis=-1)


def doubled(values):
    return jnp.concatenate([values, values], axis=-1)


def general_body(base, state, wavenumber, cutoff):
    grid_points = N
    base = base.reshape(base.shape[0], 3, base.shape[2], grid_points, grid_points)
    state = state.reshape(
        state.shape[0], state.shape[1], 3, state.shape[3], grid_points, grid_points
    )
    slab_rows = state.shape[3]
    half_rows = slab_rows // 2
    slab_count = lax.axis_size("slab")
    group_count = slab_count * lax.axis_size("comp")
    core_side = lax.axis_index("comp")
    block_number = lax.axis_index(("slab", "comp"))
    base_whole = base[0]
    base_half = lax.dynamic_slice_in_dim(base_whole, core_side * half_rows, half_rows, 1)
    own_state = state[0, 0]
    spectrum = wavenumbers(grid_points)
    one_third = grid_points // 3
    row_total = (2 * one_third + group_count) // group_count * group_count
    row_index = jnp.arange(row_total, dtype=jnp.int32)
    row_alive_mask = row_index <= 2 * one_third
    row_wave = jnp.where(row_index <= one_third, row_index, row_index - (2 * one_third + 1))
    row_wave = jnp.where(row_alive_mask, row_wave, 0)
    width = grid_points // 2
    rows_per_block = row_total // group_count
    alive_flags = row_alive_mask.astype(jnp.float32)
    grid_index = jnp.arange(grid_points, dtype=jnp.int32)
    column_index = grid_index[:width]
    angle_grid = phases(grid_index, grid_index, grid_points)
    angle_ahead = phases(grid_index, column_index, grid_points)
    angle_behind = phases(column_index, grid_index, grid_points)
    column_weight = jnp.where(column_index == 0, 1.0, 2.0).astype(jnp.float32)[:, None]
    forward_z = jnp.concatenate([jnp.cos(angle_ahead), -jnp.sin(angle_ahead)], axis=1)
    inverse_z = (
        jnp.concatenate(
            [jnp.cos(angle_behind) * column_weight, -jnp.sin(angle_behind) * column_weight], axis=0
        )
        / grid_points
    )
    phase_angle_rows = phases(row_wave, grid_index, grid_points)
    forward_transform_y = (
        jnp.stack([jnp.cos(phase_angle_rows), -jnp.sin(phase_angle_rows)])
        * alive_flags[None, :, None]
    )
    inverse_y = (
        jnp.stack([jnp.cos(phase_angle_rows).T, jnp.sin(phase_angle_rows).T])
        * alive_flags[None, None, :]
        / grid_points
    )
    forward_x = jnp.stack([jnp.cos(angle_grid), -jnp.sin(angle_grid)])
    inverse_x = jnp.stack([jnp.cos(angle_grid), jnp.sin(angle_grid)]) / grid_points
    table_ahead = forward_x.reshape(2, grid_points, slab_count, slab_rows)
    table_back = inverse_x.reshape(2, slab_count, slab_rows, grid_points)
    local_wave = lax.dynamic_slice_in_dim(row_wave, block_number * rows_per_block, rows_per_block)
    local_alive_mask = lax.dynamic_slice_in_dim(
        alive_flags, block_number * rows_per_block, rows_per_block
    )
    shape_local = (grid_points, rows_per_block, width)
    wave_x = jnp.broadcast_to(spectrum[:, None, None], shape_local)
    wave_y = jnp.broadcast_to(local_wave[None, :, None], shape_local)
    wave_z = jnp.broadcast_to(spectrum[:width][None, None, :], shape_local)
    inside = (
        (jnp.abs(wave_x) <= cutoff[0])
        & (jnp.abs(wave_y) <= cutoff[1])
        & (jnp.abs(wave_z) <= cutoff[2])
    )
    keep_mask = doubled(inside.astype(jnp.float32) * local_alive_mask[None, :, None])
    float_x = wave_x.astype(jnp.float32)
    float_y = wave_y.astype(jnp.float32)
    float_z = wave_z.astype(jnp.float32)
    ksquare = float_x * float_x + float_y * float_y + float_z * float_z
    safe_square = doubled(jnp.where(ksquare > 0, ksquare, jnp.ones_like(ksquare)))
    damping = doubled(1.0 / (1.0 + viscosity * time_step * ksquare))
    double_x = doubled(float_x)
    double_y = doubled(float_y)
    double_z = doubled(float_z)

    def project(field):
        divergence = (double_x * field[0] + double_y * field[1] + double_z * field[2]) / safe_square
        return jnp.stack(
            [
                field[0] - double_x * divergence,
                field[1] - double_y * divergence,
                field[2] - double_z * divergence,
            ]
        )

    def yz_forward(field):
        along_z = jnp.einsum("...z,zk->...k", field, forward_z, precision=highest)
        partial_value = jnp.einsum(
            "sry,...yk->s...rk", forward_transform_y, along_z, precision=highest
        )
        return combine(partial_value, width)

    def yz_inverse(modes):
        partial_value = jnp.einsum("syr,...rk->s...yk", inverse_y, modes, precision=highest)
        return jnp.einsum(
            "...k,kz->...z", combine(partial_value, width), inverse_z, precision=highest
        )

    def spectral(state_fields, base_fields):
        state_modes = yz_forward(state_fields)[:, :, None]
        base_modes = yz_forward(base_fields)[:, :, None]
        state_got = lax.all_to_all(
            state_modes, ("slab", "comp"), split_axis=4, concat_axis=2, tiled=True
        )
        base_got = lax.all_to_all(
            base_modes, ("slab", "comp"), split_axis=4, concat_axis=2, tiled=True
        )
        item_count = state_got.shape[0]
        part_count = state_got.shape[1]
        state_split = state_got.reshape(
            item_count, part_count, slab_count, 2, slab_rows, rows_per_block, 2 * width
        )
        state_partial = jnp.einsum(
            "srpx,ijpcxyk->sijcryk", table_ahead, state_split, precision=highest
        )
        base_lined = base_got.reshape(item_count, 1, grid_points, rows_per_block, 2 * width)
        base_partial = jnp.einsum("srx,ijxyk->sijryk", forward_x, base_lined, precision=highest)
        return (combine(state_partial, width), combine(base_partial, width))

    state_first, base_first = spectral(own_state[:, None], base_half[:, None])
    state_hat = state_first[:, 0] * keep_mask
    base_hat = base_first[:, 0] * keep_mask
    grad_hat = jnp.stack(
        [
            times_unit(base_hat, float_x, width),
            times_unit(base_hat, float_y, width),
            times_unit(base_hat, float_z, width),
        ],
        axis=1,
    )
    grad_hat = grad_hat.reshape(9, grid_points, rows_per_block, 2 * width)
    grad_partial = jnp.einsum("sxr,iryk->sixyk", inverse_x, grad_hat, precision=highest)
    grad_spread = combine(grad_partial, width).reshape(
        9, group_count, half_rows, rows_per_block, 2 * width
    )
    own_rows = yz_inverse(
        lax.all_to_all(grad_spread, ("slab", "comp"), split_axis=1, concat_axis=3, tiled=True)[:, 0]
    )
    other_rows = swapped(own_rows, "comp", 0)
    gradient = jnp.where(
        core_side == 0,
        jnp.concatenate([own_rows, other_rows], axis=1),
        jnp.concatenate([other_rows, own_rows], axis=1),
    )
    gradient = gradient.reshape(3, 3, slab_rows, grid_points, grid_points)
    gradient_half = lax.dynamic_slice_in_dim(gradient, core_side * half_rows, half_rows, 2)
    flux_terms = own_state[:, None] * base_whole[None, :]
    coupling_matrix = jnp.where(core_side == 0, gradient, jnp.swapaxes(gradient, 0, 1))
    coupling = jnp.sum(coupling_matrix * own_state[None, :], axis=1)
    forcing_phase = phases(wavenumber, grid_index, grid_points)[0]
    forcing = forcing_amp * jnp.sin(forcing_phase)[None, :, None]
    base_drive = jnp.sum(gradient_half * base_half[None, :], axis=1)
    base_drive = jnp.concatenate([base_drive[:1] - forcing[None], base_drive[1:]], axis=0)
    state_fields = jnp.concatenate([flux_terms, coupling[:, None]], axis=1)
    drive_modes, base_modes_two = spectral(state_fields, base_drive[:, None])
    orient = jnp.array([1.0, -1.0], dtype=jnp.float32)[None, :, None, None, None]
    divergence = (
        times_unit(drive_modes[:, 0], float_x, width)
        + times_unit(drive_modes[:, 1], float_y, width)
        + times_unit(drive_modes[:, 2], float_z, width)
    )
    state_drive = keep_mask * (orient * divergence + drive_modes[:, 3])
    new_hat = damping * project(state_hat - time_step * state_drive)
    base_new_hat = damping * project(base_hat - time_step * keep_mask * base_modes_two[:, 0])
    state_partial = jnp.einsum("spxr,icryk->sipcxyk", table_back, new_hat, precision=highest)
    state_back = combine(state_partial, width).reshape(
        3, group_count, slab_rows, rows_per_block, 2 * width
    )
    base_partial = jnp.einsum("sxr,iryk->sixyk", inverse_x, base_new_hat, precision=highest)
    base_back = combine(base_partial, width).reshape(
        3, group_count, half_rows, rows_per_block, 2 * width
    )
    state_got = lax.all_to_all(
        state_back, ("slab", "comp"), split_axis=1, concat_axis=3, tiled=True
    )
    base_got = lax.all_to_all(base_back, ("slab", "comp"), split_axis=1, concat_axis=3, tiled=True)
    state_new = yz_inverse(state_got[:, 0])
    base_new = yz_inverse(base_got[:, 0])
    base_later, later_state = shifted((base_half, own_state), "seg", -1)
    prior_state = shifted(own_state, "seg", 1)
    neighbour = jnp.where(core_side == 0, later_state, prior_state)
    base_gap = (base_new - base_later).reshape(1, 3, half_rows, grid_points * grid_points)
    state_gap = (state_new - neighbour).reshape(1, 1, 3, slab_rows, grid_points * grid_points)
    return (base_gap, state_gap)


def halves(table):
    high = table.astype(np.float32).astype(ml_dtypes.bfloat16)
    low = (table - high.astype(np.float64)).astype(ml_dtypes.bfloat16)
    return high, low


def left_table(table, depth):
    padded = np.zeros((table.shape[0], depth))
    padded[:, : table.shape[1]] = table
    high, low = halves(padded)
    return np.concatenate(
        [np.concatenate([high, high], 1), np.concatenate([low, np.zeros_like(low)], 1)], 0
    )


def right_table(table, depth):
    return np.ascontiguousarray(left_table(table.T, depth).T)


def planes_of(chunk):
    return chunk * CHUNK, min((chunk + 1) * CHUNK, NKZ)


def ky_values():
    index = np.arange(NKY)
    wave = np.where(index <= KEEP, index, index - (2 * KEEP + 1))
    alive = (index <= 2 * KEEP).astype(np.float64)
    return wave * alive, alive


@functools.cache
def tables():
    out = {}
    z = np.arange(N)
    kz = np.arange(NKZ)
    angle = 2 * np.pi * kz[:, None] * z[None, :] / N
    weight = np.where(kz == 0, 1.0, 2.0)[:, None] / N
    forward = np.zeros((2, 2, CHUNKS * CHUNK, 2, N))
    inverse = np.zeros((NKZ, 2, 2, 2, N))
    turned = np.zeros((NKZ, 2, 2, 2, N))
    slope = np.zeros((NKZ, 2, 2, 2, N))
    for y2 in range(2):
        forward[y2, 0, :NKZ, y2] = np.cos(angle)
        forward[y2, 1, :NKZ, y2] = -np.sin(angle)
        inverse[:, y2, 0, y2] = weight * np.cos(angle)
        inverse[:, y2, 1, y2] = -weight * np.sin(angle)
        turned[:, y2, 0, y2] = weight * np.sin(angle)
        turned[:, y2, 1, y2] = weight * np.cos(angle)
        slope[:, y2, 0, y2] = -weight * kz[:, None] * np.sin(angle)
        slope[:, y2, 1, y2] = -weight * kz[:, None] * np.cos(angle)
    forward = np.moveaxis(forward.reshape(4, CHUNKS, CHUNK, 2 * N), 1, 0)
    out["fz"] = left_table(forward.reshape(LINE, 2 * N), 128)
    by_kz = np.moveaxis(forward.reshape(CHUNKS, 4, CHUNK, 2 * N), 1, 0).reshape(4, -1, 2 * N)
    halved = []
    for core in range(2):
        wide = np.zeros((4, HALF_KZ + 1, 2 * N))
        wide[:, :HALF_KZ] = by_kz[:, core * HALF_KZ : (core + 1) * HALF_KZ]
        halved.append(left_table(wide.reshape(HALF_LINE, 2 * N), 128))
    out["fzh"] = np.concatenate(halved, 0)

    def by_chunk(table):
        wide = np.zeros((CHUNKS, CHUNK, 4, 2 * N))
        for chunk in range(CHUNKS):
            first, last = planes_of(chunk)
            wide[chunk, : last - first] = table.reshape(NKZ, 4, 2 * N)[first:last]
        return right_table(wide.reshape(LINE, 2 * N), 128)

    out["iz"] = by_chunk(inverse)
    out["izr"] = by_chunk(turned)

    def by_half(table):
        wide = np.zeros((2, HALF_KZ + 1, 4, 2 * N))
        wide[:, :HALF_KZ] = table.reshape(2, HALF_KZ, 4, 2 * N)
        return right_table(wide.reshape(8 * HALF_KZ + 8, 2 * N), 128)

    out["izg"] = by_half(inverse)
    out["izd"] = by_half(slope)
    ky, alive = ky_values()
    y = 2 * np.arange(HALF)[None, :] + np.arange(2)[:, None]
    phase = 2 * np.pi * ky[:, None, None] * y[None] / N
    cosine = np.cos(phase) * alive[:, None, None]
    sine = np.sin(phase) * alive[:, None, None]
    plain = np.zeros((2, NKY, 2, 2, HALF))
    plain[0, :, :, 0] = cosine
    plain[0, :, :, 1] = sine
    plain[1, :, :, 0] = -sine
    plain[1, :, :, 1] = cosine
    rotated = np.stack([-plain[1], plain[0]])
    out["fy"] = left_table(plain.reshape(ROWS, 128), 128)
    out["fyr"] = left_table(rotated.reshape(ROWS, 128), 128)
    back = np.zeros((2, 2, HALF, 2, NKY))
    cos_t = np.moveaxis(cosine, 0, -1) / N
    sin_t = np.moveaxis(sine, 0, -1) / N
    back[:, 0, :, 0] = cos_t
    back[:, 0, :, 1] = -sin_t
    back[:, 1, :, 0] = sin_t
    back[:, 1, :, 1] = cos_t
    back_slope = np.zeros_like(back)
    back_slope[..., 0, :] = ky * back[..., 1, :]
    back_slope[..., 1, :] = -ky * back[..., 0, :]
    out["iy"] = left_table(back.reshape(128, ROWS), 128)
    out["iyd"] = left_table(back_slope.reshape(128, ROWS), 128)
    grad_high, grad_low = [], []
    x = np.arange(N)
    apart = x[:HALF, None] - x[None, :]
    for cut in range(KEEP - 3, KEEP + 1):
        k = np.arange(cut + 1)
        wk = np.where(k == 0, 1.0, 2.0) / N
        arg = 2 * np.pi * apart[..., None] * k / N
        keep = (np.cos(arg) * wk).sum(-1)
        derive = (-np.sin(arg) * wk * k).sum(-1)
        table = np.zeros((2, 4, HALF, 2, 4, HALF))
        for comp in range(3):
            for side in range(2):
                rows = slice(side * HALF, (side + 1) * HALF)
                table[side, comp, :, 0, comp, :] = keep[:, rows].T
                table[side, comp, :, 1, comp, :] = derive[:, rows].T
        high, low = halves(table.reshape(256, 256))
        grad_high.append(high)
        grad_low.append(low)
    out["gxh"] = np.stack(grad_high)
    out["gxl"] = np.stack(grad_low)
    kx = np.arange(HALF)
    live = (kx <= KEEP).astype(np.float64)
    xl = np.arange(HALF)
    arg = 2 * np.pi * xl[:, None] * kx[None, :] / N
    value = np.concatenate([np.cos(arg) * live, np.sin(arg) * live], 1)
    change = np.concatenate([kx * np.sin(arg) * live, -kx * np.cos(arg) * live], 1)

    def coefficients(blocks):
        table = np.zeros((4, HALF, 2, 2 * HALF))
        for block, part, what in blocks:
            table[block, :, part] = what
        return table.reshape(LANES, LANES)

    first = coefficients([(0, 0, value), (1, 1, value), (2, 0, change), (3, 0, value)])
    last = coefficients([(0, 0, change), (1, 0, value), (2, 0, value), (3, 1, value)])
    fall = first.reshape(LANES, 2, 2, HALF)
    fall = np.stack([-kx * fall[:, :, 1], kx * fall[:, :, 0]], 2).reshape(LANES, LANES)
    out["fx"] = np.stack([right_table(part, 128) for part in (first, fall, first, last)])
    wx = np.where(kx == 0, 1.0, 2.0) * live / N
    for core in range(2):
        ix = np.zeros((4, 2, 2 * HALF, LANES))
        for side in range(2):
            xs = np.arange(HALF) + side * HALF
            arg = 2 * np.pi * kx[:, None] * xs[None, :] / N
            give = np.concatenate([np.cos(arg) * wx[:, None], np.sin(arg) * wx[:, None]], 0)
            drop = np.concatenate(
                [np.sin(arg) * (wx * kx)[:, None], -np.cos(arg) * (wx * kx)[:, None]], 0
            )
            own = slice(core * 16, core * 16 + 16)

            def put(quantity, part, lane, what):
                at = (lane + side * 64 + np.arange(what.shape[1])) % LANES
                ix[quantity, part][:, at] = what

            put(0, 0, 0, give)
            put(1, 0, 0, drop)
            put(0, 1, 32, give[:, own])
            put(1, 1, 32, drop[:, own])
            put(2, 1, 48, give[:, own])
            put(2, 0, 64, give)
            put(3, 0, 96, give)
            put(3, 1, 0, give[:, own])
        out["ix%d" % core] = np.stack(
            [right_table(part, 128) for part in ix.reshape(4, LANES, LANES)]
        )
    out["ix"] = np.stack([out.pop("ix0"), out.pop("ix1")])
    merged = {}
    merged["ahead"] = np.concatenate([out["fz"], out["fy"], out["fyr"], out["fzh"]], 0)
    gx = [out["gxh"].reshape(-1, 256), out["gxl"].reshape(-1, 256)]
    square = [out[name] for name in ("iy", "iyd", "izg", "izd", "iz", "izr")]
    merged["back"] = np.concatenate(square + gx, 0)
    merged["along"] = np.concatenate([out["fx"].reshape(-1, 256), out["ix"].reshape(-1, 256)], 0)
    return merged


def view(ref, index, rows=256, start=0):
    return ref.at[pl.ds(start + index * rows, rows), :]


def ahead_tables(ref):
    return (
        view(ref, 0, 2 * LINE),
        view(ref, 0, 2 * ROWS, 2 * LINE),
        view(ref, 1, 2 * ROWS, 2 * LINE),
    )


def ky_rows():
    row = lax.broadcasted_iota(jnp.int32, (ROWS, LANES), 0)
    index = jnp.where(row < NKY, row, row - NKY)
    wave = jnp.where(index <= KEEP, index, index - (2 * KEEP + 1))
    return jnp.where(index <= 2 * KEEP, wave, 0).astype(f32)


def kx_lanes():
    lane = lax.broadcasted_iota(jnp.int32, (1, LANES), 1) % HALF
    return jnp.where(lane <= KEEP, lane, 0).astype(f32)


def split(values):
    high = values.astype(bf16)
    low = (values - high.astype(f32)).astype(bf16)
    return high, low


def dot(a, b):
    return jnp.dot(a, b, preferred_element_type=f32)


def dot_nt(a, b):
    return lax.dot_general(a, b, (((1,), (1,)), ((), ())), preferred_element_type=f32)


def stacked(values):
    high, low = split(values)
    return jnp.concatenate([high, low], 0)


def beside(values):
    high, low = split(values)
    return jnp.concatenate([high, low], 1)


def folded(result):
    rows = result.shape[0] // 2
    return result[:rows] + result[rows:]


def folded_lanes(result):
    return result[:, :LANES] + result[:, LANES:]


def padded(values, rows=128):
    return jnp.concatenate([values, jnp.zeros((rows - values.shape[0], values.shape[1]), f32)], 0)


def triple(values, high_ref, low_ref):
    high, low = split(values)
    return dot(high, high_ref) + dot(low, high_ref) + dot(high, low_ref)


def columns(yh):
    return pl.ds(pl.multiple_of(yh * LANES, LANES), LANES)


def along_y(ref, tile, kz):
    at = kz % CHUNK
    return jnp.concatenate(
        [ref[tile, pl.ds(q * CHUNK + at, HALF, stride=4 * CHUNK), :] for q in range(4)], 0
    )


def line_rows(yh):
    return pl.ds(pl.multiple_of(yh * LINE, 8), LINE)


def lane_parts(values):
    return [values[:, at : at + LANES] for at in range(0, values.shape[1], LANES)]


def over_planes(step, first=0, last=NKZ):
    def four(index, _):
        step([first + index * 4 + k for k in range(4)])
        return 0

    count = (last - first) // 4
    lax.fori_loop(0, count, four, 0)
    if first + count * 4 < last:
        step([jnp.int32(kz) for kz in range(first + count * 4, last)])


def over_lines(step, many, first=0, last=HALF):
    def some(index, _):
        step([first + index * many + k for k in range(many)])
        return 0

    lax.fori_loop(0, (last - first) // many, some, 0)


PIECES = 4


def base_kernel(core_ref, base_hbm, ahead_hbm, out_ref, lines, base_ref, ahead_ref, arrived):
    nothing = jnp.zeros((HALF, LANES), f32)
    wide = N * N // PIECES
    table = pltpu.make_async_copy(ahead_hbm, ahead_ref, arrived.at[PIECES])
    pieces = [
        pltpu.make_async_copy(
            base_hbm.at[:, :, pl.ds(n * wide, wide)],
            base_ref.at[:, :, pl.ds(n * wide, wide)],
            arrived.at[n],
        )
        for n in range(PIECES)
    ]
    pieces[0].start()
    table.start()
    for piece in pieces[1:]:
        piece.start()
    fy_ref = ahead_tables(ahead_ref)[1]
    table.wait()
    first = 2 * LINE + 4 * ROWS + core_ref[0] * 2 * HALF_LINE
    fz = ahead_ref[pl.ds(pl.multiple_of(first, 32), 2 * HALF_LINE), :]
    many = HALF // PIECES
    for n, piece in enumerate(pieces):
        piece.wait()
        yhs = range(n * many, (n + 1) * many)
        rows = []
        for yh in yhs:
            at = slice(yh * LANES, (yh + 1) * LANES)
            rows += [base_ref[i, :, at] for i in range(3)] + [nothing]
        got = folded(dot_nt(fz, beside(jnp.concatenate(rows, 0))))
        for yh, part in zip(yhs, lane_parts(got)):
            lines[yh * HALF_LINE : (yh + 1) * HALF_LINE, :] = part
    planes = []
    for pair in range(0, HALF_KZ, 2):
        ks = range(pair, min(pair + 2, HALF_KZ))
        data = []
        for k in ks:
            starts = [q * (HALF_KZ + 1) + k for q in range(4)]
            picked = [lines[pl.ds(at, HALF, stride=HALF_LINE), :] for at in starts]
            data.append(stacked(jnp.concatenate(picked, 0)))
        data = jnp.concatenate(data, 1)
        planes += lane_parts(folded(dot(fy_ref[...], data)))
    lane = lax.broadcasted_iota(jnp.int32, (ROWS, LANES), 1)
    for k in range(SENT):
        part = planes[k]
        if k < 3 * (HALF_KZ - SENT):
            guest = pltpu.roll(planes[SENT + k // 3], (3 - k % 3) * HALF, 1)
            part = jnp.where(lane < 96, part, guest)
        out_ref[k] = part


def received(ref, k):
    if k < SENT:
        return ref[k]
    lane = lax.broadcasted_iota(jnp.int32, (ROWS, LANES), 1)
    blocks = [
        pltpu.roll(ref[3 * (k - SENT) + j], LANES - (3 - j) * HALF, 1) for j in range(3)
    ]
    return jnp.where(lane < 32, blocks[0], jnp.where(lane < 64, blocks[1], blocks[2]))


def flux_modes(lines_ref, fy_ref, fyr_ref, kzs):
    ky = ky_rows()
    lane = lax.broadcasted_iota(jnp.int32, (ROWS, LANES), 1)
    odd_block = (lane // HALF) % 2 == 1
    even = []
    for pair in range(0, len(kzs), 2):
        data = [stacked(along_y(lines_ref, 0, kz)) for kz in kzs[pair : pair + 2]]
        even += lane_parts(folded(dot(fy_ref[...], jnp.concatenate(data, 1))))
    odd = []
    for kz in kzs:
        data = [stacked(along_y(lines_ref, tile, kz)) for tile in (1, 2)]
        odd.append(lane_parts(folded(dot(fyr_ref[...], jnp.concatenate(data, 1)))))
    first, second = [], []
    for n, kz in enumerate(kzs):
        kzf = kz.astype(f32)
        plain = even[n]
        slopes = odd[n][0] * jnp.where(odd_block, kzf, ky)
        slopes = slopes + pltpu.roll(slopes, 32, 1)
        first.append(jnp.where(odd_block, slopes, plain))
        other = plain * jnp.where(lane >= 96, -kzf, -ky)
        other = other + pltpu.roll(other, 64, 1)
        second.append(jnp.where(lane >= 96, other, jnp.where(lane >= 64, odd[n][1], 0.0)))
    return first, second


def flux_kernel(
    core_ref, base_hbm, state_hbm, ahead_hbm, out_ref, out_b, out_c,
    lines_a, lines_b, lines_c, base_ref, state_ref, ahead_ref, result, arrived, left,
):
    wide = N * N // PIECES
    pieces = [pltpu.make_async_copy(ahead_hbm, ahead_ref, arrived.at[2 * PIECES])]
    for n in range(PIECES):
        for k, (source, target) in enumerate(((base_hbm, base_ref), (state_hbm, state_ref))):
            at = pl.ds(n * wide, wide)
            pieces.append(
                pltpu.make_async_copy(
                    source.at[:, :, at], target.at[:, :, at], arrived.at[2 * n + k]
                )
            )
    for piece in pieces:
        piece.start()
    fz_ref, fy_ref, fyr_ref = ahead_tables(ahead_ref)
    sigma = jnp.where(core_ref[0] == 0, -time_step, time_step).astype(f32)
    depth = LINE // CHUNKS

    def z_step(yhs):
        rows, lone = [], []
        for yh in yhs:
            b = [base_ref[i, :, columns(yh)] for i in range(3)]
            t = [sigma * state_ref[i, :, columns(yh)] for i in range(3)]
            rows += [t[2] * b[0], t[0] * b[1], t[1] * b[0], t[0] * b[2]]
            rows += [t[2] * b[1], t[2] * b[2], t[1] * b[1], t[1] * b[2]]
            lone.append(t[0] * b[0])
        got = lane_parts(folded(dot_nt(fz_ref[...], beside(jnp.concatenate(rows + lone, 0)))))
        for n, yh in enumerate(yhs):
            third = got[-1] if n == 2 else pltpu.roll(got[-1], (2 - n) % 4 * HALF, 1)
            at = pl.ds(pl.multiple_of(yh * depth, 8), depth)
            for tile, part in enumerate((got[2 * n], got[2 * n + 1], third)):
                for chunk, lines in enumerate((lines_a, lines_b, lines_c)):
                    lines[tile, at, :] = part[chunk * depth : (chunk + 1) * depth]

    pieces[0].wait()
    for n in range(PIECES):
        pieces[2 * n + 1].wait()
        pieces[2 * n + 2].wait()
        over_lines(z_step, 4, n * HALF // PIECES, (n + 1) * HALF // PIECES)
    sends = [
        pltpu.make_async_copy(lines_b, out_b, left.at[1]),
        pltpu.make_async_copy(lines_c, out_c, left.at[2]),
        pltpu.make_async_copy(result, out_ref, left.at[0]),
    ]
    sends[0].start()
    sends[1].start()

    def y_step(kzs):
        first, second = flux_modes(lines_a, fy_ref, fyr_ref, kzs)
        for n, kz in enumerate(kzs):
            result[0, kz] = first[n]
            result[1, kz] = second[n]

    over_planes(y_step, *planes_of(0))
    sends[2].start()
    for send in sends:
        send.wait()


def gradient_planes(cutoff_ref, here_ref, there_ref, back_ref, planes, start):
    cut_x, cut_y, cut_z = cutoff_ref[0], cutoff_ref[1], cutoff_ref[2]
    which = jnp.clip(cut_x - (KEEP - 3), 0, 3)
    keep_y = jnp.where(jnp.abs(ky_rows()) <= cut_y.astype(f32), 1.0, 0.0).astype(f32)
    iy_ref, iyd_ref = (view(back_ref, n) for n in range(2))
    for d in range(3):
        planes[d, HALF_KZ * LANES :, :] = jnp.zeros((LANES, LANES), f32)
    for first in range(0, HALF_KZ, 4):
        kzs = range(first, min(first + 4, HALF_KZ))
        rows = []
        for kz in kzs:
            keep = keep_y * jnp.where(start + kz <= cut_z, 1.0, 0.0).astype(f32)
            rows.append(
                jnp.concatenate([received(ref, kz) * keep for ref in (here_ref, there_ref)], 1)
            )
        high = back_ref[pl.ds(pl.multiple_of((6 + which) * 256, 256), 256), :]
        low = back_ref[pl.ds(pl.multiple_of((10 + which) * 256, 256), 256), :]
        got = triple(jnp.concatenate(rows, 0), high, low)
        data = [stacked(padded(got[n * ROWS : (n + 1) * ROWS])) for n in range(len(kzs))]
        for n, kz in enumerate(kzs):
            even = lane_parts(folded(dot(iy_ref[...], data[n])))
            planes[0, kz * LANES : (kz + 1) * LANES, :] = even[1]
            planes[2, kz * LANES : (kz + 1) * LANES, :] = even[0]
        for n in range(0, len(kzs), 2):
            both = jnp.concatenate([one[:, :LANES] for one in data[n : n + 2]], 1)
            for k, part in enumerate(lane_parts(folded(dot(iyd_ref[...], both)))):
                kz = kzs[n + k]
                planes[1, kz * LANES : (kz + 1) * LANES, :] = part


def half_kernel(core_ref, cutoff_ref, here_ref, there_ref, back_ref, planes):
    start = core_ref[0] * HALF_KZ
    gradient_planes(cutoff_ref, here_ref, there_ref, back_ref, planes, start)


def gradient_kernel(
    core_ref, cutoff_ref, wave_ref, base_ref, state_ref, own_ref, here_ref, there_ref,
    ahead_ref, back_ref, *refs
):
    *out_refs, planes, force_ref = refs
    core = core_ref[0]
    start = (1 - core) * HALF_KZ
    gradient_planes(cutoff_ref, here_ref, there_ref, back_ref, planes, start)
    fz_ref = ahead_tables(ahead_ref)[0]
    iz_ref, izd_ref = view(back_ref, 2), view(back_ref, 3)
    y = lax.broadcasted_iota(jnp.int32, (HALF, LANES), 0) * 2
    y = y + lax.broadcasted_iota(jnp.int32, (HALF, LANES), 1) // N
    phase = ((wave_ref[0] * y) % N).astype(f32) * (2.0 * np.pi / N)
    force_ref[...] = forcing_amp * jnp.sin(phase)
    nothing = jnp.zeros((HALF, LANES), f32)

    def along_halves(d, yh):
        at = pl.ds(yh, 4 * (HALF_KZ + 1), stride=HALF)
        own, other = own_ref[d, at, :], planes[d, at, :]
        low = jnp.where(core == 0, own, other)
        high = jnp.where(core == 0, other, own)
        return padded(jnp.concatenate([low, high], 0)).T

    def physical_step(yhs):
        count = len(yhs)
        flat = [along_halves(d, yh)[:96] for d in range(2) for yh in yhs]
        steep = [along_halves(2, yh)[:96] for yh in yhs]
        flat = folded_lanes(dot(beside(jnp.concatenate(flat, 0)), iz_ref[...]))
        steep = folded_lanes(dot(beside(jnp.concatenate(steep, 0)), izd_ref[...]))
        for n, yh in enumerate(yhs):
            sets = [flat[96 * n :], flat[96 * (count + n) :], steep[96 * n :]]
            grads = [[one[HALF * i : HALF * (i + 1)] for i in range(3)] for one in sets]
            b = [base_ref[i, :, columns(yh)] for i in range(3)]
            s = [state_ref[i, :, columns(yh)] for i in range(3)]
            comb, comb_base = [], []
            for i in range(3):
                coupling = sum(
                    jnp.where(core == 0, grads[j][i], grads[i][j]) * s[j] for j in range(3)
                )
                comb.append(s[i] - time_step * coupling)
                drive = sum(grads[j][i] * b[j] for j in range(3))
                if i == 0:
                    drive = drive - force_ref[pl.ds(yh, 1), :]
                comb_base.append(b[i] - time_step * drive)
            rows = [comb[1], comb_base[1], comb[2], comb_base[2]]
            rows += [comb[0], comb_base[0], nothing, nothing]
            got = folded(dot_nt(fz_ref[...], beside(jnp.concatenate(rows, 0))))
            depth = LINE // CHUNKS
            at = pl.ds(pl.multiple_of(yh * depth, 8), depth)
            for tile, part in enumerate(lane_parts(got)):
                for chunk in range(CHUNKS):
                    out_refs[chunk][tile, at, :] = part[chunk * depth : (chunk + 1) * depth]

    over_lines(physical_step, 8)


def spectral_kernel(
    chunk, core_ref, cutoff_ref, lines_ref, flux_ref,
    ahead_ref, along_ref, near_ref, far_ref,
):
    _, fy_ref, fyr_ref = ahead_tables(ahead_ref)
    core = core_ref[0]
    cut_x, cut_y, cut_z = cutoff_ref[0], cutoff_ref[1], cutoff_ref[2]
    first, last = planes_of(chunk)
    extra = last - first
    ky = ky_rows()
    kx = kx_lanes()
    keep_y = jnp.where(jnp.abs(ky) <= cut_y.astype(f32), 1.0, 0.0).astype(f32)
    keep_x = jnp.where(kx <= cut_x.astype(f32), 1.0, 0.0).astype(f32)
    keep_xy = keep_y * keep_x
    square_xy = ky * ky + kx * kx
    lane = lax.broadcasted_iota(jnp.int32, (ROWS, LANES), 1)
    near_ref[extra] = jnp.zeros((ROWS, LANES), f32)
    far_ref[extra] = jnp.zeros((ROWS, LANES), f32)

    def kept_z(kz):
        return jnp.where(kz <= cut_z, 1.0, 0.0).astype(f32)

    def spectral_step(kzs):
        fields = [[], [], []]
        if chunk == 0:
            first_flux = [flux_ref[0, kz] for kz in kzs]
            second_flux = [flux_ref[1, kz] for kz in kzs]
        else:
            first_flux, second_flux = flux_modes(flux_ref, fy_ref, fyr_ref, kzs)
        for pair in range(0, len(kzs), 2):
            ks = kzs[pair : pair + 2]
            data = [
                jnp.concatenate(
                    [stacked(along_y(lines_ref, t, kz)) for kz in ks], 1
                )
                for t in (0, 1)
            ]
            even = lane_parts(folded(dot(fy_ref[...], data[0])))
            odd = lane_parts(folded(dot(fyr_ref[...], data[1])))
            for n, kz in enumerate(ks):
                flux = first_flux[pair + n]
                fields[0].append(jnp.where(lane < 64, odd[n], second_flux[pair + n]))
                fields[1].append(jnp.where(lane < 64, even[n], flux))
                fields[2].append(jnp.where(lane < 64, flux, even[n]))
        data = [beside(jnp.concatenate(field, 0)) for field in fields]
        modes = [folded_lanes(dot(data[max(n - 1, 0)], view(along_ref, n)[...])) for n in range(4)]
        results = [[], [], [], []]
        for n, kz in enumerate(kzs):
            kzf = kz.astype(f32)
            vx, slope, uy, uz = (mode[n * ROWS : (n + 1) * ROWS] for mode in modes)
            square = square_xy + kzf * kzf
            factor = keep_xy * kept_z(kz) / (1.0 + viscosity * time_step * square)
            share = (slope + ky * uy + kzf * uz) / jnp.where(square > 0, square, 1.0)
            results[0].append(factor * vx)
            results[1].append(factor * share)
            results[2].append(factor * (uy - ky * share))
            results[3].append(factor * (uz - kzf * share))
        got = [
            dot(
                beside(jnp.concatenate(result, 0)),
                along_ref[pl.ds(pl.multiple_of((4 + core * 4 + n) * 256, 256), 256), :],
            )
            for n, result in enumerate(results)
        ]
        got = [folded_lanes(part) for part in (got[0] + got[1], got[2], got[3])]
        for n, kz in enumerate(kzs):
            x, y, z = (part[n * ROWS : (n + 1) * ROWS] for part in got)
            near_ref[kz - first] = jnp.where(lane < 48, x, jnp.where(lane < 96, y, z))
            away = jnp.where(
                (lane >= 64) & (lane < 112), x, jnp.where((lane >= 32) & (lane < 64), z, y)
            )
            far_ref[kz - first] = pltpu.roll(away, 64, 1)
            shift = (kz - first) * 16
            near_ref[extra] += pltpu.roll(jnp.where(lane < 16, z, 0.0), shift, 1)
            rest = jnp.where((lane >= 64) & (lane < 80), z, 0.0)
            far_ref[extra] += pltpu.roll(rest, (shift + 64) % LANES, 1)

    over_planes(spectral_step, first, last)


def inverse_y(near_ref, far_ref, iy_ref, planes):
    count = near_ref.shape[0] - 1
    rest = near_ref[count] + far_ref[count]
    for kz in range(count):
        turned = pltpu.roll(rest, (LANES - kz * 16) % LANES, 1) if kz else rest
        data = jnp.concatenate([near_ref[kz] + far_ref[kz], turned], 1)
        got = lane_parts(folded(dot(iy_ref[...], stacked(padded(data)))))
        for tile in range(2):
            planes[tile, kz * LANES : (kz + 1) * LANES, :] = got[tile]
    if count < CHUNK:
        blank = jnp.zeros(((CHUNK - count) * LANES, LANES), f32)
        for tile in range(2):
            planes[tile, count * LANES :, :] = blank


def inverse_kernel(near_ref, far_ref, back_ref, planes):
    inverse_y(near_ref, far_ref, view(back_ref, 0), planes)


def final_kernel(
    near_ref, far_ref, planes_a, planes_b, state_hbm, base_hbm, back_ref, base_out, state_out,
    planes_c, state_ref, base_ref, state_gap, base_gap, arrived, left,
):
    wide = N * N // PIECES
    cuts = [pl.ds(n * wide, wide) for n in range(PIECES)]

    def copies(pairs, flags):
        return [
            [
                pltpu.make_async_copy(
                    source.at[:, :, cut], target.at[:, :, cut], flags.at[2 * n + k]
                )
                for k, (source, target) in enumerate(pairs)
            ]
            for n, cut in enumerate(cuts)
        ]

    reads = copies(((state_hbm, state_ref), (base_hbm, base_ref)), arrived)
    writes = copies(((state_gap, state_out), (base_gap, base_out)), left)
    for piece in reads:
        for copy in piece:
            copy.start()
    iy_ref, iz_ref, izr_ref = (view(back_ref, n) for n in (0, 4, 5))
    inverse_y(near_ref, far_ref, iy_ref, planes_c)

    def along_chunks(tile, yh):
        parts = [
            ref[tile, pl.ds(yh, 4 * CHUNK, stride=HALF), :]
            for ref in (planes_a, planes_b, planes_c)
        ]
        return padded(jnp.concatenate(parts, 0)).T

    many = HALF // PIECES
    for piece in range(PIECES):
        yhs = range(piece * many, (piece + 1) * many)
        data = [along_chunks(0, yh) for yh in yhs]
        rest = [along_chunks(1, yh)[:16] for yh in yhs]
        turned = beside(jnp.concatenate([one[:48] for one in data], 0))
        plain = beside(jnp.concatenate([one[48:] for one in data] + rest, 0))
        turned = folded_lanes(dot(turned, izr_ref[...]))
        plain = folded_lanes(dot(plain, iz_ref[...]))
        for copy in reads[piece]:
            copy.wait()
        for n, yh in enumerate(yhs):
            at = slice(yh * LANES, (yh + 1) * LANES)
            first = turned[48 * n : 48 * n + 48]
            second = plain[80 * n : 80 * n + 80]
            third = plain[80 * many + 16 * n :][:16]
            state_gap[0, :, at] = first[:32] - state_ref[0, :, at]
            state_gap[1, :, at] = second[16:48] - state_ref[1, :, at]
            state_gap[2, :, at] = second[48:80] - state_ref[2, :, at]
            base_gap[0, :, at] = first[32:48] - base_ref[0, :, at]
            base_gap[1, :, at] = second[:16] - base_ref[1, :, at]
            base_gap[2, :, at] = third - base_ref[2, :, at]
        for copy in writes[piece]:
            copy.start()
    for piece in writes:
        for copy in piece:
            copy.wait()


interpret = False


def call(kernel, outs, scratch, inputs, room, in_smem=0, in_hbm=(), out_hbm=False):
    whole = pl.BlockSpec(memory_space=pltpu.VMEM)
    small = pl.BlockSpec(memory_space=pltpu.SMEM)
    far = pl.BlockSpec(memory_space=pltpu.HBM)
    return pl.pallas_call(
        kernel,
        out_shape=outs,
        in_specs=[
            small if n < in_smem else far if n in in_hbm else whole for n in range(len(inputs))
        ],
        out_specs=jax.tree.map(lambda _: far if out_hbm else whole, outs),
        scratch_shapes=scratch,
        compiler_params=pltpu.CompilerParams(vmem_limit_bytes=room * 2**20),
        cost_estimate=pl.CostEstimate(flops=1000, bytes_accessed=1000, transcendentals=0),
        interpret=interpret,
    )(*inputs)


def body(base, state, wavenumber, cutoff):
    t = {name: jnp.asarray(value) for name, value in tables().items()}
    core = lax.axis_index("comp")
    seg_count = lax.axis_size("seg")
    own_base = base[0]
    own_state = state[0, 0]
    base_half = lax.dynamic_slice_in_dim(own_base, core * 16, 16, 1)
    back = [((s + 1) % seg_count, s) for s in range(seg_count)]
    around = [(2 * i, 2 * o) for i, o in back] + [(2 * o + 1, 2 * i + 1) for i, o in back]
    state_next = lax.ppermute(own_state, ("seg", "comp"), around)
    sds = jax.ShapeDtypeStruct
    core_at = core.reshape(1)
    swap = [(0, 1), (1, 0)]
    here_own = call(
        base_kernel,
        sds((SENT, ROWS, LANES), f32),
        [
            pltpu.VMEM((HALF * HALF_LINE, LANES), f32),
            pltpu.VMEM(own_base.shape, f32),
            pltpu.VMEM(t["ahead"].shape, bf16),
            pltpu.SemaphoreType.DMA((PIECES + 1,)),
        ],
        [core_at, own_base, t["ahead"]],
        room=56,
        in_smem=1,
        in_hbm=(1, 2),
    )
    there_own = lax.ppermute(here_own, "slab", swap)
    here_other = lax.ppermute(here_own, "comp", swap)
    counts = [planes_of(chunk)[1] - planes_of(chunk)[0] for chunk in range(CHUNKS)]
    flux_lines = sds((3, HALF * 4 * CHUNK, LANES), f32)
    flux = call(
        flux_kernel,
        [sds((2, counts[0], ROWS, LANES), f32)] + [flux_lines] * 2,
        [
            pltpu.VMEM(flux_lines.shape, f32),
            pltpu.VMEM(flux_lines.shape, f32),
            pltpu.VMEM(flux_lines.shape, f32),
            pltpu.VMEM(own_base.shape, f32),
            pltpu.VMEM(own_state.shape, f32),
            pltpu.VMEM(t["ahead"].shape, bf16),
            pltpu.VMEM((2, counts[0], ROWS, LANES), f32),
            pltpu.SemaphoreType.DMA((2 * PIECES + 1,)),
            pltpu.SemaphoreType.DMA((CHUNKS,)),
        ],
        [core_at, own_base, own_state, t["ahead"]],
        room=56,
        in_smem=1,
        in_hbm=(1, 2, 3),
        out_hbm=True,
    )
    there_own, flux = lax.optimization_barrier((there_own, flux))
    there_other = lax.ppermute(there_own, "comp", swap)
    half_planes = sds((3, (HALF_KZ + 1) * LANES, LANES), f32)
    own_planes = call(
        half_kernel,
        half_planes,
        [],
        [core_at, cutoff, here_own, there_own, t["back"]],
        room=12,
        in_smem=2,
    )
    lines = call(
        gradient_kernel,
        [sds((2, HALF * 4 * CHUNK, LANES), f32)] * CHUNKS,
        [pltpu.VMEM(half_planes.shape, f32), pltpu.VMEM((HALF, LANES), f32)],
        [core_at, cutoff, wavenumber, own_base, own_state, own_planes, here_other, there_other]
        + [t["ahead"], t["back"]],
        room=20,
        in_smem=3,
    )
    near, far = [], []
    lines = list(lines)
    for chunk in range(CHUNKS):
        if chunk:
            near[-1], lines[chunk] = lax.optimization_barrier((near[-1], lines[chunk]))
        near_part, far_part = call(
            functools.partial(spectral_kernel, chunk),
            [sds((counts[chunk] + 1, ROWS, LANES), f32)] * 2,
            [],
            [core_at, cutoff, lines[chunk], flux[chunk], t["ahead"], t["along"]],
            room=12,
            in_smem=2,
        )
        if chunk == 0:
            base_half, near_part = lax.optimization_barrier((base_half, near_part))
            base_next = lax.ppermute(base_half, "seg", back)
        near.append(near_part)
        far.append(lax.ppermute(far_part, "slab", swap))
    planes = sds((2, CHUNK * LANES, LANES), f32)
    planes_a = call(inverse_kernel, planes, [], [near[0], far[0], t["back"]], room=8)
    near[1], planes_a = lax.optimization_barrier((near[1], planes_a))
    planes_b = call(inverse_kernel, planes, [], [near[1], far[1], t["back"]], room=8)
    base_gap, state_gap = call(
        final_kernel,
        [sds(base_next.shape, f32), sds(state_next.shape, f32)],
        [
            pltpu.VMEM((2, CHUNK * LANES, LANES), f32),
            pltpu.VMEM(state_next.shape, f32),
            pltpu.VMEM(base_next.shape, f32),
            pltpu.VMEM(state_next.shape, f32),
            pltpu.VMEM(base_next.shape, f32),
            pltpu.SemaphoreType.DMA((2 * PIECES,)),
            pltpu.SemaphoreType.DMA((2 * PIECES,)),
        ],
        [near[2], far[2], planes_a, planes_b, state_next, base_next, t["back"]],
        room=16,
        in_hbm=(4, 5),
        out_hbm=True,
    )
    return base_gap[None], state_gap[None, None]


def solution(mesh):
    paired = mesh.shape["slab"] == 2 and mesh.shape["comp"] == 2
    return jax.shard_map(
        body if paired else general_body,
        mesh=mesh,
        in_specs=(
            P(("groups", "seg"), None, "slab", None),
            P(("groups", "seg"), "comp", None, "slab", None),
            P("groups"),
            P("groups"),
        ),
        out_specs=(
            P(("groups", "seg"), None, ("slab", "comp"), None),
            P(("groups", "seg"), "comp", None, "slab", None),
        ),
        check_vma=False,
    )
```

```python
import functools

import jax
import jax.numpy as jnp
import ml_dtypes
import numpy as np
from jax import lax
from jax.experimental import pallas as pl
from jax.experimental.pallas import tpu as pltpu
from jax.sharding import PartitionSpec as P

N = 64
HALF = 32
KEEP = N // 3
NKZ = KEEP + 1
NKY = 44
ROWS = 2 * NKY
CHUNK = 8
CHUNKS = 3
LINE = CHUNKS * CHUNK * 4
HALF_KZ = NKZ // 2
HALF_LINE = 4 * (HALF_KZ + 1)
SENT = 9
LANES = 128

viscosity = 0.025
time_step = 0.02
forcing_amp = 10.0

f32 = jnp.float32
bf16 = jnp.bfloat16


highest = lax.Precision.HIGHEST


def swapped(value, axis, apart):
    mask = 2**apart
    pairs = [(source, source ^ mask) for source in range(lax.axis_size(axis))]
    return lax.ppermute(value, axis, pairs)


def shifted(block, axis, distance):
    devices = range(lax.axis_size(axis))
    route = [((i - distance) % len(devices), i) for i in devices]
    return lax.ppermute(block, axis, route)


def wavenumbers(grid_points):
    position = jnp.arange(grid_points, dtype=jnp.int32)
    return jnp.where(position < grid_points // 2, position, position - grid_points)


def phases(first, second, grid_points):
    product = jnp.mod(first[:, None] * second[None, :], grid_points)
    return product.astype(jnp.float32) * (2.0 * jnp.pi / grid_points)


def combine(partial_value, columns):
    cosine_part = partial_value[0]
    sine_part = partial_value[1]
    real_part = cosine_part[..., :columns] - sine_part[..., columns:]
    imag_part = cosine_part[..., columns:] + sine_part[..., :columns]
    return jnp.concatenate([real_part, imag_part], axis=-1)


def times_unit(values, wave, columns):
    return jnp.concatenate([-wave * values[..., columns:], wave * values[..., :columns]], axis=-1)


def doubled(values):
    return jnp.concatenate([values, values], axis=-1)


def general_body(base, state, wavenumber, cutoff):
    grid_points = N
    base = base.reshape(base.shape[0], 3, base.shape[2], grid_points, grid_points)
    state = state.reshape(
        state.shape[0], state.shape[1], 3, state.shape[3], grid_points, grid_points
    )
    slab_rows = state.shape[3]
    half_rows = slab_rows // 2
    slab_count = lax.axis_size("slab")
    group_count = slab_count * lax.axis_size("comp")
    core_side = lax.axis_index("comp")
    block_number = lax.axis_index(("slab", "comp"))
    base_whole = base[0]
    base_half = lax.dynamic_slice_in_dim(base_whole, core_side * half_rows, half_rows, 1)
    own_state = state[0, 0]
    spectrum = wavenumbers(grid_points)
    one_third = grid_points // 3
    row_total = (2 * one_third + group_count) // group_count * group_count
    row_index = jnp.arange(row_total, dtype=jnp.int32)
    row_alive_mask = row_index <= 2 * one_third
    row_wave = jnp.where(row_index <= one_third, row_index, row_index - (2 * one_third + 1))
    row_wave = jnp.where(row_alive_mask, row_wave, 0)
    width = grid_points // 2
    rows_per_block = row_total // group_count
    alive_flags = row_alive_mask.astype(jnp.float32)
    grid_index = jnp.arange(grid_points, dtype=jnp.int32)
    column_index = grid_index[:width]
    angle_grid = phases(grid_index, grid_index, grid_points)
    angle_ahead = phases(grid_index, column_index, grid_points)
    angle_behind = phases(column_index, grid_index, grid_points)
    column_weight = jnp.where(column_index == 0, 1.0, 2.0).astype(jnp.float32)[:, None]
    forward_z = jnp.concatenate([jnp.cos(angle_ahead), -jnp.sin(angle_ahead)], axis=1)
    inverse_z = (
        jnp.concatenate(
            [jnp.cos(angle_behind) * column_weight, -jnp.sin(angle_behind) * column_weight], axis=0
        )
        / grid_points
    )
    phase_angle_rows = phases(row_wave, grid_index, grid_points)
    forward_transform_y = (
        jnp.stack([jnp.cos(phase_angle_rows), -jnp.sin(phase_angle_rows)])
        * alive_flags[None, :, None]
    )
    inverse_y = (
        jnp.stack([jnp.cos(phase_angle_rows).T, jnp.sin(phase_angle_rows).T])
        * alive_flags[None, None, :]
        / grid_points
    )
    forward_x = jnp.stack([jnp.cos(angle_grid), -jnp.sin(angle_grid)])
    inverse_x = jnp.stack([jnp.cos(angle_grid), jnp.sin(angle_grid)]) / grid_points
    table_ahead = forward_x.reshape(2, grid_points, slab_count, slab_rows)
    table_back = inverse_x.reshape(2, slab_count, slab_rows, grid_points)
    local_wave = lax.dynamic_slice_in_dim(row_wave, block_number * rows_per_block, rows_per_block)
    local_alive_mask = lax.dynamic_slice_in_dim(
        alive_flags, block_number * rows_per_block, rows_per_block
    )
    shape_local = (grid_points, rows_per_block, width)
    wave_x = jnp.broadcast_to(spectrum[:, None, None], shape_local)
    wave_y = jnp.broadcast_to(local_wave[None, :, None], shape_local)
    wave_z = jnp.broadcast_to(spectrum[:width][None, None, :], shape_local)
    inside = (
        (jnp.abs(wave_x) <= cutoff[0])
        & (jnp.abs(wave_y) <= cutoff[1])
        & (jnp.abs(wave_z) <= cutoff[2])
    )
    keep_mask = doubled(inside.astype(jnp.float32) * local_alive_mask[None, :, None])
    float_x = wave_x.astype(jnp.float32)
    float_y = wave_y.astype(jnp.float32)
    float_z = wave_z.astype(jnp.float32)
    ksquare = float_x * float_x + float_y * float_y + float_z * float_z
    safe_square = doubled(jnp.where(ksquare > 0, ksquare, jnp.ones_like(ksquare)))
    damping = doubled(1.0 / (1.0 + viscosity * time_step * ksquare))
    double_x = doubled(float_x)
    double_y = doubled(float_y)
    double_z = doubled(float_z)

    def project(field):
        divergence = (double_x * field[0] + double_y * field[1] + double_z * field[2]) / safe_square
        return jnp.stack(
            [
                field[0] - double_x * divergence,
                field[1] - double_y * divergence,
                field[2] - double_z * divergence,
            ]
        )

    def yz_forward(field):
        along_z = jnp.einsum("...z,zk->...k", field, forward_z, precision=highest)
        partial_value = jnp.einsum(
            "sry,...yk->s...rk", forward_transform_y, along_z, precision=highest
        )
        return combine(partial_value, width)

    def yz_inverse(modes):
        partial_value = jnp.einsum("syr,...rk->s...yk", inverse_y, modes, precision=highest)
        return jnp.einsum(
            "...k,kz->...z", combine(partial_value, width), inverse_z, precision=highest
        )

    def spectral(state_fields, base_fields):
        state_modes = yz_forward(state_fields)[:, :, None]
        base_modes = yz_forward(base_fields)[:, :, None]
        state_got = lax.all_to_all(
            state_modes, ("slab", "comp"), split_axis=4, concat_axis=2, tiled=True
        )
        base_got = lax.all_to_all(
            base_modes, ("slab", "comp"), split_axis=4, concat_axis=2, tiled=True
        )
        item_count = state_got.shape[0]
        part_count = state_got.shape[1]
        state_split = state_got.reshape(
            item_count, part_count, slab_count, 2, slab_rows, rows_per_block, 2 * width
        )
        state_partial = jnp.einsum(
            "srpx,ijpcxyk->sijcryk", table_ahead, state_split, precision=highest
        )
        base_lined = base_got.reshape(item_count, 1, grid_points, rows_per_block, 2 * width)
        base_partial = jnp.einsum("srx,ijxyk->sijryk", forward_x, base_lined, precision=highest)
        return (combine(state_partial, width), combine(base_partial, width))

    state_first, base_first = spectral(own_state[:, None], base_half[:, None])
    state_hat = state_first[:, 0] * keep_mask
    base_hat = base_first[:, 0] * keep_mask
    grad_hat = jnp.stack(
        [
            times_unit(base_hat, float_x, width),
            times_unit(base_hat, float_y, width),
            times_unit(base_hat, float_z, width),
        ],
        axis=1,
    )
    grad_hat = grad_hat.reshape(9, grid_points, rows_per_block, 2 * width)
    grad_partial = jnp.einsum("sxr,iryk->sixyk", inverse_x, grad_hat, precision=highest)
    grad_spread = combine(grad_partial, width).reshape(
        9, group_count, half_rows, rows_per_block, 2 * width
    )
    own_rows = yz_inverse(
        lax.all_to_all(grad_spread, ("slab", "comp"), split_axis=1, concat_axis=3, tiled=True)[:, 0]
    )
    other_rows = swapped(own_rows, "comp", 0)
    gradient = jnp.where(
        core_side == 0,
        jnp.concatenate([own_rows, other_rows], axis=1),
        jnp.concatenate([other_rows, own_rows], axis=1),
    )
    gradient = gradient.reshape(3, 3, slab_rows, grid_points, grid_points)
    gradient_half = lax.dynamic_slice_in_dim(gradient, core_side * half_rows, half_rows, 2)
    flux_terms = own_state[:, None] * base_whole[None, :]
    coupling_matrix = jnp.where(core_side == 0, gradient, jnp.swapaxes(gradient, 0, 1))
    coupling = jnp.sum(coupling_matrix * own_state[None, :], axis=1)
    forcing_phase = phases(wavenumber, grid_index, grid_points)[0]
    forcing = forcing_amp * jnp.sin(forcing_phase)[None, :, None]
    base_drive = jnp.sum(gradient_half * base_half[None, :], axis=1)
    base_drive = jnp.concatenate([base_drive[:1] - forcing[None], base_drive[1:]], axis=0)
    state_fields = jnp.concatenate([flux_terms, coupling[:, None]], axis=1)
    drive_modes, base_modes_two = spectral(state_fields, base_drive[:, None])
    orient = jnp.array([1.0, -1.0], dtype=jnp.float32)[None, :, None, None, None]
    divergence = (
        times_unit(drive_modes[:, 0], float_x, width)
        + times_unit(drive_modes[:, 1], float_y, width)
        + times_unit(drive_modes[:, 2], float_z, width)
    )
    state_drive = keep_mask * (orient * divergence + drive_modes[:, 3])
    new_hat = damping * project(state_hat - time_step * state_drive)
    base_new_hat = damping * project(base_hat - time_step * keep_mask * base_modes_two[:, 0])
    state_partial = jnp.einsum("spxr,icryk->sipcxyk", table_back, new_hat, precision=highest)
    state_back = combine(state_partial, width).reshape(
        3, group_count, slab_rows, rows_per_block, 2 * width
    )
    base_partial = jnp.einsum("sxr,iryk->sixyk", inverse_x, base_new_hat, precision=highest)
    base_back = combine(base_partial, width).reshape(
        3, group_count, half_rows, rows_per_block, 2 * width
    )
    state_got = lax.all_to_all(
        state_back, ("slab", "comp"), split_axis=1, concat_axis=3, tiled=True
    )
    base_got = lax.all_to_all(base_back, ("slab", "comp"), split_axis=1, concat_axis=3, tiled=True)
    state_new = yz_inverse(state_got[:, 0])
    base_new = yz_inverse(base_got[:, 0])
    base_later, later_state = shifted((base_half, own_state), "seg", -1)
    prior_state = shifted(own_state, "seg", 1)
    neighbour = jnp.where(core_side == 0, later_state, prior_state)
    base_gap = (base_new - base_later).reshape(1, 3, half_rows, grid_points * grid_points)
    state_gap = (state_new - neighbour).reshape(1, 1, 3, slab_rows, grid_points * grid_points)
    return (base_gap, state_gap)


def halves(table):
    high = table.astype(np.float32).astype(ml_dtypes.bfloat16)
    low = (table - high.astype(np.float64)).astype(ml_dtypes.bfloat16)
    return high, low


def left_table(table, depth):
    padded = np.zeros((table.shape[0], depth))
    padded[:, : table.shape[1]] = table
    high, low = halves(padded)
    return np.concatenate(
        [np.concatenate([high, high], 1), np.concatenate([low, np.zeros_like(low)], 1)], 0
    )


def right_table(table, depth):
    return np.ascontiguousarray(left_table(table.T, depth).T)


def planes_of(chunk):
    return chunk * CHUNK, min((chunk + 1) * CHUNK, NKZ)


def ky_values():
    index = np.arange(NKY)
    wave = np.where(index <= KEEP, index, index - (2 * KEEP + 1))
    alive = (index <= 2 * KEEP).astype(np.float64)
    return wave * alive, alive


@functools.cache
def tables():
    out = {}
    z = np.arange(N)
    kz = np.arange(NKZ)
    angle = 2 * np.pi * kz[:, None] * z[None, :] / N
    weight = np.where(kz == 0, 1.0, 2.0)[:, None] / N
    forward = np.zeros((2, 2, CHUNKS * CHUNK, 2, N))
    inverse = np.zeros((NKZ, 2, 2, 2, N))
    turned = np.zeros((NKZ, 2, 2, 2, N))
    slope = np.zeros((NKZ, 2, 2, 2, N))
    for y2 in range(2):
        forward[y2, 0, :NKZ, y2] = np.cos(angle)
        forward[y2, 1, :NKZ, y2] = -np.sin(angle)
        inverse[:, y2, 0, y2] = weight * np.cos(angle)
        inverse[:, y2, 1, y2] = -weight * np.sin(angle)
        turned[:, y2, 0, y2] = weight * np.sin(angle)
        turned[:, y2, 1, y2] = weight * np.cos(angle)
        slope[:, y2, 0, y2] = -weight * kz[:, None] * np.sin(angle)
        slope[:, y2, 1, y2] = -weight * kz[:, None] * np.cos(angle)
    forward = np.moveaxis(forward.reshape(4, CHUNKS, CHUNK, 2 * N), 1, 0)
    out["fz"] = left_table(forward.reshape(LINE, 2 * N), 128)
    by_kz = np.moveaxis(forward.reshape(CHUNKS, 4, CHUNK, 2 * N), 1, 0).reshape(4, -1, 2 * N)
    halved = []
    for core in range(2):
        wide = np.zeros((4, HALF_KZ + 1, 2 * N))
        wide[:, :HALF_KZ] = by_kz[:, core * HALF_KZ : (core + 1) * HALF_KZ]
        halved.append(left_table(wide.reshape(HALF_LINE, 2 * N), 128))
    out["fzh"] = np.concatenate(halved, 0)

    def by_chunk(table):
        wide = np.zeros((CHUNKS, CHUNK, 4, 2 * N))
        for chunk in range(CHUNKS):
            first, last = planes_of(chunk)
            wide[chunk, : last - first] = table.reshape(NKZ, 4, 2 * N)[first:last]
        return right_table(wide.reshape(LINE, 2 * N), 128)

    out["iz"] = by_chunk(inverse)
    out["izr"] = by_chunk(turned)

    def last_pair(table):
        first, last = planes_of(CHUNKS - 1)
        depth = 4 * CHUNK
        wide = np.zeros((depth, 2 * N))
        wide[: 4 * (last - first)] = table.reshape(NKZ, 4, 2 * N)[first:last].reshape(-1, 2 * N)
        both = np.zeros((2, 2, 2 * depth, 4 * N), ml_dtypes.bfloat16)
        both[0, 0] = both[1, 1] = right_table(wide, depth)
        return both.reshape(2 * LANES, 256)

    out["izc"] = np.concatenate([last_pair(inverse), last_pair(turned)], 0)

    def by_half(table):
        wide = np.zeros((2, HALF_KZ + 1, 4, 2 * N))
        wide[:, :HALF_KZ] = table.reshape(2, HALF_KZ, 4, 2 * N)
        return right_table(wide.reshape(8 * HALF_KZ + 8, 2 * N), 128)

    out["izg"] = by_half(inverse)
    out["izd"] = by_half(slope)
    ky, alive = ky_values()
    y = 2 * np.arange(HALF)[None, :] + np.arange(2)[:, None]
    phase = 2 * np.pi * ky[:, None, None] * y[None] / N
    cosine = np.cos(phase) * alive[:, None, None]
    sine = np.sin(phase) * alive[:, None, None]
    plain = np.zeros((2, NKY, 2, 2, HALF))
    plain[0, :, :, 0] = cosine
    plain[0, :, :, 1] = sine
    plain[1, :, :, 0] = -sine
    plain[1, :, :, 1] = cosine
    rotated = np.stack([-plain[1], plain[0]])
    out["fy"] = left_table(plain.reshape(ROWS, 128), 128)
    out["fyr"] = left_table(rotated.reshape(ROWS, 128), 128)
    back = np.zeros((2, 2, HALF, 2, NKY))
    cos_t = np.moveaxis(cosine, 0, -1) / N
    sin_t = np.moveaxis(sine, 0, -1) / N
    back[:, 0, :, 0] = cos_t
    back[:, 0, :, 1] = -sin_t
    back[:, 1, :, 0] = sin_t
    back[:, 1, :, 1] = cos_t
    back_slope = np.zeros_like(back)
    back_slope[..., 0, :] = ky * back[..., 1, :]
    back_slope[..., 1, :] = -ky * back[..., 0, :]
    out["iy"] = left_table(back.reshape(128, ROWS), 128)
    out["iyd"] = left_table(back_slope.reshape(128, ROWS), 128)
    grad_high, grad_low = [], []
    x = np.arange(N)
    apart = x[:HALF, None] - x[None, :]
    for cut in range(KEEP - 3, KEEP + 1):
        k = np.arange(cut + 1)
        wk = np.where(k == 0, 1.0, 2.0) / N
        arg = 2 * np.pi * apart[..., None] * k / N
        keep = (np.cos(arg) * wk).sum(-1)
        derive = (-np.sin(arg) * wk * k).sum(-1)
        table = np.zeros((2, 4, HALF, 2, 4, HALF))
        for comp in range(3):
            for side in range(2):
                rows = slice(side * HALF, (side + 1) * HALF)
                table[side, comp, :, 0, comp, :] = keep[:, rows].T
                table[side, comp, :, 1, comp, :] = derive[:, rows].T
        high, low = halves(table.reshape(256, 256))
        grad_high.append(high)
        grad_low.append(low)
    out["gxh"] = np.stack(grad_high)
    out["gxl"] = np.stack(grad_low)
    kx = np.arange(HALF)
    live = (kx <= KEEP).astype(np.float64)
    xl = np.arange(HALF)
    arg = 2 * np.pi * xl[:, None] * kx[None, :] / N
    value = np.concatenate([np.cos(arg) * live, np.sin(arg) * live], 1)
    change = np.concatenate([kx * np.sin(arg) * live, -kx * np.cos(arg) * live], 1)

    def coefficients(blocks):
        table = np.zeros((4, HALF, 2, 2 * HALF))
        for block, part, what in blocks:
            table[block, :, part] = what
        return table.reshape(LANES, LANES)

    first = coefficients([(0, 0, value), (1, 1, value), (2, 0, change), (3, 0, value)])
    last = coefficients([(0, 0, change), (1, 0, value), (2, 0, value), (3, 1, value)])
    fall = first.reshape(LANES, 2, 2, HALF)
    fall = np.stack([-kx * fall[:, :, 1], kx * fall[:, :, 0]], 2).reshape(LANES, LANES)
    out["fx"] = np.stack([right_table(part, 128) for part in (first, fall, first, last)])
    wx = np.where(kx == 0, 1.0, 2.0) * live / N
    for core in range(2):
        ix = np.zeros((4, 2, 2 * HALF, LANES))
        for side in range(2):
            xs = np.arange(HALF) + side * HALF
            arg = 2 * np.pi * kx[:, None] * xs[None, :] / N
            give = np.concatenate([np.cos(arg) * wx[:, None], np.sin(arg) * wx[:, None]], 0)
            drop = np.concatenate(
                [np.sin(arg) * (wx * kx)[:, None], -np.cos(arg) * (wx * kx)[:, None]], 0
            )
            own = slice(core * 16, core * 16 + 16)

            def put(quantity, part, lane, what):
                at = (lane + side * 64 + np.arange(what.shape[1])) % LANES
                ix[quantity, part][:, at] = what

            put(0, 0, 0, give)
            put(1, 0, 0, drop)
            put(0, 1, 32, give[:, own])
            put(1, 1, 32, drop[:, own])
            put(2, 1, 48, give[:, own])
            put(2, 0, 64, give)
            put(3, 0, 96, give)
            put(3, 1, 0, give[:, own])
        out["ix%d" % core] = np.stack(
            [right_table(part, 128) for part in ix.reshape(4, LANES, LANES)]
        )
    out["ix"] = np.stack([out.pop("ix0"), out.pop("ix1")])
    merged = {}
    merged["ahead"] = np.concatenate([out["fz"], out["fy"], out["fyr"], out["fzh"]], 0)
    gx = [out["gxh"].reshape(-1, 256), out["gxl"].reshape(-1, 256)]
    square = [out[name] for name in ("iy", "iyd", "izg", "izd", "iz", "izr")]
    merged["back"] = np.concatenate(square + gx, 0)
    merged["last"] = out["izc"]
    merged["along"] = np.concatenate([out["fx"].reshape(-1, 256), out["ix"].reshape(-1, 256)], 0)
    return merged


def view(ref, index, rows=256, start=0):
    return ref.at[pl.ds(start + index * rows, rows), :]


def ahead_tables(ref):
    return (
        view(ref, 0, 2 * LINE),
        view(ref, 0, 2 * ROWS, 2 * LINE),
        view(ref, 1, 2 * ROWS, 2 * LINE),
    )


def ky_rows():
    row = lax.broadcasted_iota(jnp.int32, (ROWS, LANES), 0)
    index = jnp.where(row < NKY, row, row - NKY)
    wave = jnp.where(index <= KEEP, index, index - (2 * KEEP + 1))
    return jnp.where(index <= 2 * KEEP, wave, 0).astype(f32)


def kx_lanes():
    lane = lax.broadcasted_iota(jnp.int32, (1, LANES), 1) % HALF
    return jnp.where(lane <= KEEP, lane, 0).astype(f32)


def split(values):
    high = values.astype(bf16)
    low = (values - high.astype(f32)).astype(bf16)
    return high, low


def dot(a, b):
    return jnp.dot(a, b, preferred_element_type=f32)


def dot_nt(a, b):
    return lax.dot_general(a, b, (((1,), (1,)), ((), ())), preferred_element_type=f32)


def stacked(values):
    high, low = split(values)
    return jnp.concatenate([high, low], 0)


def beside(values):
    high, low = split(values)
    return jnp.concatenate([high, low], 1)


def folded(result):
    rows = result.shape[0] // 2
    return result[:rows] + result[rows:]


def folded_lanes(result):
    return result[:, :LANES] + result[:, LANES:]


def padded(values, rows=128):
    return jnp.concatenate([values, jnp.zeros((rows - values.shape[0], values.shape[1]), f32)], 0)


def triple(values, high_ref, low_ref):
    high, low = split(values)
    return dot(high, high_ref) + dot(low, high_ref) + dot(high, low_ref)


def columns(yh):
    return pl.ds(pl.multiple_of(yh * LANES, LANES), LANES)


def along_y(ref, tile, kz):
    at = kz % CHUNK
    return jnp.concatenate(
        [ref[tile, pl.ds(q * CHUNK + at, HALF, stride=4 * CHUNK), :] for q in range(4)], 0
    )


def line_rows(yh):
    return pl.ds(pl.multiple_of(yh * LINE, 8), LINE)


def lane_parts(values):
    return [values[:, at : at + LANES] for at in range(0, values.shape[1], LANES)]


def over_planes(step, first=0, last=NKZ):
    def four(index, _):
        step([first + index * 4 + k for k in range(4)])
        return 0

    count = (last - first) // 4
    lax.fori_loop(0, count, four, 0)
    if first + count * 4 < last:
        step([jnp.int32(kz) for kz in range(first + count * 4, last)])


def over_lines(step, many, first=0, last=HALF):
    def some(index, _):
        step([first + index * many + k for k in range(many)])
        return 0

    lax.fori_loop(0, (last - first) // many, some, 0)


PIECES = 4


def base_kernel(core_ref, base_hbm, ahead_hbm, out_ref, lines, base_ref, ahead_ref, arrived):
    nothing = jnp.zeros((HALF, LANES), f32)
    wide = N * N // PIECES
    table = pltpu.make_async_copy(ahead_hbm, ahead_ref, arrived.at[PIECES])
    pieces = [
        pltpu.make_async_copy(
            base_hbm.at[:, :, pl.ds(n * wide, wide)],
            base_ref.at[:, :, pl.ds(n * wide, wide)],
            arrived.at[n],
        )
        for n in range(PIECES)
    ]
    pieces[0].start()
    table.start()
    for piece in pieces[1:]:
        piece.start()
    fy_ref = ahead_tables(ahead_ref)[1]
    table.wait()
    first = 2 * LINE + 4 * ROWS + core_ref[0] * 2 * HALF_LINE
    fz = ahead_ref[pl.ds(pl.multiple_of(first, 32), 2 * HALF_LINE), :]
    many = HALF // PIECES
    for n, piece in enumerate(pieces):
        piece.wait()
        yhs = range(n * many, (n + 1) * many)
        rows = []
        for yh in yhs:
            at = slice(yh * LANES, (yh + 1) * LANES)
            rows += [base_ref[i, :, at] for i in range(3)] + [nothing]
        got = folded(dot_nt(fz, beside(jnp.concatenate(rows, 0))))
        for yh, part in zip(yhs, lane_parts(got)):
            lines[yh * HALF_LINE : (yh + 1) * HALF_LINE, :] = part
    planes = []
    for pair in range(0, HALF_KZ, 2):
        ks = range(pair, min(pair + 2, HALF_KZ))
        data = []
        for k in ks:
            starts = [q * (HALF_KZ + 1) + k for q in range(4)]
            picked = [lines[pl.ds(at, HALF, stride=HALF_LINE), :] for at in starts]
            data.append(stacked(jnp.concatenate(picked, 0)))
        data = jnp.concatenate(data, 1)
        planes += lane_parts(folded(dot(fy_ref[...], data)))
    lane = lax.broadcasted_iota(jnp.int32, (ROWS, LANES), 1)
    for k in range(SENT):
        part = planes[k]
        if k < 3 * (HALF_KZ - SENT):
            guest = pltpu.roll(planes[SENT + k // 3], (3 - k % 3) * HALF, 1)
            part = jnp.where(lane < 96, part, guest)
        out_ref[k] = part


def received(ref, k):
    if k < SENT:
        return ref[k]
    lane = lax.broadcasted_iota(jnp.int32, (ROWS, LANES), 1)
    blocks = [
        pltpu.roll(ref[3 * (k - SENT) + j], LANES - (3 - j) * HALF, 1) for j in range(3)
    ]
    return jnp.where(lane < 32, blocks[0], jnp.where(lane < 64, blocks[1], blocks[2]))


def flux_modes(lines_ref, fy_ref, fyr_ref, kzs):
    ky = ky_rows()
    lane = lax.broadcasted_iota(jnp.int32, (ROWS, LANES), 1)
    odd_block = (lane // HALF) % 2 == 1
    even = []
    for pair in range(0, len(kzs), 2):
        data = [stacked(along_y(lines_ref, 0, kz)) for kz in kzs[pair : pair + 2]]
        even += lane_parts(folded(dot(fy_ref[...], jnp.concatenate(data, 1))))
    odd = []
    for kz in kzs:
        data = [stacked(along_y(lines_ref, tile, kz)) for tile in (1, 2)]
        odd.append(lane_parts(folded(dot(fyr_ref[...], jnp.concatenate(data, 1)))))
    first, second = [], []
    for n, kz in enumerate(kzs):
        kzf = kz.astype(f32)
        plain = even[n]
        slopes = odd[n][0] * jnp.where(odd_block, kzf, ky)
        slopes = slopes + pltpu.roll(slopes, 32, 1)
        first.append(jnp.where(odd_block, slopes, plain))
        other = plain * jnp.where(lane >= 96, -kzf, -ky)
        other = other + pltpu.roll(other, 64, 1)
        second.append(jnp.where(lane >= 96, other, jnp.where(lane >= 64, odd[n][1], 0.0)))
    return first, second


def flux_kernel(
    core_ref, base_hbm, state_hbm, ahead_hbm, out_ref, out_b, out_c,
    lines_a, lines_b, lines_c, base_ref, state_ref, ahead_ref, result, arrived, left,
):
    wide = N * N // PIECES
    pieces = [pltpu.make_async_copy(ahead_hbm, ahead_ref, arrived.at[2 * PIECES])]
    for n in range(PIECES):
        for k, (source, target) in enumerate(((base_hbm, base_ref), (state_hbm, state_ref))):
            at = pl.ds(n * wide, wide)
            pieces.append(
                pltpu.make_async_copy(
                    source.at[:, :, at], target.at[:, :, at], arrived.at[2 * n + k]
                )
            )
    for piece in pieces:
        piece.start()
    fz_ref, fy_ref, fyr_ref = ahead_tables(ahead_ref)
    sigma = jnp.where(core_ref[0] == 0, -time_step, time_step).astype(f32)
    depth = LINE // CHUNKS

    def z_step(yhs):
        rows, lone = [], []
        for yh in yhs:
            b = [base_ref[i, :, columns(yh)] for i in range(3)]
            t = [sigma * state_ref[i, :, columns(yh)] for i in range(3)]
            rows += [t[2] * b[0], t[0] * b[1], t[1] * b[0], t[0] * b[2]]
            rows += [t[2] * b[1], t[2] * b[2], t[1] * b[1], t[1] * b[2]]
            lone.append(t[0] * b[0])
        got = lane_parts(folded(dot_nt(fz_ref[...], beside(jnp.concatenate(rows + lone, 0)))))
        for n, yh in enumerate(yhs):
            third = got[-1] if n == 2 else pltpu.roll(got[-1], (2 - n) % 4 * HALF, 1)
            at = pl.ds(pl.multiple_of(yh * depth, 8), depth)
            for tile, part in enumerate((got[2 * n], got[2 * n + 1], third)):
                for chunk, lines in enumerate((lines_a, lines_b, lines_c)):
                    lines[tile, at, :] = part[chunk * depth : (chunk + 1) * depth]

    pieces[0].wait()
    for n in range(PIECES):
        pieces[2 * n + 1].wait()
        pieces[2 * n + 2].wait()
        over_lines(z_step, 4, n * HALF // PIECES, (n + 1) * HALF // PIECES)
    sends = [
        pltpu.make_async_copy(lines_b, out_b, left.at[1]),
        pltpu.make_async_copy(lines_c, out_c, left.at[2]),
        pltpu.make_async_copy(result, out_ref, left.at[0]),
    ]
    sends[0].start()
    sends[1].start()

    def y_step(kzs):
        first, second = flux_modes(lines_a, fy_ref, fyr_ref, kzs)
        for n, kz in enumerate(kzs):
            result[0, kz] = first[n]
            result[1, kz] = second[n]

    over_planes(y_step, *planes_of(0))
    sends[2].start()
    for send in sends:
        send.wait()


def gradient_planes(cutoff_ref, here_ref, there_ref, back_ref, planes, start):
    cut_x, cut_y, cut_z = (cutoff_ref[i] for i in range(3))
    which = jnp.clip(cut_x - (KEEP - 3), 0, 3)
    keep_y = jnp.where(jnp.abs(ky_rows()) <= cut_y.astype(f32), 1.0, 0.0).astype(f32)
    tall_ref = view(back_ref, 0, 512)
    for d in range(3):
        planes[d, HALF_KZ * LANES :, :] = jnp.zeros((LANES, LANES), f32)
    for first in range(0, HALF_KZ, 4):
        kzs = range(first, min(first + 4, HALF_KZ))
        rows = []
        for kz in kzs:
            keep = keep_y * jnp.where(start + kz <= cut_z, 1.0, 0.0).astype(f32)
            rows.append(
                jnp.concatenate([received(ref, kz) * keep for ref in (here_ref, there_ref)], 1)
            )
        high = back_ref[pl.ds(pl.multiple_of((6 + which) * 256, 256), 256), :]
        low = back_ref[pl.ds(pl.multiple_of((10 + which) * 256, 256), 256), :]
        got = triple(jnp.concatenate(rows, 0), high, low)
        data = [stacked(padded(got[n * ROWS : (n + 1) * ROWS])) for n in range(len(kzs))]
        for n in range(0, len(kzs), 2):
            pair = list(enumerate(kzs))[n : n + 2]
            value = jnp.concatenate([data[k][:, :LANES] for k, _ in pair], 1)
            slope = jnp.concatenate([data[k][:, LANES:] for k, _ in pair], 1)
            both = dot(tall_ref[...], value)
            parts = [lane_parts(folded(dot(tall_ref[:256, :], slope)))]
            parts += [lane_parts(folded(both[256:])), lane_parts(folded(both[:256]))]
            for d in range(3):
                for k, (_, kz) in enumerate(pair):
                    planes[d, kz * LANES : (kz + 1) * LANES, :] = parts[d][k]


def half_kernel(core_ref, cutoff_ref, here_ref, there_ref, back_ref, planes):
    start = core_ref[0] * HALF_KZ
    gradient_planes(cutoff_ref, here_ref, there_ref, back_ref, planes, start)


def gradient_kernel(
    core_ref, cutoff_ref, wave_ref, base_ref, state_ref, own_ref, here_ref, there_ref,
    ahead_ref, back_ref, *refs
):
    *out_refs, planes, force_ref = refs
    core = core_ref[0]
    start = (1 - core) * HALF_KZ
    gradient_planes(cutoff_ref, here_ref, there_ref, back_ref, planes, start)
    fz_ref = ahead_tables(ahead_ref)[0]
    iz_ref, izd_ref = view(back_ref, 2), view(back_ref, 3)
    y = lax.broadcasted_iota(jnp.int32, (HALF, LANES), 0) * 2
    y = y + lax.broadcasted_iota(jnp.int32, (HALF, LANES), 1) // N
    phase = ((wave_ref[0] * y) % N).astype(f32) * (2.0 * np.pi / N)
    force_ref[...] = forcing_amp * jnp.sin(phase)
    nothing = jnp.zeros((HALF, LANES), f32)

    def along_halves(d, yh):
        at = pl.ds(yh, 4 * (HALF_KZ + 1), stride=HALF)
        own, other = own_ref[d, at, :], planes[d, at, :]
        low = jnp.where(core == 0, own, other)
        high = jnp.where(core == 0, other, own)
        return padded(jnp.concatenate([low, high], 0)).T

    def physical_step(yhs):
        count = len(yhs)
        flat = [along_halves(d, yh)[:96] for d in range(2) for yh in yhs]
        steep = [along_halves(2, yh)[:96] for yh in yhs]
        flat = folded_lanes(dot(beside(jnp.concatenate(flat, 0)), iz_ref[...]))
        steep = folded_lanes(dot(beside(jnp.concatenate(steep, 0)), izd_ref[...]))
        for n, yh in enumerate(yhs):
            sets = [flat[96 * n :], flat[96 * (count + n) :], steep[96 * n :]]
            grads = [[one[HALF * i : HALF * (i + 1)] for i in range(3)] for one in sets]
            b = [base_ref[i, :, columns(yh)] for i in range(3)]
            s = [state_ref[i, :, columns(yh)] for i in range(3)]
            comb, comb_base = [], []
            for i in range(3):
                coupling = sum(
                    jnp.where(core == 0, grads[j][i], grads[i][j]) * s[j] for j in range(3)
                )
                comb.append(s[i] - time_step * coupling)
                drive = sum(grads[j][i] * b[j] for j in range(3))
                if i == 0:
                    drive = drive - force_ref[pl.ds(yh, 1), :]
                comb_base.append(b[i] - time_step * drive)
            rows = [comb[1], comb_base[1], comb[2], comb_base[2]]
            rows += [comb[0], comb_base[0], nothing, nothing]
            got = folded(dot_nt(fz_ref[...], beside(jnp.concatenate(rows, 0))))
            depth = LINE // CHUNKS
            at = pl.ds(pl.multiple_of(yh * depth, 8), depth)
            for tile, part in enumerate(lane_parts(got)):
                for chunk in range(CHUNKS):
                    out_refs[chunk][tile, at, :] = part[chunk * depth : (chunk + 1) * depth]

    over_lines(physical_step, 8)


def spectral_kernel(
    chunk, core_ref, cutoff_ref, lines_ref, flux_ref,
    ahead_ref, along_ref, near_ref, far_ref,
):
    _, fy_ref, fyr_ref = ahead_tables(ahead_ref)
    core = core_ref[0]
    cut_x, cut_y, cut_z = (cutoff_ref[i] for i in range(3))
    first, last = planes_of(chunk)
    extra = last - first
    ky = ky_rows()
    kx = kx_lanes()
    keep_y = jnp.where(jnp.abs(ky) <= cut_y.astype(f32), 1.0, 0.0).astype(f32)
    keep_x = jnp.where(kx <= cut_x.astype(f32), 1.0, 0.0).astype(f32)
    keep_xy = keep_y * keep_x
    square_xy = ky * ky + kx * kx
    lane = lax.broadcasted_iota(jnp.int32, (ROWS, LANES), 1)
    near_ref[extra] = jnp.zeros((ROWS, LANES), f32)
    far_ref[extra] = jnp.zeros((ROWS, LANES), f32)

    def kept_z(kz):
        return jnp.where(kz <= cut_z, 1.0, 0.0).astype(f32)

    def spectral_step(kzs):
        fields = [[], [], []]
        if chunk == 0:
            first_flux = [flux_ref[0, kz] for kz in kzs]
            second_flux = [flux_ref[1, kz] for kz in kzs]
        else:
            first_flux, second_flux = flux_modes(flux_ref, fy_ref, fyr_ref, kzs)
        for pair in range(0, len(kzs), 2):
            ks = kzs[pair : pair + 2]
            data = [
                jnp.concatenate(
                    [stacked(along_y(lines_ref, t, kz)) for kz in ks], 1
                )
                for t in (0, 1)
            ]
            even = lane_parts(folded(dot(fy_ref[...], data[0])))
            odd = lane_parts(folded(dot(fyr_ref[...], data[1])))
            for n, kz in enumerate(ks):
                flux = first_flux[pair + n]
                fields[0].append(jnp.where(lane < 64, odd[n], second_flux[pair + n]))
                fields[1].append(jnp.where(lane < 64, even[n], flux))
                fields[2].append(jnp.where(lane < 64, flux, even[n]))
        data = [beside(jnp.concatenate(field, 0)) for field in fields]
        modes = [folded_lanes(dot(data[max(n - 1, 0)], view(along_ref, n)[...])) for n in range(4)]
        results = [[], [], [], []]
        for n, kz in enumerate(kzs):
            kzf = kz.astype(f32)
            vx, slope, uy, uz = (mode[n * ROWS : (n + 1) * ROWS] for mode in modes)
            square = square_xy + kzf * kzf
            factor = keep_xy * kept_z(kz) / (1.0 + viscosity * time_step * square)
            share = (slope + ky * uy + kzf * uz) / jnp.where(square > 0, square, 1.0)
            results[0].append(factor * vx)
            results[1].append(factor * share)
            results[2].append(factor * (uy - ky * share))
            results[3].append(factor * (uz - kzf * share))
        got = [
            dot(
                beside(jnp.concatenate(result, 0)),
                along_ref[pl.ds(pl.multiple_of((4 + core * 4 + n) * 256, 256), 256), :],
            )
            for n, result in enumerate(results)
        ]
        got = [folded_lanes(part) for part in (got[0] + got[1], got[2], got[3])]
        for n, kz in enumerate(kzs):
            x, y, z = (part[n * ROWS : (n + 1) * ROWS] for part in got)
            near_ref[kz - first] = jnp.where(lane < 48, x, jnp.where(lane < 96, y, z))
            away = jnp.where(
                (lane >= 64) & (lane < 112), x, jnp.where((lane >= 32) & (lane < 64), z, y)
            )
            far_ref[kz - first] = pltpu.roll(away, 64, 1)
            shift = (kz - first) * 16
            near_ref[extra] += pltpu.roll(jnp.where(lane < 16, z, 0.0), shift, 1)
            rest = jnp.where((lane >= 64) & (lane < 80), z, 0.0)
            far_ref[extra] += pltpu.roll(rest, (shift + 64) % LANES, 1)

    over_planes(spectral_step, first, last)


def inverse_y(near_ref, far_ref, iy_ref, planes):
    count = near_ref.shape[0] - 1
    rest = near_ref[count] + far_ref[count]
    for kz in range(count):
        turned = pltpu.roll(rest, (LANES - kz * 16) % LANES, 1) if kz else rest
        data = jnp.concatenate([near_ref[kz] + far_ref[kz], turned], 1)
        got = lane_parts(folded(dot(iy_ref[...], stacked(padded(data)))))
        for tile in range(2):
            planes[tile, kz * LANES : (kz + 1) * LANES, :] = got[tile]
    if count < CHUNK:
        blank = jnp.zeros(((CHUNK - count) * LANES, LANES), f32)
        for tile in range(2):
            planes[tile, count * LANES :, :] = blank


def inverse_kernel(near_ref, far_ref, back_ref, planes):
    inverse_y(near_ref, far_ref, view(back_ref, 0), planes)


def early_kernel(near_ref, far_ref, planes_a, back_ref, base_part, state_part, planes_b):
    inverse_y(near_ref, far_ref, view(back_ref, 0), planes_b)
    iz_ref, izr_ref = view(back_ref, 4), view(back_ref, 5)

    def along_chunks(tile, yh):
        at = pl.ds(yh, 4 * CHUNK, stride=HALF)
        return padded(jnp.concatenate([ref[tile, at, :] for ref in (planes_a, planes_b)], 0)).T

    many = HALF // PIECES
    for piece in range(PIECES):
        yhs = range(piece * many, (piece + 1) * many)
        data = [along_chunks(0, yh) for yh in yhs]
        rest = [along_chunks(1, yh)[:16] for yh in yhs]
        turned = beside(jnp.concatenate([one[:48] for one in data], 0))
        plain = beside(jnp.concatenate([one[48:] for one in data] + rest, 0))
        turned = folded_lanes(dot(turned, izr_ref[...]))
        plain = folded_lanes(dot(plain, iz_ref[...]))
        for n, yh in enumerate(yhs):
            at = slice(yh * LANES, (yh + 1) * LANES)
            first = turned[48 * n : 48 * n + 48]
            second = plain[80 * n : 80 * n + 80]
            state_part[0, :, at] = first[:32]
            state_part[1, :, at] = second[16:48]
            state_part[2, :, at] = second[48:80]
            base_part[0, :, at] = first[32:48]
            base_part[1, :, at] = second[:16]
            base_part[2, :, at] = plain[80 * many + 16 * n :][:16]


def final_kernel(
    near_ref, far_ref, base_part, state_part, state_hbm, base_hbm, back_ref, last_ref,
    base_out, state_out, planes_c, state_ref, base_ref, state_gap, base_gap, arrived, left,
):
    wide = N * N // PIECES
    cuts = [pl.ds(n * wide, wide) for n in range(PIECES)]

    def copies(pairs, flags):
        return [
            [
                pltpu.make_async_copy(
                    source.at[:, :, cut], target.at[:, :, cut], flags.at[2 * n + k]
                )
                for k, (source, target) in enumerate(pairs)
            ]
            for n, cut in enumerate(cuts)
        ]

    reads = copies(((state_hbm, state_ref), (base_hbm, base_ref)), arrived)
    writes = copies(((state_gap, state_out), (base_gap, base_out)), left)
    for piece in reads:
        for copy in piece:
            copy.start()
    inverse_y(near_ref, far_ref, view(back_ref, 0), planes_c)

    def pair_of_lines(tile, yh):
        rows = []
        for n in range(2):
            value = planes_c[tile, pl.ds(yh + n, 4 * CHUNK, stride=HALF), :]
            high = value.astype(bf16).astype(f32)
            rows += [high, value - high]
        return jnp.concatenate(rows, 0).T

    def table(n):
        rows = last_ref[n * 256 : (n + 1) * 256, :].reshape(2, LANES, 256)
        return jnp.concatenate([rows[0], rows[1]], 1)

    many = HALF // PIECES
    for piece in range(PIECES):
        yhs = range(piece * many, (piece + 1) * many, 2)
        data = [pair_of_lines(0, yh) for yh in yhs]
        rest = [pair_of_lines(1, yh)[:16] for yh in yhs]
        turned = jnp.concatenate([one[:48] for one in data], 0).astype(bf16)
        plain = jnp.concatenate([one[48:] for one in data] + rest, 0).astype(bf16)
        turned = dot(turned, table(1))
        plain = dot(plain, table(0))
        turned = [folded_lanes(turned[:, :256]), folded_lanes(turned[:, 256:])]
        plain = [folded_lanes(plain[:, :256]), folded_lanes(plain[:, 256:])]
        for copy in reads[piece]:
            copy.wait()
        for n, start in enumerate(yhs):
            for k in range(2):
                at = slice((start + k) * LANES, (start + k + 1) * LANES)
                first = turned[k][48 * n : 48 * n + 48]
                second = plain[k][80 * n : 80 * n + 80]
                third = plain[k][40 * many + 16 * n :][:16]
                states = [first[:32], second[16:48], second[48:80]]
                bases = [first[32:48], second[:16], third]
                for i in range(3):
                    part = state_part[i, :, at] - state_ref[i, :, at]
                    state_gap[i, :, at] = states[i] + part
                    part = base_part[i, :, at] - base_ref[i, :, at]
                    base_gap[i, :, at] = bases[i] + part
        for copy in writes[piece]:
            copy.start()
    for piece in writes:
        for copy in piece:
            copy.wait()


interpret = False


def call(kernel, outs, scratch, inputs, room, in_smem=0, in_hbm=(), out_hbm=False):
    whole = pl.BlockSpec(memory_space=pltpu.VMEM)
    small = pl.BlockSpec(memory_space=pltpu.SMEM)
    far = pl.BlockSpec(memory_space=pltpu.HBM)
    return pl.pallas_call(
        kernel,
        out_shape=outs,
        in_specs=[
            small if n < in_smem else far if n in in_hbm else whole for n in range(len(inputs))
        ],
        out_specs=jax.tree.map(lambda _: far if out_hbm else whole, outs),
        scratch_shapes=scratch,
        compiler_params=pltpu.CompilerParams(vmem_limit_bytes=room * 2**20),
        cost_estimate=pl.CostEstimate(flops=1000, bytes_accessed=1000, transcendentals=0),
        interpret=interpret,
    )(*inputs)


def body(base, state, wavenumber, cutoff):
    t = {name: jnp.asarray(value) for name, value in tables().items()}
    core = lax.axis_index("comp")
    seg_count = lax.axis_size("seg")
    own_base = base[0]
    own_state = state[0, 0]
    base_half = lax.dynamic_slice_in_dim(own_base, core * 16, 16, 1)
    back = [((s + 1) % seg_count, s) for s in range(seg_count)]
    around = [(2 * i, 2 * o) for i, o in back] + [(2 * o + 1, 2 * i + 1) for i, o in back]
    state_next = lax.ppermute(own_state, ("seg", "comp"), around)
    sds = jax.ShapeDtypeStruct
    core_at = core.reshape(1)
    swap = [(0, 1), (1, 0)]
    here_own = call(
        base_kernel,
        sds((SENT, ROWS, LANES), f32),
        [
            pltpu.VMEM((HALF * HALF_LINE, LANES), f32),
            pltpu.VMEM(own_base.shape, f32),
            pltpu.VMEM(t["ahead"].shape, bf16),
            pltpu.SemaphoreType.DMA((PIECES + 1,)),
        ],
        [core_at, own_base, t["ahead"]],
        room=56,
        in_smem=1,
        in_hbm=(1, 2),
    )
    there_own = lax.ppermute(here_own, "slab", swap)
    here_other = lax.ppermute(here_own, "comp", swap)
    counts = [planes_of(chunk)[1] - planes_of(chunk)[0] for chunk in range(CHUNKS)]
    flux_lines = sds((3, HALF * 4 * CHUNK, LANES), f32)
    flux = call(
        flux_kernel,
        [sds((2, counts[0], ROWS, LANES), f32)] + [flux_lines] * 2,
        [
            pltpu.VMEM(flux_lines.shape, f32),
            pltpu.VMEM(flux_lines.shape, f32),
            pltpu.VMEM(flux_lines.shape, f32),
            pltpu.VMEM(own_base.shape, f32),
            pltpu.VMEM(own_state.shape, f32),
            pltpu.VMEM(t["ahead"].shape, bf16),
            pltpu.VMEM((2, counts[0], ROWS, LANES), f32),
            pltpu.SemaphoreType.DMA((2 * PIECES + 1,)),
            pltpu.SemaphoreType.DMA((CHUNKS,)),
        ],
        [core_at, own_base, own_state, t["ahead"]],
        room=56,
        in_smem=1,
        in_hbm=(1, 2, 3),
        out_hbm=True,
    )
    there_own, flux = lax.optimization_barrier((there_own, flux))
    there_other = lax.ppermute(there_own, "comp", swap)
    half_planes = sds((3, (HALF_KZ + 1) * LANES, LANES), f32)
    own_planes = call(
        half_kernel,
        half_planes,
        [],
        [core_at, cutoff, here_own, there_own, t["back"]],
        room=12,
        in_smem=2,
    )
    lines = call(
        gradient_kernel,
        [sds((2, HALF * 4 * CHUNK, LANES), f32)] * CHUNKS,
        [pltpu.VMEM(half_planes.shape, f32), pltpu.VMEM((HALF, LANES), f32)],
        [core_at, cutoff, wavenumber, own_base, own_state, own_planes, here_other, there_other]
        + [t["ahead"], t["back"]],
        room=20,
        in_smem=3,
    )
    near, far = [], []
    lines = list(lines)
    for chunk in range(CHUNKS):
        if chunk:
            near[-1], lines[chunk] = lax.optimization_barrier((near[-1], lines[chunk]))
        near_part, far_part = call(
            functools.partial(spectral_kernel, chunk),
            [sds((counts[chunk] + 1, ROWS, LANES), f32)] * 2,
            [],
            [core_at, cutoff, lines[chunk], flux[chunk], t["ahead"], t["along"]],
            room=12,
            in_smem=2,
        )
        if chunk == 0:
            base_half, near_part = lax.optimization_barrier((base_half, near_part))
            base_next = lax.ppermute(base_half, "seg", back)
        near.append(near_part)
        far.append(lax.ppermute(far_part, "slab", swap))
    planes = sds((2, CHUNK * LANES, LANES), f32)
    planes_a = call(inverse_kernel, planes, [], [near[0], far[0], t["back"]], room=8)
    near[1], planes_a = lax.optimization_barrier((near[1], planes_a))
    base_part, state_part = call(
        early_kernel,
        [sds(base_next.shape, f32), sds(state_next.shape, f32)],
        [pltpu.VMEM(planes.shape, f32)],
        [near[1], far[1], planes_a, t["back"]],
        room=14,
    )
    base_gap, state_gap = call(
        final_kernel,
        [sds(base_next.shape, f32), sds(state_next.shape, f32)],
        [
            pltpu.VMEM((2, CHUNK * LANES, LANES), f32),
            pltpu.VMEM(state_next.shape, f32),
            pltpu.VMEM(base_next.shape, f32),
            pltpu.VMEM(state_next.shape, f32),
            pltpu.VMEM(base_next.shape, f32),
            pltpu.SemaphoreType.DMA((2 * PIECES,)),
            pltpu.SemaphoreType.DMA((2 * PIECES,)),
        ],
        [near[2], far[2], base_part, state_part, state_next, base_next, t["back"], t["last"]],
        room=16,
        in_hbm=(4, 5),
        out_hbm=True,
    )
    return base_gap[None], state_gap[None, None]


def solution(mesh):
    paired = mesh.shape["slab"] == 2 and mesh.shape["comp"] == 2
    return jax.shard_map(
        body if paired else general_body,
        mesh=mesh,
        in_specs=(
            P(("groups", "seg"), None, "slab", None),
            P(("groups", "seg"), "comp", None, "slab", None),
            P("groups"),
            P("groups"),
        ),
        out_specs=(
            P(("groups", "seg"), None, ("slab", "comp"), None),
            P(("groups", "seg"), "comp", None, "slab", None),
        ),
        check_vma=False,
    )
```

```python
import functools

import jax
import jax.numpy as jnp
import ml_dtypes
import numpy as np
from jax import lax
from jax.experimental import pallas as pl
from jax.experimental.pallas import tpu as pltpu
from jax.sharding import PartitionSpec as P

N = 64
HALF = 32
KEEP = N // 3
NKZ = KEEP + 1
NKY = 44
ROWS = 2 * NKY
CHUNK = 8
CHUNKS = 3
LINE = CHUNKS * CHUNK * 4
HALF_KZ = NKZ // 2
HALF_LINE = 4 * (HALF_KZ + 1)
SENT = 9
LANES = 128

viscosity = 0.025
time_step = 0.02
forcing_amp = 10.0

f32 = jnp.float32
bf16 = jnp.bfloat16


highest = lax.Precision.HIGHEST


def swapped(value, axis, apart):
    mask = 2**apart
    pairs = [(source, source ^ mask) for source in range(lax.axis_size(axis))]
    return lax.ppermute(value, axis, pairs)


def shifted(block, axis, distance):
    devices = range(lax.axis_size(axis))
    route = [((i - distance) % len(devices), i) for i in devices]
    return lax.ppermute(block, axis, route)


def wavenumbers(grid_points):
    position = jnp.arange(grid_points, dtype=jnp.int32)
    return jnp.where(position < grid_points // 2, position, position - grid_points)


def phases(first, second, grid_points):
    product = jnp.mod(first[:, None] * second[None, :], grid_points)
    return product.astype(jnp.float32) * (2.0 * jnp.pi / grid_points)


def combine(partial_value, columns):
    cosine_part = partial_value[0]
    sine_part = partial_value[1]
    real_part = cosine_part[..., :columns] - sine_part[..., columns:]
    imag_part = cosine_part[..., columns:] + sine_part[..., :columns]
    return jnp.concatenate([real_part, imag_part], axis=-1)


def times_unit(values, wave, columns):
    return jnp.concatenate([-wave * values[..., columns:], wave * values[..., :columns]], axis=-1)


def doubled(values):
    return jnp.concatenate([values, values], axis=-1)


def general_body(base, state, wavenumber, cutoff):
    grid_points = N
    base = base.reshape(base.shape[0], 3, base.shape[2], grid_points, grid_points)
    state = state.reshape(
        state.shape[0], state.shape[1], 3, state.shape[3], grid_points, grid_points
    )
    slab_rows = state.shape[3]
    half_rows = slab_rows // 2
    slab_count = lax.axis_size("slab")
    group_count = slab_count * lax.axis_size("comp")
    core_side = lax.axis_index("comp")
    block_number = lax.axis_index(("slab", "comp"))
    base_whole = base[0]
    base_half = lax.dynamic_slice_in_dim(base_whole, core_side * half_rows, half_rows, 1)
    own_state = state[0, 0]
    spectrum = wavenumbers(grid_points)
    one_third = grid_points // 3
    row_total = (2 * one_third + group_count) // group_count * group_count
    row_index = jnp.arange(row_total, dtype=jnp.int32)
    row_alive_mask = row_index <= 2 * one_third
    row_wave = jnp.where(row_index <= one_third, row_index, row_index - (2 * one_third + 1))
    row_wave = jnp.where(row_alive_mask, row_wave, 0)
    width = grid_points // 2
    rows_per_block = row_total // group_count
    alive_flags = row_alive_mask.astype(jnp.float32)
    grid_index = jnp.arange(grid_points, dtype=jnp.int32)
    column_index = grid_index[:width]
    angle_grid = phases(grid_index, grid_index, grid_points)
    angle_ahead = phases(grid_index, column_index, grid_points)
    angle_behind = phases(column_index, grid_index, grid_points)
    column_weight = jnp.where(column_index == 0, 1.0, 2.0).astype(jnp.float32)[:, None]
    forward_z = jnp.concatenate([jnp.cos(angle_ahead), -jnp.sin(angle_ahead)], axis=1)
    inverse_z = (
        jnp.concatenate(
            [jnp.cos(angle_behind) * column_weight, -jnp.sin(angle_behind) * column_weight], axis=0
        )
        / grid_points
    )
    phase_angle_rows = phases(row_wave, grid_index, grid_points)
    forward_transform_y = (
        jnp.stack([jnp.cos(phase_angle_rows), -jnp.sin(phase_angle_rows)])
        * alive_flags[None, :, None]
    )
    inverse_y = (
        jnp.stack([jnp.cos(phase_angle_rows).T, jnp.sin(phase_angle_rows).T])
        * alive_flags[None, None, :]
        / grid_points
    )
    forward_x = jnp.stack([jnp.cos(angle_grid), -jnp.sin(angle_grid)])
    inverse_x = jnp.stack([jnp.cos(angle_grid), jnp.sin(angle_grid)]) / grid_points
    table_ahead = forward_x.reshape(2, grid_points, slab_count, slab_rows)
    table_back = inverse_x.reshape(2, slab_count, slab_rows, grid_points)
    local_wave = lax.dynamic_slice_in_dim(row_wave, block_number * rows_per_block, rows_per_block)
    local_alive_mask = lax.dynamic_slice_in_dim(
        alive_flags, block_number * rows_per_block, rows_per_block
    )
    shape_local = (grid_points, rows_per_block, width)
    wave_x = jnp.broadcast_to(spectrum[:, None, None], shape_local)
    wave_y = jnp.broadcast_to(local_wave[None, :, None], shape_local)
    wave_z = jnp.broadcast_to(spectrum[:width][None, None, :], shape_local)
    inside = (
        (jnp.abs(wave_x) <= cutoff[0])
        & (jnp.abs(wave_y) <= cutoff[1])
        & (jnp.abs(wave_z) <= cutoff[2])
    )
    keep_mask = doubled(inside.astype(jnp.float32) * local_alive_mask[None, :, None])
    float_x = wave_x.astype(jnp.float32)
    float_y = wave_y.astype(jnp.float32)
    float_z = wave_z.astype(jnp.float32)
    ksquare = float_x * float_x + float_y * float_y + float_z * float_z
    safe_square = doubled(jnp.where(ksquare > 0, ksquare, jnp.ones_like(ksquare)))
    damping = doubled(1.0 / (1.0 + viscosity * time_step * ksquare))
    double_x = doubled(float_x)
    double_y = doubled(float_y)
    double_z = doubled(float_z)

    def project(field):
        divergence = (double_x * field[0] + double_y * field[1] + double_z * field[2]) / safe_square
        return jnp.stack(
            [
                field[0] - double_x * divergence,
                field[1] - double_y * divergence,
                field[2] - double_z * divergence,
            ]
        )

    def yz_forward(field):
        along_z = jnp.einsum("...z,zk->...k", field, forward_z, precision=highest)
        partial_value = jnp.einsum(
            "sry,...yk->s...rk", forward_transform_y, along_z, precision=highest
        )
        return combine(partial_value, width)

    def yz_inverse(modes):
        partial_value = jnp.einsum("syr,...rk->s...yk", inverse_y, modes, precision=highest)
        return jnp.einsum(
            "...k,kz->...z", combine(partial_value, width), inverse_z, precision=highest
        )

    def spectral(state_fields, base_fields):
        state_modes = yz_forward(state_fields)[:, :, None]
        base_modes = yz_forward(base_fields)[:, :, None]
        state_got = lax.all_to_all(
            state_modes, ("slab", "comp"), split_axis=4, concat_axis=2, tiled=True
        )
        base_got = lax.all_to_all(
            base_modes, ("slab", "comp"), split_axis=4, concat_axis=2, tiled=True
        )
        item_count = state_got.shape[0]
        part_count = state_got.shape[1]
        state_split = state_got.reshape(
            item_count, part_count, slab_count, 2, slab_rows, rows_per_block, 2 * width
        )
        state_partial = jnp.einsum(
            "srpx,ijpcxyk->sijcryk", table_ahead, state_split, precision=highest
        )
        base_lined = base_got.reshape(item_count, 1, grid_points, rows_per_block, 2 * width)
        base_partial = jnp.einsum("srx,ijxyk->sijryk", forward_x, base_lined, precision=highest)
        return (combine(state_partial, width), combine(base_partial, width))

    state_first, base_first = spectral(own_state[:, None], base_half[:, None])
    state_hat = state_first[:, 0] * keep_mask
    base_hat = base_first[:, 0] * keep_mask
    grad_hat = jnp.stack(
        [
            times_unit(base_hat, float_x, width),
            times_unit(base_hat, float_y, width),
            times_unit(base_hat, float_z, width),
        ],
        axis=1,
    )
    grad_hat = grad_hat.reshape(9, grid_points, rows_per_block, 2 * width)
    grad_partial = jnp.einsum("sxr,iryk->sixyk", inverse_x, grad_hat, precision=highest)
    grad_spread = combine(grad_partial, width).reshape(
        9, group_count, half_rows, rows_per_block, 2 * width
    )
    own_rows = yz_inverse(
        lax.all_to_all(grad_spread, ("slab", "comp"), split_axis=1, concat_axis=3, tiled=True)[:, 0]
    )
    other_rows = swapped(own_rows, "comp", 0)
    gradient = jnp.where(
        core_side == 0,
        jnp.concatenate([own_rows, other_rows], axis=1),
        jnp.concatenate([other_rows, own_rows], axis=1),
    )
    gradient = gradient.reshape(3, 3, slab_rows, grid_points, grid_points)
    gradient_half = lax.dynamic_slice_in_dim(gradient, core_side * half_rows, half_rows, 2)
    flux_terms = own_state[:, None] * base_whole[None, :]
    coupling_matrix = jnp.where(core_side == 0, gradient, jnp.swapaxes(gradient, 0, 1))
    coupling = jnp.sum(coupling_matrix * own_state[None, :], axis=1)
    forcing_phase = phases(wavenumber, grid_index, grid_points)[0]
    forcing = forcing_amp * jnp.sin(forcing_phase)[None, :, None]
    base_drive = jnp.sum(gradient_half * base_half[None, :], axis=1)
    base_drive = jnp.concatenate([base_drive[:1] - forcing[None], base_drive[1:]], axis=0)
    state_fields = jnp.concatenate([flux_terms, coupling[:, None]], axis=1)
    drive_modes, base_modes_two = spectral(state_fields, base_drive[:, None])
    orient = jnp.array([1.0, -1.0], dtype=jnp.float32)[None, :, None, None, None]
    divergence = (
        times_unit(drive_modes[:, 0], float_x, width)
        + times_unit(drive_modes[:, 1], float_y, width)
        + times_unit(drive_modes[:, 2], float_z, width)
    )
    state_drive = keep_mask * (orient * divergence + drive_modes[:, 3])
    new_hat = damping * project(state_hat - time_step * state_drive)
    base_new_hat = damping * project(base_hat - time_step * keep_mask * base_modes_two[:, 0])
    state_partial = jnp.einsum("spxr,icryk->sipcxyk", table_back, new_hat, precision=highest)
    state_back = combine(state_partial, width).reshape(
        3, group_count, slab_rows, rows_per_block, 2 * width
    )
    base_partial = jnp.einsum("sxr,iryk->sixyk", inverse_x, base_new_hat, precision=highest)
    base_back = combine(base_partial, width).reshape(
        3, group_count, half_rows, rows_per_block, 2 * width
    )
    state_got = lax.all_to_all(
        state_back, ("slab", "comp"), split_axis=1, concat_axis=3, tiled=True
    )
    base_got = lax.all_to_all(base_back, ("slab", "comp"), split_axis=1, concat_axis=3, tiled=True)
    state_new = yz_inverse(state_got[:, 0])
    base_new = yz_inverse(base_got[:, 0])
    base_later, later_state = shifted((base_half, own_state), "seg", -1)
    prior_state = shifted(own_state, "seg", 1)
    neighbour = jnp.where(core_side == 0, later_state, prior_state)
    base_gap = (base_new - base_later).reshape(1, 3, half_rows, grid_points * grid_points)
    state_gap = (state_new - neighbour).reshape(1, 1, 3, slab_rows, grid_points * grid_points)
    return (base_gap, state_gap)


def halves(table):
    high = table.astype(np.float32).astype(ml_dtypes.bfloat16)
    low = (table - high.astype(np.float64)).astype(ml_dtypes.bfloat16)
    return high, low


def left_table(table, depth):
    padded = np.zeros((table.shape[0], depth))
    padded[:, : table.shape[1]] = table
    high, low = halves(padded)
    return np.concatenate(
        [np.concatenate([high, high], 1), np.concatenate([low, np.zeros_like(low)], 1)], 0
    )


def right_table(table, depth):
    return np.ascontiguousarray(left_table(table.T, depth).T)


def planes_of(chunk):
    return chunk * CHUNK, min((chunk + 1) * CHUNK, NKZ)


def ky_values():
    index = np.arange(NKY)
    wave = np.where(index <= KEEP, index, index - (2 * KEEP + 1))
    alive = (index <= 2 * KEEP).astype(np.float64)
    return wave * alive, alive


@functools.cache
def tables():
    out = {}
    z = np.arange(N)
    kz = np.arange(NKZ)
    angle = 2 * np.pi * kz[:, None] * z[None, :] / N
    weight = np.where(kz == 0, 1.0, 2.0)[:, None] / N
    forward = np.zeros((2, 2, CHUNKS * CHUNK, 2, N))
    inverse = np.zeros((NKZ, 2, 2, 2, N))
    turned = np.zeros((NKZ, 2, 2, 2, N))
    slope = np.zeros((NKZ, 2, 2, 2, N))
    for y2 in range(2):
        forward[y2, 0, :NKZ, y2] = np.cos(angle)
        forward[y2, 1, :NKZ, y2] = -np.sin(angle)
        inverse[:, y2, 0, y2] = weight * np.cos(angle)
        inverse[:, y2, 1, y2] = -weight * np.sin(angle)
        turned[:, y2, 0, y2] = weight * np.sin(angle)
        turned[:, y2, 1, y2] = weight * np.cos(angle)
        slope[:, y2, 0, y2] = -weight * kz[:, None] * np.sin(angle)
        slope[:, y2, 1, y2] = -weight * kz[:, None] * np.cos(angle)
    forward = np.moveaxis(forward.reshape(4, CHUNKS, CHUNK, 2 * N), 1, 0)
    out["fz"] = left_table(forward.reshape(LINE, 2 * N), 128)
    by_kz = np.moveaxis(forward.reshape(CHUNKS, 4, CHUNK, 2 * N), 1, 0).reshape(4, -1, 2 * N)
    halved = []
    for core in range(2):
        wide = np.zeros((4, HALF_KZ + 1, 2 * N))
        wide[:, :HALF_KZ] = by_kz[:, core * HALF_KZ : (core + 1) * HALF_KZ]
        halved.append(left_table(wide.reshape(HALF_LINE, 2 * N), 128))
    out["fzh"] = np.concatenate(halved, 0)

    def by_chunk(table):
        wide = np.zeros((CHUNKS, CHUNK, 4, 2 * N))
        for chunk in range(CHUNKS):
            first, last = planes_of(chunk)
            wide[chunk, : last - first] = table.reshape(NKZ, 4, 2 * N)[first:last]
        return right_table(wide.reshape(LINE, 2 * N), 128)

    out["iz"] = by_chunk(inverse)
    out["izr"] = by_chunk(turned)

    def last_pair(table):
        first, last = planes_of(CHUNKS - 1)
        depth = 4 * CHUNK
        wide = np.zeros((depth, 2 * N))
        wide[: 4 * (last - first)] = table.reshape(NKZ, 4, 2 * N)[first:last].reshape(-1, 2 * N)
        both = np.zeros((2, 2, 2 * depth, 4 * N), ml_dtypes.bfloat16)
        both[0, 0] = both[1, 1] = right_table(wide, depth)
        return both.reshape(2 * LANES, 256)

    out["izc"] = np.concatenate([last_pair(inverse), last_pair(turned)], 0)

    def by_half(table):
        wide = np.zeros((2, HALF_KZ + 1, 4, 2 * N))
        wide[:, :HALF_KZ] = table.reshape(2, HALF_KZ, 4, 2 * N)
        return right_table(wide.reshape(8 * HALF_KZ + 8, 2 * N), 128)

    out["izg"] = by_half(inverse)
    out["izd"] = by_half(slope)
    ky, alive = ky_values()
    y = 2 * np.arange(HALF)[None, :] + np.arange(2)[:, None]
    phase = 2 * np.pi * ky[:, None, None] * y[None] / N
    cosine = np.cos(phase) * alive[:, None, None]
    sine = np.sin(phase) * alive[:, None, None]
    plain = np.zeros((2, NKY, 2, 2, HALF))
    plain[0, :, :, 0] = cosine
    plain[0, :, :, 1] = sine
    plain[1, :, :, 0] = -sine
    plain[1, :, :, 1] = cosine
    rotated = np.stack([-plain[1], plain[0]])
    out["fy"] = left_table(plain.reshape(ROWS, 128), 128)
    out["fyr"] = left_table(rotated.reshape(ROWS, 128), 128)
    back = np.zeros((2, 2, HALF, 2, NKY))
    cos_t = np.moveaxis(cosine, 0, -1) / N
    sin_t = np.moveaxis(sine, 0, -1) / N
    back[:, 0, :, 0] = cos_t
    back[:, 0, :, 1] = -sin_t
    back[:, 1, :, 0] = sin_t
    back[:, 1, :, 1] = cos_t
    back_slope = np.zeros_like(back)
    back_slope[..., 0, :] = ky * back[..., 1, :]
    back_slope[..., 1, :] = -ky * back[..., 0, :]
    out["iy"] = left_table(back.reshape(128, ROWS), 128)
    out["iyd"] = left_table(back_slope.reshape(128, ROWS), 128)
    grad_high, grad_low = [], []
    x = np.arange(N)
    apart = x[:HALF, None] - x[None, :]
    for cut in range(KEEP - 3, KEEP + 1):
        k = np.arange(cut + 1)
        wk = np.where(k == 0, 1.0, 2.0) / N
        arg = 2 * np.pi * apart[..., None] * k / N
        keep = (np.cos(arg) * wk).sum(-1)
        derive = (-np.sin(arg) * wk * k).sum(-1)
        table = np.zeros((2, 4, HALF, 2, 4, HALF))
        for comp in range(3):
            for side in range(2):
                rows = slice(side * HALF, (side + 1) * HALF)
                table[side, comp, :, 0, comp, :] = keep[:, rows].T
                table[side, comp, :, 1, comp, :] = derive[:, rows].T
        high, low = halves(table.reshape(256, 256))
        grad_high.append(high)
        grad_low.append(low)
    out["gxh"] = np.stack(grad_high)
    out["gxl"] = np.stack(grad_low)
    kx = np.arange(HALF)
    live = (kx <= KEEP).astype(np.float64)
    xl = np.arange(HALF)
    arg = 2 * np.pi * xl[:, None] * kx[None, :] / N
    value = np.concatenate([np.cos(arg) * live, np.sin(arg) * live], 1)
    change = np.concatenate([kx * np.sin(arg) * live, -kx * np.cos(arg) * live], 1)

    def coefficients(blocks):
        table = np.zeros((4, HALF, 2, 2 * HALF))
        for block, part, what in blocks:
            table[block, :, part] = what
        return table.reshape(LANES, LANES)

    first = coefficients([(0, 0, value), (1, 1, value), (2, 0, change), (3, 0, value)])
    last = coefficients([(0, 0, change), (1, 0, value), (2, 0, value), (3, 1, value)])
    fall = first.reshape(LANES, 2, 2, HALF)
    fall = np.stack([-kx * fall[:, :, 1], kx * fall[:, :, 0]], 2).reshape(LANES, LANES)
    out["fx"] = np.stack([right_table(part, 128) for part in (first, fall, first, last)])
    wx = np.where(kx == 0, 1.0, 2.0) * live / N
    for core in range(2):
        ix = np.zeros((4, 2, 2 * HALF, LANES))
        for side in range(2):
            xs = np.arange(HALF) + side * HALF
            arg = 2 * np.pi * kx[:, None] * xs[None, :] / N
            give = np.concatenate([np.cos(arg) * wx[:, None], np.sin(arg) * wx[:, None]], 0)
            drop = np.concatenate(
                [np.sin(arg) * (wx * kx)[:, None], -np.cos(arg) * (wx * kx)[:, None]], 0
            )
            own = slice(core * 16, core * 16 + 16)

            def put(quantity, part, lane, what):
                at = (lane + side * 64 + np.arange(what.shape[1])) % LANES
                ix[quantity, part][:, at] = what

            put(0, 0, 0, give)
            put(1, 0, 0, drop)
            put(0, 1, 32, give[:, own])
            put(1, 1, 32, drop[:, own])
            put(2, 1, 48, give[:, own])
            put(2, 0, 64, give)
            put(3, 0, 96, give)
            put(3, 1, 0, give[:, own])
        out["ix%d" % core] = np.stack(
            [right_table(part, 128) for part in ix.reshape(4, LANES, LANES)]
        )
    out["ix"] = np.stack([out.pop("ix0"), out.pop("ix1")])
    merged = {}
    merged["ahead"] = np.concatenate([out["fz"], out["fy"], out["fyr"], out["fzh"]], 0)
    gx = [out["gxh"].reshape(-1, 256), out["gxl"].reshape(-1, 256)]
    square = [out[name] for name in ("iy", "iyd", "izg", "izd", "iz", "izr")]
    merged["back"] = np.concatenate(square + gx, 0)
    merged["last"] = out["izc"]
    merged["along"] = np.concatenate([out["fx"].reshape(-1, 256), out["ix"].reshape(-1, 256)], 0)
    return merged


def view(ref, index, rows=256, start=0):
    return ref.at[pl.ds(start + index * rows, rows), :]


def ahead_tables(ref):
    return (
        view(ref, 0, 2 * LINE),
        view(ref, 0, 2 * ROWS, 2 * LINE),
        view(ref, 1, 2 * ROWS, 2 * LINE),
    )


def ky_rows():
    row = lax.broadcasted_iota(jnp.int32, (ROWS, LANES), 0)
    index = jnp.where(row < NKY, row, row - NKY)
    wave = jnp.where(index <= KEEP, index, index - (2 * KEEP + 1))
    return jnp.where(index <= 2 * KEEP, wave, 0).astype(f32)


def kx_lanes():
    lane = lax.broadcasted_iota(jnp.int32, (1, LANES), 1) % HALF
    return jnp.where(lane <= KEEP, lane, 0).astype(f32)


def split(values):
    high = values.astype(bf16)
    low = (values - high.astype(f32)).astype(bf16)
    return high, low


def dot(a, b):
    return jnp.dot(a, b, preferred_element_type=f32)


def dot_nt(a, b):
    return lax.dot_general(a, b, (((1,), (1,)), ((), ())), preferred_element_type=f32)


def stacked(values):
    high, low = split(values)
    return jnp.concatenate([high, low], 0)


def beside(values):
    high, low = split(values)
    return jnp.concatenate([high, low], 1)


def folded(result):
    rows = result.shape[0] // 2
    return result[:rows] + result[rows:]


def folded_lanes(result):
    return result[:, :LANES] + result[:, LANES:]


def padded(values, rows=128):
    return jnp.concatenate([values, jnp.zeros((rows - values.shape[0], values.shape[1]), f32)], 0)


def triple(values, high_ref, low_ref):
    high, low = split(values)
    return dot(high, high_ref) + dot(low, high_ref) + dot(high, low_ref)


def columns(yh):
    return pl.ds(pl.multiple_of(yh * LANES, LANES), LANES)


def along_y(ref, tile, kz):
    at = kz % CHUNK
    return jnp.concatenate(
        [ref[tile, pl.ds(q * CHUNK + at, HALF, stride=4 * CHUNK), :] for q in range(4)], 0
    )


def line_rows(yh):
    return pl.ds(pl.multiple_of(yh * LINE, 8), LINE)


def lane_parts(values):
    return [values[:, at : at + LANES] for at in range(0, values.shape[1], LANES)]


def over_planes(step, first=0, last=NKZ):
    def four(index, _):
        step([first + index * 4 + k for k in range(4)])
        return 0

    count = (last - first) // 4
    lax.fori_loop(0, count, four, 0)
    if first + count * 4 < last:
        step([jnp.int32(kz) for kz in range(first + count * 4, last)])


def over_lines(step, many, first=0, last=HALF):
    def some(index, _):
        step([first + index * many + k for k in range(many)])
        return 0

    lax.fori_loop(0, (last - first) // many, some, 0)


PIECES = 4


def base_kernel(core_ref, base_hbm, ahead_hbm, out_ref, lines, base_ref, ahead_ref, arrived):
    nothing = jnp.zeros((HALF, LANES), f32)
    wide = N * N // PIECES
    table = pltpu.make_async_copy(ahead_hbm, ahead_ref, arrived.at[PIECES])
    pieces = [
        pltpu.make_async_copy(
            base_hbm.at[:, :, pl.ds(n * wide, wide)],
            base_ref.at[:, :, pl.ds(n * wide, wide)],
            arrived.at[n],
        )
        for n in range(PIECES)
    ]
    pieces[0].start()
    table.start()
    for piece in pieces[1:]:
        piece.start()
    fy_ref = ahead_tables(ahead_ref)[1]
    table.wait()
    first = 2 * LINE + 4 * ROWS + core_ref[0] * 2 * HALF_LINE
    fz = ahead_ref[pl.ds(pl.multiple_of(first, 32), 2 * HALF_LINE), :]
    many = HALF // PIECES
    for n, piece in enumerate(pieces):
        piece.wait()
        yhs = range(n * many, (n + 1) * many)
        rows = []
        for yh in yhs:
            at = slice(yh * LANES, (yh + 1) * LANES)
            rows += [base_ref[i, :, at] for i in range(3)] + [nothing]
        got = folded(dot_nt(fz, beside(jnp.concatenate(rows, 0))))
        for yh, part in zip(yhs, lane_parts(got)):
            lines[yh * HALF_LINE : (yh + 1) * HALF_LINE, :] = part
    planes = []
    for pair in range(0, HALF_KZ, 2):
        ks = range(pair, min(pair + 2, HALF_KZ))
        data = []
        for k in ks:
            starts = [q * (HALF_KZ + 1) + k for q in range(4)]
            picked = [lines[pl.ds(at, HALF, stride=HALF_LINE), :] for at in starts]
            data.append(stacked(jnp.concatenate(picked, 0)))
        data = jnp.concatenate(data, 1)
        planes += lane_parts(folded(dot(fy_ref[...], data)))
    lane = lax.broadcasted_iota(jnp.int32, (ROWS, LANES), 1)
    for k in range(SENT):
        part = planes[k]
        if k < 3 * (HALF_KZ - SENT):
            guest = pltpu.roll(planes[SENT + k // 3], (3 - k % 3) * HALF, 1)
            part = jnp.where(lane < 96, part, guest)
        out_ref[k] = part


def received(ref, k):
    if k < SENT:
        return ref[k]
    lane = lax.broadcasted_iota(jnp.int32, (ROWS, LANES), 1)
    blocks = [
        pltpu.roll(ref[3 * (k - SENT) + j], LANES - (3 - j) * HALF, 1) for j in range(3)
    ]
    return jnp.where(lane < 32, blocks[0], jnp.where(lane < 64, blocks[1], blocks[2]))


def flux_modes(lines_ref, fy_ref, fyr_ref, kzs):
    ky = ky_rows()
    lane = lax.broadcasted_iota(jnp.int32, (ROWS, LANES), 1)
    odd_block = (lane // HALF) % 2 == 1
    even = []
    for pair in range(0, len(kzs), 2):
        data = [stacked(along_y(lines_ref, 0, kz)) for kz in kzs[pair : pair + 2]]
        even += lane_parts(folded(dot(fy_ref[...], jnp.concatenate(data, 1))))
    odd = []
    for kz in kzs:
        data = [stacked(along_y(lines_ref, tile, kz)) for tile in (1, 2)]
        odd.append(lane_parts(folded(dot(fyr_ref[...], jnp.concatenate(data, 1)))))
    first, second = [], []
    for n, kz in enumerate(kzs):
        kzf = kz.astype(f32)
        plain = even[n]
        slopes = odd[n][0] * jnp.where(odd_block, kzf, ky)
        slopes = slopes + pltpu.roll(slopes, 32, 1)
        first.append(jnp.where(odd_block, slopes, plain))
        other = plain * jnp.where(lane >= 96, -kzf, -ky)
        other = other + pltpu.roll(other, 64, 1)
        second.append(jnp.where(lane >= 96, other, jnp.where(lane >= 64, odd[n][1], 0.0)))
    return first, second


def flux_kernel(
    core_ref, base_hbm, state_hbm, ahead_hbm, out_ref, out_b, out_c,
    lines_a, lines_b, lines_c, base_ref, state_ref, ahead_ref, result, arrived, left,
):
    wide = N * N // PIECES
    pieces = [pltpu.make_async_copy(ahead_hbm, ahead_ref, arrived.at[2 * PIECES])]
    for n in range(PIECES):
        for k, (source, target) in enumerate(((base_hbm, base_ref), (state_hbm, state_ref))):
            at = pl.ds(n * wide, wide)
            pieces.append(
                pltpu.make_async_copy(
                    source.at[:, :, at], target.at[:, :, at], arrived.at[2 * n + k]
                )
            )
    for piece in pieces:
        piece.start()
    fz_ref, fy_ref, fyr_ref = ahead_tables(ahead_ref)
    sigma = jnp.where(core_ref[0] == 0, -time_step, time_step).astype(f32)
    depth = LINE // CHUNKS

    def z_step(yhs):
        rows, lone = [], []
        for yh in yhs:
            b = [base_ref[i, :, columns(yh)] for i in range(3)]
            t = [sigma * state_ref[i, :, columns(yh)] for i in range(3)]
            rows += [t[2] * b[0], t[0] * b[1], t[1] * b[0], t[0] * b[2]]
            rows += [t[2] * b[1], t[2] * b[2], t[1] * b[1], t[1] * b[2]]
            lone.append(t[0] * b[0])
        got = lane_parts(folded(dot_nt(fz_ref[...], beside(jnp.concatenate(rows + lone, 0)))))
        for n, yh in enumerate(yhs):
            third = got[-1] if n == 2 else pltpu.roll(got[-1], (2 - n) % 4 * HALF, 1)
            at = pl.ds(pl.multiple_of(yh * depth, 8), depth)
            for tile, part in enumerate((got[2 * n], got[2 * n + 1], third)):
                for chunk, lines in enumerate((lines_a, lines_b, lines_c)):
                    lines[tile, at, :] = part[chunk * depth : (chunk + 1) * depth]

    pieces[0].wait()
    for n in range(PIECES):
        pieces[2 * n + 1].wait()
        pieces[2 * n + 2].wait()
        over_lines(z_step, 4, n * HALF // PIECES, (n + 1) * HALF // PIECES)
    sends = [
        pltpu.make_async_copy(lines_b, out_b, left.at[1]),
        pltpu.make_async_copy(lines_c, out_c, left.at[2]),
        pltpu.make_async_copy(result, out_ref, left.at[0]),
    ]
    sends[0].start()
    sends[1].start()

    def y_step(kzs):
        first, second = flux_modes(lines_a, fy_ref, fyr_ref, kzs)
        for n, kz in enumerate(kzs):
            result[0, kz] = first[n]
            result[1, kz] = second[n]

    over_planes(y_step, *planes_of(0))
    sends[2].start()
    for send in sends:
        send.wait()


def gradient_planes(cutoff_ref, here_ref, there_ref, back_ref, planes, start):
    cut_x, cut_y, cut_z = cutoff_ref[0], cutoff_ref[1], cutoff_ref[2]
    which = jnp.clip(cut_x - (KEEP - 3), 0, 3)
    keep_y = jnp.where(jnp.abs(ky_rows()) <= cut_y.astype(f32), 1.0, 0.0).astype(f32)
    iy_ref, iyd_ref = (view(back_ref, n) for n in range(2))
    for d in range(3):
        planes[d, HALF_KZ * LANES :, :] = jnp.zeros((LANES, LANES), f32)
    for first in range(0, HALF_KZ, 4):
        kzs = range(first, min(first + 4, HALF_KZ))
        rows = []
        for kz in kzs:
            keep = keep_y * jnp.where(start + kz <= cut_z, 1.0, 0.0).astype(f32)
            rows.append(
                jnp.concatenate([received(ref, kz) * keep for ref in (here_ref, there_ref)], 1)
            )
        high = back_ref[pl.ds(pl.multiple_of((6 + which) * 256, 256), 256), :]
        low = back_ref[pl.ds(pl.multiple_of((10 + which) * 256, 256), 256), :]
        got = triple(jnp.concatenate(rows, 0), high, low)
        data = [stacked(padded(got[n * ROWS : (n + 1) * ROWS])) for n in range(len(kzs))]
        for n, kz in enumerate(kzs):
            even = lane_parts(folded(dot(iy_ref[...], data[n])))
            planes[0, kz * LANES : (kz + 1) * LANES, :] = even[1]
            planes[2, kz * LANES : (kz + 1) * LANES, :] = even[0]
        for n in range(0, len(kzs), 2):
            both = jnp.concatenate([one[:, :LANES] for one in data[n : n + 2]], 1)
            for k, part in enumerate(lane_parts(folded(dot(iyd_ref[...], both)))):
                kz = kzs[n + k]
                planes[1, kz * LANES : (kz + 1) * LANES, :] = part


def half_kernel(core_ref, cutoff_ref, here_ref, there_ref, back_ref, planes):
    start = core_ref[0] * HALF_KZ
    gradient_planes(cutoff_ref, here_ref, there_ref, back_ref, planes, start)


def gradient_kernel(
    core_ref, cutoff_ref, wave_ref, base_ref, state_ref, own_ref, here_ref, there_ref,
    ahead_ref, back_ref, *refs
):
    *out_refs, planes, force_ref = refs
    core = core_ref[0]
    start = (1 - core) * HALF_KZ
    gradient_planes(cutoff_ref, here_ref, there_ref, back_ref, planes, start)
    fz_ref = ahead_tables(ahead_ref)[0]
    iz_ref, izd_ref = view(back_ref, 2), view(back_ref, 3)
    y = lax.broadcasted_iota(jnp.int32, (HALF, LANES), 0) * 2
    y = y + lax.broadcasted_iota(jnp.int32, (HALF, LANES), 1) // N
    phase = ((wave_ref[0] * y) % N).astype(f32) * (2.0 * np.pi / N)
    force_ref[...] = forcing_amp * jnp.sin(phase)
    nothing = jnp.zeros((HALF, LANES), f32)

    def along_halves(d, yh):
        at = pl.ds(yh, 4 * (HALF_KZ + 1), stride=HALF)
        own, other = own_ref[d, at, :], planes[d, at, :]
        low = jnp.where(core == 0, own, other)
        high = jnp.where(core == 0, other, own)
        return padded(jnp.concatenate([low, high], 0)).T

    def physical_step(yhs):
        count = len(yhs)
        flat = [along_halves(d, yh)[:96] for d in range(2) for yh in yhs]
        steep = [along_halves(2, yh)[:96] for yh in yhs]
        flat = folded_lanes(dot(beside(jnp.concatenate(flat, 0)), iz_ref[...]))
        steep = folded_lanes(dot(beside(jnp.concatenate(steep, 0)), izd_ref[...]))
        for n, yh in enumerate(yhs):
            sets = [flat[96 * n :], flat[96 * (count + n) :], steep[96 * n :]]
            grads = [[one[HALF * i : HALF * (i + 1)] for i in range(3)] for one in sets]
            b = [base_ref[i, :, columns(yh)] for i in range(3)]
            s = [state_ref[i, :, columns(yh)] for i in range(3)]
            comb, comb_base = [], []
            for i in range(3):
                coupling = sum(
                    jnp.where(core == 0, grads[j][i], grads[i][j]) * s[j] for j in range(3)
                )
                comb.append(s[i] - time_step * coupling)
                drive = sum(grads[j][i] * b[j] for j in range(3))
                if i == 0:
                    drive = drive - force_ref[pl.ds(yh, 1), :]
                comb_base.append(b[i] - time_step * drive)
            rows = [comb[1], comb_base[1], comb[2], comb_base[2]]
            rows += [comb[0], comb_base[0], nothing, nothing]
            got = folded(dot_nt(fz_ref[...], beside(jnp.concatenate(rows, 0))))
            depth = LINE // CHUNKS
            at = pl.ds(pl.multiple_of(yh * depth, 8), depth)
            for tile, part in enumerate(lane_parts(got)):
                for chunk in range(CHUNKS):
                    out_refs[chunk][tile, at, :] = part[chunk * depth : (chunk + 1) * depth]

    over_lines(physical_step, 8)


def spectral_kernel(
    chunk, core_ref, cutoff_ref, lines_ref, flux_ref,
    ahead_ref, along_ref, near_ref, far_ref,
):
    _, fy_ref, fyr_ref = ahead_tables(ahead_ref)
    core = core_ref[0]
    cut_x, cut_y, cut_z = (cutoff_ref[i] for i in range(3))
    first, last = planes_of(chunk)
    extra = last - first
    ky = ky_rows()
    kx = kx_lanes()
    keep_y = jnp.where(jnp.abs(ky) <= cut_y.astype(f32), 1.0, 0.0).astype(f32)
    keep_x = jnp.where(kx <= cut_x.astype(f32), 1.0, 0.0).astype(f32)
    keep_xy = keep_y * keep_x
    square_xy = ky * ky + kx * kx
    lane = lax.broadcasted_iota(jnp.int32, (ROWS, LANES), 1)
    near_ref[extra] = jnp.zeros((ROWS, LANES), f32)
    far_ref[extra] = jnp.zeros((ROWS, LANES), f32)

    def kept_z(kz):
        return jnp.where(kz <= cut_z, 1.0, 0.0).astype(f32)

    def spectral_step(kzs):
        fields = [[], [], []]
        if chunk == 0:
            first_flux = [flux_ref[0, kz] for kz in kzs]
            second_flux = [flux_ref[1, kz] for kz in kzs]
        else:
            first_flux, second_flux = flux_modes(flux_ref, fy_ref, fyr_ref, kzs)
        for pair in range(0, len(kzs), 2):
            ks = kzs[pair : pair + 2]
            data = [
                jnp.concatenate(
                    [stacked(along_y(lines_ref, t, kz)) for kz in ks], 1
                )
                for t in (0, 1)
            ]
            even = lane_parts(folded(dot(fy_ref[...], data[0])))
            odd = lane_parts(folded(dot(fyr_ref[...], data[1])))
            for n, kz in enumerate(ks):
                flux = first_flux[pair + n]
                fields[0].append(jnp.where(lane < 64, odd[n], second_flux[pair + n]))
                fields[1].append(jnp.where(lane < 64, even[n], flux))
                fields[2].append(jnp.where(lane < 64, flux, even[n]))
        data = [beside(jnp.concatenate(field, 0)) for field in fields]
        modes = [folded_lanes(dot(data[max(n - 1, 0)], view(along_ref, n)[...])) for n in range(4)]
        results = [[], [], [], []]
        for n, kz in enumerate(kzs):
            kzf = kz.astype(f32)
            vx, slope, uy, uz = (mode[n * ROWS : (n + 1) * ROWS] for mode in modes)
            square = square_xy + kzf * kzf
            factor = keep_xy * kept_z(kz) / (1.0 + viscosity * time_step * square)
            share = (slope + ky * uy + kzf * uz) / jnp.where(square > 0, square, 1.0)
            results[0].append(factor * vx)
            results[1].append(factor * share)
            results[2].append(factor * (uy - ky * share))
            results[3].append(factor * (uz - kzf * share))
        got = [
            dot(
                beside(jnp.concatenate(result, 0)),
                along_ref[pl.ds(pl.multiple_of((4 + core * 4 + n) * 256, 256), 256), :],
            )
            for n, result in enumerate(results)
        ]
        got = [folded_lanes(part) for part in (got[0] + got[1], got[2], got[3])]
        for n, kz in enumerate(kzs):
            x, y, z = (part[n * ROWS : (n + 1) * ROWS] for part in got)
            near_ref[kz - first] = jnp.where(lane < 48, x, jnp.where(lane < 96, y, z))
            away = jnp.where(
                (lane >= 64) & (lane < 112), x, jnp.where((lane >= 32) & (lane < 64), z, y)
            )
            far_ref[kz - first] = pltpu.roll(away, 64, 1)
            shift = (kz - first) * 16
            near_ref[extra] += pltpu.roll(jnp.where(lane < 16, z, 0.0), shift, 1)
            rest = jnp.where((lane >= 64) & (lane < 80), z, 0.0)
            far_ref[extra] += pltpu.roll(rest, (shift + 64) % LANES, 1)

    over_planes(spectral_step, first, last)


def inverse_y(near_ref, far_ref, iy_ref, planes):
    count = near_ref.shape[0] - 1
    rest = near_ref[count] + far_ref[count]
    for kz in range(count):
        turned = pltpu.roll(rest, (LANES - kz * 16) % LANES, 1) if kz else rest
        data = jnp.concatenate([near_ref[kz] + far_ref[kz], turned], 1)
        got = lane_parts(folded(dot(iy_ref[...], stacked(padded(data)))))
        for tile in range(2):
            planes[tile, kz * LANES : (kz + 1) * LANES, :] = got[tile]
    if count < CHUNK:
        blank = jnp.zeros(((CHUNK - count) * LANES, LANES), f32)
        for tile in range(2):
            planes[tile, count * LANES :, :] = blank


def inverse_kernel(near_ref, far_ref, back_ref, planes):
    inverse_y(near_ref, far_ref, view(back_ref, 0), planes)


def early_kernel(near_ref, far_ref, planes_a, back_ref, base_part, state_part, planes_b):
    inverse_y(near_ref, far_ref, view(back_ref, 0), planes_b)
    iz_ref, izr_ref = view(back_ref, 4), view(back_ref, 5)

    def along_chunks(tile, yh):
        at = pl.ds(yh, 4 * CHUNK, stride=HALF)
        return padded(jnp.concatenate([ref[tile, at, :] for ref in (planes_a, planes_b)], 0)).T

    many = HALF // PIECES
    for piece in range(PIECES):
        yhs = range(piece * many, (piece + 1) * many)
        data = [along_chunks(0, yh) for yh in yhs]
        rest = [along_chunks(1, yh)[:16] for yh in yhs]
        turned = beside(jnp.concatenate([one[:48] for one in data], 0))
        plain = beside(jnp.concatenate([one[48:] for one in data] + rest, 0))
        turned = folded_lanes(dot(turned, izr_ref[...]))
        plain = folded_lanes(dot(plain, iz_ref[...]))
        for n, yh in enumerate(yhs):
            at = slice(yh * LANES, (yh + 1) * LANES)
            first = turned[48 * n : 48 * n + 48]
            second = plain[80 * n : 80 * n + 80]
            state_part[0, :, at] = first[:32]
            state_part[1, :, at] = second[16:48]
            state_part[2, :, at] = second[48:80]
            base_part[0, :, at] = first[32:48]
            base_part[1, :, at] = second[:16]
            base_part[2, :, at] = plain[80 * many + 16 * n :][:16]


def final_kernel(
    near_ref, far_ref, base_part, state_part, state_hbm, base_hbm, back_ref, last_ref,
    base_out, state_out, planes_c, state_ref, base_ref, state_gap, base_gap, arrived, left,
):
    wide = N * N // PIECES
    cuts = [pl.ds(n * wide, wide) for n in range(PIECES)]

    def copies(pairs, flags):
        return [
            [
                pltpu.make_async_copy(
                    source.at[:, :, cut], target.at[:, :, cut], flags.at[2 * n + k]
                )
                for k, (source, target) in enumerate(pairs)
            ]
            for n, cut in enumerate(cuts)
        ]

    reads = copies(((state_hbm, state_ref), (base_hbm, base_ref)), arrived)
    writes = copies(((state_gap, state_out), (base_gap, base_out)), left)
    for piece in reads:
        for copy in piece:
            copy.start()
    inverse_y(near_ref, far_ref, view(back_ref, 0), planes_c)

    def pair_of_lines(tile, yh):
        rows = []
        for n in range(2):
            value = planes_c[tile, pl.ds(yh + n, 4 * CHUNK, stride=HALF), :]
            high = value.astype(bf16).astype(f32)
            rows += [high, value - high]
        return jnp.concatenate(rows, 0).T

    def table(n):
        rows = last_ref[n * 256 : (n + 1) * 256, :].reshape(2, LANES, 256)
        return jnp.concatenate([rows[0], rows[1]], 1)

    many = HALF // PIECES
    for piece in range(PIECES):
        yhs = range(piece * many, (piece + 1) * many, 2)
        data = [pair_of_lines(0, yh) for yh in yhs]
        rest = [pair_of_lines(1, yh)[:16] for yh in yhs]
        turned = jnp.concatenate([one[:48] for one in data], 0).astype(bf16)
        plain = jnp.concatenate([one[48:] for one in data] + rest, 0).astype(bf16)
        turned = dot(turned, table(1))
        plain = dot(plain, table(0))
        turned = [folded_lanes(turned[:, :256]), folded_lanes(turned[:, 256:])]
        plain = [folded_lanes(plain[:, :256]), folded_lanes(plain[:, 256:])]
        for copy in reads[piece]:
            copy.wait()
        for n, start in enumerate(yhs):
            for k in range(2):
                at = slice((start + k) * LANES, (start + k + 1) * LANES)
                first = turned[k][48 * n : 48 * n + 48]
                second = plain[k][80 * n : 80 * n + 80]
                third = plain[k][40 * many + 16 * n :][:16]
                states = [first[:32], second[16:48], second[48:80]]
                bases = [first[32:48], second[:16], third]
                for i in range(3):
                    part = state_part[i, :, at] - state_ref[i, :, at]
                    state_gap[i, :, at] = states[i] + part
                    part = base_part[i, :, at] - base_ref[i, :, at]
                    base_gap[i, :, at] = bases[i] + part
        for copy in writes[piece]:
            copy.start()
    for piece in writes:
        for copy in piece:
            copy.wait()


interpret = False


def call(kernel, outs, scratch, inputs, room, in_smem=0, in_hbm=(), out_hbm=False):
    whole = pl.BlockSpec(memory_space=pltpu.VMEM)
    small = pl.BlockSpec(memory_space=pltpu.SMEM)
    far = pl.BlockSpec(memory_space=pltpu.HBM)
    return pl.pallas_call(
        kernel,
        out_shape=outs,
        in_specs=[
            small if n < in_smem else far if n in in_hbm else whole for n in range(len(inputs))
        ],
        out_specs=jax.tree.map(lambda _: far if out_hbm else whole, outs),
        scratch_shapes=scratch,
        compiler_params=pltpu.CompilerParams(vmem_limit_bytes=room * 2**20),
        cost_estimate=pl.CostEstimate(flops=1000, bytes_accessed=1000, transcendentals=0),
        interpret=interpret,
    )(*inputs)


def body(base, state, wavenumber, cutoff):
    t = {name: jnp.asarray(value) for name, value in tables().items()}
    core = lax.axis_index("comp")
    seg_count = lax.axis_size("seg")
    own_base = base[0]
    own_state = state[0, 0]
    base_half = lax.dynamic_slice_in_dim(own_base, core * 16, 16, 1)
    back = [((s + 1) % seg_count, s) for s in range(seg_count)]
    around = [(2 * i, 2 * o) for i, o in back] + [(2 * o + 1, 2 * i + 1) for i, o in back]
    state_next = lax.ppermute(own_state, ("seg", "comp"), around)
    sds = jax.ShapeDtypeStruct
    core_at = core.reshape(1)
    swap = [(0, 1), (1, 0)]
    here_own = call(
        base_kernel,
        sds((SENT, ROWS, LANES), f32),
        [
            pltpu.VMEM((HALF * HALF_LINE, LANES), f32),
            pltpu.VMEM(own_base.shape, f32),
            pltpu.VMEM(t["ahead"].shape, bf16),
            pltpu.SemaphoreType.DMA((PIECES + 1,)),
        ],
        [core_at, own_base, t["ahead"]],
        room=56,
        in_smem=1,
        in_hbm=(1, 2),
    )
    there_own = lax.ppermute(here_own, "slab", swap)
    here_other = lax.ppermute(here_own, "comp", swap)
    counts = [planes_of(chunk)[1] - planes_of(chunk)[0] for chunk in range(CHUNKS)]
    flux_lines = sds((3, HALF * 4 * CHUNK, LANES), f32)
    flux = call(
        flux_kernel,
        [sds((2, counts[0], ROWS, LANES), f32)] + [flux_lines] * 2,
        [
            pltpu.VMEM(flux_lines.shape, f32),
            pltpu.VMEM(flux_lines.shape, f32),
            pltpu.VMEM(flux_lines.shape, f32),
            pltpu.VMEM(own_base.shape, f32),
            pltpu.VMEM(own_state.shape, f32),
            pltpu.VMEM(t["ahead"].shape, bf16),
            pltpu.VMEM((2, counts[0], ROWS, LANES), f32),
            pltpu.SemaphoreType.DMA((2 * PIECES + 1,)),
            pltpu.SemaphoreType.DMA((CHUNKS,)),
        ],
        [core_at, own_base, own_state, t["ahead"]],
        room=56,
        in_smem=1,
        in_hbm=(1, 2, 3),
        out_hbm=True,
    )
    there_own, flux = lax.optimization_barrier((there_own, flux))
    there_other = lax.ppermute(there_own, "comp", swap)
    half_planes = sds((3, (HALF_KZ + 1) * LANES, LANES), f32)
    own_planes = call(
        half_kernel,
        half_planes,
        [],
        [core_at, cutoff, here_own, there_own, t["back"]],
        room=12,
        in_smem=2,
    )
    lines = call(
        gradient_kernel,
        [sds((2, HALF * 4 * CHUNK, LANES), f32)] * CHUNKS,
        [pltpu.VMEM(half_planes.shape, f32), pltpu.VMEM((HALF, LANES), f32)],
        [core_at, cutoff, wavenumber, own_base, own_state, own_planes, here_other, there_other]
        + [t["ahead"], t["back"]],
        room=20,
        in_smem=3,
    )
    near, far = [], []
    lines = list(lines)
    for chunk in range(CHUNKS):
        if chunk:
            near[-1], lines[chunk] = lax.optimization_barrier((near[-1], lines[chunk]))
        near_part, far_part = call(
            functools.partial(spectral_kernel, chunk),
            [sds((counts[chunk] + 1, ROWS, LANES), f32)] * 2,
            [],
            [core_at, cutoff, lines[chunk], flux[chunk], t["ahead"], t["along"]],
            room=12,
            in_smem=2,
        )
        if chunk == 0:
            base_half, near_part = lax.optimization_barrier((base_half, near_part))
            base_next = lax.ppermute(base_half, "seg", back)
        near.append(near_part)
        far.append(lax.ppermute(far_part, "slab", swap))
    planes = sds((2, CHUNK * LANES, LANES), f32)
    planes_a = call(inverse_kernel, planes, [], [near[0], far[0], t["back"]], room=8)
    near[1], planes_a = lax.optimization_barrier((near[1], planes_a))
    base_part, state_part = call(
        early_kernel,
        [sds(base_next.shape, f32), sds(state_next.shape, f32)],
        [pltpu.VMEM(planes.shape, f32)],
        [near[1], far[1], planes_a, t["back"]],
        room=14,
    )
    base_gap, state_gap = call(
        final_kernel,
        [sds(base_next.shape, f32), sds(state_next.shape, f32)],
        [
            pltpu.VMEM((2, CHUNK * LANES, LANES), f32),
            pltpu.VMEM(state_next.shape, f32),
            pltpu.VMEM(base_next.shape, f32),
            pltpu.VMEM(state_next.shape, f32),
            pltpu.VMEM(base_next.shape, f32),
            pltpu.SemaphoreType.DMA((2 * PIECES,)),
            pltpu.SemaphoreType.DMA((2 * PIECES,)),
        ],
        [near[2], far[2], base_part, state_part, state_next, base_next, t["back"], t["last"]],
        room=16,
        in_hbm=(4, 5),
        out_hbm=True,
    )
    return base_gap[None], state_gap[None, None]


def solution(mesh):
    paired = mesh.shape["slab"] == 2 and mesh.shape["comp"] == 2
    return jax.shard_map(
        body if paired else general_body,
        mesh=mesh,
        in_specs=(
            P(("groups", "seg"), None, "slab", None),
            P(("groups", "seg"), "comp", None, "slab", None),
            P("groups"),
            P("groups"),
        ),
        out_specs=(
            P(("groups", "seg"), None, ("slab", "comp"), None),
            P(("groups", "seg"), "comp", None, "slab", None),
        ),
        check_vma=False,
    )
```
